32 devices in a mesh: seq: 16 (over z, y, core), row: 2 (over x).
Axes of the slice: x: 2, y: 2, z: 4, core: 2. Of those that a mesh axis runs over, the one named last changes fastest.
Arguments:
- inputs: bfloat16 [2, 2048, 1024], P('row', 'seq'), may hold values from -6 to 6
- lengths: int32 [2, 4], P('row'), may hold values from 1 to 1921, 2048 in all within a row
- gain_ffn1: float32 [1024], replicated, may hold values from 0.1 to 1.9
- gain_attn: float32 [1024], replicated, may hold values from 0.1 to 1.9
- gain_conv: float32 [1024], replicated, may hold values from 0.1 to 1.9
- gain_inner: float32 [1024], replicated, may hold values from 0.1 to 1.9
- gain_ffn2: float32 [1024], replicated, may hold values from 0.1 to 1.9
- gain_out: float32 [1024], replicated, may hold values from 0.1 to 1.9
- conv_kernel: bfloat16 [31, 1024], replicated, may hold values from -1 to 1
- ffn1_in: bfloat16 [1024, 4096], P('seq'), may hold values from -0.1875 to 0.1875
- ffn1_out: bfloat16 [4096, 1024], P('seq'), may hold values from -0.09375 to 0.09375
- attn_qkv: bfloat16 [1024, 3072], P('seq'), may hold values from -0.1875 to 0.1875
- attn_out: bfloat16 [1024, 1024], P('seq'), may hold values from -6 to 6
- conv_in: bfloat16 [1024, 2048], P('seq'), may hold values from -0.1875 to 0.1875
- conv_out: bfloat16 [1024, 1024], P('seq'), may hold values from -0.1875 to 0.1875
- ffn2_in: bfloat16 [1024, 4096], P('seq'), may hold values from -0.1875 to 0.1875
- ffn2_out: bfloat16 [4096, 1024], P('seq'), may hold values from -0.09375 to 0.09375
- cotangent: bfloat16 [2, 2048, 1024], P('row', 'seq'), may hold values from -6 to 6
Outputs:
- output: bfloat16 [2, 2048, 1024], P('row', 'seq')
- input_grad: float32 [2, 2048, 1024], P('row', 'seq')
- grad_gain_ffn1: float32 [1024], replicated
- grad_gain_attn: float32 [1024], replicated
- grad_gain_conv: float32 [1024], replicated
- grad_gain_inner: float32 [1024], replicated
- grad_gain_ffn2: float32 [1024], replicated
- grad_gain_out: float32 [1024], replicated
- grad_conv_kernel: float32 [31, 1024], replicated
- grad_ffn1_in: float32 [1024, 4096], P('seq')
- grad_ffn1_out: float32 [4096, 1024], P('seq')
- grad_attn_qkv: float32 [1024, 3072], P('seq')
- grad_attn_out: float32 [1024, 1024], P('seq')
- grad_conv_in: float32 [1024, 2048], P('seq')
- grad_conv_out: float32 [1024, 1024], P('seq')
- grad_ffn2_in: float32 [1024, 4096], P('seq')
- grad_ffn2_out: float32 [4096, 1024], P('seq')
The draws below stay inside these ranges and needn't reach their ends.
Inputs may be any that keep to these rules, and one draw needn't show every extreme that they name: The 4 lengths of a row are positive and sum to 2048; the longest is exactly 1921.
All inputs are finite; a program needn't handle non-finite values.
Results may differ from the reference program's by a relative error of at most 0.023.
Values may be sent and summed in bfloat16 or wider, within the bound.
A program may use at most 256 MiB of HBM per device.

```python
import math
import jax
import jax.numpy as jnp
import numpy as np
from jax import lax

D = 1024
FF = 4096
HEADS = 16
HEAD_DIM = 64
KERNEL = 31
NSEG = 4
FR_DEV = 128
HALF = 15
FRAMES = 2048
ROWS = 2


def levels(own_key, shape, cuts, low, high):
    level, own = 1.0, jax.random.fold_in(own_key, 6)
    for axis_at, shards_of in cuts:
        heights = jnp.exp(jax.random.uniform(jax.random.fold_in(own, axis_at), (shards_of,), jnp.float32, low / len(cuts), high / len(cuts)))
        level = level * jnp.repeat(heights, shape[axis_at] // shards_of).reshape([-1 if axis == axis_at else 1 for axis in range(len(shape))])
    return level


def length_profile(count, total, limit, lean):
    portions = [(1 << 20) // math.isqrt(rank ** lean) + 1 for rank in range(2, count + 1)]
    spare, given = total - limit - (count - 1), [1] * (count - 1)
    while spare > 0:
        candidates = [i for i in range(count - 1) if given[i] < limit]
        whole, remaining = sum([portions[i] for i in candidates]), spare
        for i in candidates:
            more = min(limit - given[i], max(1, remaining * portions[i] // whole), spare)
            given[i] = given[i] + more
            spare = spare - more
    return np.array([limit] + given)


def uneven(own_key, amount, total, bound, slope):
    if amount == 2:
        one = jax.random.randint(own_key, (), max(1, total - bound), min(bound, total - 1) + 1)
        return jnp.stack([one, total - one])
    tallies = jnp.asarray(length_profile(amount, total, bound, slope), jnp.int32)
    twos = (amount - 1) // 2
    donor, receiver = tallies[1:1 + 2 * twos:2], tallies[2:2 + 2 * twos:2]
    slack = jnp.minimum(donor - 1, bound - receiver)
    moved = jax.random.randint(jax.random.fold_in(own_key, 1), (twos,), 0, 1 << 20) % (slack + 1)
    tallies = tallies.at[1:1 + 2 * twos:2].set(donor - moved).at[2:2 + 2 * twos:2].set(receiver + moved)
    return tallies[jax.random.permutation(jax.random.fold_in(own_key, 2), amount)]


def scatter_about(own_key, shape, scale, bound, cuts=(), kind=jnp.bfloat16):
    array = jax.random.normal(own_key, shape, jnp.float32) * scale
    if len(cuts) > 0:
        array = levels(own_key, shape, cuts, -0.22, 0.18) * array
    return jnp.clip(array, min=-bound, max=bound).astype(kind)


def setup_inputs(seed: int = 0) -> dict:
    splits = jax.random.split(jax.random.key(seed), 19)
    inputs = scatter_about(splits[0], (ROWS, FRAMES, D), 1.0, 6.0, ((0, 2), (1, 16)))
    lengths = jax.vmap(lambda own: uneven(own, NSEG, FRAMES, FRAMES - FR_DEV + 1, 0))(jax.random.split(splits[1], ROWS)).reshape((ROWS, NSEG)).astype(jnp.int32)
    gain_ffn1 = jnp.clip(1.0 + 0.18 * jax.random.normal(splits[2], (D,), jnp.float32), 0.1, 1.9)
    gain_attn = jnp.clip(1.0 + 0.18 * jax.random.normal(splits[3], (D,), jnp.float32), 0.1, 1.9)
    gain_conv = jnp.clip(1.0 + 0.18 * jax.random.normal(splits[4], (D,), jnp.float32), 0.1, 1.9)
    gain_inner = jnp.clip(1.0 + 0.18 * jax.random.normal(splits[5], (D,), jnp.float32), 0.1, 1.9)
    gain_ffn2 = jnp.clip(1.0 + 0.18 * jax.random.normal(splits[6], (D,), jnp.float32), 0.1, 1.9)
    gain_out = jnp.clip(1.0 + 0.18 * jax.random.normal(splits[7], (D,), jnp.float32), 0.1, 1.9)
    conv_kernel = scatter_about(splits[8], (KERNEL, D), KERNEL ** -0.5, 1.0)
    ffn1_in = scatter_about(splits[9], (D, FF), D ** -0.5, 0.1875, ((0, 16),))
    ffn1_out = scatter_about(splits[10], (FF, D), FF ** -0.5, 0.09375, ((0, 16),))
    attn_qkv = scatter_about(splits[11], (D, 3 * D), D ** -0.5, 0.1875, ((0, 16),))
    attn_out = scatter_about(splits[12], (D, D), 1 ** -0.5, 6.0, ((0, 16),))
    conv_in = scatter_about(splits[13], (D, 2 * D), D ** -0.5, 0.1875, ((0, 16),))
    conv_out = scatter_about(splits[14], (D, D), D ** -0.5, 0.1875, ((0, 16),))
    ffn2_in = scatter_about(splits[15], (D, FF), D ** -0.5, 0.1875, ((0, 16),))
    ffn2_out = scatter_about(splits[16], (FF, D), FF ** -0.5, 0.09375, ((0, 16),))
    cotangent = scatter_about(splits[17], (ROWS, FRAMES, D), 1.0, 6.0, ((0, 2), (1, 16)))
    return dict(inputs=inputs, lengths=lengths, gain_ffn1=gain_ffn1, gain_attn=gain_attn, gain_conv=gain_conv, gain_inner=gain_inner, gain_ffn2=gain_ffn2, gain_out=gain_out, conv_kernel=conv_kernel, ffn1_in=ffn1_in, ffn1_out=ffn1_out, attn_qkv=attn_qkv, attn_out=attn_out, conv_in=conv_in, conv_out=conv_out, ffn2_in=ffn2_in, ffn2_out=ffn2_out, cotangent=cotangent)


@jax.custom_vjp
def low(v):
    return lax.optimization_barrier(v.astype(jnp.bfloat16)).astype(jnp.float32)

@jax.custom_vjp
def low_back(v):
    return v

def low_keep(v):
    return (low(v), None)

def low_pass(kept, grad):
    return (grad,)

def back_keep(v):
    return (v, None)

def back_low(kept, grad):
    return (low(grad),)
low.defvjp(low_keep, low_pass)
low_back.defvjp(back_keep, back_low)
HIGH = lax.Precision.HIGHEST
EPSILON = 1e-05
MASKED = -1e+30

def segment_of(positions, seg_lengths):
    boundary = jnp.cumsum(seg_lengths)[:-1]
    return lax.optimization_barrier(jnp.sum((positions[:, None] >= boundary[None, :]).astype(jnp.int32), axis=1))

def rotary_tables(positions):
    half_dim = HEAD_DIM // 2
    inverse = jnp.exp(-jnp.log(10000.0) * jnp.arange(half_dim, dtype=jnp.float32) / half_dim)
    angles = positions.astype(jnp.float32)[:, None] * inverse[None, :]
    return (jnp.cos(angles), jnp.sin(angles))

def rotate(tensor, cos_table, sin_table):
    half_dim = HEAD_DIM // 2
    first_half = tensor[..., :half_dim]
    second_half = tensor[..., half_dim:]
    cos_heads = cos_table[:, None, :]
    sin_heads = sin_table[:, None, :]
    return jnp.concatenate([first_half * cos_heads - second_half * sin_heads, second_half * cos_heads + first_half * sin_heads], axis=-1)

def layer_norm(values, gain):
    center = values - lax.optimization_barrier(jnp.mean(values, axis=-1, keepdims=True))
    spread = lax.optimization_barrier(jnp.mean(center * center, axis=-1, keepdims=True))
    return center * lax.rsqrt(spread + EPSILON) * gain

def linear(source, weight):
    return low_back(jnp.dot(low(source), weight, precision=HIGH))

def sigmoid_linear(values):
    return values * jax.nn.sigmoid(values)

def attend(queries, key_rows, value_rows, segments):
    length = queries.shape[0]
    block_size = math.gcd(length, 512)
    scale = HEAD_DIM ** (-0.5)

    @jax.checkpoint
    def one_block(block_item):
        query_block, query_segments = block_item
        raw_scores = low_back(jnp.einsum('qhd,khd->hqk', query_block, key_rows, precision=HIGH) * scale)
        same_segment = (query_segments[:, None] == segments[None, :])[None]
        weights = low(jax.nn.softmax(jnp.where(same_segment, raw_scores, MASKED), axis=-1))
        return jnp.einsum('hqk,khd->qhd', weights, value_rows, precision=HIGH)
    blocks = lax.map(one_block, (queries.reshape(length // block_size, block_size, HEADS, HEAD_DIM), segments.reshape(length // block_size, block_size)))
    return blocks.reshape(length, HEADS, HEAD_DIM)

def depthwise(glu_values, kernel_taps, segments):
    length = glu_values.shape[0]
    padded = jnp.pad(glu_values, ((HALF, HALF), (0, 0)))
    padded_segments = jnp.pad(segments, (HALF, HALF), constant_values=-1)
    summed = jnp.zeros_like(glu_values)
    for offset in range(KERNEL):
        same_segment = (padded_segments[offset:offset + length] == segments).astype(glu_values.dtype)
        summed = summed + kernel_taps[offset] * padded[offset:offset + length] * same_segment[:, None]
    return summed

def forward(stream, segments, cos_table, sin_table, parameters):
    gain_one, gain_two, gain_three, gain_four, gain_five, gain_six, kernel_taps, ffn_one_in, ffn_one_out, qkv_weight, attn_weight, conv_weight_in, conv_weight_out, ffn_two_in, ffn_two_out = parameters
    length = stream.shape[0]
    hidden_one = linear(layer_norm(stream, gain_one), ffn_one_in)
    stream_one = stream + 0.5 * linear(sigmoid_linear(hidden_one), ffn_one_out)
    projected = linear(layer_norm(stream_one, gain_two), qkv_weight)
    shaped = projected.reshape(length, 3, HEADS, HEAD_DIM)
    query_rot = low(rotate(shaped[:, 0], cos_table, sin_table))
    key_rot = low(rotate(shaped[:, 1], cos_table, sin_table))
    value_low = low(shaped[:, 2])
    mixed = low_back(attend(query_rot, key_rot, value_low, segments)).reshape(length, D)
    stream_two = stream_one + linear(mixed, attn_weight)
    gate_up = linear(layer_norm(stream_two, gain_three), conv_weight_in)
    glu_values = low(gate_up[:, :D] * jax.nn.sigmoid(gate_up[:, D:]))
    conv_values = low_back(depthwise(glu_values, kernel_taps, segments))
    stream_three = stream_two + linear(sigmoid_linear(layer_norm(conv_values, gain_four)), conv_weight_out)
    hidden_two = linear(layer_norm(stream_three, gain_five), ffn_two_in)
    stream_four = stream_three + 0.5 * linear(sigmoid_linear(hidden_two), ffn_two_out)
    return layer_norm(stream_four, gain_six)

def reference(inputs, lengths, gain_ffn1, gain_attn, gain_conv, gain_inner, gain_ffn2, gain_out, conv_kernel, ffn1_in, ffn1_out, attn_qkv, attn_out, conv_in, conv_out, ffn2_in, ffn2_out, cotangent):
    parameters = tuple((item.astype(jnp.float32) for item in (gain_ffn1, gain_attn, gain_conv, gain_inner, gain_ffn2, gain_out, conv_kernel, ffn1_in, ffn1_out, attn_qkv, attn_out, conv_in, conv_out, ffn2_in, ffn2_out)))
    positions = jnp.arange(FRAMES, dtype=jnp.int32)
    cos_table, sin_table = rotary_tables(positions)

    def one_row(running, row_item):
        stream, seg_lengths, row_cotangent = row_item
        segments = segment_of(positions, seg_lengths)

        def row_forward(values, params_in):
            return forward(values, segments, cos_table, sin_table, params_in)
        result, pullback = jax.vjp(row_forward, stream, parameters)
        stream_grad, param_grads = pullback(row_cotangent)
        running = jax.tree.map(jnp.add, running, param_grads)
        return (running, (result.astype(jnp.bfloat16), stream_grad))
    initial = jax.tree.map(jnp.zeros_like, parameters)
    grads, (output, input_grad) = lax.scan(one_row, initial, (inputs.astype(jnp.float32), lengths, cotangent.astype(jnp.float32)))
    return (output, input_grad, grads[0], grads[1], grads[2], grads[3], grads[4], grads[5], grads[6], grads[7], grads[8], grads[9], grads[10], grads[11], grads[12], grads[13], grads[14])
```

```python
import math

import jax
import jax.numpy as jnp
from jax import lax
from jax.experimental import pallas as pl
from jax.experimental.pallas import tpu as pltpu
from jax.sharding import PartitionSpec as P

HEADS = 16
HEAD_DIM = 64
KERNEL = 31
HALF = 15


EPSILON = 1e-05
MASKED = -1e30


def with_halo(block, sides, width):
    for axis, dim in sides:
        count = lax.axis_size(axis)
        forward = [(i, i + 1) for i in range(count - 1)]
        backward = [(target, source) for source, target in forward]
        low = lax.ppermute(
            lax.slice_in_dim(block, block.shape[dim] - width, None, axis=dim), axis, forward
        )
        high = lax.ppermute(lax.slice_in_dim(block, 0, width, axis=dim), axis, backward)
        block = jnp.concatenate([low, block, high], axis=dim)
    return block


def shifted(array, axis, by):
    size = lax.axis_size(axis)
    return lax.ppermute(array, axis, [(i, (i + by) % size) for i in range(size)])


def segment_of(positions, seg_lengths):
    boundary = jnp.cumsum(seg_lengths)[:-1]
    return jnp.sum((positions[:, None] >= boundary[None, :]).astype(jnp.int32), axis=1)


def rotary_tables(positions):
    half_dim = HEAD_DIM // 2
    inverse = jnp.exp(-jnp.log(10000.0) * jnp.arange(half_dim, dtype=jnp.float32) / half_dim)
    angles = positions.astype(jnp.float32)[:, None] * inverse[None, :]
    return (jnp.cos(angles), jnp.sin(angles))


def split_heads(values):
    return values.reshape(values.shape[0], HEADS, HEAD_DIM)


def rotate(values, cos_table, sin_table):
    half_dim = HEAD_DIM // 2
    shaped = split_heads(values)
    first_half = shaped[..., :half_dim]
    second_half = shaped[..., half_dim:]
    cos_heads = cos_table[:, None, :]
    sin_heads = sin_table[:, None, :]
    turned = jnp.concatenate(
        [
            first_half * cos_heads - second_half * sin_heads,
            second_half * cos_heads + first_half * sin_heads,
        ],
        axis=-1,
    )
    return turned.reshape(values.shape)


def unrotate(grads, cos_table, sin_table):
    half_dim = HEAD_DIM // 2
    shaped = split_heads(grads)
    first_half = shaped[..., :half_dim]
    second_half = shaped[..., half_dim:]
    cos_heads = cos_table[:, None, :]
    sin_heads = sin_table[:, None, :]
    turned = jnp.concatenate(
        [
            first_half * cos_heads + second_half * sin_heads,
            second_half * cos_heads - first_half * sin_heads,
        ],
        axis=-1,
    )
    return turned.reshape(grads.shape)


def norm_forward(values, gain):
    center = values - jnp.mean(values, axis=-1, keepdims=True)
    spread = jnp.mean(center * center, axis=-1, keepdims=True)
    inverse = lax.rsqrt(spread + EPSILON)
    unit_part = center * inverse
    return (unit_part * gain, (unit_part, inverse))


def norm_backward(grads, gain, saved):
    unit_part, inverse = saved
    scaled = grads * gain
    gain_grad = jnp.sum(grads * unit_part, axis=0)
    input_part = inverse * (
        scaled
        - jnp.mean(scaled, axis=-1, keepdims=True)
        - unit_part * jnp.mean(scaled * unit_part, axis=-1, keepdims=True)
    )
    return (input_part, gain_grad)


def sigmoid_linear(values):
    return values * jax.nn.sigmoid(values)


def sigmoid_linear_grad(values):
    sigma = jax.nn.sigmoid(values)
    return sigma * (1.0 + values * (1.0 - sigma))


def project(left_side, weight):
    return (
        jnp.dot(
            left_side,
            lax.all_gather(weight, "seq", axis=0, tiled=True),
            preferred_element_type=jnp.float32,
        ),
        weight,
    )


def project_back(grad_side, weight):
    return lax.dot_general(
        grad_side,
        lax.all_gather(weight, "seq", axis=0, tiled=True),
        (((1,), (1,)), ((), ())),
        preferred_element_type=jnp.float32,
    )


def weight_grad(left_side, grad_side):
    return lax.psum_scatter(
        lax.dot_general(
            left_side, grad_side, (((0,), (0,)), ((), ())), preferred_element_type=jnp.float32
        ).astype(jnp.bfloat16),
        "seq",
        scatter_dimension=0,
        tiled=True,
    ).astype(jnp.float32)


def over_blocks(advance, running, pieces):
    total_rows = pieces[0].shape[0]
    block_size = math.gcd(total_rows, 512)
    number = total_rows // block_size
    stacked = tuple((piece.reshape((number, block_size) + piece.shape[1:]) for piece in pieces))

    def scan_step(current, block_item):
        block_index, blocks = block_item
        return (advance(current, blocks, block_index * block_size), None)

    running, unused = lax.scan(scan_step, running, (jnp.arange(number, dtype=jnp.int32), stacked))
    return running


def block_scores(query_heads, key_heads, query_segments, key_segments):
    scale = HEAD_DIM ** (-0.5)
    raw_scores = (
        jnp.einsum("qhd,khd->hqk", query_heads, key_heads, preferred_element_type=jnp.float32)
        * scale
    )
    return jnp.where((query_segments[:, None] == key_segments[None, :])[None], raw_scores, MASKED)


def pair_grads(
    query_rows, grad_rows, log_total, delta, query_segments, key_rows, value_rows, key_segments
):
    scale = HEAD_DIM ** (-0.5)
    query_heads = split_heads(query_rows)
    grad_heads = split_heads(grad_rows)
    key_heads = split_heads(key_rows)
    value_heads = split_heads(value_rows)
    probs = jnp.exp(
        block_scores(query_heads, key_heads, query_segments, key_segments) - log_total[:, :, None]
    )
    prob_grads = jnp.einsum(
        "qhd,khd->hqk", grad_heads, value_heads, preferred_element_type=jnp.float32
    )
    score_grads = (probs * (prob_grads - delta[:, :, None])).astype(jnp.bfloat16)
    query_grad = (
        jnp.einsum("hqk,khd->qhd", score_grads, key_heads, preferred_element_type=jnp.float32)
        * scale
    )
    key_grad = (
        jnp.einsum("hqk,qhd->khd", score_grads, query_heads, preferred_element_type=jnp.float32)
        * scale
    )
    value_grad = jnp.einsum(
        "hqk,qhd->khd", probs.astype(jnp.bfloat16), grad_heads, preferred_element_type=jnp.float32
    )
    return (
        query_grad.reshape(query_rows.shape),
        key_grad.reshape(key_rows.shape),
        value_grad.reshape(value_rows.shape),
    )


def local(
    inputs,
    lengths,
    gain_ffn1,
    gain_attn,
    gain_conv,
    gain_inner,
    gain_ffn2,
    gain_out,
    conv_kernel,
    ffn1_in,
    ffn1_out,
    attn_qkv,
    attn_out,
    conv_in,
    conv_out,
    ffn2_in,
    ffn2_out,
    cotangent,
):
    frame_count = inputs.shape[1]
    model_width = inputs.shape[2]
    device_count = lax.axis_size("seq")
    position_index = lax.axis_index("seq")
    seg_lengths = lengths[0]
    first_frame = position_index * frame_count
    local_frames = jnp.arange(frame_count, dtype=jnp.int32)
    positions = first_frame + local_frames
    query_segments = segment_of(positions, seg_lengths)
    cos_table, sin_table = rotary_tables(positions)
    stream = inputs[0].astype(jnp.float32)
    normed_one, saved_one = norm_forward(stream, gain_ffn1)
    normed_one_low = normed_one.astype(jnp.bfloat16)
    hidden_one, kept_ffn1_in = project(normed_one_low, ffn1_in)
    active_one = sigmoid_linear(hidden_one).astype(jnp.bfloat16)
    branch_one, kept_ffn1_out = project(active_one, ffn1_out)
    stream_one = stream + 0.5 * branch_one
    normed_two, saved_two = norm_forward(stream_one, gain_attn)
    normed_two_low = normed_two.astype(jnp.bfloat16)
    projected, kept_qkv = project(normed_two_low, attn_qkv)
    query_low = rotate(projected[:, :model_width], cos_table, sin_table).astype(jnp.bfloat16)
    key_low = rotate(projected[:, model_width : 2 * model_width], cos_table, sin_table).astype(
        jnp.bfloat16
    )
    value_low = projected[:, 2 * model_width :].astype(jnp.bfloat16)
    query_heads = split_heads(query_low)

    def stats_step(current, blocks, first_row):
        top_score, denominator = current
        key_block = blocks[0]
        key_segments = segment_of(
            first_row + jnp.arange(key_block.shape[0], dtype=jnp.int32), seg_lengths
        )
        masked = block_scores(query_heads, split_heads(key_block), query_segments, key_segments)
        new_top = jnp.maximum(top_score, jnp.max(masked, axis=-1))
        denominator = denominator * jnp.exp(top_score - new_top) + jnp.sum(
            jnp.exp(masked - new_top[:, :, None]), axis=-1
        )
        return (new_top, denominator)

    top_init = jnp.full((HEADS, frame_count), MASKED, jnp.float32)
    total_init = jnp.zeros((HEADS, frame_count), jnp.float32)
    top_score, denominator = over_blocks(
        stats_step, (top_init, total_init), (lax.all_gather(key_low, "seq", axis=0, tiled=True),)
    )
    log_total = top_score + jnp.log(denominator)

    def value_step(current, blocks, first_row):
        mixed_sum, rest_sum = current
        key_block, value_block = blocks
        key_segments = segment_of(
            first_row + jnp.arange(key_block.shape[0], dtype=jnp.int32), seg_lengths
        )
        probs = jnp.exp(
            block_scores(query_heads, split_heads(key_block), query_segments, key_segments)
            - log_total[:, :, None]
        )
        probs_high = probs.astype(jnp.bfloat16)
        probs_rest = (probs - probs_high.astype(jnp.float32)).astype(jnp.bfloat16)
        value_heads = split_heads(value_block)
        mixed_sum = mixed_sum + jnp.einsum(
            "hqk,khd->qhd", probs_high, value_heads, preferred_element_type=jnp.float32
        )
        rest_sum = rest_sum + jnp.einsum(
            "hqk,khd->qhd", probs_rest, value_heads, preferred_element_type=jnp.float32
        )
        return (mixed_sum, rest_sum)

    zero_heads = jnp.zeros((frame_count, HEADS, HEAD_DIM), jnp.float32)
    mixed_sum, rest_sum = over_blocks(
        value_step,
        (zero_heads, zero_heads),
        (
            lax.all_gather(key_low, "seq", axis=0, tiled=True),
            lax.all_gather(value_low, "seq", axis=0, tiled=True),
        ),
    )
    exact_sum = mixed_sum + rest_sum
    mixed_low = mixed_sum.reshape(frame_count, model_width).astype(jnp.bfloat16)
    branch_two, kept_attn_out = project(mixed_low, attn_out)
    stream_two = stream_one + branch_two
    normed_three, saved_three = norm_forward(stream_two, gain_conv)
    normed_three_low = normed_three.astype(jnp.bfloat16)
    gate_up, kept_conv_in = project(normed_three_low, conv_in)
    first_part = gate_up[:, :model_width]
    gate_sigma = jax.nn.sigmoid(gate_up[:, model_width:])
    glu_low = (first_part * gate_sigma).astype(jnp.bfloat16)
    padded = with_halo(glu_low, (("seq", 0),), HALF).astype(jnp.float32)
    padded_segments = segment_of(
        first_frame - HALF + jnp.arange(frame_count + 2 * HALF, dtype=jnp.int32), seg_lengths
    )
    kernel_taps = conv_kernel.astype(jnp.float32)
    conv_values = jnp.zeros((frame_count, model_width), jnp.float32)
    for offset in range(KERNEL):
        same_segment = (padded_segments[offset : offset + frame_count] == query_segments).astype(
            jnp.float32
        )
        conv_values = (
            conv_values
            + kernel_taps[offset] * padded[offset : offset + frame_count] * same_segment[:, None]
        )
    normed_four, saved_four = norm_forward(conv_values, gain_inner)
    active_four = sigmoid_linear(normed_four).astype(jnp.bfloat16)
    branch_three, kept_conv_out = project(active_four, conv_out)
    stream_three = stream_two + branch_three
    normed_five, saved_five = norm_forward(stream_three, gain_ffn2)
    normed_five_low = normed_five.astype(jnp.bfloat16)
    hidden_two, kept_ffn2_in = project(normed_five_low, ffn2_in)
    active_two = sigmoid_linear(hidden_two).astype(jnp.bfloat16)
    branch_four, kept_ffn2_out = project(active_two, ffn2_out)
    stream_four = stream_three + 0.5 * branch_four
    final_norm, saved_six = norm_forward(stream_four, gain_out)
    output = final_norm.astype(jnp.bfloat16)[None]
    grad_four, grad_gain_six = norm_backward(cotangent[0].astype(jnp.float32), gain_out, saved_six)
    out_two_low = (0.5 * grad_four).astype(jnp.bfloat16)
    grad_ffn_two_out = weight_grad(active_two, out_two_low)
    hidden_two_low = (project_back(out_two_low, ffn2_out) * sigmoid_linear_grad(hidden_two)).astype(
        jnp.bfloat16
    )
    grad_ffn_two_in = weight_grad(normed_five_low, hidden_two_low)
    input_part, grad_gain_five = norm_backward(
        project_back(hidden_two_low, ffn2_in), gain_ffn2, saved_five
    )
    grad_three = grad_four + input_part
    conv_out_low = grad_three.astype(jnp.bfloat16)
    grad_conv_weight_out = weight_grad(active_four, conv_out_low)
    active_grad = project_back(conv_out_low, conv_out) * sigmoid_linear_grad(normed_four)
    conv_grad, grad_gain_four = norm_backward(active_grad, gain_inner, saved_four)
    conv_grad_low = conv_grad.astype(jnp.bfloat16)
    conv_grad_value = conv_grad_low.astype(jnp.float32)
    rim_grad = with_halo(conv_grad_low, (("seq", 0),), HALF).astype(jnp.float32)
    tap_grads = []
    glu_grad = jnp.zeros((frame_count, model_width), jnp.float32)
    for offset in range(KERNEL):
        same_segment = (padded_segments[offset : offset + frame_count] == query_segments).astype(
            jnp.float32
        )
        tap_grads.append(
            jnp.sum(
                padded[offset : offset + frame_count] * same_segment[:, None] * conv_grad_value,
                axis=0,
            )
        )
        back_start = 2 * HALF - offset
        back_segment = (
            padded_segments[back_start : back_start + frame_count] == query_segments
        ).astype(jnp.float32)
        glu_grad = (
            glu_grad
            + kernel_taps[offset]
            * rim_grad[back_start : back_start + frame_count]
            * back_segment[:, None]
        )
    kernel_grad = jnp.stack(tap_grads, axis=0)
    gate_up_low = jnp.concatenate(
        [glu_grad * gate_sigma, glu_grad * first_part * gate_sigma * (1.0 - gate_sigma)], axis=1
    ).astype(jnp.bfloat16)
    grad_conv_weight_in = weight_grad(normed_three_low, gate_up_low)
    input_part, grad_gain_three = norm_backward(
        project_back(gate_up_low, conv_in), gain_conv, saved_three
    )
    grad_two = grad_three + input_part
    attn_grad_low = grad_two.astype(jnp.bfloat16)
    grad_attn_weight = weight_grad(mixed_low, attn_grad_low)
    mixed_grad_low = project_back(attn_grad_low, attn_out).astype(jnp.bfloat16)
    delta = jnp.transpose(
        jnp.sum(split_heads(mixed_grad_low).astype(jnp.float32) * exact_sum, axis=-1)
    )

    def key_turn(turn_index, current):
        key_rows, value_rows, key_acc, value_acc, query_acc = current
        owner = (position_index - turn_index) % device_count
        key_segments = segment_of(owner * frame_count + local_frames, seg_lengths)
        query_part, key_part, value_part = pair_grads(
            query_low,
            mixed_grad_low,
            log_total,
            delta,
            query_segments,
            key_rows,
            value_rows,
            key_segments,
        )
        key_rows, value_rows = shifted((key_rows, value_rows), "seq", 1)
        key_acc, value_acc = (
            shifted((key_acc + key_part).astype(jnp.bfloat16), "seq", 1).astype(jnp.float32),
            shifted((value_acc + value_part).astype(jnp.bfloat16), "seq", 1).astype(jnp.float32),
        )
        return (key_rows, value_rows, key_acc, value_acc, query_acc + query_part)

    zero_rows = jnp.zeros((frame_count, model_width), jnp.float32)
    unused_keys, unused_values, key_grad, value_grad, query_grad = lax.fori_loop(
        0, device_count, key_turn, (key_low, value_low, zero_rows, zero_rows, zero_rows)
    )
    projected_grad_low = jnp.concatenate(
        [
            unrotate(query_grad, cos_table, sin_table),
            unrotate(key_grad, cos_table, sin_table),
            value_grad,
        ],
        axis=1,
    ).astype(jnp.bfloat16)
    grad_qkv_weight = weight_grad(normed_two_low, projected_grad_low)
    input_part, grad_gain_two = norm_backward(
        project_back(projected_grad_low, attn_qkv), gain_attn, saved_two
    )
    grad_one = grad_two + input_part
    out_one_low = (0.5 * grad_one).astype(jnp.bfloat16)
    grad_ffn_one_out = weight_grad(active_one, out_one_low)
    hidden_one_low = (project_back(out_one_low, ffn1_out) * sigmoid_linear_grad(hidden_one)).astype(
        jnp.bfloat16
    )
    grad_ffn_one_in = weight_grad(normed_one_low, hidden_one_low)
    input_part, grad_gain_one = norm_backward(
        project_back(hidden_one_low, ffn1_in), gain_ffn1, saved_one
    )
    input_grad = (grad_one + input_part)[None]
    small_grads = lax.psum(
        (
            grad_gain_one,
            grad_gain_two,
            grad_gain_three,
            grad_gain_four,
            grad_gain_five,
            grad_gain_six,
            kernel_grad,
        ),
        ("seq", "row"),
    )
    large_grads = (
        grad_ffn_one_in,
        grad_ffn_one_out,
        grad_qkv_weight,
        grad_attn_weight,
        grad_conv_weight_in,
        grad_conv_weight_out,
        grad_ffn_two_in,
        grad_ffn_two_out,
    )
    large_grads = (
        lax.psum(grad_ffn_one_in.astype(jnp.bfloat16), "row").astype(jnp.float32),
        lax.psum(grad_ffn_one_out.astype(jnp.bfloat16), "row").astype(jnp.float32),
        lax.psum(grad_qkv_weight.astype(jnp.bfloat16), "row").astype(jnp.float32),
        lax.psum(grad_attn_weight.astype(jnp.bfloat16), "row").astype(jnp.float32),
        lax.psum(grad_conv_weight_in.astype(jnp.bfloat16), "row").astype(jnp.float32),
        lax.psum(grad_conv_weight_out.astype(jnp.bfloat16), "row").astype(jnp.float32),
        lax.psum(grad_ffn_two_in.astype(jnp.bfloat16), "row").astype(jnp.float32),
        lax.psum(grad_ffn_two_out.astype(jnp.bfloat16), "row").astype(jnp.float32),
    )
    return (
        output,
        input_grad,
        small_grads[0],
        small_grads[1],
        small_grads[2],
        small_grads[3],
        small_grads[4],
        small_grads[5],
        small_grads[6],
        large_grads[0],
        large_grads[1],
        large_grads[2],
        large_grads[3],
        large_grads[4],
        large_grads[5],
        large_grads[6],
        large_grads[7],
    )


BF16 = jnp.bfloat16
F32 = jnp.float32
PLANES = 4
VMEM = pltpu.VMEM
DMA = pltpu.SemaphoreType.DMA
VMEM_LIMIT = 60 * 1024 * 1024


class Place:
    def __init__(self):
        seq = lax.axis_index("seq")
        self.x = lax.axis_index("row")
        self.z = seq // 4
        self.yc = lax.rem(seq, 4)

    def flip(self, k):
        y, c, x = self.yc // 2, lax.rem(self.yc, 2), self.x
        c = 1 - c if k & 1 else c
        y = 1 - y if k & 2 else y
        x = 1 - x if k & 4 else x
        return x, y * 2 + c

    def dev(self, k):
        x, yc = self.flip(k)
        return {"seq": self.z * 4 + yc, "row": x}

    def slot(self, k):
        x, yc = self.flip(k)
        return x * 4 + yc

    def plane(self, k):
        return lax.rem(self.z + k, PLANES)

    def zdev(self, k):
        return {"seq": self.plane(k) * 4 + self.yc, "row": self.x}

    def enter(self):
        barrier = pltpu.get_barrier_semaphore()
        partners = [self.dev(k) for k in range(1, 8)] + [self.zdev(k) for k in range(1, PLANES)]
        for partner in partners:
            pl.semaphore_signal(barrier, inc=1, device_id=partner)
        pl.semaphore_wait(barrier, len(partners))


def remote(src, dst, send_sem, recv_sem, dev):
    return pltpu.make_async_remote_copy(src, dst, send_sem, recv_sem, device_id=dev)


def dot(left, right, left_dim=1, right_dim=0):
    return lax.dot_general(
        left, right, (((left_dim,), (right_dim,)), ((), ())), preferred_element_type=F32
    )


def all_gather(place, blocks, sems, process, order):
    send, recv = sems
    half = blocks.shape[1] // 2
    own = place.slot(0)
    sent = []

    def push(rows, to, sem):
        copy = remote(rows, rows, send.at[sem], recv.at[sem], place.dev(to))
        copy.start()
        sent.append(copy)

    def arrived(rows, sem):
        remote(rows, rows, send.at[sem], recv.at[sem], place.dev(1)).wait_recv()

    for k in (4, 2, 1):
        push(blocks.at[own], k, k)

    def fetch(k):
        slot = place.slot(k)
        rows = blocks.at[slot]
        if k == 6:
            arrived(blocks.at[slot, pl.ds(0, half)], 6)
            arrived(blocks.at[slot, pl.ds(half, half)], 8)
            push(rows, 1, 7)
        elif k:
            arrived(rows, k)
        if k == 2:
            push(blocks.at[slot, pl.ds(0, half)], 4, 6)
            push(rows, 1, 3)
        if k == 4:
            push(blocks.at[slot, pl.ds(half, half)], 2, 8)
            push(rows, 1, 5)
        return slot

    for step in order:
        if isinstance(step, tuple):
            for k, slot in [(k, fetch(k)) for k in step]:
                process(k, slot)
        else:
            step()
    return sent


class Scatter:
    def __init__(self, place, refs):
        self.place = place
        self.part, self.staged, self.sibling, self.reduced, self.received, self.send, self.recv = refs
        self.sent = []

    @staticmethod
    def scratch(rows, width):
        return [
            VMEM((4, rows, width), F32),
            VMEM((4, rows, width), BF16),
            VMEM((4, rows, width), BF16),
            VMEM((3, rows, width), BF16),
            VMEM((3, rows, width), BF16),
            DMA((8,)),
            DMA((8,)),
        ]

    def push(self, src, dst, sem, k):
        copy = remote(src, dst, self.send.at[sem], self.recv.at[sem], self.place.dev(k))
        copy.start()
        self.sent.append(copy)

    def emit(self, k, value):
        index = k // 2
        if k % 2:
            self.staged[index] = value.astype(BF16)
            self.push(self.staged.at[index], self.sibling.at[index], index, 1)
        else:
            self.part[index] = value

    def finish(self, k):
        index = k // 2
        into = self.sibling.at[index]
        remote(into, into, self.send.at[index], self.recv.at[index], self.place.dev(1)).wait_recv()
        total = self.part[index] + self.sibling[index].astype(F32)
        if k:
            self.reduced[index - 1] = total.astype(BF16)
            self.push(self.reduced.at[index - 1], self.received.at[index - 1], 3 + index, k)
        else:
            self.part[0] = total

    def total(self):
        value = self.part[0]
        for index in range(3):
            into = self.received.at[index]
            remote(
                into, into, self.send.at[4 + index], self.recv.at[4 + index], self.place.dev(1)
            ).wait_recv()
            value = value + self.received[index].astype(F32)
        return value

    def drain(self):
        for copy in self.sent:
            copy.wait_send()


class Refs:
    pass


def kernel_call(body, collective, ins, outs, scratch):
    in_names = list(ins)
    out_names = list(outs)
    scratch_names = list(scratch)
    flat_scratch = []
    counts = []
    for name in scratch_names:
        item = scratch[name]
        counts.append(len(item) if isinstance(item, list) else 0)
        flat_scratch += item if isinstance(item, list) else [item]

    def kernel(*refs):
        held = Refs()
        at = 0
        for name in in_names + out_names:
            setattr(held, name, refs[at])
            at += 1
        for name, count in zip(scratch_names, counts):
            setattr(held, name, refs[at : at + count] if count else refs[at])
            at += max(count, 1)
        body(held)

    results = pl.pallas_call(
        kernel,
        out_shape=[jax.ShapeDtypeStruct(shape, dtype) for shape, dtype, unused in outs.values()],
        in_specs=[pl.BlockSpec(memory_space=space) for unused, space in ins.values()],
        out_specs=[pl.BlockSpec(memory_space=space) for unused, unused_type, space in outs.values()],
        scratch_shapes=flat_scratch,
        compiler_params=pltpu.CompilerParams(
            collective_id=collective, has_side_effects=True, vmem_limit_bytes=VMEM_LIMIT
        ),
    )(*[array for array, unused in ins.values()])
    return dict(zip(out_names, results))


def gather_rows(place, src, dst, sems):
    send, recv, local_sem = sems
    own = pltpu.make_async_copy(src.at[place.yc], dst.at[place.z * 4 + place.yc], local_sem)
    own.start()
    copies = []
    for k in (2, 3, 1):
        unused, to = place.flip(k)
        copy = remote(
            src.at[to], dst.at[place.z * 4 + place.yc], send.at[k], recv.at[k], place.dev(k)
        )
        copy.start()
        copies.append((k, to, copy))

    def along_z():
        own.wait()
        for k, to, copy in copies:
            into = dst.at[place.z * 4 + to]
            remote(into, into, send.at[k], recv.at[k], place.dev(k)).wait_recv()
        sent = [copy for unused, unused_to, copy in copies]
        rows = dst.at[pl.ds(place.z * 4, 4)]
        for k in (1, 2, 3):
            copy = remote(rows, rows, send.at[3 + k], recv.at[3 + k], place.zdev(k))
            copy.start()
            sent.append(copy)

        def finish():
            for k in (1, 2, 3):
                into = dst.at[pl.ds(place.plane(4 - k) * 4, 4)]
                remote(into, into, send.at[3 + k], recv.at[3 + k], place.zdev(k)).wait_recv()
            for copy in sent:
                copy.wait_send()

        return finish

    return along_z


def gather_blocks(place, src, dst, sems):
    send, recv, local_sem = sems
    own = pltpu.make_async_copy(src, dst.at[place.z], local_sem)
    own.start()
    sent = []
    for k in (1, 2, 3):
        copy = remote(src, dst.at[place.z], send.at[k], recv.at[k], place.zdev(k))
        copy.start()
        sent.append(copy)

    def finish():
        own.wait()
        for k in (1, 2, 3):
            into = dst.at[place.plane(4 - k)]
            remote(into, into, send.at[k], recv.at[k], place.zdev(k)).wait_recv()
        for copy in sent:
            copy.wait_send()

    return finish


GATHER_SEMS = [DMA((8,)), DMA((8,)), DMA]


class PlaneSum:
    def __init__(self, place, refs):
        self.place = place
        self.staged, self.received, self.send, self.recv = refs
        self.sent = []

    @staticmethod
    def scratch(rows, width):
        return [VMEM((3, rows, width), BF16), VMEM((3, rows, width), BF16), DMA((4,)), DMA((4,))]

    def put(self, k, value):
        self.staged[k - 1] = value.astype(BF16)
        copy = remote(
            self.staged.at[k - 1],
            self.received.at[k - 1],
            self.send.at[k],
            self.recv.at[k],
            self.place.zdev(k),
        )
        copy.start()
        self.sent.append(copy)

    def total(self, value):
        for k in (1, 2, 3):
            into = self.received.at[k - 1]
            remote(into, into, self.send.at[k], self.recv.at[k], self.place.zdev(k)).wait_recv()
            value = value + self.received[k - 1].astype(F32)
        for copy in self.sent:
            copy.wait_send()
        return value


class Exchange:
    def __init__(self, place, refs, partners):
        self.place = place
        self.blocks, self.send, self.recv = refs
        self.partners = partners
        self.sent = []

    def start(self, source):
        own = self.place.slot(0)
        for k in self.partners:
            copy = remote(
                source(k), self.blocks.at[own], self.send.at[k], self.recv.at[k], self.place.dev(k)
            )
            copy.start()
            self.sent.append(copy)

    def wait(self):
        for k in self.partners:
            into = self.blocks.at[self.place.slot(k)]
            remote(into, into, self.send.at[k], self.recv.at[k], self.place.dev(k)).wait_recv()
        for copy in self.sent:
            copy.wait_send()


BLOCK_ORDER = ((0,), (1,), (2, 4), (3,), (5,))


def forward_blocks(place, blocks, sems, process, scatter):
    order = BLOCK_ORDER + (
        lambda: scatter.finish(2),
        lambda: scatter.finish(4),
        (6,),
        (7,),
        lambda: scatter.finish(6),
        lambda: scatter.finish(0),
    )
    return all_gather(place, blocks, sems, process, order)


def flat(ref):
    value = ref[...]
    return value.reshape(value.shape[0] * value.shape[1], value.shape[2])


def ffn_forward(place, refs, blocks, hidden, w_in, w_out, sems, scatter):
    def process(k, slot):
        value = dot(blocks[slot], flat(w_in))
        hidden[slot] = value
        active = sigmoid_linear(value).astype(BF16)
        scatter.emit(k, dot(active, flat(w_out)))

    sent = forward_blocks(place, blocks, sems, process, scatter)
    value = scatter.total()
    for copy in sent:
        copy.wait_send()
    scatter.drain()
    return value


def ffn_backward(place, blocks, grads, hidden, hidden_grads, active, w_in, w_out, sems, scatter):
    def process(k, slot):
        value = hidden[slot]
        sigma = jax.nn.sigmoid(value)
        active[slot] = (value * sigma).astype(BF16)
        back = dot(grads[slot], flat(w_out), 1, 1)
        low = (back * (sigma * (1.0 + value * (1.0 - sigma)))).astype(BF16)
        hidden_grads[slot] = low
        scatter.emit(k, dot(low, flat(w_in), 1, 1))

    return forward_blocks(place, grads, sems, process, scatter)


def token_dot(left, columns, right):
    count, rows, unused = left.shape
    taken = left[:, :, columns].reshape(count * rows, -1)
    return dot(taken, flat(right), 0, 0)


def ffn_weight_grads(place, refs, blocks, grads, hidden_grads, active):
    sum_out = PlaneSum(place, refs.sum_out)
    sum_in = PlaneSum(place, refs.sum_in)

    def out_term(plane):
        return token_dot(active, pl.ds(pl.multiple_of(plane * 128, 128), 128), grads)

    def in_term(plane):
        return token_dot(blocks, pl.ds(pl.multiple_of(plane * 256, 256), 256), hidden_grads)

    for k in (1, 2, 3):
        sum_out.put(k, out_term(place.plane(k)))
    for k in (1, 2, 3):
        sum_in.put(k, in_term(place.plane(k)))
    own_out = out_term(place.z)
    own_in = in_term(place.z)
    return sum_out, own_out, sum_in, own_in


def ffn_share_grads(place, refs, sum_out, own_out, sum_in, own_in):
    total = sum_out.total(own_out).astype(BF16)
    own = place.slot(0)
    share_out = Exchange(place, refs.share_out, (4,))
    share_out.blocks[own] = total
    share_out.start(lambda k: share_out.blocks.at[own])
    total = sum_in.total(own_in).astype(BF16)
    refs.in_total[...] = total.reshape(refs.in_total.shape)
    share_in = Exchange(place, refs.share_in, tuple(range(1, 8)))
    share_in.blocks[own] = refs.in_total[place.yc]
    share_in.start(lambda k: refs.in_total.at[place.flip(k)[1]])
    share_out.wait()
    mine = place.yc
    for x in range(2):
        refs.grad_out[pl.ds(x * 128, 128), :] = share_out.blocks[x * 4 + mine].astype(F32)
    share_in.wait()
    for slot in range(8):
        x, yc = slot // 4, slot % 4
        piece = share_in.blocks[slot].astype(F32)
        for plane in range(PLANES):
            column = ((plane * 4 + yc) * 2 + x) * 128
            refs.grad_in[:, column : column + 128] = piece[:, plane * 128 : plane * 128 + 128]


def ffn_grad_scratch():
    return dict(
        sum_out=PlaneSum.scratch(128, 1024),
        sum_in=PlaneSum.scratch(256, 512),
        in_total=VMEM((4, 64, 512), BF16),
        share_out=[VMEM((8, 128, 1024), BF16), DMA((8,)), DMA((8,))],
        share_in=[VMEM((8, 64, 512), BF16), DMA((8,)), DMA((8,))],
    )


AG_SEMS = [DMA((10,)), DMA((10,))]


def norm_rows(values, gain):
    normed, saved = norm_forward(values, gain)
    return normed.astype(BF16), saved


def norm_input_grad(grads, gain, saved):
    unit_part, inverse = saved
    scaled = grads * gain
    gain_grad = jnp.sum(grads * unit_part, axis=0, keepdims=True)
    input_part = inverse * (
        scaled
        - jnp.mean(scaled, axis=-1, keepdims=True)
        - unit_part * jnp.mean(scaled * unit_part, axis=-1, keepdims=True)
    )
    return input_part, gain_grad


def ffn1_forward_body(refs):
    place = Place()
    place.enter()
    along_z = gather_rows(place, refs.w_in_rows.at[place.x], refs.w_in, refs.gather_in)
    refs.blocks[place.slot(0)] = norm_rows(refs.stream[...], refs.gain[...])[0]
    finish_in = along_z()
    finish_out = gather_blocks(place, refs.w_out_rows.at[place.x], refs.w_out, refs.gather_out)
    finish_in()
    finish_out()
    scatter = Scatter(place, refs.scatter)
    total = ffn_forward(
        place, refs, refs.blocks, refs.hidden, refs.w_in, refs.w_out, refs.ag, scatter
    )
    refs.stream_out[...] = refs.stream[...] + 0.5 * total


def ffn1_forward(stream, gain, w_in, w_out):
    ins = dict(
        stream=(stream, VMEM),
        gain=(gain[None], VMEM),
        w_in_rows=(w_in, pl.ANY),
        w_out_rows=(w_out, pl.ANY),
    )
    outs = dict(
        stream_out=((128, 1024), F32, VMEM),
        blocks=((8, 128, 1024), BF16, VMEM),
        hidden=((8, 128, 512), F32, VMEM),
        w_in=((16, 64, 512), BF16, VMEM),
        w_out=((4, 128, 1024), BF16, VMEM),
    )
    scratch = dict(
        gather_in=GATHER_SEMS,
        gather_out=GATHER_SEMS,
        ag=AG_SEMS,
        scatter=Scatter.scratch(128, 1024),
    )
    return kernel_call(ffn1_forward_body, 1, ins, outs, scratch)


def ffn1_backward_body(refs):
    place = Place()
    place.enter()
    grad = refs.grad[...]
    refs.grads[place.slot(0)] = (0.5 * grad).astype(BF16)
    scatter = Scatter(place, refs.scatter)
    sent = ffn_backward(
        place,
        refs.blocks,
        refs.grads,
        refs.hidden,
        refs.hidden_grads,
        refs.active,
        refs.w_in,
        refs.w_out,
        refs.ag,
        scatter,
    )
    terms = ffn_weight_grads(place, refs, refs.blocks, refs.grads, refs.hidden_grads, refs.active)
    unused, saved = norm_forward(refs.stream[...], refs.gain[...])
    input_part, gain_grad = norm_input_grad(scatter.total(), refs.gain[...], saved)
    refs.grad_stream[...] = grad + input_part
    refs.grad_gain[...] = gain_grad
    for copy in sent:
        copy.wait_send()
    scatter.drain()
    ffn_share_grads(place, refs, *terms)


def ffn1_backward(grad, stream, gain, kept):
    ins = dict(
        grad=(grad, VMEM),
        stream=(stream, VMEM),
        gain=(gain[None], VMEM),
        blocks=(kept["blocks"], VMEM),
        hidden=(kept["hidden"], VMEM),
        w_in=(kept["w_in"], VMEM),
        w_out=(kept["w_out"], VMEM),
    )
    outs = dict(
        grad_stream=((128, 1024), F32, VMEM),
        grad_gain=((1, 1024), F32, VMEM),
        grad_in=((64, 4096), F32, VMEM),
        grad_out=((256, 1024), F32, VMEM),
    )
    scratch = dict(
        grads=VMEM((8, 128, 1024), BF16),
        hidden_grads=VMEM((8, 128, 512), BF16),
        active=VMEM((8, 128, 512), BF16),
        ag=AG_SEMS,
        scatter=Scatter.scratch(128, 1024),
        **ffn_grad_scratch(),
    )
    return kernel_call(ffn1_backward_body, 2, ins, outs, scratch)


def ffn2_body(refs):
    place = Place()
    place.enter()
    along_z = gather_rows(place, refs.w_in_rows.at[place.x], refs.w_in, refs.gather_in)
    own = place.slot(0)
    stream = refs.stream[...]
    low, saved = norm_rows(stream, refs.gain[...])
    refs.blocks[own] = low
    finish_in = along_z()
    finish_out = gather_blocks(place, refs.w_out_rows.at[place.x], refs.w_out, refs.gather_out)
    finish_in()
    finish_out()
    scatter = Scatter(place, refs.scatter)
    total = ffn_forward(
        place, refs, refs.blocks, refs.hidden, refs.w_in, refs.w_out, refs.ag, scatter
    )
    final, saved_final = norm_forward(stream + 0.5 * total, refs.gain_out[...])
    refs.output[...] = final.astype(BF16)
    grad, refs.grad_gain_out[...] = norm_input_grad(
        refs.cotangent[...].astype(F32), refs.gain_out[...], saved_final
    )
    refs.grads[own] = (0.5 * grad).astype(BF16)
    scatter = Scatter(place, refs.scatter_back)
    sent = ffn_backward(
        place,
        refs.blocks,
        refs.grads,
        refs.hidden,
        refs.hidden_grads,
        refs.active,
        refs.w_in,
        refs.w_out,
        refs.ag_back,
        scatter,
    )
    terms = ffn_weight_grads(place, refs, refs.blocks, refs.grads, refs.hidden_grads, refs.active)
    input_part, refs.grad_gain[...] = norm_input_grad(scatter.total(), refs.gain[...], saved)
    refs.grad_stream[...] = grad + input_part
    for copy in sent:
        copy.wait_send()
    scatter.drain()
    ffn_share_grads(place, refs, *terms)


def ffn2_both(stream, cotangent, gain, gain_out, w_in, w_out):
    ins = dict(
        stream=(stream, VMEM),
        cotangent=(cotangent, VMEM),
        gain=(gain[None], VMEM),
        gain_out=(gain_out[None], VMEM),
        w_in_rows=(w_in, pl.ANY),
        w_out_rows=(w_out, pl.ANY),
    )
    outs = dict(
        output=((128, 1024), BF16, VMEM),
        grad_stream=((128, 1024), F32, VMEM),
        grad_gain=((1, 1024), F32, VMEM),
        grad_gain_out=((1, 1024), F32, VMEM),
        grad_in=((64, 4096), F32, VMEM),
        grad_out=((256, 1024), F32, VMEM),
    )
    scratch = dict(
        blocks=VMEM((8, 128, 1024), BF16),
        hidden=VMEM((8, 128, 512), F32),
        w_in=VMEM((16, 64, 512), BF16),
        w_out=VMEM((4, 128, 1024), BF16),
        gather_in=GATHER_SEMS,
        gather_out=GATHER_SEMS,
        ag=AG_SEMS,
        scatter=Scatter.scratch(128, 1024),
        grads=VMEM((8, 128, 1024), BF16),
        hidden_grads=VMEM((8, 128, 512), BF16),
        active=VMEM((8, 128, 512), BF16),
        ag_back=AG_SEMS,
        scatter_back=Scatter.scratch(128, 1024),
        **ffn_grad_scratch(),
    )
    return kernel_call(ffn2_body, 3, ins, outs, scratch)


def ffn_rows(w_in, w_out):
    columns = w_in.reshape(64, PLANES, 4, 2, 128)
    return jnp.transpose(columns, (3, 2, 0, 1, 4)).reshape(2, 4, 64, 512), w_out.reshape(2, 128, -1)


def local_planes(
    inputs,
    lengths,
    gain_ffn1,
    gain_attn,
    gain_conv,
    gain_inner,
    gain_ffn2,
    gain_out,
    conv_kernel,
    ffn1_in,
    ffn1_out,
    attn_qkv,
    attn_out,
    conv_in,
    conv_out,
    ffn2_in,
    ffn2_out,
    cotangent,
):
    frame_count = inputs.shape[1]
    model_width = inputs.shape[2]
    device_count = lax.axis_size("seq")
    position_index = lax.axis_index("seq")
    seg_lengths = lengths[0]
    first_frame = position_index * frame_count
    local_frames = jnp.arange(frame_count, dtype=jnp.int32)
    positions = first_frame + local_frames
    query_segments = segment_of(positions, seg_lengths)
    cos_table, sin_table = rotary_tables(positions)
    stream = inputs[0].astype(jnp.float32)
    rows_one = ffn_rows(ffn1_in, ffn1_out)
    rows_two = ffn_rows(ffn2_in, ffn2_out)
    kept_one = ffn1_forward(stream, gain_ffn1, *rows_one)
    stream_one = kept_one["stream_out"]
    normed_two, saved_two = norm_forward(stream_one, gain_attn)
    normed_two_low = normed_two.astype(jnp.bfloat16)
    projected, kept_qkv = project(normed_two_low, attn_qkv)
    query_low = rotate(projected[:, :model_width], cos_table, sin_table).astype(jnp.bfloat16)
    key_low = rotate(projected[:, model_width : 2 * model_width], cos_table, sin_table).astype(
        jnp.bfloat16
    )
    value_low = projected[:, 2 * model_width :].astype(jnp.bfloat16)
    query_heads = split_heads(query_low)

    def stats_step(current, blocks, first_row):
        top_score, denominator = current
        key_block = blocks[0]
        key_segments = segment_of(
            first_row + jnp.arange(key_block.shape[0], dtype=jnp.int32), seg_lengths
        )
        masked = block_scores(query_heads, split_heads(key_block), query_segments, key_segments)
        new_top = jnp.maximum(top_score, jnp.max(masked, axis=-1))
        denominator = denominator * jnp.exp(top_score - new_top) + jnp.sum(
            jnp.exp(masked - new_top[:, :, None]), axis=-1
        )
        return (new_top, denominator)

    top_init = jnp.full((HEADS, frame_count), MASKED, jnp.float32)
    total_init = jnp.zeros((HEADS, frame_count), jnp.float32)
    top_score, denominator = over_blocks(
        stats_step, (top_init, total_init), (lax.all_gather(key_low, "seq", axis=0, tiled=True),)
    )
    log_total = top_score + jnp.log(denominator)

    def value_step(current, blocks, first_row):
        mixed_sum, rest_sum = current
        key_block, value_block = blocks
        key_segments = segment_of(
            first_row + jnp.arange(key_block.shape[0], dtype=jnp.int32), seg_lengths
        )
        probs = jnp.exp(
            block_scores(query_heads, split_heads(key_block), query_segments, key_segments)
            - log_total[:, :, None]
        )
        probs_high = probs.astype(jnp.bfloat16)
        probs_rest = (probs - probs_high.astype(jnp.float32)).astype(jnp.bfloat16)
        value_heads = split_heads(value_block)
        mixed_sum = mixed_sum + jnp.einsum(
            "hqk,khd->qhd", probs_high, value_heads, preferred_element_type=jnp.float32
        )
        rest_sum = rest_sum + jnp.einsum(
            "hqk,khd->qhd", probs_rest, value_heads, preferred_element_type=jnp.float32
        )
        return (mixed_sum, rest_sum)

    zero_heads = jnp.zeros((frame_count, HEADS, HEAD_DIM), jnp.float32)
    mixed_sum, rest_sum = over_blocks(
        value_step,
        (zero_heads, zero_heads),
        (
            lax.all_gather(key_low, "seq", axis=0, tiled=True),
            lax.all_gather(value_low, "seq", axis=0, tiled=True),
        ),
    )
    exact_sum = mixed_sum + rest_sum
    mixed_low = mixed_sum.reshape(frame_count, model_width).astype(jnp.bfloat16)
    branch_two, kept_attn_out = project(mixed_low, attn_out)
    stream_two = stream_one + branch_two
    normed_three, saved_three = norm_forward(stream_two, gain_conv)
    normed_three_low = normed_three.astype(jnp.bfloat16)
    gate_up, kept_conv_in = project(normed_three_low, conv_in)
    first_part = gate_up[:, :model_width]
    gate_sigma = jax.nn.sigmoid(gate_up[:, model_width:])
    glu_low = (first_part * gate_sigma).astype(jnp.bfloat16)
    padded = with_halo(glu_low, (("seq", 0),), HALF).astype(jnp.float32)
    padded_segments = segment_of(
        first_frame - HALF + jnp.arange(frame_count + 2 * HALF, dtype=jnp.int32), seg_lengths
    )
    kernel_taps = conv_kernel.astype(jnp.float32)
    conv_values = jnp.zeros((frame_count, model_width), jnp.float32)
    for offset in range(KERNEL):
        same_segment = (padded_segments[offset : offset + frame_count] == query_segments).astype(
            jnp.float32
        )
        conv_values = (
            conv_values
            + kernel_taps[offset] * padded[offset : offset + frame_count] * same_segment[:, None]
        )
    normed_four, saved_four = norm_forward(conv_values, gain_inner)
    active_four = sigmoid_linear(normed_four).astype(jnp.bfloat16)
    branch_three, kept_conv_out = project(active_four, conv_out)
    stream_three = stream_two + branch_three
    last = ffn2_both(stream_three, cotangent[0], gain_ffn2, gain_out, *rows_two)
    output = last["output"][None]
    grad_three = last["grad_stream"]
    grad_gain_five, grad_gain_six = last["grad_gain"][0], last["grad_gain_out"][0]
    conv_out_low = grad_three.astype(jnp.bfloat16)
    grad_conv_weight_out = weight_grad(active_four, conv_out_low)
    active_grad = project_back(conv_out_low, conv_out) * sigmoid_linear_grad(normed_four)
    conv_grad, grad_gain_four = norm_backward(active_grad, gain_inner, saved_four)
    conv_grad_low = conv_grad.astype(jnp.bfloat16)
    conv_grad_value = conv_grad_low.astype(jnp.float32)
    rim_grad = with_halo(conv_grad_low, (("seq", 0),), HALF).astype(jnp.float32)
    tap_grads = []
    glu_grad = jnp.zeros((frame_count, model_width), jnp.float32)
    for offset in range(KERNEL):
        same_segment = (padded_segments[offset : offset + frame_count] == query_segments).astype(
            jnp.float32
        )
        tap_grads.append(
            jnp.sum(
                padded[offset : offset + frame_count] * same_segment[:, None] * conv_grad_value,
                axis=0,
            )
        )
        back_start = 2 * HALF - offset
        back_segment = (
            padded_segments[back_start : back_start + frame_count] == query_segments
        ).astype(jnp.float32)
        glu_grad = (
            glu_grad
            + kernel_taps[offset]
            * rim_grad[back_start : back_start + frame_count]
            * back_segment[:, None]
        )
    kernel_grad = jnp.stack(tap_grads, axis=0)
    gate_up_low = jnp.concatenate(
        [glu_grad * gate_sigma, glu_grad * first_part * gate_sigma * (1.0 - gate_sigma)], axis=1
    ).astype(jnp.bfloat16)
    grad_conv_weight_in = weight_grad(normed_three_low, gate_up_low)
    input_part, grad_gain_three = norm_backward(
        project_back(gate_up_low, conv_in), gain_conv, saved_three
    )
    grad_two = grad_three + input_part
    attn_grad_low = grad_two.astype(jnp.bfloat16)
    grad_attn_weight = weight_grad(mixed_low, attn_grad_low)
    mixed_grad_low = project_back(attn_grad_low, attn_out).astype(jnp.bfloat16)
    delta = jnp.transpose(
        jnp.sum(split_heads(mixed_grad_low).astype(jnp.float32) * exact_sum, axis=-1)
    )

    def key_turn(turn_index, current):
        key_rows, value_rows, key_acc, value_acc, query_acc = current
        owner = (position_index - turn_index) % device_count
        key_segments = segment_of(owner * frame_count + local_frames, seg_lengths)
        query_part, key_part, value_part = pair_grads(
            query_low,
            mixed_grad_low,
            log_total,
            delta,
            query_segments,
            key_rows,
            value_rows,
            key_segments,
        )
        key_rows, value_rows = shifted((key_rows, value_rows), "seq", 1)
        key_acc, value_acc = (
            shifted((key_acc + key_part).astype(jnp.bfloat16), "seq", 1).astype(jnp.float32),
            shifted((value_acc + value_part).astype(jnp.bfloat16), "seq", 1).astype(jnp.float32),
        )
        return (key_rows, value_rows, key_acc, value_acc, query_acc + query_part)

    zero_rows = jnp.zeros((frame_count, model_width), jnp.float32)
    unused_keys, unused_values, key_grad, value_grad, query_grad = lax.fori_loop(
        0, device_count, key_turn, (key_low, value_low, zero_rows, zero_rows, zero_rows)
    )
    projected_grad_low = jnp.concatenate(
        [
            unrotate(query_grad, cos_table, sin_table),
            unrotate(key_grad, cos_table, sin_table),
            value_grad,
        ],
        axis=1,
    ).astype(jnp.bfloat16)
    grad_qkv_weight = weight_grad(normed_two_low, projected_grad_low)
    input_part, grad_gain_two = norm_backward(
        project_back(projected_grad_low, attn_qkv), gain_attn, saved_two
    )
    grad_one = grad_two + input_part
    first = ffn1_backward(grad_one, stream, gain_ffn1, kept_one)
    input_grad = first["grad_stream"][None]
    grad_gain_one = first["grad_gain"][0]
    small_grads = lax.psum(
        (
            grad_gain_one,
            grad_gain_two,
            grad_gain_three,
            grad_gain_four,
            grad_gain_five,
            grad_gain_six,
            kernel_grad,
        ),
        ("seq", "row"),
    )
    large_grads = (
        first["grad_in"],
        first["grad_out"],
        lax.psum(grad_qkv_weight.astype(jnp.bfloat16), "row").astype(jnp.float32),
        lax.psum(grad_attn_weight.astype(jnp.bfloat16), "row").astype(jnp.float32),
        lax.psum(grad_conv_weight_in.astype(jnp.bfloat16), "row").astype(jnp.float32),
        lax.psum(grad_conv_weight_out.astype(jnp.bfloat16), "row").astype(jnp.float32),
        last["grad_in"],
        last["grad_out"],
    )
    return (
        output,
        input_grad,
        small_grads[0],
        small_grads[1],
        small_grads[2],
        small_grads[3],
        small_grads[4],
        small_grads[5],
        small_grads[6],
        large_grads[0],
        large_grads[1],
        large_grads[2],
        large_grads[3],
        large_grads[4],
        large_grads[5],
        large_grads[6],
        large_grads[7],
    )


def solution(mesh):
    return jax.shard_map(
        local_planes if mesh.shape["seq"] == 16 and mesh.shape["row"] == 2 else local,
        mesh=mesh,
        in_specs=(
            P("row", "seq", None),
            P("row", None),
            P(),
            P(),
            P(),
            P(),
            P(),
            P(),
            P(),
            P("seq", None),
            P("seq", None),
            P("seq", None),
            P("seq", None),
            P("seq", None),
            P("seq", None),
            P("seq", None),
            P("seq", None),
            P("row", "seq", None),
        ),
        out_specs=(
            P("row", "seq", None),
            P("row", "seq", None),
            P(),
            P(),
            P(),
            P(),
            P(),
            P(),
            P(),
            P("seq", None),
            P("seq", None),
            P("seq", None),
            P("seq", None),
            P("seq", None),
            P("seq", None),
            P("seq", None),
            P("seq", None),
        ),
        check_vma=False,
    )
```

```python
import math

import jax
import jax.numpy as jnp
from jax import lax
from jax.experimental import pallas as pl
from jax.experimental.pallas import tpu as pltpu
from jax.sharding import PartitionSpec as P

HEADS = 16
HEAD_DIM = 64
KERNEL = 31
HALF = 15


EPSILON = 1e-05
MASKED = -1e30


def with_halo(block, sides, width):
    for axis, dim in sides:
        count = lax.axis_size(axis)
        forward = [(i, i + 1) for i in range(count - 1)]
        backward = [(target, source) for source, target in forward]
        low = lax.ppermute(
            lax.slice_in_dim(block, block.shape[dim] - width, None, axis=dim), axis, forward
        )
        high = lax.ppermute(lax.slice_in_dim(block, 0, width, axis=dim), axis, backward)
        block = jnp.concatenate([low, block, high], axis=dim)
    return block


def shifted(array, axis, by):
    size = lax.axis_size(axis)
    return lax.ppermute(array, axis, [(i, (i + by) % size) for i in range(size)])


def segment_of(positions, seg_lengths):
    boundary = jnp.cumsum(seg_lengths)[:-1]
    return jnp.sum((positions[:, None] >= boundary[None, :]).astype(jnp.int32), axis=1)


def rotary_tables(positions):
    half_dim = HEAD_DIM // 2
    inverse = jnp.exp(-jnp.log(10000.0) * jnp.arange(half_dim, dtype=jnp.float32) / half_dim)
    angles = positions.astype(jnp.float32)[:, None] * inverse[None, :]
    return (jnp.cos(angles), jnp.sin(angles))


def split_heads(values):
    return values.reshape(values.shape[0], HEADS, HEAD_DIM)


def rotate(values, cos_table, sin_table):
    half_dim = HEAD_DIM // 2
    shaped = split_heads(values)
    first_half = shaped[..., :half_dim]
    second_half = shaped[..., half_dim:]
    cos_heads = cos_table[:, None, :]
    sin_heads = sin_table[:, None, :]
    turned = jnp.concatenate(
        [
            first_half * cos_heads - second_half * sin_heads,
            second_half * cos_heads + first_half * sin_heads,
        ],
        axis=-1,
    )
    return turned.reshape(values.shape)


def unrotate(grads, cos_table, sin_table):
    half_dim = HEAD_DIM // 2
    shaped = split_heads(grads)
    first_half = shaped[..., :half_dim]
    second_half = shaped[..., half_dim:]
    cos_heads = cos_table[:, None, :]
    sin_heads = sin_table[:, None, :]
    turned = jnp.concatenate(
        [
            first_half * cos_heads + second_half * sin_heads,
            second_half * cos_heads - first_half * sin_heads,
        ],
        axis=-1,
    )
    return turned.reshape(grads.shape)


def norm_forward(values, gain):
    center = values - jnp.mean(values, axis=-1, keepdims=True)
    spread = jnp.mean(center * center, axis=-1, keepdims=True)
    inverse = lax.rsqrt(spread + EPSILON)
    unit_part = center * inverse
    return (unit_part * gain, (unit_part, inverse))


def norm_backward(grads, gain, saved):
    unit_part, inverse = saved
    scaled = grads * gain
    gain_grad = jnp.sum(grads * unit_part, axis=0)
    input_part = inverse * (
        scaled
        - jnp.mean(scaled, axis=-1, keepdims=True)
        - unit_part * jnp.mean(scaled * unit_part, axis=-1, keepdims=True)
    )
    return (input_part, gain_grad)


def sigmoid_linear(values):
    return values * jax.nn.sigmoid(values)


def sigmoid_linear_grad(values):
    sigma = jax.nn.sigmoid(values)
    return sigma * (1.0 + values * (1.0 - sigma))


def project(left_side, weight):
    return (
        jnp.dot(
            left_side,
            lax.all_gather(weight, "seq", axis=0, tiled=True),
            preferred_element_type=jnp.float32,
        ),
        weight,
    )


def project_back(grad_side, weight):
    return lax.dot_general(
        grad_side,
        lax.all_gather(weight, "seq", axis=0, tiled=True),
        (((1,), (1,)), ((), ())),
        preferred_element_type=jnp.float32,
    )


def weight_grad(left_side, grad_side):
    return lax.psum_scatter(
        lax.dot_general(
            left_side, grad_side, (((0,), (0,)), ((), ())), preferred_element_type=jnp.float32
        ).astype(jnp.bfloat16),
        "seq",
        scatter_dimension=0,
        tiled=True,
    ).astype(jnp.float32)


def over_blocks(advance, running, pieces):
    total_rows = pieces[0].shape[0]
    block_size = math.gcd(total_rows, 512)
    number = total_rows // block_size
    stacked = tuple((piece.reshape((number, block_size) + piece.shape[1:]) for piece in pieces))

    def scan_step(current, block_item):
        block_index, blocks = block_item
        return (advance(current, blocks, block_index * block_size), None)

    running, unused = lax.scan(scan_step, running, (jnp.arange(number, dtype=jnp.int32), stacked))
    return running


def block_scores(query_heads, key_heads, query_segments, key_segments):
    scale = HEAD_DIM ** (-0.5)
    raw_scores = (
        jnp.einsum("qhd,khd->hqk", query_heads, key_heads, preferred_element_type=jnp.float32)
        * scale
    )
    return jnp.where((query_segments[:, None] == key_segments[None, :])[None], raw_scores, MASKED)


def pair_grads(
    query_rows, grad_rows, log_total, delta, query_segments, key_rows, value_rows, key_segments
):
    scale = HEAD_DIM ** (-0.5)
    query_heads = split_heads(query_rows)
    grad_heads = split_heads(grad_rows)
    key_heads = split_heads(key_rows)
    value_heads = split_heads(value_rows)
    probs = jnp.exp(
        block_scores(query_heads, key_heads, query_segments, key_segments) - log_total[:, :, None]
    )
    prob_grads = jnp.einsum(
        "qhd,khd->hqk", grad_heads, value_heads, preferred_element_type=jnp.float32
    )
    score_grads = (probs * (prob_grads - delta[:, :, None])).astype(jnp.bfloat16)
    query_grad = (
        jnp.einsum("hqk,khd->qhd", score_grads, key_heads, preferred_element_type=jnp.float32)
        * scale
    )
    key_grad = (
        jnp.einsum("hqk,qhd->khd", score_grads, query_heads, preferred_element_type=jnp.float32)
        * scale
    )
    value_grad = jnp.einsum(
        "hqk,qhd->khd", probs.astype(jnp.bfloat16), grad_heads, preferred_element_type=jnp.float32
    )
    return (
        query_grad.reshape(query_rows.shape),
        key_grad.reshape(key_rows.shape),
        value_grad.reshape(value_rows.shape),
    )


def local(
    inputs,
    lengths,
    gain_ffn1,
    gain_attn,
    gain_conv,
    gain_inner,
    gain_ffn2,
    gain_out,
    conv_kernel,
    ffn1_in,
    ffn1_out,
    attn_qkv,
    attn_out,
    conv_in,
    conv_out,
    ffn2_in,
    ffn2_out,
    cotangent,
):
    frame_count = inputs.shape[1]
    model_width = inputs.shape[2]
    device_count = lax.axis_size("seq")
    position_index = lax.axis_index("seq")
    seg_lengths = lengths[0]
    first_frame = position_index * frame_count
    local_frames = jnp.arange(frame_count, dtype=jnp.int32)
    positions = first_frame + local_frames
    query_segments = segment_of(positions, seg_lengths)
    cos_table, sin_table = rotary_tables(positions)
    stream = inputs[0].astype(jnp.float32)
    normed_one, saved_one = norm_forward(stream, gain_ffn1)
    normed_one_low = normed_one.astype(jnp.bfloat16)
    hidden_one, kept_ffn1_in = project(normed_one_low, ffn1_in)
    active_one = sigmoid_linear(hidden_one).astype(jnp.bfloat16)
    branch_one, kept_ffn1_out = project(active_one, ffn1_out)
    stream_one = stream + 0.5 * branch_one
    normed_two, saved_two = norm_forward(stream_one, gain_attn)
    normed_two_low = normed_two.astype(jnp.bfloat16)
    projected, kept_qkv = project(normed_two_low, attn_qkv)
    query_low = rotate(projected[:, :model_width], cos_table, sin_table).astype(jnp.bfloat16)
    key_low = rotate(projected[:, model_width : 2 * model_width], cos_table, sin_table).astype(
        jnp.bfloat16
    )
    value_low = projected[:, 2 * model_width :].astype(jnp.bfloat16)
    query_heads = split_heads(query_low)

    def stats_step(current, blocks, first_row):
        top_score, denominator = current
        key_block = blocks[0]
        key_segments = segment_of(
            first_row + jnp.arange(key_block.shape[0], dtype=jnp.int32), seg_lengths
        )
        masked = block_scores(query_heads, split_heads(key_block), query_segments, key_segments)
        new_top = jnp.maximum(top_score, jnp.max(masked, axis=-1))
        denominator = denominator * jnp.exp(top_score - new_top) + jnp.sum(
            jnp.exp(masked - new_top[:, :, None]), axis=-1
        )
        return (new_top, denominator)

    top_init = jnp.full((HEADS, frame_count), MASKED, jnp.float32)
    total_init = jnp.zeros((HEADS, frame_count), jnp.float32)
    top_score, denominator = over_blocks(
        stats_step, (top_init, total_init), (lax.all_gather(key_low, "seq", axis=0, tiled=True),)
    )
    log_total = top_score + jnp.log(denominator)

    def value_step(current, blocks, first_row):
        mixed_sum, rest_sum = current
        key_block, value_block = blocks
        key_segments = segment_of(
            first_row + jnp.arange(key_block.shape[0], dtype=jnp.int32), seg_lengths
        )
        probs = jnp.exp(
            block_scores(query_heads, split_heads(key_block), query_segments, key_segments)
            - log_total[:, :, None]
        )
        probs_high = probs.astype(jnp.bfloat16)
        probs_rest = (probs - probs_high.astype(jnp.float32)).astype(jnp.bfloat16)
        value_heads = split_heads(value_block)
        mixed_sum = mixed_sum + jnp.einsum(
            "hqk,khd->qhd", probs_high, value_heads, preferred_element_type=jnp.float32
        )
        rest_sum = rest_sum + jnp.einsum(
            "hqk,khd->qhd", probs_rest, value_heads, preferred_element_type=jnp.float32
        )
        return (mixed_sum, rest_sum)

    zero_heads = jnp.zeros((frame_count, HEADS, HEAD_DIM), jnp.float32)
    mixed_sum, rest_sum = over_blocks(
        value_step,
        (zero_heads, zero_heads),
        (
            lax.all_gather(key_low, "seq", axis=0, tiled=True),
            lax.all_gather(value_low, "seq", axis=0, tiled=True),
        ),
    )
    exact_sum = mixed_sum + rest_sum
    mixed_low = mixed_sum.reshape(frame_count, model_width).astype(jnp.bfloat16)
    branch_two, kept_attn_out = project(mixed_low, attn_out)
    stream_two = stream_one + branch_two
    normed_three, saved_three = norm_forward(stream_two, gain_conv)
    normed_three_low = normed_three.astype(jnp.bfloat16)
    gate_up, kept_conv_in = project(normed_three_low, conv_in)
    first_part = gate_up[:, :model_width]
    gate_sigma = jax.nn.sigmoid(gate_up[:, model_width:])
    glu_low = (first_part * gate_sigma).astype(jnp.bfloat16)
    padded = with_halo(glu_low, (("seq", 0),), HALF).astype(jnp.float32)
    padded_segments = segment_of(
        first_frame - HALF + jnp.arange(frame_count + 2 * HALF, dtype=jnp.int32), seg_lengths
    )
    kernel_taps = conv_kernel.astype(jnp.float32)
    conv_values = jnp.zeros((frame_count, model_width), jnp.float32)
    for offset in range(KERNEL):
        same_segment = (padded_segments[offset : offset + frame_count] == query_segments).astype(
            jnp.float32
        )
        conv_values = (
            conv_values
            + kernel_taps[offset] * padded[offset : offset + frame_count] * same_segment[:, None]
        )
    normed_four, saved_four = norm_forward(conv_values, gain_inner)
    active_four = sigmoid_linear(normed_four).astype(jnp.bfloat16)
    branch_three, kept_conv_out = project(active_four, conv_out)
    stream_three = stream_two + branch_three
    normed_five, saved_five = norm_forward(stream_three, gain_ffn2)
    normed_five_low = normed_five.astype(jnp.bfloat16)
    hidden_two, kept_ffn2_in = project(normed_five_low, ffn2_in)
    active_two = sigmoid_linear(hidden_two).astype(jnp.bfloat16)
    branch_four, kept_ffn2_out = project(active_two, ffn2_out)
    stream_four = stream_three + 0.5 * branch_four
    final_norm, saved_six = norm_forward(stream_four, gain_out)
    output = final_norm.astype(jnp.bfloat16)[None]
    grad_four, grad_gain_six = norm_backward(cotangent[0].astype(jnp.float32), gain_out, saved_six)
    out_two_low = (0.5 * grad_four).astype(jnp.bfloat16)
    grad_ffn_two_out = weight_grad(active_two, out_two_low)
    hidden_two_low = (project_back(out_two_low, ffn2_out) * sigmoid_linear_grad(hidden_two)).astype(
        jnp.bfloat16
    )
    grad_ffn_two_in = weight_grad(normed_five_low, hidden_two_low)
    input_part, grad_gain_five = norm_backward(
        project_back(hidden_two_low, ffn2_in), gain_ffn2, saved_five
    )
    grad_three = grad_four + input_part
    conv_out_low = grad_three.astype(jnp.bfloat16)
    grad_conv_weight_out = weight_grad(active_four, conv_out_low)
    active_grad = project_back(conv_out_low, conv_out) * sigmoid_linear_grad(normed_four)
    conv_grad, grad_gain_four = norm_backward(active_grad, gain_inner, saved_four)
    conv_grad_low = conv_grad.astype(jnp.bfloat16)
    conv_grad_value = conv_grad_low.astype(jnp.float32)
    rim_grad = with_halo(conv_grad_low, (("seq", 0),), HALF).astype(jnp.float32)
    tap_grads = []
    glu_grad = jnp.zeros((frame_count, model_width), jnp.float32)
    for offset in range(KERNEL):
        same_segment = (padded_segments[offset : offset + frame_count] == query_segments).astype(
            jnp.float32
        )
        tap_grads.append(
            jnp.sum(
                padded[offset : offset + frame_count] * same_segment[:, None] * conv_grad_value,
                axis=0,
            )
        )
        back_start = 2 * HALF - offset
        back_segment = (
            padded_segments[back_start : back_start + frame_count] == query_segments
        ).astype(jnp.float32)
        glu_grad = (
            glu_grad
            + kernel_taps[offset]
            * rim_grad[back_start : back_start + frame_count]
            * back_segment[:, None]
        )
    kernel_grad = jnp.stack(tap_grads, axis=0)
    gate_up_low = jnp.concatenate(
        [glu_grad * gate_sigma, glu_grad * first_part * gate_sigma * (1.0 - gate_sigma)], axis=1
    ).astype(jnp.bfloat16)
    grad_conv_weight_in = weight_grad(normed_three_low, gate_up_low)
    input_part, grad_gain_three = norm_backward(
        project_back(gate_up_low, conv_in), gain_conv, saved_three
    )
    grad_two = grad_three + input_part
    attn_grad_low = grad_two.astype(jnp.bfloat16)
    grad_attn_weight = weight_grad(mixed_low, attn_grad_low)
    mixed_grad_low = project_back(attn_grad_low, attn_out).astype(jnp.bfloat16)
    delta = jnp.transpose(
        jnp.sum(split_heads(mixed_grad_low).astype(jnp.float32) * exact_sum, axis=-1)
    )

    def key_turn(turn_index, current):
        key_rows, value_rows, key_acc, value_acc, query_acc = current
        owner = (position_index - turn_index) % device_count
        key_segments = segment_of(owner * frame_count + local_frames, seg_lengths)
        query_part, key_part, value_part = pair_grads(
            query_low,
            mixed_grad_low,
            log_total,
            delta,
            query_segments,
            key_rows,
            value_rows,
            key_segments,
        )
        key_rows, value_rows = shifted((key_rows, value_rows), "seq", 1)
        key_acc, value_acc = (
            shifted((key_acc + key_part).astype(jnp.bfloat16), "seq", 1).astype(jnp.float32),
            shifted((value_acc + value_part).astype(jnp.bfloat16), "seq", 1).astype(jnp.float32),
        )
        return (key_rows, value_rows, key_acc, value_acc, query_acc + query_part)

    zero_rows = jnp.zeros((frame_count, model_width), jnp.float32)
    unused_keys, unused_values, key_grad, value_grad, query_grad = lax.fori_loop(
        0, device_count, key_turn, (key_low, value_low, zero_rows, zero_rows, zero_rows)
    )
    projected_grad_low = jnp.concatenate(
        [
            unrotate(query_grad, cos_table, sin_table),
            unrotate(key_grad, cos_table, sin_table),
            value_grad,
        ],
        axis=1,
    ).astype(jnp.bfloat16)
    grad_qkv_weight = weight_grad(normed_two_low, projected_grad_low)
    input_part, grad_gain_two = norm_backward(
        project_back(projected_grad_low, attn_qkv), gain_attn, saved_two
    )
    grad_one = grad_two + input_part
    out_one_low = (0.5 * grad_one).astype(jnp.bfloat16)
    grad_ffn_one_out = weight_grad(active_one, out_one_low)
    hidden_one_low = (project_back(out_one_low, ffn1_out) * sigmoid_linear_grad(hidden_one)).astype(
        jnp.bfloat16
    )
    grad_ffn_one_in = weight_grad(normed_one_low, hidden_one_low)
    input_part, grad_gain_one = norm_backward(
        project_back(hidden_one_low, ffn1_in), gain_ffn1, saved_one
    )
    input_grad = (grad_one + input_part)[None]
    small_grads = lax.psum(
        (
            grad_gain_one,
            grad_gain_two,
            grad_gain_three,
            grad_gain_four,
            grad_gain_five,
            grad_gain_six,
            kernel_grad,
        ),
        ("seq", "row"),
    )
    large_grads = (
        grad_ffn_one_in,
        grad_ffn_one_out,
        grad_qkv_weight,
        grad_attn_weight,
        grad_conv_weight_in,
        grad_conv_weight_out,
        grad_ffn_two_in,
        grad_ffn_two_out,
    )
    large_grads = (
        lax.psum(grad_ffn_one_in.astype(jnp.bfloat16), "row").astype(jnp.float32),
        lax.psum(grad_ffn_one_out.astype(jnp.bfloat16), "row").astype(jnp.float32),
        lax.psum(grad_qkv_weight.astype(jnp.bfloat16), "row").astype(jnp.float32),
        lax.psum(grad_attn_weight.astype(jnp.bfloat16), "row").astype(jnp.float32),
        lax.psum(grad_conv_weight_in.astype(jnp.bfloat16), "row").astype(jnp.float32),
        lax.psum(grad_conv_weight_out.astype(jnp.bfloat16), "row").astype(jnp.float32),
        lax.psum(grad_ffn_two_in.astype(jnp.bfloat16), "row").astype(jnp.float32),
        lax.psum(grad_ffn_two_out.astype(jnp.bfloat16), "row").astype(jnp.float32),
    )
    return (
        output,
        input_grad,
        small_grads[0],
        small_grads[1],
        small_grads[2],
        small_grads[3],
        small_grads[4],
        small_grads[5],
        small_grads[6],
        large_grads[0],
        large_grads[1],
        large_grads[2],
        large_grads[3],
        large_grads[4],
        large_grads[5],
        large_grads[6],
        large_grads[7],
    )


BF16 = jnp.bfloat16
F32 = jnp.float32
PLANES = 4
VMEM = pltpu.VMEM
DMA = pltpu.SemaphoreType.DMA
VMEM_LIMIT = 60 * 1024 * 1024


class Place:
    def __init__(self):
        seq = lax.axis_index("seq")
        self.x = lax.axis_index("row")
        self.z = seq // 4
        self.yc = lax.rem(seq, 4)

    def flip(self, k):
        y, c, x = self.yc // 2, lax.rem(self.yc, 2), self.x
        c = 1 - c if k & 1 else c
        y = 1 - y if k & 2 else y
        x = 1 - x if k & 4 else x
        return x, y * 2 + c

    def dev(self, k):
        x, yc = self.flip(k)
        return {"seq": self.z * 4 + yc, "row": x}

    def slot(self, k):
        x, yc = self.flip(k)
        return x * 4 + yc

    def plane(self, k):
        return lax.rem(self.z + k, PLANES)

    def zdev(self, k):
        return {"seq": self.plane(k) * 4 + self.yc, "row": self.x}

    def enter(self):
        barrier = pltpu.get_barrier_semaphore()
        partners = [self.dev(k) for k in range(1, 8)] + [self.zdev(k) for k in range(1, PLANES)]
        for partner in partners:
            pl.semaphore_signal(barrier, inc=1, device_id=partner)
        pl.semaphore_wait(barrier, len(partners))


def remote(src, dst, send_sem, recv_sem, dev):
    return pltpu.make_async_remote_copy(src, dst, send_sem, recv_sem, device_id=dev)


def dot(left, right, left_dim=1, right_dim=0):
    return lax.dot_general(
        left, right, (((left_dim,), (right_dim,)), ((), ())), preferred_element_type=F32
    )


def all_gather(place, blocks, sems, process, order):
    send, recv = sems
    half = blocks.shape[1] // 2
    own = place.slot(0)
    sent = []

    def push(rows, to, sem):
        copy = remote(rows, rows, send.at[sem], recv.at[sem], place.dev(to))
        copy.start()
        sent.append(copy)

    def arrived(rows, sem):
        remote(rows, rows, send.at[sem], recv.at[sem], place.dev(1)).wait_recv()

    for k in (4, 2, 1):
        push(blocks.at[own], k, k)

    def fetch(k):
        slot = place.slot(k)
        rows = blocks.at[slot]
        if k == 6:
            arrived(blocks.at[slot, pl.ds(0, half)], 6)
            arrived(blocks.at[slot, pl.ds(half, half)], 8)
            push(rows, 1, 7)
        elif k:
            arrived(rows, k)
        if k == 2:
            push(blocks.at[slot, pl.ds(0, half)], 4, 6)
            push(rows, 1, 3)
        if k == 4:
            push(blocks.at[slot, pl.ds(half, half)], 2, 8)
            push(rows, 1, 5)
        return slot

    for step in order:
        if isinstance(step, tuple):
            for k, slot in [(k, fetch(k)) for k in step]:
                process(k, slot)
        else:
            step()
    return sent


class Scatter:
    def __init__(self, place, refs):
        self.place = place
        self.part, self.staged, self.sibling, self.reduced, self.received, self.send, self.recv = refs
        self.sent = []

    @staticmethod
    def scratch(rows, width):
        return [
            VMEM((4, rows, width), F32),
            VMEM((4, rows, width), BF16),
            VMEM((4, rows, width), BF16),
            VMEM((3, rows, width), BF16),
            VMEM((3, rows, width), BF16),
            DMA((8,)),
            DMA((8,)),
        ]

    def push(self, src, dst, sem, k):
        copy = remote(src, dst, self.send.at[sem], self.recv.at[sem], self.place.dev(k))
        copy.start()
        self.sent.append(copy)

    def emit(self, k, value):
        index = k // 2
        if k % 2:
            self.staged[index] = value.astype(BF16)
            self.push(self.staged.at[index], self.sibling.at[index], index, 1)
        else:
            self.part[index] = value

    def finish(self, k):
        index = k // 2
        into = self.sibling.at[index]
        remote(into, into, self.send.at[index], self.recv.at[index], self.place.dev(1)).wait_recv()
        total = self.part[index] + self.sibling[index].astype(F32)
        if k:
            self.reduced[index - 1] = total.astype(BF16)
            self.push(self.reduced.at[index - 1], self.received.at[index - 1], 3 + index, k)
        else:
            self.part[0] = total

    def total(self):
        value = self.part[0]
        for index in range(3):
            into = self.received.at[index]
            remote(
                into, into, self.send.at[4 + index], self.recv.at[4 + index], self.place.dev(1)
            ).wait_recv()
            value = value + self.received[index].astype(F32)
        return value

    def drain(self):
        for copy in self.sent:
            copy.wait_send()


class Refs:
    pass


def kernel_call(body, collective, ins, outs, scratch):
    in_names = list(ins)
    out_names = list(outs)
    scratch_names = list(scratch)
    flat_scratch = []
    counts = []
    for name in scratch_names:
        item = scratch[name]
        counts.append(len(item) if isinstance(item, list) else 0)
        flat_scratch += item if isinstance(item, list) else [item]

    def kernel(*refs):
        held = Refs()
        at = 0
        for name in in_names + out_names:
            setattr(held, name, refs[at])
            at += 1
        for name, count in zip(scratch_names, counts):
            setattr(held, name, refs[at : at + count] if count else refs[at])
            at += max(count, 1)
        body(held)

    results = pl.pallas_call(
        kernel,
        out_shape=[jax.ShapeDtypeStruct(shape, dtype) for shape, dtype, unused in outs.values()],
        in_specs=[pl.BlockSpec(memory_space=space) for unused, space in ins.values()],
        out_specs=[pl.BlockSpec(memory_space=space) for unused, unused_type, space in outs.values()],
        scratch_shapes=flat_scratch,
        compiler_params=pltpu.CompilerParams(
            collective_id=collective, has_side_effects=True, vmem_limit_bytes=VMEM_LIMIT
        ),
    )(*[array for array, unused in ins.values()])
    return dict(zip(out_names, results))


def gather_rows(place, src, dst, sems):
    send, recv, local_sem = sems
    own = pltpu.make_async_copy(src.at[place.yc], dst.at[place.z * 4 + place.yc], local_sem)
    own.start()
    copies = []
    for k in (2, 3, 1):
        unused, to = place.flip(k)
        copy = remote(
            src.at[to], dst.at[place.z * 4 + place.yc], send.at[k], recv.at[k], place.dev(k)
        )
        copy.start()
        copies.append((k, to, copy))

    def along_z():
        own.wait()
        for k, to, copy in copies:
            into = dst.at[place.z * 4 + to]
            remote(into, into, send.at[k], recv.at[k], place.dev(k)).wait_recv()
        sent = [copy for unused, unused_to, copy in copies]
        rows = dst.at[pl.ds(place.z * 4, 4)]
        for k in (1, 2, 3):
            copy = remote(rows, rows, send.at[3 + k], recv.at[3 + k], place.zdev(k))
            copy.start()
            sent.append(copy)

        def finish():
            for k in (1, 2, 3):
                into = dst.at[pl.ds(place.plane(4 - k) * 4, 4)]
                remote(into, into, send.at[3 + k], recv.at[3 + k], place.zdev(k)).wait_recv()
            for copy in sent:
                copy.wait_send()

        return finish

    return along_z


def gather_blocks(place, src, dst, sems):
    send, recv, local_sem = sems
    own = pltpu.make_async_copy(src, dst.at[place.z], local_sem)
    own.start()
    sent = []
    for k in (1, 2, 3):
        copy = remote(src, dst.at[place.z], send.at[k], recv.at[k], place.zdev(k))
        copy.start()
        sent.append(copy)

    def finish():
        own.wait()
        for k in (1, 2, 3):
            into = dst.at[place.plane(4 - k)]
            remote(into, into, send.at[k], recv.at[k], place.zdev(k)).wait_recv()
        for copy in sent:
            copy.wait_send()

    return finish


GATHER_SEMS = [DMA((8,)), DMA((8,)), DMA]


class PlaneSum:
    def __init__(self, place, refs):
        self.place = place
        self.staged, self.received, self.send, self.recv = refs
        self.sent = []

    @staticmethod
    def scratch(rows, width):
        return [VMEM((3, rows, width), BF16), VMEM((3, rows, width), BF16), DMA((4,)), DMA((4,))]

    def put(self, k, value):
        self.staged[k - 1] = value.astype(BF16)
        copy = remote(
            self.staged.at[k - 1],
            self.received.at[k - 1],
            self.send.at[k],
            self.recv.at[k],
            self.place.zdev(k),
        )
        copy.start()
        self.sent.append(copy)

    def total(self, value):
        for k in (1, 2, 3):
            into = self.received.at[k - 1]
            remote(into, into, self.send.at[k], self.recv.at[k], self.place.zdev(k)).wait_recv()
            value = value + self.received[k - 1].astype(F32)
        for copy in self.sent:
            copy.wait_send()
        return value


class Exchange:
    def __init__(self, place, refs, partners):
        self.place = place
        self.blocks, self.send, self.recv = refs
        self.partners = partners
        self.sent = []

    def start(self, source):
        own = self.place.slot(0)
        for k in self.partners:
            copy = remote(
                source(k), self.blocks.at[own], self.send.at[k], self.recv.at[k], self.place.dev(k)
            )
            copy.start()
            self.sent.append(copy)

    def wait(self):
        for k in self.partners:
            into = self.blocks.at[self.place.slot(k)]
            remote(into, into, self.send.at[k], self.recv.at[k], self.place.dev(k)).wait_recv()
        for copy in self.sent:
            copy.wait_send()


BLOCK_ORDER = ((0,), (1,), (2, 4), (3,), (5,))


def forward_blocks(place, blocks, sems, process, scatter):
    order = BLOCK_ORDER + (
        lambda: scatter.finish(2),
        lambda: scatter.finish(4),
        (6,),
        (7,),
        lambda: scatter.finish(6),
        lambda: scatter.finish(0),
    )
    return all_gather(place, blocks, sems, process, order)


def flat(ref):
    value = ref[...]
    return value.reshape(value.shape[0] * value.shape[1], value.shape[2])


def ffn_forward(place, refs, blocks, hidden, w_in, w_out, sems, scatter):
    def process(k, slot):
        value = dot(blocks[slot], flat(w_in))
        hidden[slot] = value
        active = sigmoid_linear(value).astype(BF16)
        scatter.emit(k, dot(active, flat(w_out)))

    sent = forward_blocks(place, blocks, sems, process, scatter)
    value = scatter.total()
    for copy in sent:
        copy.wait_send()
    scatter.drain()
    return value


def ffn_backward(place, blocks, grads, hidden, hidden_grads, active, w_in, w_out, sems, scatter):
    def process(k, slot):
        value = hidden[slot]
        sigma = jax.nn.sigmoid(value)
        active[slot] = (value * sigma).astype(BF16)
        back = dot(grads[slot], flat(w_out), 1, 1)
        low = (back * (sigma * (1.0 + value * (1.0 - sigma)))).astype(BF16)
        hidden_grads[slot] = low
        scatter.emit(k, dot(low, flat(w_in), 1, 1))

    return forward_blocks(place, grads, sems, process, scatter)


def token_dot(left, columns, right):
    count, rows, unused = left.shape
    taken = left[:, :, columns].reshape(count * rows, -1)
    return dot(taken, flat(right), 0, 0)


def ffn_weight_grads(place, refs, blocks, grads, hidden_grads, active):
    sum_out = PlaneSum(place, refs.sum_out)
    sum_in = PlaneSum(place, refs.sum_in)

    def out_term(plane):
        return token_dot(active, pl.ds(pl.multiple_of(plane * 128, 128), 128), grads)

    def in_term(plane):
        return token_dot(blocks, pl.ds(pl.multiple_of(plane * 256, 256), 256), hidden_grads)

    for k in (1, 2, 3):
        sum_out.put(k, out_term(place.plane(k)))
    for k in (1, 2, 3):
        sum_in.put(k, in_term(place.plane(k)))
    own_out = out_term(place.z)
    own_in = in_term(place.z)
    return sum_out, own_out, sum_in, own_in


def ffn_share_grads(place, refs, sum_out, own_out, sum_in, own_in):
    total = sum_out.total(own_out).astype(BF16)
    own = place.slot(0)
    share_out = Exchange(place, refs.share_out, (4,))
    share_out.blocks[own] = total
    share_out.start(lambda k: share_out.blocks.at[own])
    total = sum_in.total(own_in).astype(BF16)
    refs.in_total[...] = total.reshape(refs.in_total.shape)
    share_in = Exchange(place, refs.share_in, tuple(range(1, 8)))
    share_in.blocks[own] = refs.in_total[place.yc]
    share_in.start(lambda k: refs.in_total.at[place.flip(k)[1]])
    share_out.wait()
    mine = place.yc
    for x in range(2):
        refs.grad_out[pl.ds(x * 128, 128), :] = share_out.blocks[x * 4 + mine].astype(F32)
    share_in.wait()
    for slot in range(8):
        x, yc = slot // 4, slot % 4
        piece = share_in.blocks[slot].astype(F32)
        for plane in range(PLANES):
            column = ((plane * 4 + yc) * 2 + x) * 128
            refs.grad_in[:, column : column + 128] = piece[:, plane * 128 : plane * 128 + 128]


def ffn_grad_scratch():
    return dict(
        sum_out=PlaneSum.scratch(128, 1024),
        sum_in=PlaneSum.scratch(256, 512),
        in_total=VMEM((4, 64, 512), BF16),
        share_out=[VMEM((8, 128, 1024), BF16), DMA((8,)), DMA((8,))],
        share_in=[VMEM((8, 64, 512), BF16), DMA((8,)), DMA((8,))],
    )


AG_SEMS = [DMA((10,)), DMA((10,))]


def norm_rows(values, gain):
    normed, saved = norm_forward(values, gain)
    return normed.astype(BF16), saved


def norm_input_grad(grads, gain, saved):
    unit_part, inverse = saved
    scaled = grads * gain
    gain_grad = jnp.sum(grads * unit_part, axis=0, keepdims=True)
    input_part = inverse * (
        scaled
        - jnp.mean(scaled, axis=-1, keepdims=True)
        - unit_part * jnp.mean(scaled * unit_part, axis=-1, keepdims=True)
    )
    return input_part, gain_grad


def ffn1_forward_body(refs):
    place = Place()
    place.enter()
    along_z = gather_rows(place, refs.w_in_rows.at[place.x], refs.w_in, refs.gather_in)
    refs.blocks[place.slot(0)] = norm_rows(refs.stream[...], refs.gain[...])[0]
    finish_in = along_z()
    finish_out = gather_blocks(place, refs.w_out_rows.at[place.x], refs.w_out, refs.gather_out)
    finish_in()
    finish_out()
    scatter = Scatter(place, refs.scatter)
    total = ffn_forward(
        place, refs, refs.blocks, refs.hidden, refs.w_in, refs.w_out, refs.ag, scatter
    )
    refs.stream_out[...] = refs.stream[...] + 0.5 * total


def ffn1_forward(stream, gain, w_in, w_out):
    ins = dict(
        stream=(stream, VMEM),
        gain=(gain[None], VMEM),
        w_in_rows=(w_in, pl.ANY),
        w_out_rows=(w_out, pl.ANY),
    )
    outs = dict(
        stream_out=((128, 1024), F32, VMEM),
        blocks=((8, 128, 1024), BF16, VMEM),
        hidden=((8, 128, 512), F32, VMEM),
        w_in=((16, 64, 512), BF16, VMEM),
        w_out=((4, 128, 1024), BF16, VMEM),
    )
    scratch = dict(
        gather_in=GATHER_SEMS,
        gather_out=GATHER_SEMS,
        ag=AG_SEMS,
        scatter=Scatter.scratch(128, 1024),
    )
    return kernel_call(ffn1_forward_body, 1, ins, outs, scratch)


def ffn1_backward_body(refs):
    place = Place()
    place.enter()
    grad = refs.grad[...]
    refs.grads[place.slot(0)] = (0.5 * grad).astype(BF16)
    scatter = Scatter(place, refs.scatter)
    sent = ffn_backward(
        place,
        refs.blocks,
        refs.grads,
        refs.hidden,
        refs.hidden_grads,
        refs.active,
        refs.w_in,
        refs.w_out,
        refs.ag,
        scatter,
    )
    terms = ffn_weight_grads(place, refs, refs.blocks, refs.grads, refs.hidden_grads, refs.active)
    unused, saved = norm_forward(refs.stream[...], refs.gain[...])
    input_part, gain_grad = norm_input_grad(scatter.total(), refs.gain[...], saved)
    refs.grad_stream[...] = grad + input_part
    refs.grad_gain[...] = gain_grad
    for copy in sent:
        copy.wait_send()
    scatter.drain()
    ffn_share_grads(place, refs, *terms)


def ffn1_backward(grad, stream, gain, kept):
    ins = dict(
        grad=(grad, VMEM),
        stream=(stream, VMEM),
        gain=(gain[None], VMEM),
        blocks=(kept["blocks"], VMEM),
        hidden=(kept["hidden"], VMEM),
        w_in=(kept["w_in"], VMEM),
        w_out=(kept["w_out"], VMEM),
    )
    outs = dict(
        grad_stream=((128, 1024), F32, VMEM),
        grad_gain=((1, 1024), F32, VMEM),
        grad_in=((64, 4096), F32, VMEM),
        grad_out=((256, 1024), F32, VMEM),
    )
    scratch = dict(
        grads=VMEM((8, 128, 1024), BF16),
        hidden_grads=VMEM((8, 128, 512), BF16),
        active=VMEM((8, 128, 512), BF16),
        ag=AG_SEMS,
        scatter=Scatter.scratch(128, 1024),
        **ffn_grad_scratch(),
    )
    return kernel_call(ffn1_backward_body, 2, ins, outs, scratch)


def ffn2_body(refs):
    place = Place()
    place.enter()
    along_z = gather_rows(place, refs.w_in_rows.at[place.x], refs.w_in, refs.gather_in)
    own = place.slot(0)
    stream = refs.stream[...]
    low, saved = norm_rows(stream, refs.gain[...])
    refs.blocks[own] = low
    finish_in = along_z()
    finish_out = gather_blocks(place, refs.w_out_rows.at[place.x], refs.w_out, refs.gather_out)
    finish_in()
    finish_out()
    scatter = Scatter(place, refs.scatter)
    total = ffn_forward(
        place, refs, refs.blocks, refs.hidden, refs.w_in, refs.w_out, refs.ag, scatter
    )
    final, saved_final = norm_forward(stream + 0.5 * total, refs.gain_out[...])
    refs.output[...] = final.astype(BF16)
    grad, refs.grad_gain_out[...] = norm_input_grad(
        refs.cotangent[...].astype(F32), refs.gain_out[...], saved_final
    )
    refs.grads[own] = (0.5 * grad).astype(BF16)
    scatter = Scatter(place, refs.scatter_back)
    sent = ffn_backward(
        place,
        refs.blocks,
        refs.grads,
        refs.hidden,
        refs.hidden_grads,
        refs.active,
        refs.w_in,
        refs.w_out,
        refs.ag_back,
        scatter,
    )
    terms = ffn_weight_grads(place, refs, refs.blocks, refs.grads, refs.hidden_grads, refs.active)
    input_part, refs.grad_gain[...] = norm_input_grad(scatter.total(), refs.gain[...], saved)
    refs.grad_stream[...] = grad + input_part
    for copy in sent:
        copy.wait_send()
    scatter.drain()
    ffn_share_grads(place, refs, *terms)


def ffn2_both(stream, cotangent, gain, gain_out, w_in, w_out):
    ins = dict(
        stream=(stream, VMEM),
        cotangent=(cotangent, VMEM),
        gain=(gain[None], VMEM),
        gain_out=(gain_out[None], VMEM),
        w_in_rows=(w_in, pl.ANY),
        w_out_rows=(w_out, pl.ANY),
    )
    outs = dict(
        output=((128, 1024), BF16, VMEM),
        grad_stream=((128, 1024), F32, VMEM),
        grad_gain=((1, 1024), F32, VMEM),
        grad_gain_out=((1, 1024), F32, VMEM),
        grad_in=((64, 4096), F32, VMEM),
        grad_out=((256, 1024), F32, VMEM),
    )
    scratch = dict(
        blocks=VMEM((8, 128, 1024), BF16),
        hidden=VMEM((8, 128, 512), F32),
        w_in=VMEM((16, 64, 512), BF16),
        w_out=VMEM((4, 128, 1024), BF16),
        gather_in=GATHER_SEMS,
        gather_out=GATHER_SEMS,
        ag=AG_SEMS,
        scatter=Scatter.scratch(128, 1024),
        grads=VMEM((8, 128, 1024), BF16),
        hidden_grads=VMEM((8, 128, 512), BF16),
        active=VMEM((8, 128, 512), BF16),
        ag_back=AG_SEMS,
        scatter_back=Scatter.scratch(128, 1024),
        **ffn_grad_scratch(),
    )
    return kernel_call(ffn2_body, 3, ins, outs, scratch)


def ffn_rows(w_in, w_out):
    columns = w_in.reshape(64, PLANES, 4, 2, 128)
    return jnp.transpose(columns, (3, 2, 0, 1, 4)).reshape(2, 4, 64, 512), w_out.reshape(2, 128, -1)


def gather_half(place, src, dst, sems):
    send, recv, local_sem = sems
    mine = place.z // 2 == place.x
    at = lax.rem(place.z, 2)
    own = pltpu.make_async_copy(src, dst.at[at], local_sem)
    copies = [
        remote(src, dst.at[at], send.at[k], recv.at[at], place.zdev(k)) for k in (1, 2, 3)
    ]

    @pl.when(mine)
    def start():
        own.start()
        for copy in copies:
            copy.start()

    def finish():
        for half in range(2):

            @pl.when(place.z != place.x * 2 + half)
            def arrive():
                into = dst.at[half]
                remote(into, into, send.at[0], recv.at[half], place.zdev(1)).wait_recv()

        @pl.when(mine)
        def done():
            own.wait()
            for copy in copies:
                copy.wait_send()

    return finish


class HalfSum:
    def __init__(self, place, refs):
        self.place = place
        self.staged, self.received, self.result, self.send, self.recv, self.last = refs

    @staticmethod
    def scratch(width):
        return [
            VMEM((2, 64, width), BF16),
            VMEM((PLANES, 64, width), BF16),
            VMEM((64, width), BF16),
            DMA((2,)),
            DMA((PLANES,)),
            DMA((2,)),
        ]

    def copies(self):
        place = self.place
        for half in range(2):
            plane = place.x * 2 + half
            yield (
                plane,
                remote(
                    self.staged.at[half],
                    self.received.at[place.z],
                    self.send.at[half],
                    self.recv.at[place.z],
                    {"seq": plane * 4 + place.yc, "row": place.x},
                ),
            )

    def put(self, value):
        self.staged[...] = value.astype(BF16).reshape(self.staged.shape)
        for plane, copy in self.copies():

            @pl.when(self.place.z != plane)
            def start(copy=copy):
                copy.start()

    def add(self):
        place = self.place

        @pl.when(place.z // 2 == place.x)
        def reduce():
            self.received[place.z] = self.staged[lax.rem(place.z, 2)]
            for plane in range(PLANES):

                @pl.when(place.z != plane)
                def arrive():
                    into = self.received.at[plane]
                    remote(
                        into, into, self.send.at[0], self.recv.at[plane], place.zdev(1)
                    ).wait_recv()

            value = self.received[0].astype(F32)
            for plane in range(1, PLANES):
                value = value + self.received[plane].astype(F32)
            self.result[...] = value.astype(BF16)
            self.hand_over().start()

        for plane, copy in self.copies():

            @pl.when(self.place.z != plane)
            def drain(copy=copy):
                copy.wait_send()

    def hand_over(self):
        return remote(
            self.result, self.result, self.last.at[0], self.last.at[1], self.place.dev(4)
        )

    def wait(self):
        mine = self.place.z // 2 == self.place.x

        @pl.when(mine)
        def sent():
            self.hand_over().wait_send()

        @pl.when(jnp.logical_not(mine))
        def arrived():
            self.hand_over().wait_recv()

        return self.result[...].astype(F32)


class Turn:
    def __init__(self, place, refs):
        self.place = place
        self.staged, self.received, self.send, self.recv = refs
        self.sent = []

    @staticmethod
    def scratch(rows):
        return [VMEM((PLANES, rows, 128), BF16), VMEM((PLANES, rows, 128), BF16), DMA((4,)), DMA((4,))]

    def start(self):
        place = self.place
        for k in (2, 1, 3):
            copy = remote(
                self.staged.at[place.plane(k)],
                self.received.at[place.z],
                self.send.at[k],
                self.recv.at[k],
                place.zdev(k),
            )
            copy.start()
            self.sent.append(copy)
        self.received[place.z] = self.staged[place.z]

    def wait(self):
        for k in (1, 2, 3):
            into = self.received.at[self.place.plane(4 - k)]
            remote(into, into, self.send.at[k], self.recv.at[k], self.place.zdev(k)).wait_recv()
        for copy in self.sent:
            copy.wait_send()


def swap_halves(values):
    lane = lax.broadcasted_iota(jnp.int32, values.shape, 1)
    return jnp.where(lane % 64 < 32, pltpu.roll(values, 96, 1), pltpu.roll(values, 32, 1))


def head_part(values, head):
    return values[:, head * 64 : head * 64 + 64]


def pack_wide(turn, pair, left, right):
    row, head = divmod(pair, 2)
    for block in range(4):
        turn.staged[pair, block * 128 : block * 128 + 128, :] = jnp.concatenate(
            [head_part(left[row * 4 + block], head), head_part(right[row * 4 + block], head)], axis=1
        )


def pack_narrow(turn, pair, values):
    row, head = divmod(pair, 2)
    for block in range(2):
        turn.staged[pair, block * 128 : block * 128 + 128, :] = jnp.concatenate(
            [
                head_part(values[row * 4 + block], head),
                head_part(values[row * 4 + block + 2], head),
            ],
            axis=1,
        )


def unpack_narrow(turn, row, block):
    rows = slice((block % 2) * 128, (block % 2) * 128 + 128)
    return jnp.concatenate(
        [head_part(turn.received[row * 2 + head, rows, :], block // 2) for head in range(2)], axis=1
    )


def unpack_wide(turn, row, block, side):
    rows = slice(block * 128, block * 128 + 128)
    return jnp.concatenate(
        [head_part(turn.received[row * 2 + head, rows, :], side) for head in range(2)], axis=1
    )


QUERY_BLOCK = 256


def open_heads(refs, turn_qk, turn_v):
    for plane in range(PLANES):
        rows = slice(plane * 512, plane * 512 + 512)
        pair = turn_qk.received[plane]
        scaled = (pair[:, :64].astype(F32) * HEAD_DIM ** (-0.5)).astype(BF16)
        refs.queries[rows, :] = jnp.concatenate([scaled, refs.seg_query[rows, :]], axis=1)
        refs.keys[rows, :] = jnp.concatenate([pair[:, 64:], refs.seg_key[rows, :]], axis=1)
        both = turn_v.received[plane]
        turned = jnp.transpose(both.astype(F32)).astype(BF16)
        refs.values[plane * 512 : plane * 512 + 256, :] = both[:, :64]
        refs.values[plane * 512 + 256 : plane * 512 + 512, :] = both[:, 64:]
        refs.values_t[:, plane * 512 : plane * 512 + 256] = turned[:64]
        refs.values_t[:, plane * 512 + 256 : plane * 512 + 512] = turned[64:]


def attend(refs, turn_mix):
    def plane_step(plane, unused):
        parts = []
        for half in range(2):
            first = plane * 512 + half * 256
            query = refs.queries[pl.ds(pl.multiple_of(first, 256), QUERY_BLOCK), :]
            scores = dot(refs.keys[...], query, 1, 1)
            top = jnp.max(scores, axis=0, keepdims=True)
            weights = jnp.exp(scores - top)
            total = jnp.sum(weights, axis=0, keepdims=True)
            low = (weights * (1.0 / total)).astype(BF16)
            parts.append(jnp.transpose(dot(refs.values_t[...], low)))
            refs.log_total[plane * 2 + half] = jnp.broadcast_to(top + jnp.log(total), (8, 256))
        turn_mix.staged[plane] = jnp.concatenate(parts, axis=1).astype(BF16)
        return unused

    lax.fori_loop(0, PLANES, plane_step, 0)


OUT_ORDER = (1, 3, 5, 7, 2, 4, 6, 0)


def attention_forward(place, refs, stream, scatter):
    blocks = refs.attn_blocks
    blocks[place.slot(0)] = norm_rows(stream, refs.gain_attn[...])[0]
    refs.finish_qkv()

    def process(k, slot):
        value = dot(blocks[slot], flat(refs.w_qkv))
        rows = pl.ds(pl.multiple_of(lax.rem(slot, 4) * 128, 128), 128)
        cos, sin = refs.cos[rows, :], refs.sin[rows, :]
        query, key = value[:, :128], value[:, 128:256]
        refs.q_rows[slot] = (query * cos + swap_halves(query) * sin).astype(BF16)
        refs.k_rows[slot] = (key * cos + swap_halves(key) * sin).astype(BF16)
        refs.v_rows[slot] = value[:, 256:].astype(BF16)

    sent = all_gather(
        place, blocks, refs.attn_ag, process, BLOCK_ORDER + ((6,), (7,))
    )
    turn_qk, turn_v = Turn(place, refs.turn_qk), Turn(place, refs.turn_v)
    for pair in range(PLANES):
        pack_wide(turn_qk, pair, refs.q_rows, refs.k_rows)
        pack_narrow(turn_v, pair, refs.v_rows)
    turn_qk.start()
    turn_v.start()
    turn_qk.wait()
    turn_v.wait()
    open_heads(refs, turn_qk, turn_v)
    turn_mix = Turn(place, refs.turn_mix)
    attend(refs, turn_mix)
    turn_mix.start()
    refs.finish_wo()
    turn_mix.wait()
    for slot in range(8):
        refs.mixed[slot] = unpack_narrow(turn_mix, slot // 4, slot % 4)
    for k in OUT_ORDER:
        scatter.emit(k, dot(refs.mixed[place.slot(k)], flat(refs.w_o)))
    for k in (6, 2, 4, 0):
        scatter.finish(k)
    for copy in sent:
        copy.wait_send()
    total = scatter.total()
    scatter.drain()
    return stream + total


def attention_forward_body(refs):
    place = Place()
    place.enter()
    along_z = gather_rows(place, refs.qkv_rows.at[place.x], refs.w_qkv, refs.gather_qkv)
    refs.finish_qkv = along_z()
    refs.finish_wo = gather_half(place, refs.o_rows, refs.w_o, refs.gather_o)
    scatter = Scatter(place, refs.scatter)
    refs.stream_out[...] = attention_forward(place, refs, refs.stream[...], scatter)


def attention_kept():
    return dict(
        attn_blocks=((8, 128, 1024), BF16, VMEM),
        w_qkv=((16, 64, 384), BF16, VMEM),
        w_o=((2, 64, 1024), BF16, VMEM),
        queries=((2048, 128), BF16, VMEM),
        keys=((2048, 128), BF16, VMEM),
        values=((2048, 64), BF16, VMEM),
        log_total=((8, 8, 256), F32, VMEM),
        mixed=((8, 128, 128), BF16, VMEM),
    )


def attention_forward_call(stream, gain, rows, tables, features):
    ins = dict(
        stream=(stream, VMEM),
        gain_attn=(gain[None], VMEM),
        qkv_rows=(rows[0], pl.ANY),
        o_rows=(rows[1], pl.ANY),
        cos=(tables[0], VMEM),
        sin=(tables[1], VMEM),
        seg_query=(features[0], VMEM),
        seg_key=(features[1], VMEM),
    )
    outs = dict(stream_out=((128, 1024), F32, VMEM), **attention_kept())
    scratch = dict(
        gather_qkv=GATHER_SEMS,
        gather_o=GATHER_SEMS,
        attn_ag=AG_SEMS,
        q_rows=VMEM((8, 128, 128), BF16),
        k_rows=VMEM((8, 128, 128), BF16),
        v_rows=VMEM((8, 128, 128), BF16),
        turn_qk=Turn.scratch(512),
        turn_v=Turn.scratch(256),
        turn_mix=Turn.scratch(256),
        values_t=VMEM((64, 2048), BF16),
        scatter=Scatter.scratch(128, 1024),
    )
    return kernel_call(attention_forward_body, 4, ins, outs, scratch)


def attend_back(refs, turn_qk, turn_v):
    refs.key_grad[...] = jnp.zeros_like(refs.key_grad)
    refs.value_grad[...] = jnp.zeros_like(refs.value_grad)

    def plane_step(plane, unused):
        parts = []
        for half in range(2):
            first = pl.multiple_of(plane * 512 + half * 256, 256)
            query = refs.queries[pl.ds(first, QUERY_BLOCK), :]
            grad = refs.mix_grads[pl.ds(first, QUERY_BLOCK), :]
            log_total = refs.log_total[plane * 2 + half][:1]
            probs = jnp.exp(dot(refs.keys[...], query, 1, 1) - log_total)
            prob_grads = dot(refs.values[...], grad, 1, 1)
            delta = jnp.sum(probs * prob_grads, axis=0, keepdims=True)
            low = (probs * (prob_grads - delta)).astype(BF16)
            refs.key_grad[...] += dot(low, query[:, :64])
            refs.value_grad[...] += dot(probs.astype(BF16), grad)
            parts.append(jnp.transpose(dot(refs.keys_t[...], low)) * HEAD_DIM ** (-0.5))
        refs.query_grad[pl.ds(pl.multiple_of(plane * 512, 512), 512), :] = jnp.concatenate(
            parts, axis=0
        )
        return unused

    lax.fori_loop(0, PLANES, plane_step, 0)
    for plane in range(PLANES):
        rows = slice(plane * 512, plane * 512 + 512)
        turn_qk.staged[plane] = jnp.concatenate(
            [refs.query_grad[rows, :], refs.key_grad[rows, :]], axis=1
        ).astype(BF16)
        first = plane * 512
        turn_v.staged[plane] = jnp.concatenate(
            [refs.value_grad[first : first + 256, :], refs.value_grad[first + 256 : first + 512, :]],
            axis=1,
        ).astype(BF16)


def attention_backward(place, refs, grad, stream, scatter):
    grads = refs.attn_grads
    grads[place.slot(0)] = grad.astype(BF16)

    def process(k, slot):
        refs.mix_rows[slot] = dot(grads[slot], flat(refs.w_o), 1, 1).astype(BF16)

    sent = all_gather(place, grads, refs.attn_ag, process, BLOCK_ORDER + ((6,), (7,)))
    turn_mix = Turn(place, refs.turn_mix)
    for pair in range(PLANES):
        pack_narrow(turn_mix, pair, refs.mix_rows)
    turn_mix.start()
    sum_o = HalfSum(place, refs.sum_o)
    sum_o.put(dot(flat(refs.mixed), flat(grads), 0, 0))
    turned = jnp.transpose(refs.keys[...].astype(F32))
    refs.keys_t[...] = turned[:64].astype(BF16)
    turn_mix.wait()
    for plane in range(PLANES):
        both = turn_mix.received[plane]
        refs.mix_grads[plane * 512 : plane * 512 + 256, :] = both[:, :64]
        refs.mix_grads[plane * 512 + 256 : plane * 512 + 512, :] = both[:, 64:]
    turn_qk, turn_v = Turn(place, refs.turn_qk), Turn(place, refs.turn_v)
    attend_back(refs, turn_qk, turn_v)
    turn_qk.start()
    turn_v.start()
    sum_o.add()
    turn_qk.wait()
    turn_v.wait()
    for slot in range(8):
        row, block = divmod(slot, 4)
        cos = refs.cos[block * 128 : block * 128 + 128, :]
        sin = refs.sin[block * 128 : block * 128 + 128, :]
        query = unpack_wide(turn_qk, row, block, 0).astype(F32)
        key = unpack_wide(turn_qk, row, block, 1).astype(F32)
        refs.qkv_grads[slot] = jnp.concatenate(
            [
                (query * cos - swap_halves(query) * sin).astype(BF16),
                (key * cos - swap_halves(key) * sin).astype(BF16),
                unpack_narrow(turn_v, row, block),
            ],
            axis=1,
        )
    for k in OUT_ORDER:
        scatter.emit(k, dot(refs.qkv_grads[place.slot(k)], flat(refs.w_qkv), 1, 1))
    for k in (6, 2, 4, 0):
        scatter.finish(k)
    sum_qkv = PlaneSum(place, refs.sum_qkv)

    def term(plane):
        return token_dot(
            refs.attn_blocks, pl.ds(pl.multiple_of(plane * 256, 256), 256), refs.qkv_grads
        )

    for k in (1, 2, 3):
        sum_qkv.put(k, term(place.plane(k)))
    own_term = term(place.z)
    unused, saved = norm_forward(stream, refs.gain_attn[...])
    input_part, gain_grad = norm_input_grad(scatter.total(), refs.gain_attn[...], saved)
    for copy in sent:
        copy.wait_send()
    scatter.drain()
    return grad + input_part, gain_grad, sum_o, sum_qkv, own_term


def share_rows(place, total, total_ref, share):
    total_ref[...] = total.astype(BF16).reshape(total_ref.shape)
    share.blocks[place.slot(0)] = total_ref[place.yc]
    share.start(lambda k: total_ref.at[place.flip(k)[1]])


def attention_backward_body(refs):
    place = Place()
    place.enter()
    scatter = Scatter(place, refs.scatter)
    refs.grad_stream[...], refs.grad_gain[...], sum_o, sum_qkv, own_term = attention_backward(
        place, refs, refs.grad[...], refs.stream[...], scatter
    )
    share = Exchange(place, refs.share_qkv, tuple(range(1, 8)))
    share_rows(place, sum_qkv.total(own_term), refs.qkv_total, share)
    refs.grad_o[...] = sum_o.wait()
    share.wait()
    for slot in range(8):
        x, yc = divmod(slot, 4)
        piece = share.blocks[slot].astype(F32)
        for kind in range(3):
            for head in range(2):
                column = kind * 1024 + ((x * 2 + head) * 4 + yc) * 64
                start = kind * 128 + head * 64
                refs.grad_qkv[:, column : column + 64] = piece[:, start : start + 64]


def attention_backward_call(grad, stream, gain, tables, kept):
    ins = dict(
        grad=(grad, VMEM),
        stream=(stream, VMEM),
        gain_attn=(gain[None], VMEM),
        cos=(tables[0], VMEM),
        sin=(tables[1], VMEM),
        **{name: (kept[name], VMEM) for name in attention_kept()},
    )
    outs = dict(
        grad_stream=((128, 1024), F32, VMEM),
        grad_gain=((1, 1024), F32, VMEM),
        grad_qkv=((64, 3072), F32, VMEM),
        grad_o=((64, 1024), F32, VMEM),
    )
    scratch = dict(
        attn_ag=AG_SEMS,
        attn_grads=VMEM((8, 128, 1024), BF16),
        mix_rows=VMEM((8, 128, 128), BF16),
        mix_grads=VMEM((2048, 64), BF16),
        keys_t=VMEM((64, 2048), BF16),
        turn_qk=Turn.scratch(512),
        turn_v=Turn.scratch(256),
        turn_mix=Turn.scratch(256),
        query_grad=VMEM((2048, 64), F32),
        key_grad=VMEM((2048, 64), F32),
        value_grad=VMEM((2048, 64), F32),
        qkv_grads=VMEM((8, 128, 384), BF16),
        scatter=Scatter.scratch(128, 1024),
        sum_o=HalfSum.scratch(1024),
        sum_qkv=PlaneSum.scratch(256, 384),
        qkv_total=VMEM((4, 64, 384), BF16),
        share_qkv=[VMEM((8, 64, 384), BF16), DMA((8,)), DMA((8,))],
    )
    return kernel_call(attention_backward_body, 5, ins, outs, scratch)


def head_rows(w_qkv):
    columns = w_qkv.reshape(64, 3, 2, 2, 4, 64)
    return jnp.transpose(columns, (2, 4, 0, 1, 3, 5)).reshape(2, 4, 64, 384)


def plane_tables(frames):
    cos, sin = rotary_tables(frames)
    return jnp.tile(cos, (1, 4)), jnp.tile(jnp.concatenate([-sin, sin], axis=1), (1, 2))


def segment_features(segments):
    same = (segments[:, None] == jnp.arange(64)[None, :]).astype(F32)
    inside = (jnp.arange(64) < 4).astype(F32)[None, :]
    return (-MASKED * (1.0 - same) * inside).astype(BF16), (-same).astype(BF16)


class Edges:
    def __init__(self, place, refs):
        self.place = place
        self.staged, self.received, self.send, self.recv = refs

    @staticmethod
    def scratch():
        return [VMEM((2, 2, 16, 128), BF16), VMEM((2, 2, 16, 128), BF16), DMA((2,)), DMA((2,))]

    def copies(self):
        place = self.place
        for side, inside, step in ((0, place.z < PLANES - 1, 1), (1, place.z > 0, -1)):
            plane = jnp.clip(place.z + step, 0, PLANES - 1)
            yield (
                side,
                inside,
                remote(
                    self.staged.at[side],
                    self.received.at[side],
                    self.send.at[side],
                    self.recv.at[side],
                    {"seq": plane * 4 + place.yc, "row": place.x},
                ),
            )

    def start(self, blocks):
        for row in range(2):
            self.staged[0, row] = blocks[row * 4 + 3, 112:128, :]
            self.staged[1, row] = blocks[row * 4, 0:16, :]
        for side, inside, copy in self.copies():

            @pl.when(inside)
            def start(copy=copy):
                copy.start()

    def wait(self, blocks, padded):
        for slot in range(8):
            row, block = divmod(slot, 4)
            padded[slot, 16:144, :] = blocks[slot].astype(F32)
            if block > 0:
                padded[slot, 0:16, :] = blocks[slot - 1, 112:128, :].astype(F32)
            if block < 3:
                padded[slot, 144:160, :] = blocks[slot + 1, 0:16, :].astype(F32)
        place = self.place
        for side, outside in ((0, place.z == 0), (1, place.z == PLANES - 1)):
            first, rows = ((0, slice(0, 16)), (3, slice(144, 160)))[side]
            into = self.received.at[side]

            @pl.when(outside)
            def nothing():
                for row in range(2):
                    padded[row * 4 + first, rows, :] = jnp.zeros((16, 128), F32)

            @pl.when(jnp.logical_not(outside))
            def arrive():
                remote(
                    into, into, self.send.at[side], self.recv.at[side], place.zdev(1)
                ).wait_recv()
                for row in range(2):
                    padded[row * 4 + first, rows, :] = self.received[side, row].astype(F32)

        for side, inside, copy in self.copies():

            @pl.when(inside)
            def drain(copy=copy):
                copy.wait_send()


def lane_is(index):
    return lax.broadcasted_iota(jnp.int32, (128, 128), 1) == index


def put_columns(tile, slot, first, second):
    return jnp.where(lane_is(slot), first, jnp.where(lane_is(slot + 8), second, tile))


def share_columns(place, refs, tile):
    share = Exchange(place, refs, tuple(range(1, 8)))
    own = place.slot(0)
    share.blocks[own] = jnp.transpose(tile)[:16]
    share.start(lambda k: share.blocks.at[own])
    share.wait()
    return share.blocks[...]


def back_to_columns(first, second):
    rows = jnp.concatenate([first, second, jnp.zeros((112, 128), F32)], axis=0)
    return jnp.transpose(rows)


def column(tile, slot):
    return jnp.sum(jnp.where(lane_is(slot), tile, 0.0), axis=1, keepdims=True)


def kept_frames(value, offset, before, after):
    if offset < 0:
        return jnp.where(before <= offset, value, 0.0)
    if offset > 0:
        return jnp.where(after > offset, value, 0.0)
    return value


CHUNK = 64


def convolve(refs):
    taps = [refs.taps[j : j + 1, :] for j in range(KERNEL)]

    def step(slot, tile):
        for first in range(0, 128, CHUNK):
            rows = slice(first, first + CHUNK)
            before, after = refs.before[slot, rows, :], refs.after[slot, rows, :]
            total = jnp.zeros((CHUNK, 128), F32)
            for j in range(KERNEL):
                start = first + j + 1
                value = refs.glu_padded[slot, start : start + CHUNK, :]
                total = total + taps[j] * kept_frames(value, j - HALF, before, after)
            refs.conv[slot, rows, :] = total
        value = refs.conv[slot]
        mean = jnp.mean(value, axis=1, keepdims=True)
        center = value - mean
        return put_columns(tile, slot, mean, jnp.sum(center * center, axis=1, keepdims=True))

    return lax.fori_loop(0, 8, step, jnp.zeros((128, 128), F32))


def inner_norm(refs, slot):
    mean, inverse = column(refs.inner_stats[...], slot), column(refs.inner_stats[...], slot + 8)
    unit_part = (refs.conv[slot] - mean) * inverse
    return unit_part, inverse


def conv_forward(place, refs, stream, scatter):
    blocks = refs.conv_blocks
    blocks[place.slot(0)] = norm_rows(stream, refs.gain_conv[...])[0]
    refs.finish_ci()

    def process(k, slot):
        value = dot(blocks[slot], flat(refs.w_ci))
        refs.gate_up[slot] = value
        refs.glu[slot] = (value[:, :128] * jax.nn.sigmoid(value[:, 128:])).astype(BF16)

    sent = all_gather(place, blocks, refs.conv_ag, process, BLOCK_ORDER + ((6,), (7,)))
    edges = Edges(place, refs.edges)
    edges.start(refs.glu)
    edges.wait(refs.glu, refs.glu_padded)
    stats = share_columns(place, refs.stats, convolve(refs))
    means, spreads = stats[:, :8], stats[:, 8:]
    mean = jnp.mean(means, axis=0)
    spread = jnp.sum(spreads + 128.0 * jnp.square(means - mean[None]), axis=0) / 1024.0
    refs.inner_stats[...] = back_to_columns(mean, lax.rsqrt(spread + EPSILON))
    refs.finish_co()
    for k in OUT_ORDER:
        slot = place.slot(k)
        unit_part, unused = inner_norm(refs, slot)
        active = sigmoid_linear(unit_part * refs.gain_inner[...]).astype(BF16)
        refs.conv_active[slot] = active
        scatter.emit(k, dot(active, flat(refs.w_co)))
    for k in (6, 2, 4, 0):
        scatter.finish(k)
    for copy in sent:
        copy.wait_send()
    total = scatter.total()
    scatter.drain()
    return stream + total


def conv_forward_body(refs):
    place = Place()
    place.enter()
    along_z = gather_rows(place, refs.ci_rows.at[place.x], refs.w_ci, refs.gather_ci)
    refs.finish_ci = along_z()
    refs.finish_co = gather_half(place, refs.co_rows, refs.w_co, refs.gather_co)
    scatter = Scatter(place, refs.scatter)
    refs.stream_out[...] = conv_forward(place, refs, refs.stream[...], scatter)


def conv_kept():
    return dict(
        conv_blocks=((8, 128, 1024), BF16, VMEM),
        w_ci=((16, 64, 256), BF16, VMEM),
        w_co=((2, 64, 1024), BF16, VMEM),
        gate_up=((8, 128, 256), F32, VMEM),
        glu_padded=((8, 160, 128), F32, VMEM),
        conv=((8, 128, 128), F32, VMEM),
        inner_stats=((128, 128), F32, VMEM),
        conv_active=((8, 128, 128), BF16, VMEM),
    )


STATS = [VMEM((8, 16, 128), F32), DMA((8,)), DMA((8,))]


def conv_inputs(gain, inner, taps, reach):
    return dict(
        gain_conv=(gain[None], VMEM),
        gain_inner=(inner, VMEM),
        taps=(taps, VMEM),
        before=(reach[0], VMEM),
        after=(reach[1], VMEM),
    )


def conv_forward_call(stream, rows, inputs):
    ins = dict(
        stream=(stream, VMEM), ci_rows=(rows[0], pl.ANY), co_rows=(rows[1], pl.ANY), **inputs
    )
    outs = dict(stream_out=((128, 1024), F32, VMEM), **conv_kept())
    scratch = dict(
        gather_ci=GATHER_SEMS,
        gather_co=GATHER_SEMS,
        conv_ag=AG_SEMS,
        glu=VMEM((8, 128, 128), BF16),
        edges=Edges.scratch(),
        stats=STATS,
        scatter=Scatter.scratch(128, 1024),
    )
    return kernel_call(conv_forward_body, 6, ins, outs, scratch)


def convolve_back(refs):
    taps = [refs.taps[j : j + 1, :] for j in range(KERNEL)]
    refs.tap_sums[...] = jnp.zeros_like(refs.tap_sums)

    def step(slot, unused):
        for first in range(0, 128, CHUNK):
            rows = slice(first, first + CHUNK)
            before, after = refs.before[slot, rows, :], refs.after[slot, rows, :]
            total = jnp.zeros((CHUNK, 128), F32)
            grad = refs.conv_grad_padded[slot, first + 16 : first + 16 + CHUNK, :]
            for j in range(KERNEL):
                offset = j - HALF
                start = first + 16 - offset
                value = refs.conv_grad_padded[slot, start : start + CHUNK, :]
                total = total + taps[j] * kept_frames(value, -offset, before, after)
                start = first + 16 + offset
                value = refs.glu_padded[slot, start : start + CHUNK, :]
                product = kept_frames(value * grad, offset, before, after)
                refs.tap_sums[j] += jnp.sum(product.reshape(CHUNK // 8, 8, 128), axis=0)
            refs.glu_grad[slot, rows, :] = total
        return unused

    lax.fori_loop(0, 8, step, 0)
    return jnp.sum(refs.tap_sums[...], axis=1)


def conv_backward(place, refs, grad, stream, scatter):
    grads = refs.conv_grads
    grads[place.slot(0)] = grad.astype(BF16)
    gain = refs.gain_inner[...]

    def process(k, slot):
        back = dot(grads[slot], flat(refs.w_co), 1, 1)
        unit_part, unused = inner_norm(refs, slot)
        refs.inner_grad[slot] = back * sigmoid_linear_grad(unit_part * gain)

    sent = all_gather(place, grads, refs.conv_ag, process, BLOCK_ORDER + ((6,), (7,)))

    def sums(slot, current):
        tile, gain_grad = current
        value = refs.inner_grad[slot]
        unit_part, unused = inner_norm(refs, slot)
        scaled = value * gain
        tile = put_columns(
            tile,
            slot,
            jnp.sum(scaled, axis=1, keepdims=True),
            jnp.sum(scaled * unit_part, axis=1, keepdims=True),
        )
        return tile, gain_grad + jnp.sum(value * unit_part, axis=0, keepdims=True)

    tile, inner_gain_grad = lax.fori_loop(
        0, 8, sums, (jnp.zeros((128, 128), F32), jnp.zeros((1, 128), F32))
    )
    stats = share_columns(place, refs.stats, tile)
    means = jnp.sum(stats, axis=0) / 1024.0
    refs.grad_stats[...] = back_to_columns(means[:8], means[8:])
    sum_co = HalfSum(place, refs.sum_co)
    sum_co.put(dot(flat(refs.conv_active), flat(grads), 0, 0))

    def input_grad(slot, unused):
        unit_part, inverse = inner_norm(refs, slot)
        tile = refs.grad_stats[...]
        refs.conv_grad[slot] = (
            inverse
            * (
                refs.inner_grad[slot] * gain
                - column(tile, slot)
                - unit_part * column(tile, slot + 8)
            )
        ).astype(BF16)
        return unused

    lax.fori_loop(0, 8, input_grad, 0)
    edges = Edges(place, refs.edges)
    edges.start(refs.conv_grad)
    edges.wait(refs.conv_grad, refs.conv_grad_padded)
    tap_grads = convolve_back(refs)
    for k in OUT_ORDER:
        slot = place.slot(k)
        value = refs.gate_up[slot]
        glu_grad, sigma = refs.glu_grad[slot], jax.nn.sigmoid(value[:, 128:])
        refs.gate_grads[slot] = jnp.concatenate(
            [glu_grad * sigma, glu_grad * value[:, :128] * sigma * (1.0 - sigma)], axis=1
        ).astype(BF16)
        scatter.emit(k, dot(refs.gate_grads[slot], flat(refs.w_ci), 1, 1))
    for k in (6, 2, 4, 0):
        scatter.finish(k)
    sum_ci = PlaneSum(place, refs.sum_ci)

    def term(plane):
        return token_dot(
            refs.conv_blocks, pl.ds(pl.multiple_of(plane * 256, 256), 256), refs.gate_grads
        )

    for k in (1, 2, 3):
        sum_ci.put(k, term(place.plane(k)))
    own_term = term(place.z)
    unused, saved = norm_forward(stream, refs.gain_conv[...])
    input_part, gain_grad = norm_input_grad(scatter.total(), refs.gain_conv[...], saved)
    for copy in sent:
        copy.wait_send()
    scatter.drain()
    sum_co.add()
    return grad + input_part, gain_grad, inner_gain_grad, tap_grads, sum_co, sum_ci, own_term


def conv_backward_body(refs):
    place = Place()
    place.enter()
    scatter = Scatter(place, refs.scatter)
    (
        refs.grad_stream[...],
        refs.grad_gain[...],
        refs.grad_inner[...],
        refs.grad_taps[...],
        sum_co,
        sum_ci,
        own_term,
    ) = conv_backward(place, refs, refs.grad[...], refs.stream[...], scatter)
    share = Exchange(place, refs.share_ci, tuple(range(1, 8)))
    share_rows(place, sum_ci.total(own_term), refs.ci_total, share)
    refs.grad_co[...] = sum_co.wait()
    share.wait()
    for slot in range(8):
        x, yc = divmod(slot, 4)
        piece = share.blocks[slot].astype(F32)
        for kind in range(2):
            for half in range(2):
                column_at = kind * 1024 + ((x * 2 + half) * 4 + yc) * 64
                start = kind * 128 + half * 64
                refs.grad_ci[:, column_at : column_at + 64] = piece[:, start : start + 64]


def conv_backward_call(grad, stream, inputs, kept):
    ins = dict(
        grad=(grad, VMEM),
        stream=(stream, VMEM),
        **inputs,
        **{name: (kept[name], VMEM) for name in conv_kept()},
    )
    outs = dict(
        grad_stream=((128, 1024), F32, VMEM),
        grad_gain=((1, 1024), F32, VMEM),
        grad_inner=((1, 128), F32, VMEM),
        grad_taps=((32, 128), F32, VMEM),
        grad_ci=((64, 2048), F32, VMEM),
        grad_co=((64, 1024), F32, VMEM),
    )
    scratch = dict(
        conv_ag=AG_SEMS,
        conv_grads=VMEM((8, 128, 1024), BF16),
        inner_grad=VMEM((8, 128, 128), F32),
        grad_stats=VMEM((128, 128), F32),
        conv_grad=VMEM((8, 128, 128), BF16),
        conv_grad_padded=VMEM((8, 160, 128), F32),
        glu_grad=VMEM((8, 128, 128), F32),
        gate_grads=VMEM((8, 128, 256), BF16),
        tap_sums=VMEM((32, 8, 128), F32),
        edges=Edges.scratch(),
        stats=STATS,
        scatter=Scatter.scratch(128, 1024),
        sum_co=HalfSum.scratch(1024),
        sum_ci=PlaneSum.scratch(256, 256),
        ci_total=VMEM((4, 64, 256), BF16),
        share_ci=[VMEM((8, 64, 256), BF16), DMA((8,)), DMA((8,))],
    )
    return kernel_call(conv_backward_body, 7, ins, outs, scratch)


def channel_rows(w_in):
    columns = w_in.reshape(64, 2, 2, 2, 4, 64)
    return jnp.transpose(columns, (2, 4, 0, 1, 3, 5)).reshape(2, 4, 64, 256)


def own_channels(array, x, yc):
    split = array.reshape(array.shape[:-1] + (2, 2, 4, 64))
    split = lax.dynamic_index_in_dim(split, x, split.ndim - 4, keepdims=False)
    split = lax.dynamic_index_in_dim(split, yc, split.ndim - 2, keepdims=False)
    return split.reshape(array.shape[:-1] + (128,))


def all_channels(array, x, yc):
    lead = array.shape[:-1]
    split = array.reshape(lead + (1, 2, 1, 64))
    at_x = (jnp.arange(2) == x).reshape(2, 1, 1, 1)
    at_yc = (jnp.arange(4) == yc).reshape(4, 1)
    return jnp.where(jnp.logical_and(at_x, at_yc), split, 0.0).reshape(lead + (1024,))


def segment_reach(frames, lengths):
    ends = jnp.cumsum(lengths, axis=1)
    starts = ends - lengths
    place = frames[None, :]
    inside = jnp.logical_and(place[:, :, None] >= starts[:, None, :], place[:, :, None] < ends[:, None, :])
    before = jnp.sum(jnp.where(inside, starts[:, None, :], 0), axis=2) - place
    after = jnp.sum(jnp.where(inside, ends[:, None, :], 0), axis=2) - place

    def wide(array):
        return jnp.broadcast_to(array.astype(jnp.int32).reshape(8, 128, 1), (8, 128, 128))

    return wide(before), wide(after)


def local_planes(
    inputs,
    lengths,
    gain_ffn1,
    gain_attn,
    gain_conv,
    gain_inner,
    gain_ffn2,
    gain_out,
    conv_kernel,
    ffn1_in,
    ffn1_out,
    attn_qkv,
    attn_out,
    conv_in,
    conv_out,
    ffn2_in,
    ffn2_out,
    cotangent,
):
    position_index = lax.axis_index("seq")
    stream = inputs[0].astype(jnp.float32)
    rows_one = ffn_rows(ffn1_in, ffn1_out)
    rows_two = ffn_rows(ffn2_in, ffn2_out)
    kept_one = ffn1_forward(stream, gain_ffn1, *rows_one)
    stream_one = kept_one["stream_out"]
    plane = position_index // 4
    all_lengths = lax.all_gather(lengths[0], "row", axis=0)
    head_lengths = lax.dynamic_index_in_dim(all_lengths, plane // 2, 0, keepdims=False)
    features = segment_features(segment_of(jnp.arange(2048, dtype=jnp.int32), head_lengths))
    tables = plane_tables(plane * 512 + jnp.arange(512, dtype=jnp.int32))
    kept_two = attention_forward_call(
        stream_one, gain_attn, (head_rows(attn_qkv), attn_out), tables, features
    )
    stream_two = kept_two["stream_out"]
    reach = segment_reach(plane * 512 + jnp.arange(512, dtype=jnp.int32), all_lengths)
    row_index, column_index = lax.axis_index("row"), lax.rem(position_index, 4)
    taps = own_channels(conv_kernel.astype(jnp.float32), row_index, column_index)
    inner = own_channels(gain_inner[None], row_index, column_index)
    conv_args = conv_inputs(gain_conv, inner, taps, reach)
    kept_three = conv_forward_call(stream_two, (channel_rows(conv_in), conv_out), conv_args)
    stream_three = kept_three["stream_out"]
    last = ffn2_both(stream_three, cotangent[0], gain_ffn2, gain_out, *rows_two)
    output = last["output"][None]
    grad_three = last["grad_stream"]
    grad_gain_five, grad_gain_six = last["grad_gain"][0], last["grad_gain_out"][0]
    third = conv_backward_call(grad_three, stream_two, conv_args, kept_three)
    grad_two = third["grad_stream"]
    grad_gain_three = third["grad_gain"][0]
    grad_gain_four = all_channels(third["grad_inner"], row_index, column_index)[0]
    kernel_grad = all_channels(third["grad_taps"][:KERNEL], row_index, column_index)
    second = attention_backward_call(grad_two, stream_one, gain_attn, tables, kept_two)
    grad_one = second["grad_stream"]
    grad_gain_two = second["grad_gain"][0]
    first = ffn1_backward(grad_one, stream, gain_ffn1, kept_one)
    input_grad = first["grad_stream"][None]
    grad_gain_one = first["grad_gain"][0]
    small_grads = lax.psum(
        (
            grad_gain_one,
            grad_gain_two,
            grad_gain_three,
            grad_gain_four,
            grad_gain_five,
            grad_gain_six,
            kernel_grad,
        ),
        ("seq", "row"),
    )
    large_grads = (
        first["grad_in"],
        first["grad_out"],
        second["grad_qkv"],
        second["grad_o"],
        third["grad_ci"],
        third["grad_co"],
        last["grad_in"],
        last["grad_out"],
    )
    return (
        output,
        input_grad,
        small_grads[0],
        small_grads[1],
        small_grads[2],
        small_grads[3],
        small_grads[4],
        small_grads[5],
        small_grads[6],
        large_grads[0],
        large_grads[1],
        large_grads[2],
        large_grads[3],
        large_grads[4],
        large_grads[5],
        large_grads[6],
        large_grads[7],
    )


def solution(mesh):
    return jax.shard_map(
        local_planes if mesh.shape["seq"] == 16 and mesh.shape["row"] == 2 else local,
        mesh=mesh,
        in_specs=(
            P("row", "seq", None),
            P("row", None),
            P(),
            P(),
            P(),
            P(),
            P(),
            P(),
            P(),
            P("seq", None),
            P("seq", None),
            P("seq", None),
            P("seq", None),
            P("seq", None),
            P("seq", None),
            P("seq", None),
            P("seq", None),
            P("row", "seq", None),
        ),
        out_specs=(
            P("row", "seq", None),
            P("row", "seq", None),
            P(),
            P(),
            P(),
            P(),
            P(),
            P(),
            P(),
            P("seq", None),
            P("seq", None),
            P("seq", None),
            P("seq", None),
            P("seq", None),
            P("seq", None),
            P("seq", None),
            P("seq", None),
        ),
        check_vma=False,
    )
```

```python
import math

import jax
import jax.numpy as jnp
from jax import lax
from jax.experimental import pallas as pl
from jax.experimental.pallas import tpu as pltpu
from jax.sharding import PartitionSpec as P

HEADS = 16
HEAD_DIM = 64
KERNEL = 31
HALF = 15


EPSILON = 1e-05
MASKED = -1e30


def with_halo(block, sides, width):
    for axis, dim in sides:
        count = lax.axis_size(axis)
        forward = [(i, i + 1) for i in range(count - 1)]
        backward = [(target, source) for source, target in forward]
        low = lax.ppermute(
            lax.slice_in_dim(block, block.shape[dim] - width, None, axis=dim), axis, forward
        )
        high = lax.ppermute(lax.slice_in_dim(block, 0, width, axis=dim), axis, backward)
        block = jnp.concatenate([low, block, high], axis=dim)
    return block


def shifted(array, axis, by):
    size = lax.axis_size(axis)
    return lax.ppermute(array, axis, [(i, (i + by) % size) for i in range(size)])


def segment_of(positions, seg_lengths):
    boundary = jnp.cumsum(seg_lengths)[:-1]
    return jnp.sum((positions[:, None] >= boundary[None, :]).astype(jnp.int32), axis=1)


def rotary_tables(positions):
    half_dim = HEAD_DIM // 2
    inverse = jnp.exp(-jnp.log(10000.0) * jnp.arange(half_dim, dtype=jnp.float32) / half_dim)
    angles = positions.astype(jnp.float32)[:, None] * inverse[None, :]
    return (jnp.cos(angles), jnp.sin(angles))


def split_heads(values):
    return values.reshape(values.shape[0], HEADS, HEAD_DIM)


def rotate(values, cos_table, sin_table):
    half_dim = HEAD_DIM // 2
    shaped = split_heads(values)
    first_half = shaped[..., :half_dim]
    second_half = shaped[..., half_dim:]
    cos_heads = cos_table[:, None, :]
    sin_heads = sin_table[:, None, :]
    turned = jnp.concatenate(
        [
            first_half * cos_heads - second_half * sin_heads,
            second_half * cos_heads + first_half * sin_heads,
        ],
        axis=-1,
    )
    return turned.reshape(values.shape)


def unrotate(grads, cos_table, sin_table):
    half_dim = HEAD_DIM // 2
    shaped = split_heads(grads)
    first_half = shaped[..., :half_dim]
    second_half = shaped[..., half_dim:]
    cos_heads = cos_table[:, None, :]
    sin_heads = sin_table[:, None, :]
    turned = jnp.concatenate(
        [
            first_half * cos_heads + second_half * sin_heads,
            second_half * cos_heads - first_half * sin_heads,
        ],
        axis=-1,
    )
    return turned.reshape(grads.shape)


def norm_forward(values, gain):
    center = values - jnp.mean(values, axis=-1, keepdims=True)
    spread = jnp.mean(center * center, axis=-1, keepdims=True)
    inverse = lax.rsqrt(spread + EPSILON)
    unit_part = center * inverse
    return (unit_part * gain, (unit_part, inverse))


def norm_backward(grads, gain, saved):
    unit_part, inverse = saved
    scaled = grads * gain
    gain_grad = jnp.sum(grads * unit_part, axis=0)
    input_part = inverse * (
        scaled
        - jnp.mean(scaled, axis=-1, keepdims=True)
        - unit_part * jnp.mean(scaled * unit_part, axis=-1, keepdims=True)
    )
    return (input_part, gain_grad)


def sigmoid_linear(values):
    return values * jax.nn.sigmoid(values)


def sigmoid_linear_grad(values):
    sigma = jax.nn.sigmoid(values)
    return sigma * (1.0 + values * (1.0 - sigma))


def project(left_side, weight):
    return (
        jnp.dot(
            left_side,
            lax.all_gather(weight, "seq", axis=0, tiled=True),
            preferred_element_type=jnp.float32,
        ),
        weight,
    )


def project_back(grad_side, weight):
    return lax.dot_general(
        grad_side,
        lax.all_gather(weight, "seq", axis=0, tiled=True),
        (((1,), (1,)), ((), ())),
        preferred_element_type=jnp.float32,
    )


def weight_grad(left_side, grad_side):
    return lax.psum_scatter(
        lax.dot_general(
            left_side, grad_side, (((0,), (0,)), ((), ())), preferred_element_type=jnp.float32
        ).astype(jnp.bfloat16),
        "seq",
        scatter_dimension=0,
        tiled=True,
    ).astype(jnp.float32)


def over_blocks(advance, running, pieces):
    total_rows = pieces[0].shape[0]
    block_size = math.gcd(total_rows, 512)
    number = total_rows // block_size
    stacked = tuple((piece.reshape((number, block_size) + piece.shape[1:]) for piece in pieces))

    def scan_step(current, block_item):
        block_index, blocks = block_item
        return (advance(current, blocks, block_index * block_size), None)

    running, unused = lax.scan(scan_step, running, (jnp.arange(number, dtype=jnp.int32), stacked))
    return running


def block_scores(query_heads, key_heads, query_segments, key_segments):
    scale = HEAD_DIM ** (-0.5)
    raw_scores = (
        jnp.einsum("qhd,khd->hqk", query_heads, key_heads, preferred_element_type=jnp.float32)
        * scale
    )
    return jnp.where((query_segments[:, None] == key_segments[None, :])[None], raw_scores, MASKED)


def pair_grads(
    query_rows, grad_rows, log_total, delta, query_segments, key_rows, value_rows, key_segments
):
    scale = HEAD_DIM ** (-0.5)
    query_heads = split_heads(query_rows)
    grad_heads = split_heads(grad_rows)
    key_heads = split_heads(key_rows)
    value_heads = split_heads(value_rows)
    probs = jnp.exp(
        block_scores(query_heads, key_heads, query_segments, key_segments) - log_total[:, :, None]
    )
    prob_grads = jnp.einsum(
        "qhd,khd->hqk", grad_heads, value_heads, preferred_element_type=jnp.float32
    )
    score_grads = (probs * (prob_grads - delta[:, :, None])).astype(jnp.bfloat16)
    query_grad = (
        jnp.einsum("hqk,khd->qhd", score_grads, key_heads, preferred_element_type=jnp.float32)
        * scale
    )
    key_grad = (
        jnp.einsum("hqk,qhd->khd", score_grads, query_heads, preferred_element_type=jnp.float32)
        * scale
    )
    value_grad = jnp.einsum(
        "hqk,qhd->khd", probs.astype(jnp.bfloat16), grad_heads, preferred_element_type=jnp.float32
    )
    return (
        query_grad.reshape(query_rows.shape),
        key_grad.reshape(key_rows.shape),
        value_grad.reshape(value_rows.shape),
    )


def local(
    inputs,
    lengths,
    gain_ffn1,
    gain_attn,
    gain_conv,
    gain_inner,
    gain_ffn2,
    gain_out,
    conv_kernel,
    ffn1_in,
    ffn1_out,
    attn_qkv,
    attn_out,
    conv_in,
    conv_out,
    ffn2_in,
    ffn2_out,
    cotangent,
):
    frame_count = inputs.shape[1]
    model_width = inputs.shape[2]
    device_count = lax.axis_size("seq")
    position_index = lax.axis_index("seq")
    seg_lengths = lengths[0]
    first_frame = position_index * frame_count
    local_frames = jnp.arange(frame_count, dtype=jnp.int32)
    positions = first_frame + local_frames
    query_segments = segment_of(positions, seg_lengths)
    cos_table, sin_table = rotary_tables(positions)
    stream = inputs[0].astype(jnp.float32)
    normed_one, saved_one = norm_forward(stream, gain_ffn1)
    normed_one_low = normed_one.astype(jnp.bfloat16)
    hidden_one, kept_ffn1_in = project(normed_one_low, ffn1_in)
    active_one = sigmoid_linear(hidden_one).astype(jnp.bfloat16)
    branch_one, kept_ffn1_out = project(active_one, ffn1_out)
    stream_one = stream + 0.5 * branch_one
    normed_two, saved_two = norm_forward(stream_one, gain_attn)
    normed_two_low = normed_two.astype(jnp.bfloat16)
    projected, kept_qkv = project(normed_two_low, attn_qkv)
    query_low = rotate(projected[:, :model_width], cos_table, sin_table).astype(jnp.bfloat16)
    key_low = rotate(projected[:, model_width : 2 * model_width], cos_table, sin_table).astype(
        jnp.bfloat16
    )
    value_low = projected[:, 2 * model_width :].astype(jnp.bfloat16)
    query_heads = split_heads(query_low)

    def stats_step(current, blocks, first_row):
        top_score, denominator = current
        key_block = blocks[0]
        key_segments = segment_of(
            first_row + jnp.arange(key_block.shape[0], dtype=jnp.int32), seg_lengths
        )
        masked = block_scores(query_heads, split_heads(key_block), query_segments, key_segments)
        new_top = jnp.maximum(top_score, jnp.max(masked, axis=-1))
        denominator = denominator * jnp.exp(top_score - new_top) + jnp.sum(
            jnp.exp(masked - new_top[:, :, None]), axis=-1
        )
        return (new_top, denominator)

    top_init = jnp.full((HEADS, frame_count), MASKED, jnp.float32)
    total_init = jnp.zeros((HEADS, frame_count), jnp.float32)
    top_score, denominator = over_blocks(
        stats_step, (top_init, total_init), (lax.all_gather(key_low, "seq", axis=0, tiled=True),)
    )
    log_total = top_score + jnp.log(denominator)

    def value_step(current, blocks, first_row):
        mixed_sum, rest_sum = current
        key_block, value_block = blocks
        key_segments = segment_of(
            first_row + jnp.arange(key_block.shape[0], dtype=jnp.int32), seg_lengths
        )
        probs = jnp.exp(
            block_scores(query_heads, split_heads(key_block), query_segments, key_segments)
            - log_total[:, :, None]
        )
        probs_high = probs.astype(jnp.bfloat16)
        probs_rest = (probs - probs_high.astype(jnp.float32)).astype(jnp.bfloat16)
        value_heads = split_heads(value_block)
        mixed_sum = mixed_sum + jnp.einsum(
            "hqk,khd->qhd", probs_high, value_heads, preferred_element_type=jnp.float32
        )
        rest_sum = rest_sum + jnp.einsum(
            "hqk,khd->qhd", probs_rest, value_heads, preferred_element_type=jnp.float32
        )
        return (mixed_sum, rest_sum)

    zero_heads = jnp.zeros((frame_count, HEADS, HEAD_DIM), jnp.float32)
    mixed_sum, rest_sum = over_blocks(
        value_step,
        (zero_heads, zero_heads),
        (
            lax.all_gather(key_low, "seq", axis=0, tiled=True),
            lax.all_gather(value_low, "seq", axis=0, tiled=True),
        ),
    )
    exact_sum = mixed_sum + rest_sum
    mixed_low = mixed_sum.reshape(frame_count, model_width).astype(jnp.bfloat16)
    branch_two, kept_attn_out = project(mixed_low, attn_out)
    stream_two = stream_one + branch_two
    normed_three, saved_three = norm_forward(stream_two, gain_conv)
    normed_three_low = normed_three.astype(jnp.bfloat16)
    gate_up, kept_conv_in = project(normed_three_low, conv_in)
    first_part = gate_up[:, :model_width]
    gate_sigma = jax.nn.sigmoid(gate_up[:, model_width:])
    glu_low = (first_part * gate_sigma).astype(jnp.bfloat16)
    padded = with_halo(glu_low, (("seq", 0),), HALF).astype(jnp.float32)
    padded_segments = segment_of(
        first_frame - HALF + jnp.arange(frame_count + 2 * HALF, dtype=jnp.int32), seg_lengths
    )
    kernel_taps = conv_kernel.astype(jnp.float32)
    conv_values = jnp.zeros((frame_count, model_width), jnp.float32)
    for offset in range(KERNEL):
        same_segment = (padded_segments[offset : offset + frame_count] == query_segments).astype(
            jnp.float32
        )
        conv_values = (
            conv_values
            + kernel_taps[offset] * padded[offset : offset + frame_count] * same_segment[:, None]
        )
    normed_four, saved_four = norm_forward(conv_values, gain_inner)
    active_four = sigmoid_linear(normed_four).astype(jnp.bfloat16)
    branch_three, kept_conv_out = project(active_four, conv_out)
    stream_three = stream_two + branch_three
    normed_five, saved_five = norm_forward(stream_three, gain_ffn2)
    normed_five_low = normed_five.astype(jnp.bfloat16)
    hidden_two, kept_ffn2_in = project(normed_five_low, ffn2_in)
    active_two = sigmoid_linear(hidden_two).astype(jnp.bfloat16)
    branch_four, kept_ffn2_out = project(active_two, ffn2_out)
    stream_four = stream_three + 0.5 * branch_four
    final_norm, saved_six = norm_forward(stream_four, gain_out)
    output = final_norm.astype(jnp.bfloat16)[None]
    grad_four, grad_gain_six = norm_backward(cotangent[0].astype(jnp.float32), gain_out, saved_six)
    out_two_low = (0.5 * grad_four).astype(jnp.bfloat16)
    grad_ffn_two_out = weight_grad(active_two, out_two_low)
    hidden_two_low = (project_back(out_two_low, ffn2_out) * sigmoid_linear_grad(hidden_two)).astype(
        jnp.bfloat16
    )
    grad_ffn_two_in = weight_grad(normed_five_low, hidden_two_low)
    input_part, grad_gain_five = norm_backward(
        project_back(hidden_two_low, ffn2_in), gain_ffn2, saved_five
    )
    grad_three = grad_four + input_part
    conv_out_low = grad_three.astype(jnp.bfloat16)
    grad_conv_weight_out = weight_grad(active_four, conv_out_low)
    active_grad = project_back(conv_out_low, conv_out) * sigmoid_linear_grad(normed_four)
    conv_grad, grad_gain_four = norm_backward(active_grad, gain_inner, saved_four)
    conv_grad_low = conv_grad.astype(jnp.bfloat16)
    conv_grad_value = conv_grad_low.astype(jnp.float32)
    rim_grad = with_halo(conv_grad_low, (("seq", 0),), HALF).astype(jnp.float32)
    tap_grads = []
    glu_grad = jnp.zeros((frame_count, model_width), jnp.float32)
    for offset in range(KERNEL):
        same_segment = (padded_segments[offset : offset + frame_count] == query_segments).astype(
            jnp.float32
        )
        tap_grads.append(
            jnp.sum(
                padded[offset : offset + frame_count] * same_segment[:, None] * conv_grad_value,
                axis=0,
            )
        )
        back_start = 2 * HALF - offset
        back_segment = (
            padded_segments[back_start : back_start + frame_count] == query_segments
        ).astype(jnp.float32)
        glu_grad = (
            glu_grad
            + kernel_taps[offset]
            * rim_grad[back_start : back_start + frame_count]
            * back_segment[:, None]
        )
    kernel_grad = jnp.stack(tap_grads, axis=0)
    gate_up_low = jnp.concatenate(
        [glu_grad * gate_sigma, glu_grad * first_part * gate_sigma * (1.0 - gate_sigma)], axis=1
    ).astype(jnp.bfloat16)
    grad_conv_weight_in = weight_grad(normed_three_low, gate_up_low)
    input_part, grad_gain_three = norm_backward(
        project_back(gate_up_low, conv_in), gain_conv, saved_three
    )
    grad_two = grad_three + input_part
    attn_grad_low = grad_two.astype(jnp.bfloat16)
    grad_attn_weight = weight_grad(mixed_low, attn_grad_low)
    mixed_grad_low = project_back(attn_grad_low, attn_out).astype(jnp.bfloat16)
    delta = jnp.transpose(
        jnp.sum(split_heads(mixed_grad_low).astype(jnp.float32) * exact_sum, axis=-1)
    )

    def key_turn(turn_index, current):
        key_rows, value_rows, key_acc, value_acc, query_acc = current
        owner = (position_index - turn_index) % device_count
        key_segments = segment_of(owner * frame_count + local_frames, seg_lengths)
        query_part, key_part, value_part = pair_grads(
            query_low,
            mixed_grad_low,
            log_total,
            delta,
            query_segments,
            key_rows,
            value_rows,
            key_segments,
        )
        key_rows, value_rows = shifted((key_rows, value_rows), "seq", 1)
        key_acc, value_acc = (
            shifted((key_acc + key_part).astype(jnp.bfloat16), "seq", 1).astype(jnp.float32),
            shifted((value_acc + value_part).astype(jnp.bfloat16), "seq", 1).astype(jnp.float32),
        )
        return (key_rows, value_rows, key_acc, value_acc, query_acc + query_part)

    zero_rows = jnp.zeros((frame_count, model_width), jnp.float32)
    unused_keys, unused_values, key_grad, value_grad, query_grad = lax.fori_loop(
        0, device_count, key_turn, (key_low, value_low, zero_rows, zero_rows, zero_rows)
    )
    projected_grad_low = jnp.concatenate(
        [
            unrotate(query_grad, cos_table, sin_table),
            unrotate(key_grad, cos_table, sin_table),
            value_grad,
        ],
        axis=1,
    ).astype(jnp.bfloat16)
    grad_qkv_weight = weight_grad(normed_two_low, projected_grad_low)
    input_part, grad_gain_two = norm_backward(
        project_back(projected_grad_low, attn_qkv), gain_attn, saved_two
    )
    grad_one = grad_two + input_part
    out_one_low = (0.5 * grad_one).astype(jnp.bfloat16)
    grad_ffn_one_out = weight_grad(active_one, out_one_low)
    hidden_one_low = (project_back(out_one_low, ffn1_out) * sigmoid_linear_grad(hidden_one)).astype(
        jnp.bfloat16
    )
    grad_ffn_one_in = weight_grad(normed_one_low, hidden_one_low)
    input_part, grad_gain_one = norm_backward(
        project_back(hidden_one_low, ffn1_in), gain_ffn1, saved_one
    )
    input_grad = (grad_one + input_part)[None]
    small_grads = lax.psum(
        (
            grad_gain_one,
            grad_gain_two,
            grad_gain_three,
            grad_gain_four,
            grad_gain_five,
            grad_gain_six,
            kernel_grad,
        ),
        ("seq", "row"),
    )
    large_grads = (
        grad_ffn_one_in,
        grad_ffn_one_out,
        grad_qkv_weight,
        grad_attn_weight,
        grad_conv_weight_in,
        grad_conv_weight_out,
        grad_ffn_two_in,
        grad_ffn_two_out,
    )
    large_grads = (
        lax.psum(grad_ffn_one_in.astype(jnp.bfloat16), "row").astype(jnp.float32),
        lax.psum(grad_ffn_one_out.astype(jnp.bfloat16), "row").astype(jnp.float32),
        lax.psum(grad_qkv_weight.astype(jnp.bfloat16), "row").astype(jnp.float32),
        lax.psum(grad_attn_weight.astype(jnp.bfloat16), "row").astype(jnp.float32),
        lax.psum(grad_conv_weight_in.astype(jnp.bfloat16), "row").astype(jnp.float32),
        lax.psum(grad_conv_weight_out.astype(jnp.bfloat16), "row").astype(jnp.float32),
        lax.psum(grad_ffn_two_in.astype(jnp.bfloat16), "row").astype(jnp.float32),
        lax.psum(grad_ffn_two_out.astype(jnp.bfloat16), "row").astype(jnp.float32),
    )
    return (
        output,
        input_grad,
        small_grads[0],
        small_grads[1],
        small_grads[2],
        small_grads[3],
        small_grads[4],
        small_grads[5],
        small_grads[6],
        large_grads[0],
        large_grads[1],
        large_grads[2],
        large_grads[3],
        large_grads[4],
        large_grads[5],
        large_grads[6],
        large_grads[7],
    )


BF16 = jnp.bfloat16
F32 = jnp.float32
PLANES = 4
VMEM = pltpu.VMEM
DMA = pltpu.SemaphoreType.DMA
VMEM_LIMIT = 60 * 1024 * 1024


class Place:
    def __init__(self):
        seq = lax.axis_index("seq")
        self.x = lax.axis_index("row")
        self.z = seq // 4
        self.yc = lax.rem(seq, 4)

    def flip(self, k):
        y, c, x = self.yc // 2, lax.rem(self.yc, 2), self.x
        c = 1 - c if k & 1 else c
        y = 1 - y if k & 2 else y
        x = 1 - x if k & 4 else x
        return x, y * 2 + c

    def dev(self, k):
        x, yc = self.flip(k)
        return {"seq": self.z * 4 + yc, "row": x}

    def slot(self, k):
        x, yc = self.flip(k)
        return x * 4 + yc

    def plane(self, k):
        return lax.rem(self.z + k, PLANES)

    def zdev(self, k):
        return {"seq": self.plane(k) * 4 + self.yc, "row": self.x}

    def enter(self):
        barrier = pltpu.get_barrier_semaphore()
        partners = [self.dev(k) for k in range(1, 8)] + [self.zdev(k) for k in range(1, PLANES)]
        for partner in partners:
            pl.semaphore_signal(barrier, inc=1, device_id=partner)
        pl.semaphore_wait(barrier, len(partners))


def remote(src, dst, send_sem, recv_sem, dev):
    return pltpu.make_async_remote_copy(src, dst, send_sem, recv_sem, device_id=dev)


def dot(left, right, left_dim=1, right_dim=0):
    return lax.dot_general(
        left, right, (((left_dim,), (right_dim,)), ((), ())), preferred_element_type=F32
    )


def all_gather(place, blocks, sems, process, order):
    send, recv = sems
    half = blocks.shape[1] // 2
    own = place.slot(0)
    sent = []
    slots = {}

    def push(rows, to, sem):
        copy = remote(rows, rows, send.at[sem], recv.at[sem], place.dev(to))
        copy.start()
        sent.append(copy)

    def arrived(rows, sem):
        remote(rows, rows, send.at[sem], recv.at[sem], place.dev(1)).wait_recv()

    for k in (4, 2, 1):
        push(blocks.at[own], k, k)

    def fetch(k):
        slot = place.slot(k)
        rows = blocks.at[slot]
        if k == 6:
            arrived(blocks.at[slot, pl.ds(0, half)], 6)
            arrived(blocks.at[slot, pl.ds(half, half)], 8)
            push(rows, 1, 7)
        elif k:
            arrived(rows, k)
        if k == 2:
            push(blocks.at[slot, pl.ds(0, half)], 4, 6)
            push(rows, 1, 3)
        if k == 4:
            push(blocks.at[slot, pl.ds(half, half)], 2, 8)
            push(rows, 1, 5)
        return slot

    for step in order:
        if callable(step):
            step()
        elif step in slots:
            process(step, slots[step])
        else:
            slots[step] = fetch(step)
    return sent


class Scatter:
    def __init__(self, place, buffers, sems):
        self.place = place
        self.part, self.staged, self.sibling, self.reduced, self.received = buffers
        self.send, self.recv = sems
        self.sent = []

    @staticmethod
    def scratch(rows, width):
        return [
            VMEM((4, rows, width), F32),
            VMEM((4, rows, width), BF16),
            VMEM((4, rows, width), BF16),
            VMEM((3, rows, width), BF16),
            VMEM((3, rows, width), BF16),
        ]

    def push(self, src, dst, sem, k):
        copy = remote(src, dst, self.send.at[sem], self.recv.at[sem], self.place.dev(k))
        copy.start()
        self.sent.append(copy)

    def emit(self, k, value):
        index = k // 2
        if k % 2:
            self.staged[index] = value.astype(BF16)
            self.push(self.staged.at[index], self.sibling.at[index], index, 1)
        else:
            self.part[index] = value

    def finish(self, k):
        index = k // 2
        into = self.sibling.at[index]
        remote(into, into, self.send.at[index], self.recv.at[index], self.place.dev(1)).wait_recv()
        total = self.part[index] + self.sibling[index].astype(F32)
        if k:
            self.reduced[index - 1] = total.astype(BF16)
            self.push(self.reduced.at[index - 1], self.received.at[index - 1], 3 + index, k)
        else:
            self.part[0] = total

    def total(self):
        value = self.part[0]
        for index in range(3):
            into = self.received.at[index]
            remote(
                into, into, self.send.at[4 + index], self.recv.at[4 + index], self.place.dev(1)
            ).wait_recv()
            value = value + self.received[index].astype(F32)
        return value

    def drain(self):
        for copy in self.sent:
            copy.wait_send()


class Refs:
    pass


def kernel_call(body, collective, ins, outs, scratch):
    in_names = list(ins)
    out_names = list(outs)
    scratch_names = list(scratch)
    flat_scratch = []
    counts = []
    for name in scratch_names:
        item = scratch[name]
        counts.append(len(item) if isinstance(item, list) else 0)
        flat_scratch += item if isinstance(item, list) else [item]

    def kernel(*refs):
        held = Refs()
        at = 0
        for name in in_names + out_names:
            setattr(held, name, refs[at])
            at += 1
        for name, count in zip(scratch_names, counts):
            setattr(held, name, refs[at : at + count] if count else refs[at])
            at += max(count, 1)
        body(held)

    results = pl.pallas_call(
        kernel,
        out_shape=[jax.ShapeDtypeStruct(shape, dtype) for shape, dtype, unused in outs.values()],
        in_specs=[pl.BlockSpec(memory_space=space) for unused, space in ins.values()],
        out_specs=[pl.BlockSpec(memory_space=space) for unused, unused_type, space in outs.values()],
        scratch_shapes=flat_scratch,
        compiler_params=pltpu.CompilerParams(
            collective_id=collective, has_side_effects=True, vmem_limit_bytes=VMEM_LIMIT
        ),
    )(*[array for array, unused in ins.values()])
    return dict(zip(out_names, results))


def gather_rows(place, src, dst, sems):
    send, recv, local_sem = sems
    own = pltpu.make_async_copy(src.at[place.yc], dst.at[place.z * 4 + place.yc], local_sem)
    own.start()
    copies = []
    for k in (2, 3, 1):
        unused, to = place.flip(k)
        copy = remote(
            src.at[to], dst.at[place.z * 4 + place.yc], send.at[k], recv.at[k], place.dev(k)
        )
        copy.start()
        copies.append((k, to, copy))

    def along_z():
        own.wait()
        for k, to, copy in copies:
            into = dst.at[place.z * 4 + to]
            remote(into, into, send.at[k], recv.at[k], place.dev(k)).wait_recv()
        sent = [copy for unused, unused_to, copy in copies]
        rows = dst.at[pl.ds(place.z * 4, 4)]
        for k in (1, 2, 3):
            copy = remote(rows, rows, send.at[3 + k], recv.at[3 + k], place.zdev(k))
            copy.start()
            sent.append(copy)

        def finish():
            for k in (1, 2, 3):
                into = dst.at[pl.ds(place.plane(4 - k) * 4, 4)]
                remote(into, into, send.at[3 + k], recv.at[3 + k], place.zdev(k)).wait_recv()
            for copy in sent:
                copy.wait_send()

        return finish

    return along_z


def gather_blocks(place, src, dst, sems):
    send, recv, local_sem = sems
    own = pltpu.make_async_copy(src, dst.at[place.z], local_sem)
    own.start()
    sent = []
    for k in (1, 2, 3):
        copy = remote(src, dst.at[place.z], send.at[k], recv.at[k], place.zdev(k))
        copy.start()
        sent.append(copy)

    def finish():
        own.wait()
        for k in (1, 2, 3):
            into = dst.at[place.plane(4 - k)]
            remote(into, into, send.at[k], recv.at[k], place.zdev(k)).wait_recv()
        for copy in sent:
            copy.wait_send()

    return finish


GATHER_SEMS = [DMA((8,)), DMA((8,)), DMA]


class PlaneSum:
    def __init__(self, place, refs):
        self.place = place
        self.own, self.staged, self.received, self.send, self.recv = refs
        self.sent = []

    @staticmethod
    def scratch(rows, width):
        return [
            VMEM((rows, width), F32),
            VMEM((3, rows, width), BF16),
            VMEM((3, rows, width), BF16),
            DMA((4,)),
            DMA((4,)),
        ]

    def terms(self, term):
        for k in (2, 1, 3):
            self.put(k, term(self.place.plane(k)))
        self.own[...] = term(self.place.z)

    def put(self, k, value):
        self.staged[k - 1] = value.astype(BF16)
        copy = remote(
            self.staged.at[k - 1],
            self.received.at[k - 1],
            self.send.at[k],
            self.recv.at[k],
            self.place.zdev(k),
        )
        copy.start()
        self.sent.append(copy)

    def total(self):
        value = self.own[...]
        for k in (1, 2, 3):
            into = self.received.at[k - 1]
            remote(into, into, self.send.at[k], self.recv.at[k], self.place.zdev(k)).wait_recv()
            value = value + self.received[k - 1].astype(F32)
        for copy in self.sent:
            copy.wait_send()
        return value


class Exchange:
    def __init__(self, place, blocks, sems, partners=tuple(range(1, 8)), slot=None):
        self.place = place
        self.blocks = blocks
        self.send, self.recv = sems
        self.partners = partners
        self.slot = slot or place.slot
        self.sent = []

    def start(self, source):
        own = self.slot(0)
        for k in self.partners:
            copy = remote(
                source(k), self.blocks.at[own], self.send.at[k], self.recv.at[k], self.place.dev(k)
            )
            copy.start()
            self.sent.append(copy)

    def wait(self):
        for k in self.partners:
            into = self.blocks.at[self.slot(k)]
            remote(into, into, self.send.at[k], self.recv.at[k], self.place.dev(k)).wait_recv()
        for copy in self.sent:
            copy.wait_send()


FETCH_ORDER = (0, 1, 0, 1, 2, 4, 3, 5, 2, 4, 3, 5, 6, 7, 6, 7)


def forward_blocks(place, blocks, sems, process, scatter):
    order = FETCH_ORDER[:12] + (
        lambda: scatter.finish(2),
        lambda: scatter.finish(4),
        *FETCH_ORDER[12:],
        lambda: scatter.finish(6),
        lambda: scatter.finish(0),
    )
    return all_gather(place, blocks, sems, process, order)


def flat(ref):
    value = ref[...]
    return value.reshape(value.shape[0] * value.shape[1], value.shape[2])


def ffn_forward(place, refs, blocks, hidden, w_in, w_out, sems, scatter, ready):
    def process(k, slot):
        value = dot(blocks[slot], flat(w_in))
        hidden[slot] = value
        active = sigmoid_linear(value).astype(BF16)
        scatter.emit(k, dot(active, flat(w_out)))

    def gathered(k, slot):
        if k == 0:
            ready()
        process(k, slot)

    sent = forward_blocks(place, blocks, sems, gathered, scatter)
    value = scatter.total()
    for copy in sent:
        copy.wait_send()
    scatter.drain()
    return value


def ffn_backward(place, blocks, grads, hidden, hidden_grads, active, w_in, w_out, sems, scatter, ready):
    def process(k, slot):
        if k == 0:
            ready()
        value = hidden[slot]
        sigma = jax.nn.sigmoid(value)
        active[slot] = (value * sigma).astype(BF16)
        back = dot(grads[slot], flat(w_out), 1, 1)
        low = (back * (sigma * (1.0 + value * (1.0 - sigma)))).astype(BF16)
        hidden_grads[slot] = low
        scatter.emit(k, dot(low, flat(w_in), 1, 1))

    return forward_blocks(place, grads, sems, process, scatter)


def token_dot(left, columns, right):
    count, rows, unused = left.shape
    taken = left[:, :, columns].reshape(count * rows, -1)
    return dot(taken, flat(right), 0, 0)


def columns_of(plane, width):
    return pl.ds(pl.multiple_of(plane * width, width), width)


class WeightGrads:
    def __init__(self, place, refs, name, sums, wide):
        self.place = place
        self.sum_in = PlaneSum(place, getattr(refs, sums + "_sum_in"))
        self.total_in = getattr(refs, name + "_total_in")
        self.share_in = Exchange(
            place, getattr(refs, name + "_grad_in"), getattr(refs, name + "_share_in")
        )
        self.wide = wide
        if wide:
            self.sum_out = PlaneSum(place, getattr(refs, sums + "_sum_out"))
            self.share_out = Exchange(
                place,
                getattr(refs, name + "_grad_out"),
                getattr(refs, name + "_share_out"),
                (4,),
                lambda k: place.flip(k)[0],
            )
        else:
            self.sum_out = HalfSum(
                place, getattr(refs, sums + "_sum_out"), getattr(refs, name + "_grad_out")
            )

    def put_out(self, active, grads):
        if self.wide:
            self.sum_out.terms(lambda plane: token_dot(active, columns_of(plane, 128), grads))
        else:
            self.sum_out.put(dot(flat(active), flat(grads), 0, 0))

    def put_in(self, blocks, grads):
        self.sum_in.terms(lambda plane: token_dot(blocks, columns_of(plane, 256), grads))

    def share(self):
        if self.wide:
            self.share_out.blocks[self.place.x] = self.sum_out.total().astype(BF16)
            self.share_out.start(lambda k: self.share_out.blocks.at[self.place.x])
        else:
            self.sum_out.add()
        self.total_in[...] = self.sum_in.total().astype(BF16).reshape(self.total_in.shape)
        self.share_in.blocks[self.place.slot(0)] = self.total_in[self.place.yc]
        self.share_in.start(lambda k: self.total_in.at[self.place.flip(k)[1]])

    def wait(self):
        (self.share_out if self.wide else self.sum_out).wait()
        self.share_in.wait()

    @staticmethod
    def sums(name, width, wide):
        return {
            name + "_sum_in": PlaneSum.scratch(256, width),
            name + "_sum_out": PlaneSum.scratch(128, 1024) if wide else HalfSum.scratch(1024),
        }

    @staticmethod
    def scratch(name, width, wide):
        held = {
            name + "_total_in": VMEM((4, 64, width), BF16),
            name + "_share_in": [DMA((8,)), DMA((8,))],
        }
        if wide:
            held[name + "_share_out"] = [DMA((8,)), DMA((8,))]
        return held

    @staticmethod
    def outs(name, width, wide):
        return {
            name + "_grad_in": ((8, 64, width), BF16, VMEM),
            name + "_grad_out": ((2, 128, 1024) if wide else (64, 1024), BF16, VMEM),
        }


AG_SEMS = [DMA((10,)), DMA((10,))]


def norm_rows(values, gain):
    normed, saved = norm_forward(values, gain)
    return normed.astype(BF16), saved


def norm_input_grad(grads, gain, saved):
    unit_part, inverse = saved
    scaled = grads * gain
    gain_grad = jnp.sum(grads * unit_part, axis=0, keepdims=True)
    input_part = inverse * (
        scaled
        - jnp.mean(scaled, axis=-1, keepdims=True)
        - unit_part * jnp.mean(scaled * unit_part, axis=-1, keepdims=True)
    )
    return input_part, gain_grad


def ffn_rows(w_in, w_out):
    columns = w_in.reshape(64, PLANES, 4, 2, 128)
    return jnp.transpose(columns, (3, 2, 0, 1, 4)).reshape(2, 4, 64, 512), w_out.reshape(2, 128, -1)


def gather_half(place, src, dst, sems):
    send, recv, local_sem = sems
    mine = place.z // 2 == place.x
    at = lax.rem(place.z, 2)
    own = pltpu.make_async_copy(src, dst.at[at], local_sem)
    copies = [
        remote(src, dst.at[at], send.at[k], recv.at[at], place.zdev(k)) for k in (1, 2, 3)
    ]

    @pl.when(mine)
    def start():
        own.start()
        for copy in copies:
            copy.start()

    def finish():
        for half in range(2):

            @pl.when(place.z != place.x * 2 + half)
            def arrive():
                into = dst.at[half]
                remote(into, into, send.at[0], recv.at[half], place.zdev(1)).wait_recv()

        @pl.when(mine)
        def done():
            own.wait()
            for copy in copies:
                copy.wait_send()

    return finish


class HalfSum:
    def __init__(self, place, refs, result):
        self.place = place
        self.staged, self.received, self.send, self.recv, self.last = refs
        self.result = result

    @staticmethod
    def scratch(width):
        return [
            VMEM((2, 64, width), BF16),
            VMEM((PLANES, 64, width), BF16),
            DMA((2,)),
            DMA((PLANES,)),
            DMA((2,)),
        ]

    def copies(self):
        place = self.place
        for half in range(2):
            plane = place.x * 2 + half
            yield (
                plane,
                remote(
                    self.staged.at[half],
                    self.received.at[place.z],
                    self.send.at[half],
                    self.recv.at[place.z],
                    {"seq": plane * 4 + place.yc, "row": place.x},
                ),
            )

    def put(self, value):
        self.staged[...] = value.astype(BF16).reshape(self.staged.shape)
        for plane, copy in self.copies():

            @pl.when(self.place.z != plane)
            def start(copy=copy):
                copy.start()

    def add(self):
        place = self.place

        @pl.when(place.z // 2 == place.x)
        def reduce():
            self.received[place.z] = self.staged[lax.rem(place.z, 2)]
            for plane in range(PLANES):

                @pl.when(place.z != plane)
                def arrive():
                    into = self.received.at[plane]
                    remote(
                        into, into, self.send.at[0], self.recv.at[plane], place.zdev(1)
                    ).wait_recv()

            value = self.received[0].astype(F32)
            for plane in range(1, PLANES):
                value = value + self.received[plane].astype(F32)
            self.result[...] = value.astype(BF16)
            self.hand_over().start()

        for plane, copy in self.copies():

            @pl.when(self.place.z != plane)
            def drain(copy=copy):
                copy.wait_send()

    def hand_over(self):
        return remote(
            self.result, self.result, self.last.at[0], self.last.at[1], self.place.dev(4)
        )

    def wait(self):
        mine = self.place.z // 2 == self.place.x

        @pl.when(mine)
        def sent():
            self.hand_over().wait_send()

        @pl.when(jnp.logical_not(mine))
        def arrived():
            self.hand_over().wait_recv()


class Turn:
    def __init__(self, place, refs):
        self.place = place
        self.staged, self.received, self.send, self.recv = refs
        self.sent = []

    @staticmethod
    def scratch(rows):
        return [VMEM((PLANES, rows, 128), BF16), VMEM((PLANES, rows, 128), BF16), DMA((4,)), DMA((4,))]

    def start(self):
        place = self.place
        for k in (2, 1, 3):
            copy = remote(
                self.staged.at[place.plane(k)],
                self.received.at[place.z],
                self.send.at[k],
                self.recv.at[k],
                place.zdev(k),
            )
            copy.start()
            self.sent.append(copy)
        self.received[place.z] = self.staged[place.z]

    def wait(self):
        for k in (1, 2, 3):
            into = self.received.at[self.place.plane(4 - k)]
            remote(into, into, self.send.at[k], self.recv.at[k], self.place.zdev(k)).wait_recv()
        for copy in self.sent:
            copy.wait_send()


def swap_halves(values):
    lane = lax.broadcasted_iota(jnp.int32, values.shape, 1)
    return jnp.where(lane % 64 < 32, pltpu.roll(values, 96, 1), pltpu.roll(values, 32, 1))


def head_part(values, head):
    return values[:, head * 64 : head * 64 + 64]


def pack_wide(turn, pair, left, right):
    row, head = divmod(pair, 2)
    for block in range(4):
        turn.staged[pair, block * 128 : block * 128 + 128, :] = jnp.concatenate(
            [head_part(left[row * 4 + block], head), head_part(right[row * 4 + block], head)], axis=1
        )


def pack_narrow(turn, pair, values):
    row, head = divmod(pair, 2)
    for block in range(2):
        turn.staged[pair, block * 128 : block * 128 + 128, :] = jnp.concatenate(
            [
                head_part(values[row * 4 + block], head),
                head_part(values[row * 4 + block + 2], head),
            ],
            axis=1,
        )


def unpack_narrow(turn, row, block):
    rows = slice((block % 2) * 128, (block % 2) * 128 + 128)
    return jnp.concatenate(
        [head_part(turn.received[row * 2 + head, rows, :], block // 2) for head in range(2)], axis=1
    )


def unpack_wide(turn, row, block, side):
    rows = slice(block * 128, block * 128 + 128)
    return jnp.concatenate(
        [head_part(turn.received[row * 2 + head, rows, :], side) for head in range(2)], axis=1
    )


QUERY_BLOCK = 256


def open_heads(refs, turn_qk, turn_v):
    for plane in range(PLANES):
        rows = slice(plane * 512, plane * 512 + 512)
        pair = turn_qk.received[plane]
        scaled = (pair[:, :64].astype(F32) * HEAD_DIM ** (-0.5)).astype(BF16)
        refs.queries[rows, :] = jnp.concatenate([scaled, refs.seg_query[rows, :]], axis=1)
        refs.keys[rows, :] = jnp.concatenate([pair[:, 64:], refs.seg_key[rows, :]], axis=1)
        both = turn_v.received[plane]
        turned = jnp.transpose(both.astype(F32)).astype(BF16)
        refs.values[plane * 512 : plane * 512 + 256, :] = both[:, :64]
        refs.values[plane * 512 + 256 : plane * 512 + 512, :] = both[:, 64:]
        refs.values_t[:, plane * 512 : plane * 512 + 256] = turned[:64]
        refs.values_t[:, plane * 512 + 256 : plane * 512 + 512] = turned[64:]


def attend(refs, turn_mix):
    def plane_step(plane, unused):
        parts = []
        for half in range(2):
            first = plane * 512 + half * 256
            query = refs.queries[pl.ds(pl.multiple_of(first, 256), QUERY_BLOCK), :]
            scores = dot(refs.keys[...], query, 1, 1)
            top = jnp.max(scores, axis=0, keepdims=True)
            weights = jnp.exp(scores - top)
            total = jnp.sum(weights, axis=0, keepdims=True)
            low = (weights * (1.0 / total)).astype(BF16)
            parts.append(jnp.transpose(dot(refs.values_t[...], low)))
            refs.log_total[plane * 2 + half] = jnp.broadcast_to(top + jnp.log(total), (8, 256))
        turn_mix.staged[plane] = jnp.concatenate(parts, axis=1).astype(BF16)
        return unused

    lax.fori_loop(0, PLANES, plane_step, 0)


OUT_ORDER = (1, 3, 5, 7, 2, 4, 6, 0)


def attention_forward(place, refs, stream, scatter):
    blocks = refs.attn_blocks
    blocks[place.slot(0)] = norm_rows(stream, refs.gain_attn[...])[0]

    def process(k, slot):
        if k == 0:
            refs.finish_qkv()
        value = dot(blocks[slot], flat(refs.w_qkv))
        rows = pl.ds(pl.multiple_of(lax.rem(slot, 4) * 128, 128), 128)
        cos, sin = refs.cos[rows, :], refs.sin[rows, :]
        query, key = value[:, :128], value[:, 128:256]
        refs.q_rows[slot] = (query * cos + swap_halves(query) * sin).astype(BF16)
        refs.k_rows[slot] = (key * cos + swap_halves(key) * sin).astype(BF16)
        refs.v_rows[slot] = value[:, 256:].astype(BF16)

    sent = all_gather(
        place, blocks, refs.attn_ag, process, FETCH_ORDER
    )
    turn_qk, turn_v = Turn(place, refs.turn_qk), Turn(place, refs.turn_v)
    for pair in range(PLANES):
        pack_wide(turn_qk, pair, refs.q_rows, refs.k_rows)
        pack_narrow(turn_v, pair, refs.v_rows)
    turn_qk.start()
    turn_v.start()
    turn_qk.wait()
    turn_v.wait()
    refs.after_turn()
    open_heads(refs, turn_qk, turn_v)
    turn_mix = Turn(place, refs.turn_mix)
    attend(refs, turn_mix)
    turn_mix.start()
    turn_mix.wait()
    refs.after_mix()
    for slot in range(8):
        refs.mixed[slot] = unpack_narrow(turn_mix, slot // 4, slot % 4)
    for k in OUT_ORDER:
        scatter.emit(k, dot(refs.mixed[place.slot(k)], flat(refs.w_o)))
    for k in (6, 2, 4, 0):
        scatter.finish(k)
    for copy in sent:
        copy.wait_send()
    total = scatter.total()
    scatter.drain()
    return stream + total


def attention_kept():
    return dict(
        attn_blocks=((8, 128, 1024), BF16),
        w_qkv=((16, 64, 384), BF16),
        w_o=((2, 64, 1024), BF16),
        queries=((2048, 128), BF16),
        keys=((2048, 128), BF16),
        values=((2048, 64), BF16),
        log_total=((8, 8, 256), F32),
        mixed=((8, 128, 128), BF16),
    )


def attend_back(refs, turn_qk, turn_v):
    refs.key_grad[...] = jnp.zeros_like(refs.key_grad)
    refs.value_grad[...] = jnp.zeros_like(refs.value_grad)

    def plane_step(plane, unused):
        parts = []
        for half in range(2):
            first = pl.multiple_of(plane * 512 + half * 256, 256)
            query = refs.queries[pl.ds(first, QUERY_BLOCK), :]
            grad = refs.mix_grads[pl.ds(first, QUERY_BLOCK), :]
            log_total = refs.log_total[plane * 2 + half][:1]
            probs = jnp.exp(dot(refs.keys[...], query, 1, 1) - log_total)
            prob_grads = dot(refs.values[...], grad, 1, 1)
            delta = jnp.sum(probs * prob_grads, axis=0, keepdims=True)
            low = (probs * (prob_grads - delta)).astype(BF16)
            refs.key_grad[...] += dot(low, query[:, :64])
            refs.value_grad[...] += dot(probs.astype(BF16), grad)
            parts.append(jnp.transpose(dot(refs.keys_t[...], low)) * HEAD_DIM ** (-0.5))
        refs.query_grad[pl.ds(pl.multiple_of(plane * 512, 512), 512), :] = jnp.concatenate(
            parts, axis=0
        )
        return unused

    lax.fori_loop(0, PLANES, plane_step, 0)
    for plane in range(PLANES):
        rows = slice(plane * 512, plane * 512 + 512)
        turn_qk.staged[plane] = jnp.concatenate(
            [refs.query_grad[rows, :], refs.key_grad[rows, :]], axis=1
        ).astype(BF16)
        first = plane * 512
        turn_v.staged[plane] = jnp.concatenate(
            [refs.value_grad[first : first + 256, :], refs.value_grad[first + 256 : first + 512, :]],
            axis=1,
        ).astype(BF16)


def attention_backward(place, refs, grad, stream, scatter):
    grads = refs.grads_even
    grads[place.slot(0)] = grad.astype(BF16)

    def process(k, slot):
        if k == 0:
            refs.finish_attn()
        refs.mix_rows[slot] = dot(grads[slot], flat(refs.w_o), 1, 1).astype(BF16)

    sent = all_gather(place, grads, refs.attn_ag, process, FETCH_ORDER)
    turn_mix = Turn(place, refs.turn_mix)
    for pair in range(PLANES):
        pack_narrow(turn_mix, pair, refs.mix_rows)
    turn_mix.start()
    weights = WeightGrads(place, refs, "qkv", "qkv", False)
    weights.put_out(refs.mixed, grads)
    turned = jnp.transpose(refs.keys[...].astype(F32))
    refs.keys_t[...] = turned[:64].astype(BF16)
    turn_mix.wait()
    for plane in range(PLANES):
        both = turn_mix.received[plane]
        refs.mix_grads[plane * 512 : plane * 512 + 256, :] = both[:, :64]
        refs.mix_grads[plane * 512 + 256 : plane * 512 + 512, :] = both[:, 64:]
    refs.before_attend()
    turn_qk, turn_v = Turn(place, refs.turn_qk), Turn(place, refs.turn_v)
    attend_back(refs, turn_qk, turn_v)
    turn_qk.start()
    turn_v.start()
    turn_qk.wait()
    turn_v.wait()
    for slot in range(8):
        row, block = divmod(slot, 4)
        cos = refs.cos[block * 128 : block * 128 + 128, :]
        sin = refs.sin[block * 128 : block * 128 + 128, :]
        query = unpack_wide(turn_qk, row, block, 0).astype(F32)
        key = unpack_wide(turn_qk, row, block, 1).astype(F32)
        refs.qkv_grads[slot] = jnp.concatenate(
            [
                (query * cos - swap_halves(query) * sin).astype(BF16),
                (key * cos - swap_halves(key) * sin).astype(BF16),
                unpack_narrow(turn_v, row, block),
            ],
            axis=1,
        )
    for k in OUT_ORDER:
        scatter.emit(k, dot(refs.qkv_grads[place.slot(k)], flat(refs.w_qkv), 1, 1))
    for k in (6, 2, 4, 0):
        scatter.finish(k)
    weights.put_in(refs.attn_blocks, refs.qkv_grads)
    unused, saved = norm_forward(stream, refs.gain_attn[...])
    input_part, gain_grad = norm_input_grad(scatter.total(), refs.gain_attn[...], saved)
    for copy in sent:
        copy.wait_send()
    scatter.drain()
    return grad + input_part, gain_grad, weights


def head_rows(w_qkv):
    columns = w_qkv.reshape(64, 3, 2, 2, 4, 64)
    return jnp.transpose(columns, (2, 4, 0, 1, 3, 5)).reshape(2, 4, 64, 384)


def plane_tables(frames):
    cos, sin = rotary_tables(frames)
    return jnp.tile(cos, (1, 4)), jnp.tile(jnp.concatenate([-sin, sin], axis=1), (1, 2))


def segment_features(segments):
    same = (segments[:, None] == jnp.arange(64)[None, :]).astype(F32)
    inside = (jnp.arange(64) < 4).astype(F32)[None, :]
    return (-MASKED * (1.0 - same) * inside).astype(BF16), (-same).astype(BF16)


class Edges:
    def __init__(self, place, refs):
        self.place = place
        self.staged, self.received, self.send, self.recv = refs

    @staticmethod
    def scratch():
        return [VMEM((2, 2, 16, 128), BF16), VMEM((2, 2, 16, 128), BF16), DMA((2,)), DMA((2,))]

    def copies(self):
        place = self.place
        for side, inside, step in ((0, place.z < PLANES - 1, 1), (1, place.z > 0, -1)):
            plane = jnp.clip(place.z + step, 0, PLANES - 1)
            yield (
                side,
                inside,
                remote(
                    self.staged.at[side],
                    self.received.at[side],
                    self.send.at[side],
                    self.recv.at[side],
                    {"seq": plane * 4 + place.yc, "row": place.x},
                ),
            )

    def start(self, blocks):
        for row in range(2):
            self.staged[0, row] = blocks[row * 4 + 3, 112:128, :]
            self.staged[1, row] = blocks[row * 4, 0:16, :]
        for side, inside, copy in self.copies():

            @pl.when(inside)
            def start(copy=copy):
                copy.start()

    def wait(self, blocks, padded):
        for slot in range(8):
            row, block = divmod(slot, 4)
            padded[slot, 16:144, :] = blocks[slot].astype(F32)
            if block > 0:
                padded[slot, 0:16, :] = blocks[slot - 1, 112:128, :].astype(F32)
            if block < 3:
                padded[slot, 144:160, :] = blocks[slot + 1, 0:16, :].astype(F32)
        place = self.place
        for side, outside in ((0, place.z == 0), (1, place.z == PLANES - 1)):
            first, rows = ((0, slice(0, 16)), (3, slice(144, 160)))[side]
            into = self.received.at[side]

            @pl.when(outside)
            def nothing():
                for row in range(2):
                    padded[row * 4 + first, rows, :] = jnp.zeros((16, 128), F32)

            @pl.when(jnp.logical_not(outside))
            def arrive():
                remote(
                    into, into, self.send.at[side], self.recv.at[side], place.zdev(1)
                ).wait_recv()
                for row in range(2):
                    padded[row * 4 + first, rows, :] = self.received[side, row].astype(F32)

        for side, inside, copy in self.copies():

            @pl.when(inside)
            def drain(copy=copy):
                copy.wait_send()


def lane_is(index):
    return lax.broadcasted_iota(jnp.int32, (128, 128), 1) == index


def put_columns(tile, slot, first, second):
    return jnp.where(lane_is(slot), first, jnp.where(lane_is(slot + 8), second, tile))


def share_columns(place, refs, tile):
    share = Exchange(place, refs[0], refs[1:])
    own = place.slot(0)
    share.blocks[own] = jnp.transpose(tile)[:16]
    share.start(lambda k: share.blocks.at[own])
    share.wait()
    return share.blocks[...]


def back_to_columns(first, second):
    rows = jnp.concatenate([first, second, jnp.zeros((112, 128), F32)], axis=0)
    return jnp.transpose(rows)


def column(tile, slot):
    return jnp.sum(jnp.where(lane_is(slot), tile, 0.0), axis=1, keepdims=True)


def kept_frames(value, offset, before, after):
    if offset < 0:
        return jnp.where(before <= offset, value, 0.0)
    if offset > 0:
        return jnp.where(after > offset, value, 0.0)
    return value


CHUNK = 64


def convolve(refs):
    taps = [refs.taps[j : j + 1, :] for j in range(KERNEL)]

    def step(slot, tile):
        for first in range(0, 128, CHUNK):
            rows = slice(first, first + CHUNK)
            before, after = refs.before[slot, rows, :], refs.after[slot, rows, :]
            total = jnp.zeros((CHUNK, 128), F32)
            for j in range(KERNEL):
                start = first + j + 1
                value = refs.glu_padded[slot, start : start + CHUNK, :]
                total = total + taps[j] * kept_frames(value, j - HALF, before, after)
            refs.conv[slot, rows, :] = total
        value = refs.conv[slot]
        mean = jnp.mean(value, axis=1, keepdims=True)
        center = value - mean
        return put_columns(tile, slot, mean, jnp.sum(center * center, axis=1, keepdims=True))

    return lax.fori_loop(0, 8, step, jnp.zeros((128, 128), F32))


def inner_norm(refs, slot):
    mean, inverse = column(refs.inner_stats[...], slot), column(refs.inner_stats[...], slot + 8)
    unit_part = (refs.conv[slot] - mean) * inverse
    return unit_part, inverse


def conv_forward(place, refs, stream, scatter):
    blocks = refs.conv_blocks
    blocks[place.slot(0)] = norm_rows(stream, refs.gain_conv[...])[0]

    def process(k, slot):
        if k == 0:
            refs.finish_ci()
        value = dot(blocks[slot], flat(refs.w_ci))
        refs.gate_up[slot] = value
        refs.glu[slot] = (value[:, :128] * jax.nn.sigmoid(value[:, 128:])).astype(BF16)

    sent = all_gather(place, blocks, refs.conv_ag, process, FETCH_ORDER)
    edges = Edges(place, refs.edges)
    edges.start(refs.glu)
    edges.wait(refs.glu, refs.glu_padded)
    stats = share_columns(place, refs.stats, convolve(refs))
    means, spreads = stats[:, :8], stats[:, 8:]
    mean = jnp.mean(means, axis=0)
    spread = jnp.sum(spreads + 128.0 * jnp.square(means - mean[None]), axis=0) / 1024.0
    refs.inner_stats[...] = back_to_columns(mean, lax.rsqrt(spread + EPSILON))
    refs.finish_co()
    for k in OUT_ORDER:
        slot = place.slot(k)
        unit_part, unused = inner_norm(refs, slot)
        active = sigmoid_linear(unit_part * refs.gain_inner[...]).astype(BF16)
        refs.conv_active[slot] = active
        scatter.emit(k, dot(active, flat(refs.w_co)))
    for k in (6, 2, 4, 0):
        scatter.finish(k)
    for copy in sent:
        copy.wait_send()
    total = scatter.total()
    scatter.drain()
    return stream + total


def conv_kept():
    return dict(
        conv_blocks=((8, 128, 1024), BF16),
        w_ci=((16, 64, 256), BF16),
        w_co=((2, 64, 1024), BF16),
        gate_up=((8, 128, 256), F32),
        glu_padded=((8, 160, 128), F32),
        conv=((8, 128, 128), F32),
        inner_stats=((128, 128), F32),
        conv_active=((8, 128, 128), BF16),
    )


STATS = [VMEM((8, 16, 128), F32), DMA((8,)), DMA((8,))]


def conv_inputs(gain, inner, taps, reach):
    return dict(
        gain_conv=(gain[None], VMEM),
        gain_inner=(inner, VMEM),
        taps=(taps, VMEM),
        before=(reach[0], VMEM),
        after=(reach[1], VMEM),
    )


def convolve_back(refs):
    taps = [refs.taps[j : j + 1, :] for j in range(KERNEL)]
    refs.tap_sums[...] = jnp.zeros_like(refs.tap_sums)

    def step(slot, unused):
        for first in range(0, 128, CHUNK):
            rows = slice(first, first + CHUNK)
            before, after = refs.before[slot, rows, :], refs.after[slot, rows, :]
            total = jnp.zeros((CHUNK, 128), F32)
            grad = refs.conv_grad_padded[slot, first + 16 : first + 16 + CHUNK, :]
            for j in range(KERNEL):
                offset = j - HALF
                start = first + 16 - offset
                value = refs.conv_grad_padded[slot, start : start + CHUNK, :]
                total = total + taps[j] * kept_frames(value, -offset, before, after)
                start = first + 16 + offset
                value = refs.glu_padded[slot, start : start + CHUNK, :]
                product = kept_frames(value * grad, offset, before, after)
                refs.tap_sums[j] += jnp.sum(product.reshape(CHUNK // 8, 8, 128), axis=0)
            refs.glu_grad[slot, rows, :] = total
        return unused

    lax.fori_loop(0, 8, step, 0)
    return jnp.sum(refs.tap_sums[...], axis=1)


def conv_backward(place, refs, grad, stream, scatter):
    grads = refs.grads_odd
    grads[place.slot(0)] = grad.astype(BF16)
    gain = refs.gain_inner[...]

    def process(k, slot):
        if k == 0:
            refs.finish_conv()
        back = dot(grads[slot], flat(refs.w_co), 1, 1)
        unit_part, unused = inner_norm(refs, slot)
        refs.inner_grad[slot] = back * sigmoid_linear_grad(unit_part * gain)

    sent = all_gather(place, grads, refs.conv_ag, process, FETCH_ORDER)

    def sums(slot, current):
        tile, gain_grad = current
        value = refs.inner_grad[slot]
        unit_part, unused = inner_norm(refs, slot)
        scaled = value * gain
        tile = put_columns(
            tile,
            slot,
            jnp.sum(scaled, axis=1, keepdims=True),
            jnp.sum(scaled * unit_part, axis=1, keepdims=True),
        )
        return tile, gain_grad + jnp.sum(value * unit_part, axis=0, keepdims=True)

    tile, inner_gain_grad = lax.fori_loop(
        0, 8, sums, (jnp.zeros((128, 128), F32), jnp.zeros((1, 128), F32))
    )
    stats = share_columns(place, refs.stats, tile)
    means = jnp.sum(stats, axis=0) / 1024.0
    refs.grad_stats[...] = back_to_columns(means[:8], means[8:])
    weights = WeightGrads(place, refs, "conv", "conv", False)
    weights.put_out(refs.conv_active, grads)

    def input_grad(slot, unused):
        unit_part, inverse = inner_norm(refs, slot)
        tile = refs.grad_stats[...]
        refs.conv_grad[slot] = (
            inverse
            * (
                refs.inner_grad[slot] * gain
                - column(tile, slot)
                - unit_part * column(tile, slot + 8)
            )
        ).astype(BF16)
        return unused

    lax.fori_loop(0, 8, input_grad, 0)
    edges = Edges(place, refs.edges)
    edges.start(refs.conv_grad)
    edges.wait(refs.conv_grad, refs.conv_grad_padded)
    tap_grads = convolve_back(refs)
    for k in OUT_ORDER:
        slot = place.slot(k)
        value = refs.gate_up[slot]
        glu_grad, sigma = refs.glu_grad[slot], jax.nn.sigmoid(value[:, 128:])
        refs.gate_grads[slot] = jnp.concatenate(
            [glu_grad * sigma, glu_grad * value[:, :128] * sigma * (1.0 - sigma)], axis=1
        ).astype(BF16)
        scatter.emit(k, dot(refs.gate_grads[slot], flat(refs.w_ci), 1, 1))
    for k in (6, 2, 4, 0):
        scatter.finish(k)
    weights.put_in(refs.conv_blocks, refs.gate_grads)
    unused, saved = norm_forward(stream, refs.gain_conv[...])
    input_part, gain_grad = norm_input_grad(scatter.total(), refs.gain_conv[...], saved)
    for copy in sent:
        copy.wait_send()
    scatter.drain()
    return grad + input_part, gain_grad, inner_gain_grad, tap_grads, weights


def channel_rows(w_in):
    columns = w_in.reshape(64, 2, 2, 2, 4, 64)
    return jnp.transpose(columns, (2, 4, 0, 1, 3, 5)).reshape(2, 4, 64, 256)


def own_channels(array, x, yc):
    split = array.reshape(array.shape[:-1] + (2, 2, 4, 64))
    split = lax.dynamic_index_in_dim(split, x, split.ndim - 4, keepdims=False)
    split = lax.dynamic_index_in_dim(split, yc, split.ndim - 2, keepdims=False)
    return split.reshape(array.shape[:-1] + (128,))


def all_channels(array, x, yc):
    lead = array.shape[:-1]
    split = array.reshape(lead + (1, 2, 1, 64))
    at_x = (jnp.arange(2) == x).reshape(2, 1, 1, 1)
    at_yc = (jnp.arange(4) == yc).reshape(4, 1)
    return jnp.where(jnp.logical_and(at_x, at_yc), split, 0.0).reshape(lead + (1024,))


def segment_reach(frames, lengths):
    ends = jnp.cumsum(lengths, axis=1)
    starts = ends - lengths
    place = frames[None, :]
    inside = jnp.logical_and(place[:, :, None] >= starts[:, None, :], place[:, :, None] < ends[:, None, :])
    before = jnp.sum(jnp.where(inside, starts[:, None, :], 0), axis=2) - place
    after = jnp.sum(jnp.where(inside, ends[:, None, :], 0), axis=2) - place

    def wide(array):
        return jnp.broadcast_to(array.astype(jnp.int32).reshape(8, 128, 1), (8, 128, 128))

    return wide(before), wide(after)


class Traffic:
    def __init__(self, refs, sems):
        self.refs, self.sems = refs, sems
        self.count = 0

    def start(self, pairs):
        copies = []
        for source, target in pairs:
            copy = pltpu.make_async_copy(source, target, self.sems.at[self.count])
            copy.start()
            copies.append(copy)
            self.count += 1

        def finish():
            for copy in copies:
                copy.wait()

        return finish

    def save(self, names):
        return self.start(
            [(getattr(self.refs, name), getattr(self.refs, "keep_" + name)) for name in names]
        )

    def load(self, names):
        return self.start(
            [(getattr(self.refs, "keep_" + name), getattr(self.refs, name)) for name in names]
        )


def ffn_kept():
    return dict(
        blocks=((8, 128, 1024), BF16),
        hidden=((8, 128, 512), F32),
        w_in=((16, 64, 512), BF16),
        w_out=((4, 128, 1024), BF16),
    )


SCATTER_SEMS = [DMA((8,)), DMA((8,))]


def forward_body(refs):
    place = Place()
    place.enter()
    own = place.slot(0)
    traffic = Traffic(refs, refs.traffic)
    along_in = gather_rows(place, refs.w_in_rows.at[place.x], refs.w_in, refs.gather_in)
    stream = refs.stream[...].astype(F32)
    refs.blocks[own] = norm_rows(stream, refs.gain_ffn1[...])[0]
    held = Refs()

    def process_in(k, slot):
        if k == 0:
            held.finish_in()
        value = dot(refs.blocks[slot], flat(refs.w_in))
        refs.hidden[slot] = value
        refs.active[slot] = sigmoid_linear(value).astype(BF16)

    def begin():
        held.finish_in = along_in()
        held.finish_out = gather_blocks(
            place, refs.w_out_rows.at[place.x], refs.w_out, refs.gather_out
        )
        held.along_qkv = gather_rows(
            place, refs.qkv_rows.at[place.x], refs.w_qkv, refs.gather_qkv
        )
        held.finish_wo = gather_half(place, refs.o_rows, refs.w_o, refs.gather_o)

    order = (begin, 0, 1, 2, 4, 3, 5, 6, 7, 0, 1, 2, 4, 3, 5, 6, 7)
    sent = all_gather(place, refs.blocks, refs.ffn_ag, process_in, order)
    refs.finish_qkv = held.along_qkv()
    held.finish_out()
    scatter = Scatter(place, refs.scatter, refs.ffn_scatter)
    for k in OUT_ORDER:
        scatter.emit(k, dot(refs.active[place.slot(k)], flat(refs.w_out)))
    for k in (6, 2, 4, 0):
        scatter.finish(k)
    saved = [traffic.save(ffn_kept())]
    along_ci = gather_rows(place, refs.ci_rows.at[place.x], refs.w_ci, refs.gather_ci)
    along_next = gather_rows(place, refs.next_in_rows.at[place.x], refs.next_in, refs.gather_next)
    total = scatter.total()
    for copy in sent:
        copy.wait_send()
    scatter.drain()
    stream = stream + 0.5 * total
    refs.stream_one[...] = stream

    def after_turn():
        refs.finish_ci = along_ci()
        refs.finish_co = gather_half(place, refs.co_rows, refs.w_co, refs.gather_co)

    def after_mix():
        held.finish_wo()
        held.finish_next_in = along_next()
        held.finish_next_out = gather_blocks(
            place, refs.next_out_rows.at[place.x], refs.next_out, refs.gather_next_out
        )

    refs.after_turn, refs.after_mix = after_turn, after_mix
    stream = attention_forward(
        place, refs, stream, Scatter(place, refs.scatter, refs.attn_scatter)
    )
    saved.append(traffic.save(attention_kept()))
    refs.stream_two[...] = stream
    stream = conv_forward(place, refs, stream, Scatter(place, refs.scatter, refs.conv_scatter))
    saved.append(traffic.save(conv_kept()))
    refs.stream_three[...] = stream
    held.finish_next_in()
    held.finish_next_out()
    for finish in saved:
        finish()


def scratch_of(kept):
    return {name: VMEM(shape, dtype) for name, (shape, dtype) in kept.items()}


def forward_call(ins):
    kept = {**ffn_kept(), **attention_kept(), **conv_kept()}
    outs = dict(
        stream_one=((128, 1024), F32, VMEM),
        stream_two=((128, 1024), F32, VMEM),
        stream_three=((128, 1024), F32, VMEM),
        next_in=((16, 64, 512), BF16, pl.ANY),
        next_out=((4, 128, 1024), BF16, pl.ANY),
    )
    for name, (shape, dtype) in kept.items():
        outs["keep_" + name] = (shape, dtype, pl.ANY)
    scratch = dict(
        scratch_of(kept),
        active=VMEM((8, 128, 512), BF16),
        gather_in=GATHER_SEMS,
        gather_out=GATHER_SEMS,
        gather_qkv=GATHER_SEMS,
        gather_o=GATHER_SEMS,
        gather_ci=GATHER_SEMS,
        gather_co=GATHER_SEMS,
        gather_next=GATHER_SEMS,
        gather_next_out=GATHER_SEMS,
        traffic=DMA((len(kept),)),
        scatter=Scatter.scratch(128, 1024),
        ffn_ag=AG_SEMS,
        attn_ag=AG_SEMS,
        conv_ag=AG_SEMS,
        ffn_scatter=SCATTER_SEMS,
        attn_scatter=SCATTER_SEMS,
        conv_scatter=SCATTER_SEMS,
        q_rows=VMEM((8, 128, 128), BF16),
        k_rows=VMEM((8, 128, 128), BF16),
        v_rows=VMEM((8, 128, 128), BF16),
        turn_qk=Turn.scratch(512),
        turn_v=Turn.scratch(256),
        turn_mix=Turn.scratch(256),
        values_t=VMEM((64, 2048), BF16),
        glu=VMEM((8, 128, 128), BF16),
        edges=Edges.scratch(),
        stats=STATS,
    )
    return kernel_call(forward_body, 1, ins, outs, scratch)


class SmallSum:
    def __init__(self, place, refs):
        self.place, self.refs = place, refs
        self.first = Exchange(place, refs.small_first, refs.small_first_sems)
        self.last = Exchange(place, refs.small, refs.small_last_sems)
        self.sent = []

    def start(self):
        refs, place = self.refs, self.place

        def part(slot):
            return refs.gain_grads.at[:, columns_of(slot, 128)]

        self.first.blocks[place.slot(0)] = refs.gain_grads[:, columns_of(place.slot(0), 128)]
        self.first.start(lambda k: part(place.slot(k)))

    def along_z(self):
        refs, place = self.refs, self.place
        self.first.wait()
        refs.small_planes[place.z, 0:8, :] = jnp.sum(self.first.blocks[...], axis=0)
        refs.small_planes[place.z, 8:48, :] = refs.channel_grads[...]
        send, recv = refs.small_z_sems
        rows = refs.small_planes.at[place.z]
        for k in (1, 2, 3):
            copy = remote(rows, rows, send.at[k], recv.at[k], place.zdev(k))
            copy.start()
            self.sent.append(copy)

    def spread(self):
        refs, place = self.refs, self.place
        send, recv = refs.small_z_sems
        for k in (1, 2, 3):
            into = refs.small_planes.at[place.plane(4 - k)]
            remote(into, into, send.at[k], recv.at[k], place.zdev(k)).wait_recv()
        for copy in self.sent:
            copy.wait_send()
        own = place.slot(0)
        self.last.blocks[own] = jnp.sum(refs.small_planes[...], axis=0)
        self.last.start(lambda k: self.last.blocks.at[own])

    def wait(self):
        self.last.wait()


def backward_body(refs):
    place = Place()
    place.enter()
    own = place.slot(0)
    traffic = Traffic(refs, refs.traffic)
    ready = traffic.start([(refs.next_in, refs.w_in), (refs.next_out, refs.w_out)])
    refs.finish_conv = traffic.load(conv_kept())
    refs.finish_attn = traffic.load(attention_kept())
    refs.gain_grads[...] = jnp.zeros_like(refs.gain_grads)
    refs.channel_grads[...] = jnp.zeros_like(refs.channel_grads)
    stream = refs.stream_three[...]
    low, saved = norm_rows(stream, refs.gain_ffn2[...])
    refs.blocks[own] = low
    total = ffn_forward(
        place,
        refs,
        refs.blocks,
        refs.hidden,
        refs.w_in,
        refs.w_out,
        refs.ffn2_ag,
        Scatter(place, refs.scatter, refs.ffn2_scatter),
        ready,
    )
    final, saved_final = norm_forward(stream + 0.5 * total, refs.gain_out[...])
    refs.output[...] = final.astype(BF16)
    grad, refs.gain_grads[4:5, :] = norm_input_grad(
        refs.cotangent[...].astype(F32), refs.gain_out[...], saved_final
    )
    refs.grads_even[own] = (0.5 * grad).astype(BF16)
    scatter = Scatter(place, refs.scatter, refs.ffn2_scatter_back)
    sent = ffn_backward(
        place,
        refs.blocks,
        refs.grads_even,
        refs.hidden,
        refs.hidden_grads,
        refs.active,
        refs.w_in,
        refs.w_out,
        refs.ffn2_ag_back,
        scatter,
        lambda: None,
    )
    weights_two = WeightGrads(place, refs, "ffn2", "ffn", True)
    weights_two.put_out(refs.active, refs.grads_even)
    weights_two.put_in(refs.blocks, refs.hidden_grads)
    input_part, refs.gain_grads[3:4, :] = norm_input_grad(
        scatter.total(), refs.gain_ffn2[...], saved
    )
    grad = grad + input_part
    for copy in sent:
        copy.wait_send()
    scatter.drain()
    load_first = traffic.load(ffn_kept())
    grad, refs.gain_grads[2:3, :], inner, taps, weights_three = conv_backward(
        place, refs, grad, refs.stream_two[...], Scatter(place, refs.scatter, refs.conv_scatter)
    )
    refs.channel_grads[0:32, :] = taps
    refs.channel_grads[32:33, :] = inner

    def before_attend():
        weights_two.share()
        weights_three.share()

    refs.before_attend = before_attend
    grad, refs.gain_grads[1:2, :], weights_four = attention_backward(
        place, refs, grad, refs.stream_one[...], Scatter(place, refs.scatter, refs.attn_scatter)
    )
    weights_two.wait()
    weights_three.wait()
    refs.grads_odd[own] = (0.5 * grad).astype(BF16)
    scatter = Scatter(place, refs.scatter, refs.ffn1_scatter)
    sent = ffn_backward(
        place,
        refs.blocks,
        refs.grads_odd,
        refs.hidden,
        refs.hidden_grads,
        refs.active,
        refs.w_in,
        refs.w_out,
        refs.ffn1_ag,
        scatter,
        load_first,
    )
    weights_one = WeightGrads(place, refs, "ffn1", "ffn", True)
    weights_one.put_out(refs.active, refs.grads_odd)
    weights_one.put_in(refs.blocks, refs.hidden_grads)
    weights_four.share()
    unused, saved = norm_forward(refs.stream[...].astype(F32), refs.gain_ffn1[...])
    input_part, refs.gain_grads[0:1, :] = norm_input_grad(
        scatter.total(), refs.gain_ffn1[...], saved
    )
    small = SmallSum(place, refs)
    small.start()
    refs.grad_stream[...] = grad + input_part
    for copy in sent:
        copy.wait_send()
    scatter.drain()
    small.along_z()
    small.spread()
    weights_four.wait()
    weights_one.share()
    small.wait()
    weights_one.wait()


MODULES = (("ffn1", 512, True), ("qkv", 384, False), ("conv", 256, False), ("ffn2", 512, True))


def backward_call(ins):
    kept = {**ffn_kept(), **attention_kept(), **conv_kept()}
    outs = dict(
        output=((128, 1024), BF16, VMEM),
        grad_stream=((128, 1024), F32, VMEM),
        small=((8, 48, 128), F32, VMEM),
    )
    scratch = dict(
        scratch_of(kept),
        active=VMEM((8, 128, 512), BF16),
        hidden_grads=VMEM((8, 128, 512), BF16),
        grads_even=VMEM((8, 128, 1024), BF16),
        grads_odd=VMEM((8, 128, 1024), BF16),
        traffic=DMA((2 + len(kept),)),
        scatter=Scatter.scratch(128, 1024),
        ffn2_ag=AG_SEMS,
        ffn2_ag_back=AG_SEMS,
        conv_ag=AG_SEMS,
        attn_ag=AG_SEMS,
        ffn1_ag=AG_SEMS,
        ffn2_scatter=SCATTER_SEMS,
        ffn2_scatter_back=SCATTER_SEMS,
        conv_scatter=SCATTER_SEMS,
        attn_scatter=SCATTER_SEMS,
        ffn1_scatter=SCATTER_SEMS,
        mix_rows=VMEM((8, 128, 128), BF16),
        mix_grads=VMEM((2048, 64), BF16),
        keys_t=VMEM((64, 2048), BF16),
        turn_qk=Turn.scratch(512),
        turn_v=Turn.scratch(256),
        turn_mix=Turn.scratch(256),
        query_grad=VMEM((2048, 64), F32),
        key_grad=VMEM((2048, 64), F32),
        value_grad=VMEM((2048, 64), F32),
        qkv_grads=VMEM((8, 128, 384), BF16),
        inner_grad=VMEM((8, 128, 128), F32),
        grad_stats=VMEM((128, 128), F32),
        conv_grad=VMEM((8, 128, 128), BF16),
        conv_grad_padded=VMEM((8, 160, 128), F32),
        glu_grad=VMEM((8, 128, 128), F32),
        gate_grads=VMEM((8, 128, 256), BF16),
        tap_sums=VMEM((32, 8, 128), F32),
        edges=Edges.scratch(),
        stats=STATS,
        gain_grads=VMEM((8, 1024), F32),
        channel_grads=VMEM((40, 128), F32),
        small_first=VMEM((8, 8, 128), F32),
        small_planes=VMEM((PLANES, 48, 128), F32),
        small_first_sems=[DMA((8,)), DMA((8,))],
        small_z_sems=[DMA((4,)), DMA((4,))],
        small_last_sems=[DMA((8,)), DMA((8,))],
        **WeightGrads.sums("ffn", 512, True),
        **WeightGrads.sums("qkv", 384, False),
        **WeightGrads.sums("conv", 256, False),
    )
    for name, width, wide in MODULES:
        outs.update(WeightGrads.outs(name, width, wide))
        scratch.update(WeightGrads.scratch(name, width, wide))
    return kernel_call(backward_body, 2, ins, outs, scratch)


def ffn_grads(grad_in, grad_out):
    columns = grad_in.reshape(2, 4, 64, PLANES, 128).transpose(2, 3, 1, 0, 4)
    return columns.reshape(64, 4096).astype(F32), grad_out.reshape(256, 1024).astype(F32)


def half_grads(grad_in, kinds):
    columns = grad_in.reshape(2, 4, 64, kinds, 2, 64).transpose(2, 3, 0, 4, 1, 5)
    return columns.reshape(64, kinds * 1024).astype(F32)


def spread_channels(values):
    rows = values.shape[1]
    return values.reshape(2, 4, rows, 2, 64).transpose(2, 0, 3, 1, 4).reshape(rows, 1024)


def local_planes(
    inputs,
    lengths,
    gain_ffn1,
    gain_attn,
    gain_conv,
    gain_inner,
    gain_ffn2,
    gain_out,
    conv_kernel,
    ffn1_in,
    ffn1_out,
    attn_qkv,
    attn_out,
    conv_in,
    conv_out,
    ffn2_in,
    ffn2_out,
    cotangent,
):
    position_index = lax.axis_index("seq")
    plane, column_index = position_index // 4, lax.rem(position_index, 4)
    row_index = lax.axis_index("row")
    all_lengths = lax.all_gather(lengths[0], "row", axis=0)
    head_lengths = lax.dynamic_index_in_dim(all_lengths, plane // 2, 0, keepdims=False)
    features = segment_features(segment_of(jnp.arange(2048, dtype=jnp.int32), head_lengths))
    frames = plane * 512 + jnp.arange(512, dtype=jnp.int32)
    tables = plane_tables(frames)
    reach = segment_reach(frames, all_lengths)
    rows_one = ffn_rows(ffn1_in, ffn1_out)
    rows_two = ffn_rows(ffn2_in, ffn2_out)
    shared = dict(
        stream=(inputs[0], VMEM),
        gain_ffn1=(gain_ffn1[None], VMEM),
        gain_attn=(gain_attn[None], VMEM),
        cos=(tables[0], VMEM),
        sin=(tables[1], VMEM),
        **conv_inputs(
            gain_conv,
            own_channels(gain_inner[None], row_index, column_index),
            own_channels(conv_kernel.astype(F32), row_index, column_index),
            reach,
        ),
    )
    forward = forward_call(
        dict(
            shared,
            seg_query=(features[0], VMEM),
            seg_key=(features[1], VMEM),
            w_in_rows=(rows_one[0], pl.ANY),
            w_out_rows=(rows_one[1], pl.ANY),
            qkv_rows=(head_rows(attn_qkv), pl.ANY),
            o_rows=(attn_out, pl.ANY),
            ci_rows=(channel_rows(conv_in), pl.ANY),
            co_rows=(conv_out, pl.ANY),
            next_in_rows=(rows_two[0], pl.ANY),
            next_out_rows=(rows_two[1], pl.ANY),
        )
    )
    ins = dict(
        shared,
        cotangent=(cotangent[0], VMEM),
        gain_ffn2=(gain_ffn2[None], VMEM),
        gain_out=(gain_out[None], VMEM),
    )
    for name, array in forward.items():
        ins[name] = (array, VMEM if name.startswith("stream") else pl.ANY)
    backward = backward_call(ins)
    small = backward["small"]
    gains = small[:, :8].transpose(1, 0, 2).reshape(8, 1024)
    channels = spread_channels(small[:, 8:41])
    return (
        backward["output"][None],
        backward["grad_stream"][None],
        gains[0],
        gains[1],
        gains[2],
        channels[32],
        gains[3],
        gains[4],
        channels[:KERNEL],
        *ffn_grads(backward["ffn1_grad_in"], backward["ffn1_grad_out"]),
        half_grads(backward["qkv_grad_in"], 3),
        backward["qkv_grad_out"].astype(F32),
        half_grads(backward["conv_grad_in"], 2),
        backward["conv_grad_out"].astype(F32),
        *ffn_grads(backward["ffn2_grad_in"], backward["ffn2_grad_out"]),
    )


def solution(mesh):
    return jax.shard_map(
        local_planes if mesh.shape["seq"] == 16 and mesh.shape["row"] == 2 else local,
        mesh=mesh,
        in_specs=(
            P("row", "seq", None),
            P("row", None),
            P(),
            P(),
            P(),
            P(),
            P(),
            P(),
            P(),
            P("seq", None),
            P("seq", None),
            P("seq", None),
            P("seq", None),
            P("seq", None),
            P("seq", None),
            P("seq", None),
            P("seq", None),
            P("row", "seq", None),
        ),
        out_specs=(
            P("row", "seq", None),
            P("row", "seq", None),
            P(),
            P(),
            P(),
            P(),
            P(),
            P(),
            P(),
            P("seq", None),
            P("seq", None),
            P("seq", None),
            P("seq", None),
            P("seq", None),
            P("seq", None),
            P("seq", None),
            P("seq", None),
        ),
        check_vma=False,
    )
```

```python
import functools
import math

import jax
import jax.numpy as jnp
from jax import lax
from jax.experimental import pallas as pl
from jax.experimental.pallas import tpu as pltpu
from jax.sharding import PartitionSpec as P

HEADS = 16
HEAD_DIM = 64
KERNEL = 31
HALF = 15


EPSILON = 1e-05
MASKED = -1e30


def with_halo(block, sides, width):
    for axis, dim in sides:
        count = lax.axis_size(axis)
        forward = [(i, i + 1) for i in range(count - 1)]
        backward = [(target, source) for source, target in forward]
        low = lax.ppermute(
            lax.slice_in_dim(block, block.shape[dim] - width, None, axis=dim), axis, forward
        )
        high = lax.ppermute(lax.slice_in_dim(block, 0, width, axis=dim), axis, backward)
        block = jnp.concatenate([low, block, high], axis=dim)
    return block


def shifted(array, axis, by):
    size = lax.axis_size(axis)
    return lax.ppermute(array, axis, [(i, (i + by) % size) for i in range(size)])


def segment_of(positions, seg_lengths):
    boundary = jnp.cumsum(seg_lengths)[:-1]
    return jnp.sum((positions[:, None] >= boundary[None, :]).astype(jnp.int32), axis=1)


def rotary_tables(positions):
    half_dim = HEAD_DIM // 2
    inverse = jnp.exp(-jnp.log(10000.0) * jnp.arange(half_dim, dtype=jnp.float32) / half_dim)
    angles = positions.astype(jnp.float32)[:, None] * inverse[None, :]
    return (jnp.cos(angles), jnp.sin(angles))


def split_heads(values):
    return values.reshape(values.shape[0], HEADS, HEAD_DIM)


def rotate(values, cos_table, sin_table):
    half_dim = HEAD_DIM // 2
    shaped = split_heads(values)
    first_half = shaped[..., :half_dim]
    second_half = shaped[..., half_dim:]
    cos_heads = cos_table[:, None, :]
    sin_heads = sin_table[:, None, :]
    turned = jnp.concatenate(
        [
            first_half * cos_heads - second_half * sin_heads,
            second_half * cos_heads + first_half * sin_heads,
        ],
        axis=-1,
    )
    return turned.reshape(values.shape)


def unrotate(grads, cos_table, sin_table):
    half_dim = HEAD_DIM // 2
    shaped = split_heads(grads)
    first_half = shaped[..., :half_dim]
    second_half = shaped[..., half_dim:]
    cos_heads = cos_table[:, None, :]
    sin_heads = sin_table[:, None, :]
    turned = jnp.concatenate(
        [
            first_half * cos_heads + second_half * sin_heads,
            second_half * cos_heads - first_half * sin_heads,
        ],
        axis=-1,
    )
    return turned.reshape(grads.shape)


def norm_forward(values, gain):
    center = values - jnp.mean(values, axis=-1, keepdims=True)
    spread = jnp.mean(center * center, axis=-1, keepdims=True)
    inverse = lax.rsqrt(spread + EPSILON)
    unit_part = center * inverse
    return (unit_part * gain, (unit_part, inverse))


def norm_backward(grads, gain, saved):
    unit_part, inverse = saved
    scaled = grads * gain
    gain_grad = jnp.sum(grads * unit_part, axis=0)
    input_part = inverse * (
        scaled
        - jnp.mean(scaled, axis=-1, keepdims=True)
        - unit_part * jnp.mean(scaled * unit_part, axis=-1, keepdims=True)
    )
    return (input_part, gain_grad)


def sigmoid_linear(values):
    return values * jax.nn.sigmoid(values)


def sigmoid_linear_grad(values):
    sigma = jax.nn.sigmoid(values)
    return sigma * (1.0 + values * (1.0 - sigma))


def project(left_side, weight):
    return (
        jnp.dot(
            left_side,
            lax.all_gather(weight, "seq", axis=0, tiled=True),
            preferred_element_type=jnp.float32,
        ),
        weight,
    )


def project_back(grad_side, weight):
    return lax.dot_general(
        grad_side,
        lax.all_gather(weight, "seq", axis=0, tiled=True),
        (((1,), (1,)), ((), ())),
        preferred_element_type=jnp.float32,
    )


def weight_grad(left_side, grad_side):
    return lax.psum_scatter(
        lax.dot_general(
            left_side, grad_side, (((0,), (0,)), ((), ())), preferred_element_type=jnp.float32
        ).astype(jnp.bfloat16),
        "seq",
        scatter_dimension=0,
        tiled=True,
    ).astype(jnp.float32)


def over_blocks(advance, running, pieces):
    total_rows = pieces[0].shape[0]
    block_size = math.gcd(total_rows, 512)
    number = total_rows // block_size
    stacked = tuple((piece.reshape((number, block_size) + piece.shape[1:]) for piece in pieces))

    def scan_step(current, block_item):
        block_index, blocks = block_item
        return (advance(current, blocks, block_index * block_size), None)

    running, unused = lax.scan(scan_step, running, (jnp.arange(number, dtype=jnp.int32), stacked))
    return running


def block_scores(query_heads, key_heads, query_segments, key_segments):
    scale = HEAD_DIM ** (-0.5)
    raw_scores = (
        jnp.einsum("qhd,khd->hqk", query_heads, key_heads, preferred_element_type=jnp.float32)
        * scale
    )
    return jnp.where((query_segments[:, None] == key_segments[None, :])[None], raw_scores, MASKED)


def pair_grads(
    query_rows, grad_rows, log_total, delta, query_segments, key_rows, value_rows, key_segments
):
    scale = HEAD_DIM ** (-0.5)
    query_heads = split_heads(query_rows)
    grad_heads = split_heads(grad_rows)
    key_heads = split_heads(key_rows)
    value_heads = split_heads(value_rows)
    probs = jnp.exp(
        block_scores(query_heads, key_heads, query_segments, key_segments) - log_total[:, :, None]
    )
    prob_grads = jnp.einsum(
        "qhd,khd->hqk", grad_heads, value_heads, preferred_element_type=jnp.float32
    )
    score_grads = (probs * (prob_grads - delta[:, :, None])).astype(jnp.bfloat16)
    query_grad = (
        jnp.einsum("hqk,khd->qhd", score_grads, key_heads, preferred_element_type=jnp.float32)
        * scale
    )
    key_grad = (
        jnp.einsum("hqk,qhd->khd", score_grads, query_heads, preferred_element_type=jnp.float32)
        * scale
    )
    value_grad = jnp.einsum(
        "hqk,qhd->khd", probs.astype(jnp.bfloat16), grad_heads, preferred_element_type=jnp.float32
    )
    return (
        query_grad.reshape(query_rows.shape),
        key_grad.reshape(key_rows.shape),
        value_grad.reshape(value_rows.shape),
    )


def local(
    inputs,
    lengths,
    gain_ffn1,
    gain_attn,
    gain_conv,
    gain_inner,
    gain_ffn2,
    gain_out,
    conv_kernel,
    ffn1_in,
    ffn1_out,
    attn_qkv,
    attn_out,
    conv_in,
    conv_out,
    ffn2_in,
    ffn2_out,
    cotangent,
):
    frame_count = inputs.shape[1]
    model_width = inputs.shape[2]
    device_count = lax.axis_size("seq")
    position_index = lax.axis_index("seq")
    seg_lengths = lengths[0]
    first_frame = position_index * frame_count
    local_frames = jnp.arange(frame_count, dtype=jnp.int32)
    positions = first_frame + local_frames
    query_segments = segment_of(positions, seg_lengths)
    cos_table, sin_table = rotary_tables(positions)
    stream = inputs[0].astype(jnp.float32)
    normed_one, saved_one = norm_forward(stream, gain_ffn1)
    normed_one_low = normed_one.astype(jnp.bfloat16)
    hidden_one, kept_ffn1_in = project(normed_one_low, ffn1_in)
    active_one = sigmoid_linear(hidden_one).astype(jnp.bfloat16)
    branch_one, kept_ffn1_out = project(active_one, ffn1_out)
    stream_one = stream + 0.5 * branch_one
    normed_two, saved_two = norm_forward(stream_one, gain_attn)
    normed_two_low = normed_two.astype(jnp.bfloat16)
    projected, kept_qkv = project(normed_two_low, attn_qkv)
    query_low = rotate(projected[:, :model_width], cos_table, sin_table).astype(jnp.bfloat16)
    key_low = rotate(projected[:, model_width : 2 * model_width], cos_table, sin_table).astype(
        jnp.bfloat16
    )
    value_low = projected[:, 2 * model_width :].astype(jnp.bfloat16)
    query_heads = split_heads(query_low)

    def stats_step(current, blocks, first_row):
        top_score, denominator = current
        key_block = blocks[0]
        key_segments = segment_of(
            first_row + jnp.arange(key_block.shape[0], dtype=jnp.int32), seg_lengths
        )
        masked = block_scores(query_heads, split_heads(key_block), query_segments, key_segments)
        new_top = jnp.maximum(top_score, jnp.max(masked, axis=-1))
        denominator = denominator * jnp.exp(top_score - new_top) + jnp.sum(
            jnp.exp(masked - new_top[:, :, None]), axis=-1
        )
        return (new_top, denominator)

    top_init = jnp.full((HEADS, frame_count), MASKED, jnp.float32)
    total_init = jnp.zeros((HEADS, frame_count), jnp.float32)
    top_score, denominator = over_blocks(
        stats_step, (top_init, total_init), (lax.all_gather(key_low, "seq", axis=0, tiled=True),)
    )
    log_total = top_score + jnp.log(denominator)

    def value_step(current, blocks, first_row):
        mixed_sum, rest_sum = current
        key_block, value_block = blocks
        key_segments = segment_of(
            first_row + jnp.arange(key_block.shape[0], dtype=jnp.int32), seg_lengths
        )
        probs = jnp.exp(
            block_scores(query_heads, split_heads(key_block), query_segments, key_segments)
            - log_total[:, :, None]
        )
        probs_high = probs.astype(jnp.bfloat16)
        probs_rest = (probs - probs_high.astype(jnp.float32)).astype(jnp.bfloat16)
        value_heads = split_heads(value_block)
        mixed_sum = mixed_sum + jnp.einsum(
            "hqk,khd->qhd", probs_high, value_heads, preferred_element_type=jnp.float32
        )
        rest_sum = rest_sum + jnp.einsum(
            "hqk,khd->qhd", probs_rest, value_heads, preferred_element_type=jnp.float32
        )
        return (mixed_sum, rest_sum)

    zero_heads = jnp.zeros((frame_count, HEADS, HEAD_DIM), jnp.float32)
    mixed_sum, rest_sum = over_blocks(
        value_step,
        (zero_heads, zero_heads),
        (
            lax.all_gather(key_low, "seq", axis=0, tiled=True),
            lax.all_gather(value_low, "seq", axis=0, tiled=True),
        ),
    )
    exact_sum = mixed_sum + rest_sum
    mixed_low = mixed_sum.reshape(frame_count, model_width).astype(jnp.bfloat16)
    branch_two, kept_attn_out = project(mixed_low, attn_out)
    stream_two = stream_one + branch_two
    normed_three, saved_three = norm_forward(stream_two, gain_conv)
    normed_three_low = normed_three.astype(jnp.bfloat16)
    gate_up, kept_conv_in = project(normed_three_low, conv_in)
    first_part = gate_up[:, :model_width]
    gate_sigma = jax.nn.sigmoid(gate_up[:, model_width:])
    glu_low = (first_part * gate_sigma).astype(jnp.bfloat16)
    padded = with_halo(glu_low, (("seq", 0),), HALF).astype(jnp.float32)
    padded_segments = segment_of(
        first_frame - HALF + jnp.arange(frame_count + 2 * HALF, dtype=jnp.int32), seg_lengths
    )
    kernel_taps = conv_kernel.astype(jnp.float32)
    conv_values = jnp.zeros((frame_count, model_width), jnp.float32)
    for offset in range(KERNEL):
        same_segment = (padded_segments[offset : offset + frame_count] == query_segments).astype(
            jnp.float32
        )
        conv_values = (
            conv_values
            + kernel_taps[offset] * padded[offset : offset + frame_count] * same_segment[:, None]
        )
    normed_four, saved_four = norm_forward(conv_values, gain_inner)
    active_four = sigmoid_linear(normed_four).astype(jnp.bfloat16)
    branch_three, kept_conv_out = project(active_four, conv_out)
    stream_three = stream_two + branch_three
    normed_five, saved_five = norm_forward(stream_three, gain_ffn2)
    normed_five_low = normed_five.astype(jnp.bfloat16)
    hidden_two, kept_ffn2_in = project(normed_five_low, ffn2_in)
    active_two = sigmoid_linear(hidden_two).astype(jnp.bfloat16)
    branch_four, kept_ffn2_out = project(active_two, ffn2_out)
    stream_four = stream_three + 0.5 * branch_four
    final_norm, saved_six = norm_forward(stream_four, gain_out)
    output = final_norm.astype(jnp.bfloat16)[None]
    grad_four, grad_gain_six = norm_backward(cotangent[0].astype(jnp.float32), gain_out, saved_six)
    out_two_low = (0.5 * grad_four).astype(jnp.bfloat16)
    grad_ffn_two_out = weight_grad(active_two, out_two_low)
    hidden_two_low = (project_back(out_two_low, ffn2_out) * sigmoid_linear_grad(hidden_two)).astype(
        jnp.bfloat16
    )
    grad_ffn_two_in = weight_grad(normed_five_low, hidden_two_low)
    input_part, grad_gain_five = norm_backward(
        project_back(hidden_two_low, ffn2_in), gain_ffn2, saved_five
    )
    grad_three = grad_four + input_part
    conv_out_low = grad_three.astype(jnp.bfloat16)
    grad_conv_weight_out = weight_grad(active_four, conv_out_low)
    active_grad = project_back(conv_out_low, conv_out) * sigmoid_linear_grad(normed_four)
    conv_grad, grad_gain_four = norm_backward(active_grad, gain_inner, saved_four)
    conv_grad_low = conv_grad.astype(jnp.bfloat16)
    conv_grad_value = conv_grad_low.astype(jnp.float32)
    rim_grad = with_halo(conv_grad_low, (("seq", 0),), HALF).astype(jnp.float32)
    tap_grads = []
    glu_grad = jnp.zeros((frame_count, model_width), jnp.float32)
    for offset in range(KERNEL):
        same_segment = (padded_segments[offset : offset + frame_count] == query_segments).astype(
            jnp.float32
        )
        tap_grads.append(
            jnp.sum(
                padded[offset : offset + frame_count] * same_segment[:, None] * conv_grad_value,
                axis=0,
            )
        )
        back_start = 2 * HALF - offset
        back_segment = (
            padded_segments[back_start : back_start + frame_count] == query_segments
        ).astype(jnp.float32)
        glu_grad = (
            glu_grad
            + kernel_taps[offset]
            * rim_grad[back_start : back_start + frame_count]
            * back_segment[:, None]
        )
    kernel_grad = jnp.stack(tap_grads, axis=0)
    gate_up_low = jnp.concatenate(
        [glu_grad * gate_sigma, glu_grad * first_part * gate_sigma * (1.0 - gate_sigma)], axis=1
    ).astype(jnp.bfloat16)
    grad_conv_weight_in = weight_grad(normed_three_low, gate_up_low)
    input_part, grad_gain_three = norm_backward(
        project_back(gate_up_low, conv_in), gain_conv, saved_three
    )
    grad_two = grad_three + input_part
    attn_grad_low = grad_two.astype(jnp.bfloat16)
    grad_attn_weight = weight_grad(mixed_low, attn_grad_low)
    mixed_grad_low = project_back(attn_grad_low, attn_out).astype(jnp.bfloat16)
    delta = jnp.transpose(
        jnp.sum(split_heads(mixed_grad_low).astype(jnp.float32) * exact_sum, axis=-1)
    )

    def key_turn(turn_index, current):
        key_rows, value_rows, key_acc, value_acc, query_acc = current
        owner = (position_index - turn_index) % device_count
        key_segments = segment_of(owner * frame_count + local_frames, seg_lengths)
        query_part, key_part, value_part = pair_grads(
            query_low,
            mixed_grad_low,
            log_total,
            delta,
            query_segments,
            key_rows,
            value_rows,
            key_segments,
        )
        key_rows, value_rows = shifted((key_rows, value_rows), "seq", 1)
        key_acc, value_acc = (
            shifted((key_acc + key_part).astype(jnp.bfloat16), "seq", 1).astype(jnp.float32),
            shifted((value_acc + value_part).astype(jnp.bfloat16), "seq", 1).astype(jnp.float32),
        )
        return (key_rows, value_rows, key_acc, value_acc, query_acc + query_part)

    zero_rows = jnp.zeros((frame_count, model_width), jnp.float32)
    unused_keys, unused_values, key_grad, value_grad, query_grad = lax.fori_loop(
        0, device_count, key_turn, (key_low, value_low, zero_rows, zero_rows, zero_rows)
    )
    projected_grad_low = jnp.concatenate(
        [
            unrotate(query_grad, cos_table, sin_table),
            unrotate(key_grad, cos_table, sin_table),
            value_grad,
        ],
        axis=1,
    ).astype(jnp.bfloat16)
    grad_qkv_weight = weight_grad(normed_two_low, projected_grad_low)
    input_part, grad_gain_two = norm_backward(
        project_back(projected_grad_low, attn_qkv), gain_attn, saved_two
    )
    grad_one = grad_two + input_part
    out_one_low = (0.5 * grad_one).astype(jnp.bfloat16)
    grad_ffn_one_out = weight_grad(active_one, out_one_low)
    hidden_one_low = (project_back(out_one_low, ffn1_out) * sigmoid_linear_grad(hidden_one)).astype(
        jnp.bfloat16
    )
    grad_ffn_one_in = weight_grad(normed_one_low, hidden_one_low)
    input_part, grad_gain_one = norm_backward(
        project_back(hidden_one_low, ffn1_in), gain_ffn1, saved_one
    )
    input_grad = (grad_one + input_part)[None]
    small_grads = lax.psum(
        (
            grad_gain_one,
            grad_gain_two,
            grad_gain_three,
            grad_gain_four,
            grad_gain_five,
            grad_gain_six,
            kernel_grad,
        ),
        ("seq", "row"),
    )
    large_grads = (
        grad_ffn_one_in,
        grad_ffn_one_out,
        grad_qkv_weight,
        grad_attn_weight,
        grad_conv_weight_in,
        grad_conv_weight_out,
        grad_ffn_two_in,
        grad_ffn_two_out,
    )
    large_grads = (
        lax.psum(grad_ffn_one_in.astype(jnp.bfloat16), "row").astype(jnp.float32),
        lax.psum(grad_ffn_one_out.astype(jnp.bfloat16), "row").astype(jnp.float32),
        lax.psum(grad_qkv_weight.astype(jnp.bfloat16), "row").astype(jnp.float32),
        lax.psum(grad_attn_weight.astype(jnp.bfloat16), "row").astype(jnp.float32),
        lax.psum(grad_conv_weight_in.astype(jnp.bfloat16), "row").astype(jnp.float32),
        lax.psum(grad_conv_weight_out.astype(jnp.bfloat16), "row").astype(jnp.float32),
        lax.psum(grad_ffn_two_in.astype(jnp.bfloat16), "row").astype(jnp.float32),
        lax.psum(grad_ffn_two_out.astype(jnp.bfloat16), "row").astype(jnp.float32),
    )
    return (
        output,
        input_grad,
        small_grads[0],
        small_grads[1],
        small_grads[2],
        small_grads[3],
        small_grads[4],
        small_grads[5],
        small_grads[6],
        large_grads[0],
        large_grads[1],
        large_grads[2],
        large_grads[3],
        large_grads[4],
        large_grads[5],
        large_grads[6],
        large_grads[7],
    )


BF16 = jnp.bfloat16
F32 = jnp.float32
PLANES = 4
VMEM = pltpu.VMEM
DMA = pltpu.SemaphoreType.DMA
VMEM_LIMIT = 60 * 1024 * 1024


class Place:
    def __init__(self):
        seq = lax.axis_index("seq")
        self.x = lax.axis_index("row")
        self.z = seq // 4
        self.yc = lax.rem(seq, 4)
        self.core = lax.rem(self.yc, 2)
        inside = lax.rem(self.z + self.z // 2, 2)
        self.end, self.middle = inside == 0, inside == 1
        self.beside, self.across, self.opposite = self.line(1 - inside), self.line(2), self.line(3)

    def flip(self, k):
        y, c, x = self.yc // 2, lax.rem(self.yc, 2), self.x
        c = 1 - c if k & 1 else c
        y = 1 - y if k & 2 else y
        x = 1 - x if k & 4 else x
        return x, y * 2 + c

    def dev(self, k):
        x, yc = self.flip(k)
        return {"seq": self.z * 4 + yc, "row": x}

    def slot(self, k):
        x, yc = self.flip(k)
        return x * 4 + yc

    def zdev(self, k):
        return self.at(lax.rem(self.z + k, PLANES))

    def at(self, plane, yc=None):
        return {"seq": plane * 4 + (self.yc if yc is None else yc), "row": self.x}

    def line(self, index):
        return index + self.z // 2 * (3 - 2 * index)

    def pair(self, x=None, yc=None):
        x = self.x if x is None else x
        yc = self.yc if yc is None else yc
        return (x * 2 + lax.rem(yc, 2)) * 2 + yc // 2

    def enter(self):
        barrier = pltpu.get_barrier_semaphore()
        partners = [self.dev(k) for k in range(1, 8)]
        for k in range(1, PLANES):
            plane = lax.rem(self.z + k, PLANES)
            partners += [self.at(plane), self.at(plane, self.flip(1)[1])]
        for partner in partners:
            pl.semaphore_signal(barrier, inc=1, device_id=partner)
        pl.semaphore_wait(barrier, len(partners))


def remote(src, dst, send_sem, recv_sem, dev):
    return pltpu.make_async_remote_copy(src, dst, send_sem, recv_sem, device_id=dev)


def dot(left, right, left_dim=1, right_dim=0):
    return lax.dot_general(
        left, right, (((left_dim,), (right_dim,)), ((), ())), preferred_element_type=F32
    )


def all_gather(place, blocks, sems, process, order):
    send, recv = sems
    half = blocks.shape[1] // 2
    own = place.slot(0)
    sent = []
    slots = {}

    def push(rows, to, sem):
        copy = remote(rows, rows, send.at[sem], recv.at[sem], place.dev(to))
        copy.start()
        sent.append(copy)

    def arrived(rows, sem):
        remote(rows, rows, send.at[sem], recv.at[sem], place.dev(1)).wait_recv()

    for k in (4, 2, 1):
        push(blocks.at[own], k, k)

    def fetch(k):
        slot = place.slot(k)
        rows = blocks.at[slot]
        if k == 6:
            arrived(blocks.at[slot, pl.ds(0, half)], 6)
            arrived(blocks.at[slot, pl.ds(half, half)], 8)
            push(rows, 1, 7)
        elif k:
            arrived(rows, k)
        if k == 2:
            push(blocks.at[slot, pl.ds(0, half)], 4, 6)
            push(rows, 1, 3)
        if k == 4:
            push(blocks.at[slot, pl.ds(half, half)], 2, 8)
            push(rows, 1, 5)
        return slot

    for step in order:
        if callable(step):
            step()
        elif step in slots:
            process(step, slots[step])
        else:
            slots[step] = fetch(step)
    return sent


class Scatter:
    def __init__(self, place, buffers, sems):
        self.place = place
        self.part, self.staged, self.sibling, self.reduced, self.received = buffers
        self.send, self.recv = sems
        self.sent = []

    @staticmethod
    def scratch(rows, width):
        return [
            VMEM((4, rows, width), F32),
            VMEM((4, rows, width), BF16),
            VMEM((4, rows, width), BF16),
            VMEM((3, rows, width), BF16),
            VMEM((3, rows, width), BF16),
        ]

    def push(self, src, dst, sem, k):
        copy = remote(src, dst, self.send.at[sem], self.recv.at[sem], self.place.dev(k))
        copy.start()
        self.sent.append(copy)

    def emit(self, k, value):
        index = k // 2
        if k % 2:
            self.staged[index] = value.astype(BF16)
            self.push(self.staged.at[index], self.sibling.at[index], index, 1)
        else:
            self.part[index] = value

    def finish(self, k):
        index = k // 2
        into = self.sibling.at[index]
        remote(into, into, self.send.at[index], self.recv.at[index], self.place.dev(1)).wait_recv()
        total = self.part[index] + self.sibling[index].astype(F32)
        if k:
            self.reduced[index - 1] = total.astype(BF16)
            self.push(self.reduced.at[index - 1], self.received.at[index - 1], 3 + index, k)
        else:
            self.part[0] = total

    def total(self):
        value = self.part[0]
        for index in range(3):
            into = self.received.at[index]
            remote(
                into, into, self.send.at[4 + index], self.recv.at[4 + index], self.place.dev(1)
            ).wait_recv()
            value = value + self.received[index].astype(F32)
        return value

    def drain(self):
        for copy in self.sent:
            copy.wait_send()


class Refs:
    pass


def kernel_call(body, collective, ins, outs, scratch):
    in_names = list(ins)
    out_names = list(outs)
    scratch_names = list(scratch)
    flat_scratch = []
    counts = []
    for name in scratch_names:
        item = scratch[name]
        counts.append(len(item) if isinstance(item, list) else 0)
        flat_scratch += item if isinstance(item, list) else [item]

    def kernel(*refs):
        held = Refs()
        at = 0
        for name in in_names + out_names:
            setattr(held, name, refs[at])
            at += 1
        for name, count in zip(scratch_names, counts):
            setattr(held, name, refs[at : at + count] if count else refs[at])
            at += max(count, 1)
        body(held)

    results = pl.pallas_call(
        kernel,
        out_shape=[jax.ShapeDtypeStruct(shape, dtype) for shape, dtype, unused in outs.values()],
        in_specs=[pl.BlockSpec(memory_space=space) for unused, space in ins.values()],
        out_specs=[pl.BlockSpec(memory_space=space) for unused, unused_type, space in outs.values()],
        scratch_shapes=flat_scratch,
        compiler_params=pltpu.CompilerParams(
            collective_id=collective, has_side_effects=True, vmem_limit_bytes=VMEM_LIMIT
        ),
    )(*[array for array, unused in ins.values()])
    return dict(zip(out_names, results))


class AlongZ:
    def __init__(self, place, sems, block):
        self.place = place
        self.send, self.recv = sems
        self.block = block
        self.sent = []

    def copy(self, source, owner, plane, sem):
        into = self.block(owner)
        return remote(
            source, into, self.send.at[sem], self.recv.at[owner], self.place.at(plane)
        )

    def arrive(self, owner):
        self.copy(self.block(owner), owner, owner, 0).wait_recv()

    def start(self, source):
        place = self.place
        self.sent = [
            self.copy(source, place.z, place.across, 0),
            self.copy(source, place.z, place.beside, 1),
        ]
        self.last = [
            self.copy(source, place.z, place.opposite, 2),
            self.copy(self.block(place.opposite), place.opposite, place.line(0), 3),
        ]
        for copy in self.sent:
            copy.start()

        @pl.when(place.middle)
        def start():
            self.last[0].start()

    def relay(self):
        @pl.when(self.place.middle)
        def hand_on():
            self.arrive(self.place.opposite)
            self.last[1].start()

    def finish(self):
        place = self.place
        self.arrive(place.beside)
        self.arrive(place.across)

        @pl.when(place.end)
        def last():
            self.arrive(place.opposite)

        for copy in self.sent:
            copy.wait_send()

        @pl.when(place.middle)
        def drain():
            for copy in self.last:
                copy.wait_send()


class GatherRows:
    def __init__(self, place, src, dst, sems, pieces):
        self.place, self.dst = place, dst
        self.send, self.recv, self.local = sems[:3]
        self.along = AlongZ(place, sems[3:], lambda plane: dst.at[pl.ds(plane * 4, 4)])
        mine = place.z * 4 + place.yc
        for k in (0, 2, 3, 1):
            x, to = place.flip(k)
            for index, column in enumerate(pieces(place, to)):
                source = src.at[:, pl.ds(pl.multiple_of(column * 128, 128), 128)]
                into = dst.at[mine, :, pl.ds(index * 128, 128)]
                if k:
                    remote(source, into, self.send.at[k], self.recv.at[k], place.dev(k)).start()
                else:
                    pltpu.make_async_copy(source, into, self.local).start()

    def along_z(self):
        place = self.place
        mine = self.dst.at[place.z * 4 + place.yc]
        pltpu.make_async_copy(mine, mine, self.local).wait()
        for k in (2, 3, 1):
            into = self.dst.at[place.z * 4 + place.flip(k)[1]]
            remote(into, into, self.send.at[k], self.recv.at[k], place.dev(k)).wait_recv()
        self.along.start(self.dst.at[pl.ds(place.z * 4, 4)])

    def relay(self):
        self.along.relay()

    def finish(self):
        place = self.place
        self.along.finish()
        mine = self.dst.at[place.z * 4 + place.yc]
        for k in (2, 3, 1):
            remote(mine, mine, self.send.at[k], self.recv.at[k], place.dev(k)).wait_send()

    @staticmethod
    def scratch():
        return [DMA((4,)), DMA((4,)), DMA, DMA((4,)), DMA((PLANES,))]


def ffn_pieces(place, yc):
    return [(plane * 4 + yc) * 2 + place.x for plane in range(PLANES)]


def head_pieces(place, yc):
    return [kind * 8 + place.pair(None, yc) for kind in range(3)]


def channel_pieces(place, yc):
    return [kind * 8 + place.pair(None, yc) for kind in range(2)]


class GatherBlocks:
    def __init__(self, place, src, dst, sems):
        self.along = AlongZ(place, sems[1:], lambda plane: dst.at[plane])
        self.own = pltpu.make_async_copy(src, dst.at[place.z], sems[0])
        self.own.start()
        self.along.start(src)

    def relay(self):
        self.along.relay()

    def finish(self):
        self.own.wait()
        self.along.finish()

    @staticmethod
    def scratch():
        return [DMA, DMA((4,)), DMA((PLANES,))]


class PlaneSum:
    def __init__(self, place, refs):
        self.place = place
        self.own, self.staged, self.received, self.relayed, self.send, self.recv = refs

    @staticmethod
    def scratch(rows, width):
        return [
            VMEM((rows, width), F32),
            VMEM((3, rows, width), BF16),
            VMEM((3, rows, width), BF16),
            VMEM((rows, width), BF16),
            DMA((4,)),
            DMA((4,)),
        ]

    def term_copy(self, index, plane):
        slot = lax.rem(plane + 3 - self.place.z, PLANES)
        return remote(
            self.staged.at[index],
            self.received.at[slot],
            self.send.at[index],
            self.recv.at[slot],
            self.place.at(plane),
        )

    def relay_copy(self):
        return remote(
            self.staged.at[0],
            self.relayed,
            self.send.at[3],
            self.recv.at[3],
            self.place.at(self.place.beside),
        )

    def terms(self, term):
        place = self.place
        self.staged[0] = term(place.opposite).astype(BF16)

        @pl.when(place.end)
        def start():
            self.relay_copy().start()

        self.staged[1] = term(place.across).astype(BF16)
        self.term_copy(1, place.across).start()
        self.staged[2] = term(place.beside).astype(BF16)
        self.term_copy(2, place.beside).start()
        self.own[...] = term(place.z)

    def relay(self):
        @pl.when(self.place.middle)
        def add():
            self.relay_copy().wait_recv()
            self.staged[0] = (
                self.staged[0].astype(F32) + self.relayed[...].astype(F32)
            ).astype(BF16)
            self.term_copy(0, self.place.opposite).start()

    def arrive(self, plane):
        slot = lax.rem(self.place.z + 3 - plane, PLANES)
        into = self.received.at[slot]
        remote(
            into, into, self.send.at[0], self.recv.at[slot], self.place.at(plane)
        ).wait_recv()

    def total(self):
        place = self.place
        self.arrive(place.beside)
        self.arrive(place.across)

        @pl.when(place.middle)
        def last():
            self.arrive(place.opposite)
            self.term_copy(0, place.opposite).wait_send()

        @pl.when(place.end)
        def nothing():
            self.received[lax.rem(place.z + 3 - place.opposite, PLANES)] = jnp.zeros(
                self.received.shape[1:], BF16
            )
            self.relay_copy().wait_send()

        self.term_copy(1, place.across).wait_send()
        self.term_copy(2, place.beside).wait_send()
        value = self.own[...]
        for index in range(3):
            value = value + self.received[index].astype(F32)
        return value


class Exchange:
    def __init__(self, place, blocks, sems, partners=tuple(range(1, 8)), slot=None):
        self.place = place
        self.blocks = blocks
        self.send, self.recv = sems
        self.partners = partners
        self.slot = slot or place.slot
        self.sent = []

    def start(self, source):
        own = self.slot(0)
        for k in self.partners:
            copy = remote(
                source(k), self.blocks.at[own], self.send.at[k], self.recv.at[k], self.place.dev(k)
            )
            copy.start()
            self.sent.append(copy)

    def wait(self):
        for k in self.partners:
            into = self.blocks.at[self.slot(k)]
            remote(into, into, self.send.at[k], self.recv.at[k], self.place.dev(k)).wait_recv()
        for copy in self.sent:
            copy.wait_send()


FETCH_ORDER = (0, 1, 0, 1, 2, 4, 3, 5, 2, 4, 3, 5, 6, 7, 6, 7)


def forward_blocks(place, blocks, sems, process, scatter):
    order = FETCH_ORDER[:12] + (
        lambda: scatter.finish(2),
        lambda: scatter.finish(4),
        *FETCH_ORDER[12:],
        lambda: scatter.finish(6),
        lambda: scatter.finish(0),
    )
    return all_gather(place, blocks, sems, process, order)


def flat(ref):
    value = ref[...]
    return value.reshape(value.shape[0] * value.shape[1], value.shape[2])


def ffn_forward(place, refs, blocks, hidden, w_in, w_out, sems, scatter, ready):
    def process(k, slot):
        value = dot(blocks[slot], flat(w_in))
        hidden[slot] = value
        active = sigmoid_linear(value).astype(BF16)
        scatter.emit(k, dot(active, flat(w_out)))

    def gathered(k, slot):
        if k == 0:
            ready()
        process(k, slot)

    sent = forward_blocks(place, blocks, sems, gathered, scatter)
    value = scatter.total()
    for copy in sent:
        copy.wait_send()
    scatter.drain()
    return value


def ffn_backward(place, blocks, grads, hidden, hidden_grads, active, w_in, w_out, sems, scatter, ready):
    def process(k, slot):
        if k == 0:
            ready()
        value = hidden[slot]
        sigma = jax.nn.sigmoid(value)
        active[slot] = (value * sigma).astype(BF16)
        back = dot(grads[slot], flat(w_out), 1, 1)
        low = (back * (sigma * (1.0 + value * (1.0 - sigma)))).astype(BF16)
        hidden_grads[slot] = low
        scatter.emit(k, dot(low, flat(w_in), 1, 1))

    return forward_blocks(place, grads, sems, process, scatter)


def token_dot(left, columns, right):
    count, rows, unused = left.shape
    taken = left[:, :, columns].reshape(count * rows, -1)
    return dot(taken, flat(right), 0, 0)


def columns_of(plane, width):
    return pl.ds(pl.multiple_of(plane * width, width), width)


class WeightGrads:
    def __init__(self, place, refs, name, sums, wide):
        self.place = place
        self.sum_in = PlaneSum(place, getattr(refs, sums + "_sum_in"))
        self.total_in = getattr(refs, name + "_total_in")
        self.share_in = Exchange(
            place, getattr(refs, name + "_grad_in"), getattr(refs, name + "_share_in")
        )
        self.wide = wide
        if wide:
            self.sum_out = PlaneSum(place, getattr(refs, sums + "_sum_out"))
            self.share_out = Exchange(
                place,
                getattr(refs, name + "_grad_out"),
                getattr(refs, name + "_share_out"),
                (4,),
                lambda k: place.flip(k)[0],
            )
        else:
            self.sum_out = HalfSum(
                place, getattr(refs, sums + "_sum_out"), getattr(refs, name + "_grad_out")
            )

    def put_out(self, active, grads):
        if self.wide:
            self.sum_out.terms(lambda plane: token_dot(active, columns_of(plane, 128), grads))
        else:
            self.sum_out.put(dot(flat(active), flat(grads), 0, 0))

    def put_in(self, blocks, grads):
        self.sum_in.terms(lambda plane: token_dot(blocks, columns_of(plane, 256), grads))

    def relay(self):
        self.sum_out.relay()
        self.sum_in.relay()

    def share(self):
        if self.wide:
            self.share_out.blocks[self.place.x] = self.sum_out.total().astype(BF16)
            self.share_out.start(lambda k: self.share_out.blocks.at[self.place.x])
        else:
            self.sum_out.add()
        self.total_in[...] = self.sum_in.total().astype(BF16).reshape(self.total_in.shape)
        self.share_in.blocks[self.place.slot(0)] = self.total_in[self.place.yc]
        self.share_in.start(lambda k: self.total_in.at[self.place.flip(k)[1]])

    def wait(self):
        (self.share_out if self.wide else self.sum_out).wait()
        self.share_in.wait()

    @staticmethod
    def sums(name, width, wide):
        return {
            name + "_sum_in": PlaneSum.scratch(256, width),
            name + "_sum_out": PlaneSum.scratch(128, 1024) if wide else HalfSum.scratch(1024),
        }

    @staticmethod
    def scratch(name, width, wide):
        held = {
            name + "_total_in": VMEM((4, 64, width), BF16),
            name + "_share_in": [DMA((8,)), DMA((8,))],
        }
        if wide:
            held[name + "_share_out"] = [DMA((8,)), DMA((8,))]
        return held

    @staticmethod
    def outs(name, width, wide):
        return {
            name + "_grad_in": ((8, 64, width), BF16, VMEM),
            name + "_grad_out": ((2, 128, 1024) if wide else (64, 1024), BF16, VMEM),
        }


AG_SEMS = [DMA((10,)), DMA((10,))]


def norm_rows(values, gain):
    normed, saved = norm_forward(values, gain)
    return normed.astype(BF16), saved


def norm_input_grad(grads, gain, saved):
    unit_part, inverse = saved
    scaled = grads * gain
    gain_grad = jnp.sum(grads * unit_part, axis=0, keepdims=True)
    input_part = inverse * (
        scaled
        - jnp.mean(scaled, axis=-1, keepdims=True)
        - unit_part * jnp.mean(scaled * unit_part, axis=-1, keepdims=True)
    )
    return input_part, gain_grad


class GatherHalf:
    def __init__(self, place, src, dst, sems):
        self.place, self.dst = place, dst
        self.send, self.recv, self.local = sems
        self.source = place.z // 2 == place.x
        self.first, self.last = 2 - place.x, 3 - 3 * place.x
        target = place.yc // 2 * 2 + lax.rem(place.z, 2)
        self.same = lax.rem(place.z, 2) == place.core
        self.own = pltpu.make_async_copy(src, dst.at[place.core], self.local)

        def copy(sem, plane):
            return remote(
                src,
                dst.at[place.core],
                self.send.at[sem],
                self.recv.at[place.core],
                place.at(plane, target),
            )

        self.far, self.near, self.sibling = (
            copy(0, self.first),
            copy(1, place.x * 2 + 1 - lax.rem(place.z, 2)),
            copy(2, place.z),
        )

        @pl.when(self.source)
        def start():
            self.far.start()
            self.near.start()

            @pl.when(self.same)
            def local():
                self.own.start()

            @pl.when(jnp.logical_not(self.same))
            def sibling():
                self.sibling.start()

    def on(self, half):
        rows = self.dst.at[half]
        return remote(
            rows, rows, self.send.at[half], self.recv.at[half], self.place.at(self.last)
        )

    def relay(self):
        @pl.when(self.place.z == self.first)
        def hand_on():
            for half in range(2):
                self.on(half).wait_recv()
                self.on(half).start()

    def finish(self):
        place = self.place
        at_home = place.z == place.x * 2 + place.core
        for half in range(2):
            here = jnp.logical_or(
                jnp.logical_and(at_home, place.core == half), place.z == self.first
            )

            @pl.when(jnp.logical_not(here))
            def arrive():
                self.on(half).wait_recv()

        @pl.when(self.source)
        def drain():
            self.far.wait_send()
            self.near.wait_send()

            @pl.when(self.same)
            def local():
                self.own.wait()

            @pl.when(jnp.logical_not(self.same))
            def sibling():
                self.sibling.wait_send()

        @pl.when(place.z == self.first)
        def drain_on():
            for half in range(2):
                self.on(half).wait_send()

    @staticmethod
    def scratch():
        return [DMA((3,)), DMA((2,)), DMA]


class HalfSum:
    def __init__(self, place, refs, result):
        self.place = place
        self.staged, self.received, self.relayed, self.send, self.recv, self.last = refs
        self.result = result
        self.near = place.z // 2 == place.x
        self.far_middle, self.far_end = 2 - place.x, 3 - 3 * place.x
        self.home = place.x * 2 + place.core

    @staticmethod
    def scratch(width):
        return [
            VMEM((2, 64, width), BF16),
            VMEM((3, 64, width), BF16),
            VMEM((2, 64, width), BF16),
            DMA((3,)),
            DMA((4,)),
            DMA((2,)),
        ]

    def term_copy(self, half, slot):
        place = self.place
        return remote(
            self.staged.at[half],
            self.received.at[slot],
            self.send.at[half],
            self.recv.at[slot],
            place.at(self.home, place.yc // 2 * 2 + half),
        )

    def relay_copy(self):
        return remote(
            self.staged,
            self.relayed,
            self.send.at[2],
            self.recv.at[3],
            self.place.at(self.far_middle),
        )

    def near_copies(self):
        place = self.place
        for half in range(2):
            here = jnp.logical_and(place.z == self.home, place.core == half)
            slot = lax.rem(place.z + self.home, 2)
            yield jnp.logical_and(self.near, jnp.logical_not(here)), self.term_copy(half, slot)

    def put(self, value):
        place = self.place
        self.staged[...] = value.astype(BF16).reshape(self.staged.shape)

        @pl.when(place.z == self.far_end)
        def relay():
            self.relay_copy().start()

        for away, copy in self.near_copies():

            @pl.when(away)
            def start(copy=copy):
                copy.start()

    def relay(self):
        @pl.when(self.place.z == self.far_middle)
        def add():
            self.relay_copy().wait_recv()
            self.staged[...] = (
                self.staged[...].astype(F32) + self.relayed[...].astype(F32)
            ).astype(BF16)
            for half in range(2):
                self.term_copy(half, 2).start()

    def add(self):
        place = self.place
        at_home = jnp.logical_and(self.near, place.z == self.home)

        @pl.when(self.near)
        def reduce():
            @pl.when(at_home)
            def own():
                self.received[0] = self.staged[place.core]

            for slot in range(3):

                def arrive():
                    into = self.received.at[slot]
                    remote(
                        into, into, self.send.at[0], self.recv.at[slot], place.at(place.z)
                    ).wait_recv()

                if slot:
                    arrive()
                else:
                    pl.when(jnp.logical_not(at_home))(arrive)
            value = self.received[0].astype(F32)
            for slot in range(1, 3):
                value = value + self.received[slot].astype(F32)
            self.result[...] = value.astype(BF16)
            self.hand_over().start()

        for away, copy in self.near_copies():

            @pl.when(away)
            def drain(copy=copy):
                copy.wait_send()

        @pl.when(place.z == self.far_middle)
        def drain_sums():
            for half in range(2):
                self.term_copy(half, 2).wait_send()

        @pl.when(place.z == self.far_end)
        def drain_relay():
            self.relay_copy().wait_send()

    def hand_over(self):
        return remote(
            self.result, self.result, self.last.at[0], self.last.at[1], self.place.dev(4)
        )

    def wait(self):
        @pl.when(self.near)
        def sent():
            self.hand_over().wait_send()

        @pl.when(jnp.logical_not(self.near))
        def arrived():
            self.hand_over().wait_recv()


class Turn:
    def __init__(self, place, refs):
        self.place = place
        self.staged, self.received, self.send, self.recv = refs
        self.sent = []

    @staticmethod
    def scratch(rows):
        return [VMEM((PLANES, rows, 128), BF16), VMEM((PLANES, rows, 128), BF16), DMA((4,)), DMA((4,))]

    def start(self):
        place = self.place
        for k in (2, 1, 3):
            copy = remote(
                self.staged.at[lax.rem(place.z + k, PLANES)],
                self.received.at[place.z],
                self.send.at[k],
                self.recv.at[k],
                place.zdev(k),
            )
            copy.start()
            self.sent.append(copy)
        self.received[place.z] = self.staged[place.z]

    def wait(self):
        for k in (1, 2, 3):
            into = self.received.at[lax.rem(self.place.z + 4 - k, PLANES)]
            remote(into, into, self.send.at[k], self.recv.at[k], self.place.zdev(k)).wait_recv()
        for copy in self.sent:
            copy.wait_send()


def swap_halves(values):
    lane = lax.broadcasted_iota(jnp.int32, values.shape, 1)
    return jnp.where(lane % 64 < 32, pltpu.roll(values, 96, 1), pltpu.roll(values, 32, 1))


def head_part(values, head):
    return values[:, head * 64 : head * 64 + 64]


def pack_wide(turn, pair, left, right):
    row, head = divmod(pair, 2)
    for block in range(4):
        turn.staged[pair, block * 128 : block * 128 + 128, :] = jnp.concatenate(
            [head_part(left[row * 4 + block], head), head_part(right[row * 4 + block], head)], axis=1
        )


def pack_narrow(turn, pair, values):
    row, head = divmod(pair, 2)
    for block in range(2):
        turn.staged[pair, block * 128 : block * 128 + 128, :] = jnp.concatenate(
            [
                head_part(values[row * 4 + block], head),
                head_part(values[row * 4 + block + 2], head),
            ],
            axis=1,
        )


def unpack_narrow(turn, row, block):
    rows = slice((block % 2) * 128, (block % 2) * 128 + 128)
    return jnp.concatenate(
        [head_part(turn.received[row * 2 + head, rows, :], block // 2) for head in range(2)], axis=1
    )


def unpack_wide(turn, row, block, side):
    rows = slice(block * 128, block * 128 + 128)
    return jnp.concatenate(
        [head_part(turn.received[row * 2 + head, rows, :], side) for head in range(2)], axis=1
    )


QUERY_BLOCK = 256


def segment_ends(refs, row):
    lengths = refs.row_lengths[row]
    ends = [lengths[0:1, 0:1]]
    for index in range(1, 4):
        ends.append(ends[-1] + lengths[0:1, index : index + 1])
    return ends


def segment_features(refs, plane, row):
    frame = (plane * 512 + lax.broadcasted_iota(jnp.int32, (512, 64), 0)).astype(F32)
    lane = lax.broadcasted_iota(jnp.int32, (512, 64), 1).astype(F32)
    segment = jnp.zeros((512, 64), F32)
    for end in segment_ends(refs, row)[:3]:
        segment = segment + jnp.where(frame >= end, 1.0, 0.0)
    other = jnp.where(lane < 4.0, -MASKED, 0.0)
    return (
        jnp.where(lane == segment, 0.0, other).astype(BF16),
        jnp.where(lane == segment, -1.0, 0.0).astype(BF16),
    )


def segment_reach(place, refs, slot):
    row, block = slot // 4, slot % 4
    frame = place.z * 512 + block * 128 + lax.broadcasted_iota(jnp.int32, (128, 128), 0)
    frame = frame.astype(F32)
    ends = segment_ends(refs, row)
    first, last = jnp.zeros((128, 128), F32), ends[3]
    for end in ends[:3]:
        first = jnp.where(frame >= end, end, first)
    for end in ends[2::-1]:
        last = jnp.where(frame < end, end, last)
    return first - frame, last - frame


def open_heads(place, refs, turn_qk, turn_v):
    for plane in range(PLANES):
        seg_query, seg_key = segment_features(refs, plane, place.z // 2)
        rows = slice(plane * 512, plane * 512 + 512)
        pair = turn_qk.received[plane]
        scaled = (pair[:, :64].astype(F32) * HEAD_DIM ** (-0.5)).astype(BF16)
        refs.queries[rows, :] = jnp.concatenate([scaled, seg_query], axis=1)
        refs.keys[rows, :] = jnp.concatenate([pair[:, 64:], seg_key], axis=1)
        both = turn_v.received[plane]
        turned = jnp.transpose(both.astype(F32)).astype(BF16)
        refs.values[plane * 512 : plane * 512 + 256, :] = both[:, :64]
        refs.values[plane * 512 + 256 : plane * 512 + 512, :] = both[:, 64:]
        refs.values_t[:, plane * 512 : plane * 512 + 256] = turned[:64]
        refs.values_t[:, plane * 512 + 256 : plane * 512 + 512] = turned[64:]


def attend(refs, turn_mix):
    def plane_step(plane, unused):
        parts = []
        for half in range(2):
            first = plane * 512 + half * 256
            query = refs.queries[pl.ds(pl.multiple_of(first, 256), QUERY_BLOCK), :]
            scores = dot(refs.keys[...], query, 1, 1)
            top = jnp.max(scores, axis=0, keepdims=True)
            weights = jnp.exp(scores - top)
            total = jnp.sum(weights, axis=0, keepdims=True)
            low = (weights * (1.0 / total)).astype(BF16)
            parts.append(jnp.transpose(dot(refs.values_t[...], low)))
            refs.log_total[plane * 2 + half] = jnp.broadcast_to(top + jnp.log(total), (8, 256))
        turn_mix.staged[plane] = jnp.concatenate(parts, axis=1).astype(BF16)
        return unused

    lax.fori_loop(0, PLANES, plane_step, 0)


OUT_ORDER = (1, 3, 5, 7, 2, 4, 6, 0)


def attention_forward(place, refs, stream, scatter):
    blocks = refs.attn_blocks
    blocks[place.slot(0)] = norm_rows(stream, refs.gain_attn[...])[0]

    def process(k, slot):
        if k == 0:
            refs.finish_qkv()
        value = dot(blocks[slot], flat(refs.w_qkv))
        rows = pl.ds(pl.multiple_of(lax.rem(slot, 4) * 128, 128), 128)
        cos, sin = refs.cos[rows, :], refs.sin[rows, :]
        query, key = value[:, :128], value[:, 128:256]
        refs.q_rows[slot] = (query * cos + swap_halves(query) * sin).astype(BF16)
        refs.k_rows[slot] = (key * cos + swap_halves(key) * sin).astype(BF16)
        refs.v_rows[slot] = value[:, 256:].astype(BF16)

    sent = all_gather(
        place, blocks, refs.attn_ag, process, FETCH_ORDER
    )
    turn_qk, turn_v = Turn(place, refs.turn_qk), Turn(place, refs.turn_v)
    for pair in range(PLANES):
        pack_wide(turn_qk, pair, refs.q_rows, refs.k_rows)
        pack_narrow(turn_v, pair, refs.v_rows)
    turn_qk.start()
    turn_v.start()
    turn_qk.wait()
    turn_v.wait()
    refs.after_turn()
    open_heads(place, refs, turn_qk, turn_v)
    turn_mix = Turn(place, refs.turn_mix)
    attend(refs, turn_mix)
    turn_mix.start()
    turn_mix.wait()
    refs.after_mix()
    for slot in range(8):
        refs.mixed[slot] = unpack_narrow(turn_mix, slot // 4, slot % 4)
    for k in OUT_ORDER:
        scatter.emit(k, dot(refs.mixed[place.slot(k)], flat(refs.w_o)))
    for k in (6, 2, 4, 0):
        scatter.finish(k)
    for copy in sent:
        copy.wait_send()
    total = scatter.total()
    scatter.drain()
    return stream + total


def attention_kept():
    return dict(
        attn_blocks=((8, 128, 1024), BF16),
        w_qkv=((16, 64, 384), BF16),
        w_o=((2, 64, 1024), BF16),
        queries=((2048, 128), BF16),
        keys=((2048, 128), BF16),
        values=((2048, 64), BF16),
        log_total=((8, 8, 256), F32),
        mixed=((8, 128, 128), BF16),
    )


def attend_back(refs, turn_qk, turn_v):
    refs.key_grad[...] = jnp.zeros_like(refs.key_grad)
    refs.value_grad[...] = jnp.zeros_like(refs.value_grad)

    def plane_step(plane, unused):
        parts = []
        for half in range(2):
            first = pl.multiple_of(plane * 512 + half * 256, 256)
            query = refs.queries[pl.ds(first, QUERY_BLOCK), :]
            grad = refs.mix_grads[pl.ds(first, QUERY_BLOCK), :]
            log_total = refs.log_total[plane * 2 + half][:1]
            probs = jnp.exp(dot(refs.keys[...], query, 1, 1) - log_total)
            prob_grads = dot(refs.values[...], grad, 1, 1)
            delta = jnp.sum(probs * prob_grads, axis=0, keepdims=True)
            low = (probs * (prob_grads - delta)).astype(BF16)
            refs.key_grad[...] += dot(low, query[:, :64])
            refs.value_grad[...] += dot(probs.astype(BF16), grad)
            parts.append(jnp.transpose(dot(refs.keys_t[...], low)) * HEAD_DIM ** (-0.5))
        turn_qk.staged[plane, :, 0:64] = jnp.concatenate(parts, axis=0).astype(BF16)
        return unused

    lax.fori_loop(0, PLANES, plane_step, 0)
    for plane in range(PLANES):
        rows = slice(plane * 512, plane * 512 + 512)
        turn_qk.staged[plane, :, 64:128] = refs.key_grad[rows, :].astype(BF16)
        first = plane * 512
        turn_v.staged[plane] = jnp.concatenate(
            [refs.value_grad[first : first + 256, :], refs.value_grad[first + 256 : first + 512, :]],
            axis=1,
        ).astype(BF16)


def attention_backward(place, refs, grad, stream, scatter):
    grads = refs.grads_even
    grads[place.slot(0)] = grad.astype(BF16)

    def process(k, slot):
        if k == 0:
            refs.finish_attn()
        refs.mix_rows[slot] = dot(grads[slot], flat(refs.w_o), 1, 1).astype(BF16)

    sent = all_gather(place, grads, refs.attn_ag, process, FETCH_ORDER)
    turn_mix = Turn(place, refs.turn_mix)
    for pair in range(PLANES):
        pack_narrow(turn_mix, pair, refs.mix_rows)
    turn_mix.start()
    weights = WeightGrads(place, refs, "qkv", "qkv", False)
    weights.put_out(refs.mixed, grads)
    turned = jnp.transpose(refs.keys[...].astype(F32))
    refs.keys_t[...] = turned[:64].astype(BF16)
    turn_mix.wait()
    for plane in range(PLANES):
        both = turn_mix.received[plane]
        refs.mix_grads[plane * 512 : plane * 512 + 256, :] = both[:, :64]
        refs.mix_grads[plane * 512 + 256 : plane * 512 + 512, :] = both[:, 64:]
    weights.sum_out.relay()
    refs.before_attend()
    turn_qk, turn_v = Turn(place, refs.turn_qk), Turn(place, refs.turn_v)
    attend_back(refs, turn_qk, turn_v)
    turn_qk.start()
    turn_v.start()
    refs.after_attend()
    turn_qk.wait()
    turn_v.wait()
    for slot in range(8):
        row, block = divmod(slot, 4)
        cos = refs.cos[block * 128 : block * 128 + 128, :]
        sin = refs.sin[block * 128 : block * 128 + 128, :]
        query = unpack_wide(turn_qk, row, block, 0).astype(F32)
        key = unpack_wide(turn_qk, row, block, 1).astype(F32)
        refs.qkv_grads[slot] = jnp.concatenate(
            [
                (query * cos - swap_halves(query) * sin).astype(BF16),
                (key * cos - swap_halves(key) * sin).astype(BF16),
                unpack_narrow(turn_v, row, block),
            ],
            axis=1,
        )
    for k in OUT_ORDER:
        scatter.emit(k, dot(refs.qkv_grads[place.slot(k)], flat(refs.w_qkv), 1, 1))
    for k in (6, 2, 4, 0):
        scatter.finish(k)
    weights.put_in(refs.attn_blocks, refs.qkv_grads)
    unused, saved = norm_forward(stream, refs.gain_attn[...])
    input_part, gain_grad = norm_input_grad(scatter.total(), refs.gain_attn[...], saved)
    for copy in sent:
        copy.wait_send()
    scatter.drain()
    return grad + input_part, gain_grad, weights


def fill_tables(refs):
    cos, sin = refs.cos_rows[...], refs.sin_rows[...]
    refs.cos[...] = jnp.concatenate([cos] * 4, axis=1)
    refs.sin[...] = jnp.concatenate([-sin, sin] * 2, axis=1)


def fill_channels(place, refs):
    columns = columns_of(place.pair(), 128)
    refs.taps[0:KERNEL, :] = refs.all_taps[:, columns].astype(F32)
    refs.gain_inner[...] = refs.all_inner[:, columns]
    for slot in range(8):
        refs.before[slot], refs.after[slot] = segment_reach(place, refs, slot)


def table_scratch():
    return dict(
        cos=VMEM((512, 128), F32),
        sin=VMEM((512, 128), F32),
        taps=VMEM((32, 128), F32),
        gain_inner=VMEM((1, 128), F32),
        before=VMEM((8, 128, 128), F32),
        after=VMEM((8, 128, 128), F32),
    )


class Edges:
    def __init__(self, place, refs):
        self.place = place
        self.staged, self.received, self.send, self.recv = refs

    @staticmethod
    def scratch():
        return [VMEM((2, 2, 16, 128), BF16), VMEM((2, 2, 16, 128), BF16), DMA((2,)), DMA((2,))]

    def copies(self):
        place = self.place
        for side, inside, step in ((0, place.z < PLANES - 1, 1), (1, place.z > 0, -1)):
            plane = jnp.clip(place.z + step, 0, PLANES - 1)
            yield (
                side,
                inside,
                remote(
                    self.staged.at[side],
                    self.received.at[side],
                    self.send.at[side],
                    self.recv.at[side],
                    {"seq": plane * 4 + place.yc, "row": place.x},
                ),
            )

    def start(self, blocks):
        for row in range(2):
            self.staged[0, row] = blocks[row * 4 + 3, 112:128, :]
            self.staged[1, row] = blocks[row * 4, 0:16, :]
        for side, inside, copy in self.copies():

            @pl.when(inside)
            def start(copy=copy):
                copy.start()

    def wait(self, blocks, padded):
        for slot in range(8):
            row, block = divmod(slot, 4)
            padded[slot, 16:144, :] = blocks[slot].astype(F32)
            if block > 0:
                padded[slot, 0:16, :] = blocks[slot - 1, 112:128, :].astype(F32)
            if block < 3:
                padded[slot, 144:160, :] = blocks[slot + 1, 0:16, :].astype(F32)
        place = self.place
        for side, outside in ((0, place.z == 0), (1, place.z == PLANES - 1)):
            first, rows = ((0, slice(0, 16)), (3, slice(144, 160)))[side]
            into = self.received.at[side]

            @pl.when(outside)
            def nothing():
                for row in range(2):
                    padded[row * 4 + first, rows, :] = jnp.zeros((16, 128), F32)

            @pl.when(jnp.logical_not(outside))
            def arrive():
                remote(
                    into, into, self.send.at[side], self.recv.at[side], place.zdev(1)
                ).wait_recv()
                for row in range(2):
                    padded[row * 4 + first, rows, :] = self.received[side, row].astype(F32)

        for side, inside, copy in self.copies():

            @pl.when(inside)
            def drain(copy=copy):
                copy.wait_send()


def lane_is(index):
    return lax.broadcasted_iota(jnp.int32, (128, 128), 1) == index


def put_columns(tile, slot, first, second):
    return jnp.where(lane_is(slot), first, jnp.where(lane_is(slot + 8), second, tile))


def share_columns(place, refs, tile):
    share = Exchange(place, refs[0], refs[1:])
    own = place.slot(0)
    share.blocks[own] = jnp.transpose(tile)[:16]
    share.start(lambda k: share.blocks.at[own])
    share.wait()
    return share.blocks[...]


def back_to_columns(first, second):
    rows = jnp.concatenate([first, second, jnp.zeros((112, 128), F32)], axis=0)
    return jnp.transpose(rows)


def column(tile, slot):
    return jnp.sum(jnp.where(lane_is(slot), tile, 0.0), axis=1, keepdims=True)


def kept_frames(value, offset, before, after):
    if offset < 0:
        return jnp.where(before <= offset, value, 0.0)
    if offset > 0:
        return jnp.where(after > offset, value, 0.0)
    return value


CHUNK = 64


def convolve(refs):
    taps = [refs.taps[j : j + 1, :] for j in range(KERNEL)]

    def step(slot, tile):
        for first in range(0, 128, CHUNK):
            rows = slice(first, first + CHUNK)
            before, after = refs.before[slot, rows, :], refs.after[slot, rows, :]
            total = jnp.zeros((CHUNK, 128), F32)
            for j in range(KERNEL):
                start = first + j + 1
                value = refs.glu_padded[slot, start : start + CHUNK, :]
                total = total + taps[j] * kept_frames(value, j - HALF, before, after)
            refs.conv[slot, rows, :] = total
        value = refs.conv[slot]
        mean = jnp.mean(value, axis=1, keepdims=True)
        center = value - mean
        return put_columns(tile, slot, mean, jnp.sum(center * center, axis=1, keepdims=True))

    return lax.fori_loop(0, 8, step, jnp.zeros((128, 128), F32))


def inner_norm(refs, slot):
    mean, inverse = column(refs.inner_stats[...], slot), column(refs.inner_stats[...], slot + 8)
    unit_part = (refs.conv[slot] - mean) * inverse
    return unit_part, inverse


def conv_forward(place, refs, stream, scatter):
    blocks = refs.conv_blocks
    blocks[place.slot(0)] = norm_rows(stream, refs.gain_conv[...])[0]

    def process(k, slot):
        if k == 0:
            refs.finish_ci()
        value = dot(blocks[slot], flat(refs.w_ci))
        refs.gate_up[slot] = value
        refs.glu[slot] = (value[:, :128] * jax.nn.sigmoid(value[:, 128:])).astype(BF16)

    sent = all_gather(place, blocks, refs.conv_ag, process, FETCH_ORDER)
    edges = Edges(place, refs.edges)
    edges.start(refs.glu)
    edges.wait(refs.glu, refs.glu_padded)
    stats = share_columns(place, refs.stats, convolve(refs))
    refs.conv_middle()
    means, spreads = stats[:, :8], stats[:, 8:]
    mean = jnp.mean(means, axis=0)
    spread = jnp.sum(spreads + 128.0 * jnp.square(means - mean[None]), axis=0) / 1024.0
    refs.inner_stats[...] = back_to_columns(mean, lax.rsqrt(spread + EPSILON))
    refs.finish_co()
    for k in OUT_ORDER:
        slot = place.slot(k)
        unit_part, unused = inner_norm(refs, slot)
        active = sigmoid_linear(unit_part * refs.gain_inner[...]).astype(BF16)
        refs.conv_active[slot] = active
        scatter.emit(k, dot(active, flat(refs.w_co)))
    for k in (6, 2, 4, 0):
        scatter.finish(k)
    for copy in sent:
        copy.wait_send()
    total = scatter.total()
    scatter.drain()
    return stream + total


def conv_kept():
    return dict(
        conv_blocks=((8, 128, 1024), BF16),
        w_ci=((16, 64, 256), BF16),
        w_co=((2, 64, 1024), BF16),
        gate_up=((8, 128, 256), F32),
        glu_padded=((8, 160, 128), F32),
        conv=((8, 128, 128), F32),
        inner_stats=((128, 128), F32),
        conv_active=((8, 128, 128), BF16),
    )


STATS = [VMEM((8, 16, 128), F32), DMA((8,)), DMA((8,))]


def convolve_back(refs):
    taps = [refs.taps[j : j + 1, :] for j in range(KERNEL)]
    refs.tap_sums[...] = jnp.zeros_like(refs.tap_sums)

    def step(slot, unused):
        for first in range(0, 128, CHUNK):
            rows = slice(first, first + CHUNK)
            before, after = refs.before[slot, rows, :], refs.after[slot, rows, :]
            total = jnp.zeros((CHUNK, 128), F32)
            grad = refs.conv_grad_padded[slot, first + 16 : first + 16 + CHUNK, :]
            for j in range(KERNEL):
                offset = j - HALF
                start = first + 16 - offset
                value = refs.conv_grad_padded[slot, start : start + CHUNK, :]
                total = total + taps[j] * kept_frames(value, -offset, before, after)
                start = first + 16 + offset
                value = refs.glu_padded[slot, start : start + CHUNK, :]
                product = kept_frames(value * grad, offset, before, after)
                refs.tap_sums[j] += jnp.sum(product.reshape(CHUNK // 8, 8, 128), axis=0)
            refs.glu_grad[slot, rows, :] = total
        return unused

    lax.fori_loop(0, 8, step, 0)
    return jnp.sum(refs.tap_sums[...], axis=1)


def conv_backward(place, refs, grad, stream, scatter):
    grads = refs.grads_odd
    grads[place.slot(0)] = grad.astype(BF16)
    gain = refs.gain_inner[...]

    def process(k, slot):
        if k == 0:
            refs.finish_conv()
        back = dot(grads[slot], flat(refs.w_co), 1, 1)
        unit_part, unused = inner_norm(refs, slot)
        refs.inner_grad[slot] = back * sigmoid_linear_grad(unit_part * gain)

    sent = all_gather(place, grads, refs.conv_ag, process, FETCH_ORDER)

    refs.conv_begin()

    def sums(slot, current):
        tile, gain_grad = current
        value = refs.inner_grad[slot]
        unit_part, unused = inner_norm(refs, slot)
        scaled = value * gain
        tile = put_columns(
            tile,
            slot,
            jnp.sum(scaled, axis=1, keepdims=True),
            jnp.sum(scaled * unit_part, axis=1, keepdims=True),
        )
        return tile, gain_grad + jnp.sum(value * unit_part, axis=0, keepdims=True)

    tile, inner_gain_grad = lax.fori_loop(
        0, 8, sums, (jnp.zeros((128, 128), F32), jnp.zeros((1, 128), F32))
    )
    stats = share_columns(place, refs.stats, tile)
    means = jnp.sum(stats, axis=0) / 1024.0
    refs.grad_stats[...] = back_to_columns(means[:8], means[8:])
    weights = WeightGrads(place, refs, "conv", "conv", False)
    weights.put_out(refs.conv_active, grads)

    def input_grad(slot, unused):
        unit_part, inverse = inner_norm(refs, slot)
        tile = refs.grad_stats[...]
        refs.conv_grad[slot] = (
            inverse
            * (
                refs.inner_grad[slot] * gain
                - column(tile, slot)
                - unit_part * column(tile, slot + 8)
            )
        ).astype(BF16)
        return unused

    lax.fori_loop(0, 8, input_grad, 0)
    edges = Edges(place, refs.edges)
    edges.start(refs.conv_grad)
    edges.wait(refs.conv_grad, refs.conv_grad_padded)
    refs.conv_middle()
    tap_grads = convolve_back(refs)
    for k in OUT_ORDER:
        slot = place.slot(k)
        value = refs.gate_up[slot]
        glu_grad, sigma = refs.glu_grad[slot], jax.nn.sigmoid(value[:, 128:])
        refs.gate_grads[slot] = jnp.concatenate(
            [glu_grad * sigma, glu_grad * value[:, :128] * sigma * (1.0 - sigma)], axis=1
        ).astype(BF16)
        scatter.emit(k, dot(refs.gate_grads[slot], flat(refs.w_ci), 1, 1))
    for k in (6, 2, 4, 0):
        scatter.finish(k)
    weights.put_in(refs.conv_blocks, refs.gate_grads)
    unused, saved = norm_forward(stream, refs.gain_conv[...])
    input_part, gain_grad = norm_input_grad(scatter.total(), refs.gain_conv[...], saved)
    for copy in sent:
        copy.wait_send()
    scatter.drain()
    return grad + input_part, gain_grad, inner_gain_grad, tap_grads, weights


class Traffic:
    def __init__(self, refs, sems):
        self.refs, self.sems = refs, sems
        self.count = 0

    def start(self, pairs):
        copies = []
        for source, target in pairs:
            copy = pltpu.make_async_copy(source, target, self.sems.at[self.count])
            copy.start()
            copies.append(copy)
            self.count += 1

        def finish():
            for copy in copies:
                copy.wait()

        return finish

    def save(self, names):
        return self.start(
            [(getattr(self.refs, name), getattr(self.refs, "keep_" + name)) for name in names]
        )

    def load(self, names):
        return self.start(
            [(getattr(self.refs, "keep_" + name), getattr(self.refs, name)) for name in names]
        )


def ffn_kept():
    return dict(
        blocks=((8, 128, 1024), BF16),
        hidden=((8, 128, 512), F32),
        w_in=((16, 64, 512), BF16),
        w_out=((4, 128, 1024), BF16),
    )


SCATTER_SEMS = [DMA((8,)), DMA((8,))]


def forward_body(refs):
    place = Place()
    place.enter()
    own = place.slot(0)
    traffic = Traffic(refs, refs.traffic)
    gather_in = GatherRows(place, refs.w_in_rows, refs.w_in, refs.gather_in, ffn_pieces)
    refs.row_lengths[place.x] = refs.own_lengths[...]
    lengths = remote(
        refs.own_lengths,
        refs.row_lengths.at[place.x],
        refs.length_sems.at[0],
        refs.length_sems.at[1],
        place.dev(4),
    )
    lengths.start()
    stream = refs.stream[...].astype(F32)
    refs.blocks[own] = norm_rows(stream, refs.gain_ffn1[...])[0]
    held = Refs()
    rows = pl.ds(place.x * 128, 128)

    def process_in(k, slot):
        if k == 0:
            gather_in.relay()
            gather_in.finish()
            held.qkv.along_z()
            held.o = GatherHalf(place, refs.o_rows, refs.w_o, refs.gather_o)
        value = dot(refs.blocks[slot], flat(refs.w_in))
        refs.hidden[slot] = value
        refs.active[slot] = sigmoid_linear(value).astype(BF16)

    def begin():
        gather_in.along_z()
        held.out = GatherBlocks(place, refs.w_out_rows.at[rows], refs.w_out, refs.gather_out)
        held.qkv = GatherRows(place, refs.qkv_rows, refs.w_qkv, refs.gather_qkv, head_pieces)
        lengths.wait()
        fill_tables(refs)
        fill_channels(place, refs)

    order = (begin, 0, 1, 2, 4, 3, 5, 6, 7, 0, 1, 2, 4, 3, 5, 6, 7)
    sent = all_gather(place, refs.blocks, refs.ffn_ag, process_in, order)
    held.out.relay()
    held.out.finish()
    scatter = Scatter(place, refs.scatter, refs.ffn_scatter)
    for k in OUT_ORDER:
        scatter.emit(k, dot(refs.active[place.slot(k)], flat(refs.w_out)))
    for k in (6, 2, 4, 0):
        scatter.finish(k)
    saved = [traffic.save(ffn_kept())]
    gather_ci = GatherRows(place, refs.ci_rows, refs.w_ci, refs.gather_ci, channel_pieces)
    gather_next = GatherRows(place, refs.next_in_rows, refs.next_in, refs.gather_next, ffn_pieces)
    total = scatter.total()
    held.qkv.relay()
    held.o.relay()
    gather_ci.along_z()
    gather_co = GatherHalf(place, refs.co_rows, refs.w_co, refs.gather_co)
    for copy in sent:
        copy.wait_send()
    scatter.drain()
    stream = stream + 0.5 * total
    refs.stream_one[...] = stream

    def after_turn():
        gather_ci.relay()
        gather_co.relay()

    def after_mix():
        held.o.finish()
        gather_next.along_z()
        held.next_out = GatherBlocks(
            place, refs.next_out_rows.at[rows], refs.next_out, refs.gather_next_out
        )

    def conv_middle():
        gather_next.relay()
        held.next_out.relay()

    refs.after_turn, refs.after_mix, refs.conv_middle = after_turn, after_mix, conv_middle
    refs.finish_qkv, refs.finish_ci, refs.finish_co = (
        held.qkv.finish,
        gather_ci.finish,
        gather_co.finish,
    )
    stream = attention_forward(
        place, refs, stream, Scatter(place, refs.scatter, refs.attn_scatter)
    )
    saved.append(traffic.save(attention_kept()))
    refs.stream_two[...] = stream
    stream = conv_forward(place, refs, stream, Scatter(place, refs.scatter, refs.conv_scatter))
    saved.append(traffic.save(conv_kept()))
    refs.stream_three[...] = stream
    gather_next.finish()
    held.next_out.finish()
    for finish in saved:
        finish()


def scratch_of(kept):
    return {name: VMEM(shape, dtype) for name, (shape, dtype) in kept.items()}


def forward_call(ins):
    kept = {**ffn_kept(), **attention_kept(), **conv_kept()}
    outs = dict(
        stream_one=((128, 1024), F32, VMEM),
        stream_two=((128, 1024), F32, VMEM),
        stream_three=((128, 1024), F32, VMEM),
        next_in=((16, 64, 512), BF16, pl.ANY),
        next_out=((4, 128, 1024), BF16, pl.ANY),
    )
    outs["row_lengths"] = ((2, 8, 128), F32, VMEM)
    for name, (shape, dtype) in kept.items():
        outs["keep_" + name] = (shape, dtype, pl.ANY)
    scratch = dict(
        scratch_of(kept),
        active=VMEM((8, 128, 512), BF16),
        gather_in=GatherRows.scratch(),
        gather_out=GatherBlocks.scratch(),
        gather_qkv=GatherRows.scratch(),
        gather_o=GatherHalf.scratch(),
        gather_ci=GatherRows.scratch(),
        gather_co=GatherHalf.scratch(),
        gather_next=GatherRows.scratch(),
        gather_next_out=GatherBlocks.scratch(),
        length_sems=DMA((2,)),
        **table_scratch(),
        traffic=DMA((len(kept),)),
        scatter=Scatter.scratch(128, 1024),
        ffn_ag=AG_SEMS,
        attn_ag=AG_SEMS,
        conv_ag=AG_SEMS,
        ffn_scatter=SCATTER_SEMS,
        attn_scatter=SCATTER_SEMS,
        conv_scatter=SCATTER_SEMS,
        q_rows=VMEM((8, 128, 128), BF16),
        k_rows=VMEM((8, 128, 128), BF16),
        v_rows=VMEM((8, 128, 128), BF16),
        turn_qk=Turn.scratch(512),
        turn_v=Turn.scratch(256),
        turn_mix=Turn.scratch(256),
        values_t=VMEM((64, 2048), BF16),
        glu=VMEM((8, 128, 128), BF16),
        edges=Edges.scratch(),
        stats=STATS,
    )
    return kernel_call(forward_body, 1, ins, outs, scratch)


class SmallSum:
    def __init__(self, place, refs):
        self.place, self.refs = place, refs
        self.first = Exchange(place, refs.small_first, refs.small_first_sems)
        self.last = Exchange(place, refs.small, refs.small_last_sems)
        self.sent = []

    def start(self):
        refs, place = self.refs, self.place

        def part(slot):
            return refs.gain_grads.at[:, columns_of(slot, 128)]

        self.first.blocks[place.slot(0)] = refs.gain_grads[:, columns_of(place.slot(0), 128)]
        self.first.start(lambda k: part(place.slot(k)))

    def along_z(self):
        refs, place = self.refs, self.place
        self.first.wait()
        refs.small_planes[place.z, 0:8, :] = jnp.sum(self.first.blocks[...], axis=0)
        refs.small_planes[place.z, 8:48, :] = refs.channel_grads[...]
        send, recv = refs.small_z_sems
        rows = refs.small_planes.at[place.z]
        for k in (1, 2, 3):
            copy = remote(rows, rows, send.at[k], recv.at[k], place.zdev(k))
            copy.start()
            self.sent.append(copy)

    def spread(self):
        refs, place = self.refs, self.place
        send, recv = refs.small_z_sems
        for k in (1, 2, 3):
            into = refs.small_planes.at[lax.rem(place.z + 4 - k, PLANES)]
            remote(into, into, send.at[k], recv.at[k], place.zdev(k)).wait_recv()
        for copy in self.sent:
            copy.wait_send()
        own = place.slot(0)
        self.last.blocks[own] = jnp.sum(refs.small_planes[...], axis=0)
        self.last.start(lambda k: self.last.blocks.at[own])

    def wait(self):
        self.last.wait()


def backward_body(refs):
    place = Place()
    place.enter()
    own = place.slot(0)
    traffic = Traffic(refs, refs.traffic)
    ready = traffic.start([(refs.next_in, refs.w_in), (refs.next_out, refs.w_out)])
    refs.finish_conv = traffic.load(conv_kept())
    refs.finish_attn = traffic.load(attention_kept())
    fill_tables(refs)
    fill_channels(place, refs)
    refs.gain_grads[...] = jnp.zeros_like(refs.gain_grads)
    refs.channel_grads[...] = jnp.zeros_like(refs.channel_grads)
    stream = refs.stream_three[...]
    low, saved = norm_rows(stream, refs.gain_ffn2[...])
    refs.blocks[own] = low
    total = ffn_forward(
        place,
        refs,
        refs.blocks,
        refs.hidden,
        refs.w_in,
        refs.w_out,
        refs.ffn2_ag,
        Scatter(place, refs.scatter, refs.ffn2_scatter),
        ready,
    )
    final, saved_final = norm_forward(stream + 0.5 * total, refs.gain_out[...])
    refs.output[...] = final.astype(BF16)
    grad, refs.gain_grads[4:5, :] = norm_input_grad(
        refs.cotangent[...].astype(F32), refs.gain_out[...], saved_final
    )
    refs.grads_even[own] = (0.5 * grad).astype(BF16)
    scatter = Scatter(place, refs.scatter, refs.ffn2_scatter_back)
    sent = ffn_backward(
        place,
        refs.blocks,
        refs.grads_even,
        refs.hidden,
        refs.hidden_grads,
        refs.active,
        refs.w_in,
        refs.w_out,
        refs.ffn2_ag_back,
        scatter,
        lambda: None,
    )
    weights_two = WeightGrads(place, refs, "ffn2", "ffn", True)
    weights_two.put_out(refs.active, refs.grads_even)
    weights_two.put_in(refs.blocks, refs.hidden_grads)
    input_part, refs.gain_grads[3:4, :] = norm_input_grad(
        scatter.total(), refs.gain_ffn2[...], saved
    )
    grad = grad + input_part
    for copy in sent:
        copy.wait_send()
    scatter.drain()
    load_first = traffic.load(ffn_kept())
    refs.conv_begin, refs.conv_middle = weights_two.sum_out.relay, weights_two.sum_in.relay
    grad, refs.gain_grads[2:3, :], inner, taps, weights_three = conv_backward(
        place, refs, grad, refs.stream_two[...], Scatter(place, refs.scatter, refs.conv_scatter)
    )
    refs.channel_grads[0:32, :] = taps
    refs.channel_grads[32:33, :] = inner

    def before_attend():
        weights_two.share()
        weights_three.relay()

    refs.before_attend, refs.after_attend = before_attend, weights_three.share
    grad, refs.gain_grads[1:2, :], weights_four = attention_backward(
        place, refs, grad, refs.stream_one[...], Scatter(place, refs.scatter, refs.attn_scatter)
    )
    weights_two.wait()
    weights_three.wait()
    refs.grads_odd[own] = (0.5 * grad).astype(BF16)
    scatter = Scatter(place, refs.scatter, refs.ffn1_scatter)
    sent = ffn_backward(
        place,
        refs.blocks,
        refs.grads_odd,
        refs.hidden,
        refs.hidden_grads,
        refs.active,
        refs.w_in,
        refs.w_out,
        refs.ffn1_ag,
        scatter,
        load_first,
    )
    weights_one = WeightGrads(place, refs, "ffn1", "ffn", True)
    weights_one.put_out(refs.active, refs.grads_odd)
    weights_one.put_in(refs.blocks, refs.hidden_grads)
    weights_four.sum_in.relay()
    weights_four.share()
    unused, saved = norm_forward(refs.stream[...].astype(F32), refs.gain_ffn1[...])
    input_part, refs.gain_grads[0:1, :] = norm_input_grad(
        scatter.total(), refs.gain_ffn1[...], saved
    )
    small = SmallSum(place, refs)
    small.start()
    refs.grad_stream[...] = grad + input_part
    for copy in sent:
        copy.wait_send()
    scatter.drain()
    weights_one.relay()
    small.along_z()
    small.spread()
    weights_four.wait()
    weights_one.share()
    small.wait()
    weights_one.wait()


MODULES = (("ffn1", 512, True), ("qkv", 384, False), ("conv", 256, False), ("ffn2", 512, True))


def backward_call(ins):
    kept = {**ffn_kept(), **attention_kept(), **conv_kept()}
    outs = dict(
        output=((128, 1024), BF16, VMEM),
        grad_stream=((128, 1024), F32, VMEM),
        small=((8, 48, 128), F32, VMEM),
    )
    scratch = dict(
        scratch_of(kept),
        active=VMEM((8, 128, 512), BF16),
        hidden_grads=VMEM((8, 128, 512), BF16),
        grads_even=VMEM((8, 128, 1024), BF16),
        grads_odd=VMEM((8, 128, 1024), BF16),
        traffic=DMA((2 + len(kept),)),
        scatter=Scatter.scratch(128, 1024),
        ffn2_ag=AG_SEMS,
        ffn2_ag_back=AG_SEMS,
        conv_ag=AG_SEMS,
        attn_ag=AG_SEMS,
        ffn1_ag=AG_SEMS,
        ffn2_scatter=SCATTER_SEMS,
        ffn2_scatter_back=SCATTER_SEMS,
        conv_scatter=SCATTER_SEMS,
        attn_scatter=SCATTER_SEMS,
        ffn1_scatter=SCATTER_SEMS,
        mix_rows=VMEM((8, 128, 128), BF16),
        mix_grads=VMEM((2048, 64), BF16),
        keys_t=VMEM((64, 2048), BF16),
        turn_qk=Turn.scratch(512),
        turn_v=Turn.scratch(256),
        turn_mix=Turn.scratch(256),
        key_grad=VMEM((2048, 64), F32),
        value_grad=VMEM((2048, 64), F32),
        qkv_grads=VMEM((8, 128, 384), BF16),
        **table_scratch(),
        inner_grad=VMEM((8, 128, 128), F32),
        grad_stats=VMEM((128, 128), F32),
        conv_grad=VMEM((8, 128, 128), BF16),
        conv_grad_padded=VMEM((8, 160, 128), F32),
        glu_grad=VMEM((8, 128, 128), F32),
        gate_grads=VMEM((8, 128, 256), BF16),
        tap_sums=VMEM((32, 8, 128), F32),
        edges=Edges.scratch(),
        stats=STATS,
        gain_grads=VMEM((8, 1024), F32),
        channel_grads=VMEM((40, 128), F32),
        small_first=VMEM((8, 8, 128), F32),
        small_planes=VMEM((PLANES, 48, 128), F32),
        small_first_sems=[DMA((8,)), DMA((8,))],
        small_z_sems=[DMA((4,)), DMA((4,))],
        small_last_sems=[DMA((8,)), DMA((8,))],
        **WeightGrads.sums("ffn", 512, True),
        **WeightGrads.sums("qkv", 384, False),
        **WeightGrads.sums("conv", 256, False),
    )
    for name, width, wide in MODULES:
        outs.update(WeightGrads.outs(name, width, wide))
        scratch.update(WeightGrads.scratch(name, width, wide))
    return kernel_call(backward_body, 2, ins, outs, scratch)


def unpack_body(count, *refs):
    sources, outs = refs[:count], refs[count : 2 * count + 8]
    (
        output,
        grad_stream,
        small,
        ffn1_in,
        ffn1_out,
        qkv_in,
        qkv_out,
        conv_in,
        conv_out,
        ffn2_in,
        ffn2_out,
    ) = sources
    outs[0][...] = output[...]
    outs[1][...] = grad_stream[...]
    for slot in range(8):
        x, yc = divmod(slot, 4)
        pair = ((x * 2 + yc % 2) * 2 + yc // 2) * 128
        for index, row in enumerate((0, 1, 2, None, 3, 4)):
            if row is not None:
                outs[2 + index][:, slot * 128 : slot * 128 + 128] = small[slot, row : row + 1, :]
        outs[5][:, pair : pair + 128] = small[slot, 40:41, :]
        outs[8][:, pair : pair + 128] = small[slot, 8 : 8 + KERNEL, :]
        for source, out in ((ffn1_in, outs[9]), (ffn2_in, outs[15])):
            for plane in range(PLANES):
                column = ((plane * 4 + yc) * 2 + x) * 128
                out[:, column : column + 128] = source[
                    slot, :, plane * 128 : plane * 128 + 128
                ].astype(F32)
        for source, out, kinds in ((qkv_in, outs[11], 3), (conv_in, outs[13], 2)):
            for kind in range(kinds):
                column = kind * 1024 + pair
                out[:, column : column + 128] = source[slot, :, kind * 128 : kind * 128 + 128].astype(
                    F32
                )
    for source, out in ((ffn1_out, outs[10]), (ffn2_out, outs[16])):
        out[0:128, :] = source[0].astype(F32)
        out[128:256, :] = source[1].astype(F32)
    outs[12][...] = qkv_out[...].astype(F32)
    outs[14][...] = conv_out[...].astype(F32)


def unpack_call(backward):
    arrays = list(backward.values())
    gain = jax.ShapeDtypeStruct((1, 1024), F32)
    shapes = [
        jax.ShapeDtypeStruct((128, 1024), BF16),
        jax.ShapeDtypeStruct((128, 1024), F32),
        *[gain] * 6,
        jax.ShapeDtypeStruct((KERNEL, 1024), F32),
    ] + [
        jax.ShapeDtypeStruct(shape, F32)
        for shape in (
            (64, 4096),
            (256, 1024),
            (64, 3072),
            (64, 1024),
            (64, 2048),
            (64, 1024),
            (64, 4096),
            (256, 1024),
        )
    ]
    whole = pl.BlockSpec(memory_space=VMEM)
    return pl.pallas_call(
        functools.partial(unpack_body, len(arrays)),
        out_shape=shapes,
        in_specs=[whole] * len(arrays),
        out_specs=[whole] * len(shapes),
        compiler_params=pltpu.CompilerParams(vmem_limit_bytes=VMEM_LIMIT),
    )(*arrays)


def local_planes(
    inputs,
    lengths,
    gain_ffn1,
    gain_attn,
    gain_conv,
    gain_inner,
    gain_ffn2,
    gain_out,
    conv_kernel,
    ffn1_in,
    ffn1_out,
    attn_qkv,
    attn_out,
    conv_in,
    conv_out,
    ffn2_in,
    ffn2_out,
    cotangent,
):
    plane = lax.axis_index("seq") // 4
    cos, sin = rotary_tables(plane * 512 + jnp.arange(512, dtype=jnp.int32))
    shared = dict(
        stream=(inputs[0], VMEM),
        gain_ffn1=(gain_ffn1[None], VMEM),
        gain_attn=(gain_attn[None], VMEM),
        gain_conv=(gain_conv[None], VMEM),
        all_inner=(gain_inner[None], VMEM),
        all_taps=(conv_kernel, VMEM),
        cos_rows=(cos, VMEM),
        sin_rows=(sin, VMEM),
    )
    forward = forward_call(
        dict(
            shared,
            own_lengths=(jnp.pad(lengths.astype(F32), ((0, 7), (0, 124))), VMEM),
            w_in_rows=(ffn1_in, pl.ANY),
            w_out_rows=(ffn1_out, pl.ANY),
            qkv_rows=(attn_qkv, pl.ANY),
            o_rows=(attn_out, pl.ANY),
            ci_rows=(conv_in, pl.ANY),
            co_rows=(conv_out, pl.ANY),
            next_in_rows=(ffn2_in, pl.ANY),
            next_out_rows=(ffn2_out, pl.ANY),
        )
    )
    ins = dict(
        shared,
        cotangent=(cotangent[0], VMEM),
        gain_ffn2=(gain_ffn2[None], VMEM),
        gain_out=(gain_out[None], VMEM),
    )
    for name, array in forward.items():
        held = name.startswith("stream") or name == "row_lengths"
        ins[name] = (array, VMEM if held else pl.ANY)
    results = unpack_call(backward_call(ins))
    return (
        results[0][None],
        results[1][None],
        *[gain[0] for gain in results[2:8]],
        *results[8:],
    )


def solution(mesh):
    return jax.shard_map(
        local_planes if mesh.shape["seq"] == 16 and mesh.shape["row"] == 2 else local,
        mesh=mesh,
        in_specs=(
            P("row", "seq", None),
            P("row", None),
            P(),
            P(),
            P(),
            P(),
            P(),
            P(),
            P(),
            P("seq", None),
            P("seq", None),
            P("seq", None),
            P("seq", None),
            P("seq", None),
            P("seq", None),
            P("seq", None),
            P("seq", None),
            P("row", "seq", None),
        ),
        out_specs=(
            P("row", "seq", None),
            P("row", "seq", None),
            P(),
            P(),
            P(),
            P(),
            P(),
            P(),
            P(),
            P("seq", None),
            P("seq", None),
            P("seq", None),
            P("seq", None),
            P("seq", None),
            P("seq", None),
            P("seq", None),
            P("seq", None),
        ),
        check_vma=False,
    )
```

```python
import functools
import math

import jax
import jax.numpy as jnp
from jax import lax
from jax.experimental import pallas as pl
from jax.experimental.pallas import tpu as pltpu
from jax.sharding import PartitionSpec as P

HEADS = 16
HEAD_DIM = 64
KERNEL = 31
HALF = 15


EPSILON = 1e-05
MASKED = -1e30


def with_halo(block, sides, width):
    for axis, dim in sides:
        count = lax.axis_size(axis)
        forward = [(i, i + 1) for i in range(count - 1)]
        backward = [(target, source) for source, target in forward]
        low = lax.ppermute(
            lax.slice_in_dim(block, block.shape[dim] - width, None, axis=dim), axis, forward
        )
        high = lax.ppermute(lax.slice_in_dim(block, 0, width, axis=dim), axis, backward)
        block = jnp.concatenate([low, block, high], axis=dim)
    return block


def shifted(array, axis, by):
    size = lax.axis_size(axis)
    return lax.ppermute(array, axis, [(i, (i + by) % size) for i in range(size)])


def segment_of(positions, seg_lengths):
    boundary = jnp.cumsum(seg_lengths)[:-1]
    return jnp.sum((positions[:, None] >= boundary[None, :]).astype(jnp.int32), axis=1)


def rotary_tables(positions):
    half_dim = HEAD_DIM // 2
    inverse = jnp.exp(-jnp.log(10000.0) * jnp.arange(half_dim, dtype=jnp.float32) / half_dim)
    angles = positions.astype(jnp.float32)[:, None] * inverse[None, :]
    return (jnp.cos(angles), jnp.sin(angles))


def split_heads(values):
    return values.reshape(values.shape[0], HEADS, HEAD_DIM)


def rotate(values, cos_table, sin_table):
    half_dim = HEAD_DIM // 2
    shaped = split_heads(values)
    first_half = shaped[..., :half_dim]
    second_half = shaped[..., half_dim:]
    cos_heads = cos_table[:, None, :]
    sin_heads = sin_table[:, None, :]
    turned = jnp.concatenate(
        [
            first_half * cos_heads - second_half * sin_heads,
            second_half * cos_heads + first_half * sin_heads,
        ],
        axis=-1,
    )
    return turned.reshape(values.shape)


def unrotate(grads, cos_table, sin_table):
    half_dim = HEAD_DIM // 2
    shaped = split_heads(grads)
    first_half = shaped[..., :half_dim]
    second_half = shaped[..., half_dim:]
    cos_heads = cos_table[:, None, :]
    sin_heads = sin_table[:, None, :]
    turned = jnp.concatenate(
        [
            first_half * cos_heads + second_half * sin_heads,
            second_half * cos_heads - first_half * sin_heads,
        ],
        axis=-1,
    )
    return turned.reshape(grads.shape)


def norm_forward(values, gain):
    center = values - jnp.mean(values, axis=-1, keepdims=True)
    spread = jnp.mean(center * center, axis=-1, keepdims=True)
    inverse = lax.rsqrt(spread + EPSILON)
    unit_part = center * inverse
    return (unit_part * gain, (unit_part, inverse))


def norm_backward(grads, gain, saved):
    unit_part, inverse = saved
    scaled = grads * gain
    gain_grad = jnp.sum(grads * unit_part, axis=0)
    input_part = inverse * (
        scaled
        - jnp.mean(scaled, axis=-1, keepdims=True)
        - unit_part * jnp.mean(scaled * unit_part, axis=-1, keepdims=True)
    )
    return (input_part, gain_grad)


def sigmoid_linear(values):
    return values * jax.nn.sigmoid(values)


def sigmoid_linear_grad(values):
    sigma = jax.nn.sigmoid(values)
    return sigma * (1.0 + values * (1.0 - sigma))


def project(left_side, weight):
    return (
        jnp.dot(
            left_side,
            lax.all_gather(weight, "seq", axis=0, tiled=True),
            preferred_element_type=jnp.float32,
        ),
        weight,
    )


def project_back(grad_side, weight):
    return lax.dot_general(
        grad_side,
        lax.all_gather(weight, "seq", axis=0, tiled=True),
        (((1,), (1,)), ((), ())),
        preferred_element_type=jnp.float32,
    )


def weight_grad(left_side, grad_side):
    return lax.psum_scatter(
        lax.dot_general(
            left_side, grad_side, (((0,), (0,)), ((), ())), preferred_element_type=jnp.float32
        ).astype(jnp.bfloat16),
        "seq",
        scatter_dimension=0,
        tiled=True,
    ).astype(jnp.float32)


def over_blocks(advance, running, pieces):
    total_rows = pieces[0].shape[0]
    block_size = math.gcd(total_rows, 512)
    number = total_rows // block_size
    stacked = tuple((piece.reshape((number, block_size) + piece.shape[1:]) for piece in pieces))

    def scan_step(current, block_item):
        block_index, blocks = block_item
        return (advance(current, blocks, block_index * block_size), None)

    running, unused = lax.scan(scan_step, running, (jnp.arange(number, dtype=jnp.int32), stacked))
    return running


def block_scores(query_heads, key_heads, query_segments, key_segments):
    scale = HEAD_DIM ** (-0.5)
    raw_scores = (
        jnp.einsum("qhd,khd->hqk", query_heads, key_heads, preferred_element_type=jnp.float32)
        * scale
    )
    return jnp.where((query_segments[:, None] == key_segments[None, :])[None], raw_scores, MASKED)


def pair_grads(
    query_rows, grad_rows, log_total, delta, query_segments, key_rows, value_rows, key_segments
):
    scale = HEAD_DIM ** (-0.5)
    query_heads = split_heads(query_rows)
    grad_heads = split_heads(grad_rows)
    key_heads = split_heads(key_rows)
    value_heads = split_heads(value_rows)
    probs = jnp.exp(
        block_scores(query_heads, key_heads, query_segments, key_segments) - log_total[:, :, None]
    )
    prob_grads = jnp.einsum(
        "qhd,khd->hqk", grad_heads, value_heads, preferred_element_type=jnp.float32
    )
    score_grads = (probs * (prob_grads - delta[:, :, None])).astype(jnp.bfloat16)
    query_grad = (
        jnp.einsum("hqk,khd->qhd", score_grads, key_heads, preferred_element_type=jnp.float32)
        * scale
    )
    key_grad = (
        jnp.einsum("hqk,qhd->khd", score_grads, query_heads, preferred_element_type=jnp.float32)
        * scale
    )
    value_grad = jnp.einsum(
        "hqk,qhd->khd", probs.astype(jnp.bfloat16), grad_heads, preferred_element_type=jnp.float32
    )
    return (
        query_grad.reshape(query_rows.shape),
        key_grad.reshape(key_rows.shape),
        value_grad.reshape(value_rows.shape),
    )


def local(
    inputs,
    lengths,
    gain_ffn1,
    gain_attn,
    gain_conv,
    gain_inner,
    gain_ffn2,
    gain_out,
    conv_kernel,
    ffn1_in,
    ffn1_out,
    attn_qkv,
    attn_out,
    conv_in,
    conv_out,
    ffn2_in,
    ffn2_out,
    cotangent,
):
    frame_count = inputs.shape[1]
    model_width = inputs.shape[2]
    device_count = lax.axis_size("seq")
    position_index = lax.axis_index("seq")
    seg_lengths = lengths[0]
    first_frame = position_index * frame_count
    local_frames = jnp.arange(frame_count, dtype=jnp.int32)
    positions = first_frame + local_frames
    query_segments = segment_of(positions, seg_lengths)
    cos_table, sin_table = rotary_tables(positions)
    stream = inputs[0].astype(jnp.float32)
    normed_one, saved_one = norm_forward(stream, gain_ffn1)
    normed_one_low = normed_one.astype(jnp.bfloat16)
    hidden_one, kept_ffn1_in = project(normed_one_low, ffn1_in)
    active_one = sigmoid_linear(hidden_one).astype(jnp.bfloat16)
    branch_one, kept_ffn1_out = project(active_one, ffn1_out)
    stream_one = stream + 0.5 * branch_one
    normed_two, saved_two = norm_forward(stream_one, gain_attn)
    normed_two_low = normed_two.astype(jnp.bfloat16)
    projected, kept_qkv = project(normed_two_low, attn_qkv)
    query_low = rotate(projected[:, :model_width], cos_table, sin_table).astype(jnp.bfloat16)
    key_low = rotate(projected[:, model_width : 2 * model_width], cos_table, sin_table).astype(
        jnp.bfloat16
    )
    value_low = projected[:, 2 * model_width :].astype(jnp.bfloat16)
    query_heads = split_heads(query_low)

    def stats_step(current, blocks, first_row):
        top_score, denominator = current
        key_block = blocks[0]
        key_segments = segment_of(
            first_row + jnp.arange(key_block.shape[0], dtype=jnp.int32), seg_lengths
        )
        masked = block_scores(query_heads, split_heads(key_block), query_segments, key_segments)
        new_top = jnp.maximum(top_score, jnp.max(masked, axis=-1))
        denominator = denominator * jnp.exp(top_score - new_top) + jnp.sum(
            jnp.exp(masked - new_top[:, :, None]), axis=-1
        )
        return (new_top, denominator)

    top_init = jnp.full((HEADS, frame_count), MASKED, jnp.float32)
    total_init = jnp.zeros((HEADS, frame_count), jnp.float32)
    top_score, denominator = over_blocks(
        stats_step, (top_init, total_init), (lax.all_gather(key_low, "seq", axis=0, tiled=True),)
    )
    log_total = top_score + jnp.log(denominator)

    def value_step(current, blocks, first_row):
        mixed_sum, rest_sum = current
        key_block, value_block = blocks
        key_segments = segment_of(
            first_row + jnp.arange(key_block.shape[0], dtype=jnp.int32), seg_lengths
        )
        probs = jnp.exp(
            block_scores(query_heads, split_heads(key_block), query_segments, key_segments)
            - log_total[:, :, None]
        )
        probs_high = probs.astype(jnp.bfloat16)
        probs_rest = (probs - probs_high.astype(jnp.float32)).astype(jnp.bfloat16)
        value_heads = split_heads(value_block)
        mixed_sum = mixed_sum + jnp.einsum(
            "hqk,khd->qhd", probs_high, value_heads, preferred_element_type=jnp.float32
        )
        rest_sum = rest_sum + jnp.einsum(
            "hqk,khd->qhd", probs_rest, value_heads, preferred_element_type=jnp.float32
        )
        return (mixed_sum, rest_sum)

    zero_heads = jnp.zeros((frame_count, HEADS, HEAD_DIM), jnp.float32)
    mixed_sum, rest_sum = over_blocks(
        value_step,
        (zero_heads, zero_heads),
        (
            lax.all_gather(key_low, "seq", axis=0, tiled=True),
            lax.all_gather(value_low, "seq", axis=0, tiled=True),
        ),
    )
    exact_sum = mixed_sum + rest_sum
    mixed_low = mixed_sum.reshape(frame_count, model_width).astype(jnp.bfloat16)
    branch_two, kept_attn_out = project(mixed_low, attn_out)
    stream_two = stream_one + branch_two
    normed_three, saved_three = norm_forward(stream_two, gain_conv)
    normed_three_low = normed_three.astype(jnp.bfloat16)
    gate_up, kept_conv_in = project(normed_three_low, conv_in)
    first_part = gate_up[:, :model_width]
    gate_sigma = jax.nn.sigmoid(gate_up[:, model_width:])
    glu_low = (first_part * gate_sigma).astype(jnp.bfloat16)
    padded = with_halo(glu_low, (("seq", 0),), HALF).astype(jnp.float32)
    padded_segments = segment_of(
        first_frame - HALF + jnp.arange(frame_count + 2 * HALF, dtype=jnp.int32), seg_lengths
    )
    kernel_taps = conv_kernel.astype(jnp.float32)
    conv_values = jnp.zeros((frame_count, model_width), jnp.float32)
    for offset in range(KERNEL):
        same_segment = (padded_segments[offset : offset + frame_count] == query_segments).astype(
            jnp.float32
        )
        conv_values = (
            conv_values
            + kernel_taps[offset] * padded[offset : offset + frame_count] * same_segment[:, None]
        )
    normed_four, saved_four = norm_forward(conv_values, gain_inner)
    active_four = sigmoid_linear(normed_four).astype(jnp.bfloat16)
    branch_three, kept_conv_out = project(active_four, conv_out)
    stream_three = stream_two + branch_three
    normed_five, saved_five = norm_forward(stream_three, gain_ffn2)
    normed_five_low = normed_five.astype(jnp.bfloat16)
    hidden_two, kept_ffn2_in = project(normed_five_low, ffn2_in)
    active_two = sigmoid_linear(hidden_two).astype(jnp.bfloat16)
    branch_four, kept_ffn2_out = project(active_two, ffn2_out)
    stream_four = stream_three + 0.5 * branch_four
    final_norm, saved_six = norm_forward(stream_four, gain_out)
    output = final_norm.astype(jnp.bfloat16)[None]
    grad_four, grad_gain_six = norm_backward(cotangent[0].astype(jnp.float32), gain_out, saved_six)
    out_two_low = (0.5 * grad_four).astype(jnp.bfloat16)
    grad_ffn_two_out = weight_grad(active_two, out_two_low)
    hidden_two_low = (project_back(out_two_low, ffn2_out) * sigmoid_linear_grad(hidden_two)).astype(
        jnp.bfloat16
    )
    grad_ffn_two_in = weight_grad(normed_five_low, hidden_two_low)
    input_part, grad_gain_five = norm_backward(
        project_back(hidden_two_low, ffn2_in), gain_ffn2, saved_five
    )
    grad_three = grad_four + input_part
    conv_out_low = grad_three.astype(jnp.bfloat16)
    grad_conv_weight_out = weight_grad(active_four, conv_out_low)
    active_grad = project_back(conv_out_low, conv_out) * sigmoid_linear_grad(normed_four)
    conv_grad, grad_gain_four = norm_backward(active_grad, gain_inner, saved_four)
    conv_grad_low = conv_grad.astype(jnp.bfloat16)
    conv_grad_value = conv_grad_low.astype(jnp.float32)
    rim_grad = with_halo(conv_grad_low, (("seq", 0),), HALF).astype(jnp.float32)
    tap_grads = []
    glu_grad = jnp.zeros((frame_count, model_width), jnp.float32)
    for offset in range(KERNEL):
        same_segment = (padded_segments[offset : offset + frame_count] == query_segments).astype(
            jnp.float32
        )
        tap_grads.append(
            jnp.sum(
                padded[offset : offset + frame_count] * same_segment[:, None] * conv_grad_value,
                axis=0,
            )
        )
        back_start = 2 * HALF - offset
        back_segment = (
            padded_segments[back_start : back_start + frame_count] == query_segments
        ).astype(jnp.float32)
        glu_grad = (
            glu_grad
            + kernel_taps[offset]
            * rim_grad[back_start : back_start + frame_count]
            * back_segment[:, None]
        )
    kernel_grad = jnp.stack(tap_grads, axis=0)
    gate_up_low = jnp.concatenate(
        [glu_grad * gate_sigma, glu_grad * first_part * gate_sigma * (1.0 - gate_sigma)], axis=1
    ).astype(jnp.bfloat16)
    grad_conv_weight_in = weight_grad(normed_three_low, gate_up_low)
    input_part, grad_gain_three = norm_backward(
        project_back(gate_up_low, conv_in), gain_conv, saved_three
    )
    grad_two = grad_three + input_part
    attn_grad_low = grad_two.astype(jnp.bfloat16)
    grad_attn_weight = weight_grad(mixed_low, attn_grad_low)
    mixed_grad_low = project_back(attn_grad_low, attn_out).astype(jnp.bfloat16)
    delta = jnp.transpose(
        jnp.sum(split_heads(mixed_grad_low).astype(jnp.float32) * exact_sum, axis=-1)
    )

    def key_turn(turn_index, current):
        key_rows, value_rows, key_acc, value_acc, query_acc = current
        owner = (position_index - turn_index) % device_count
        key_segments = segment_of(owner * frame_count + local_frames, seg_lengths)
        query_part, key_part, value_part = pair_grads(
            query_low,
            mixed_grad_low,
            log_total,
            delta,
            query_segments,
            key_rows,
            value_rows,
            key_segments,
        )
        key_rows, value_rows = shifted((key_rows, value_rows), "seq", 1)
        key_acc, value_acc = (
            shifted((key_acc + key_part).astype(jnp.bfloat16), "seq", 1).astype(jnp.float32),
            shifted((value_acc + value_part).astype(jnp.bfloat16), "seq", 1).astype(jnp.float32),
        )
        return (key_rows, value_rows, key_acc, value_acc, query_acc + query_part)

    zero_rows = jnp.zeros((frame_count, model_width), jnp.float32)
    unused_keys, unused_values, key_grad, value_grad, query_grad = lax.fori_loop(
        0, device_count, key_turn, (key_low, value_low, zero_rows, zero_rows, zero_rows)
    )
    projected_grad_low = jnp.concatenate(
        [
            unrotate(query_grad, cos_table, sin_table),
            unrotate(key_grad, cos_table, sin_table),
            value_grad,
        ],
        axis=1,
    ).astype(jnp.bfloat16)
    grad_qkv_weight = weight_grad(normed_two_low, projected_grad_low)
    input_part, grad_gain_two = norm_backward(
        project_back(projected_grad_low, attn_qkv), gain_attn, saved_two
    )
    grad_one = grad_two + input_part
    out_one_low = (0.5 * grad_one).astype(jnp.bfloat16)
    grad_ffn_one_out = weight_grad(active_one, out_one_low)
    hidden_one_low = (project_back(out_one_low, ffn1_out) * sigmoid_linear_grad(hidden_one)).astype(
        jnp.bfloat16
    )
    grad_ffn_one_in = weight_grad(normed_one_low, hidden_one_low)
    input_part, grad_gain_one = norm_backward(
        project_back(hidden_one_low, ffn1_in), gain_ffn1, saved_one
    )
    input_grad = (grad_one + input_part)[None]
    small_grads = lax.psum(
        (
            grad_gain_one,
            grad_gain_two,
            grad_gain_three,
            grad_gain_four,
            grad_gain_five,
            grad_gain_six,
            kernel_grad,
        ),
        ("seq", "row"),
    )
    large_grads = (
        grad_ffn_one_in,
        grad_ffn_one_out,
        grad_qkv_weight,
        grad_attn_weight,
        grad_conv_weight_in,
        grad_conv_weight_out,
        grad_ffn_two_in,
        grad_ffn_two_out,
    )
    large_grads = (
        lax.psum(grad_ffn_one_in.astype(jnp.bfloat16), "row").astype(jnp.float32),
        lax.psum(grad_ffn_one_out.astype(jnp.bfloat16), "row").astype(jnp.float32),
        lax.psum(grad_qkv_weight.astype(jnp.bfloat16), "row").astype(jnp.float32),
        lax.psum(grad_attn_weight.astype(jnp.bfloat16), "row").astype(jnp.float32),
        lax.psum(grad_conv_weight_in.astype(jnp.bfloat16), "row").astype(jnp.float32),
        lax.psum(grad_conv_weight_out.astype(jnp.bfloat16), "row").astype(jnp.float32),
        lax.psum(grad_ffn_two_in.astype(jnp.bfloat16), "row").astype(jnp.float32),
        lax.psum(grad_ffn_two_out.astype(jnp.bfloat16), "row").astype(jnp.float32),
    )
    return (
        output,
        input_grad,
        small_grads[0],
        small_grads[1],
        small_grads[2],
        small_grads[3],
        small_grads[4],
        small_grads[5],
        small_grads[6],
        large_grads[0],
        large_grads[1],
        large_grads[2],
        large_grads[3],
        large_grads[4],
        large_grads[5],
        large_grads[6],
        large_grads[7],
    )


BF16 = jnp.bfloat16
F32 = jnp.float32
PLANES = 4
VMEM = pltpu.VMEM
DMA = pltpu.SemaphoreType.DMA
VMEM_LIMIT = 60 * 1024 * 1024
FORWARD_PARTS = 1
BACKWARD_PARTS = 1


class Place:
    def __init__(self, parts):
        self.parts = Parts(parts)
        seq = lax.axis_index("seq")
        self.x = lax.axis_index("row")
        self.z = seq // 4
        self.yc = lax.rem(seq, 4)
        self.core = lax.rem(self.yc, 2)
        inside = lax.rem(self.z + self.z // 2, 2)
        self.end, self.middle = inside == 0, inside == 1
        self.beside, self.across, self.opposite = self.line(1 - inside), self.line(2), self.line(3)

    def flip(self, k):
        y, c, x = self.yc // 2, lax.rem(self.yc, 2), self.x
        c = 1 - c if k & 1 else c
        y = 1 - y if k & 2 else y
        x = 1 - x if k & 4 else x
        return x, y * 2 + c

    def dev(self, k):
        x, yc = self.flip(k)
        return {"seq": self.z * 4 + yc, "row": x}

    def slot(self, k):
        x, yc = self.flip(k)
        return x * 4 + yc

    def zdev(self, k):
        return self.at(lax.rem(self.z + k, PLANES))

    def at(self, plane, yc=None):
        return {"seq": plane * 4 + (self.yc if yc is None else yc), "row": self.x}

    def line(self, index):
        return index + self.z // 2 * (3 - 2 * index)

    def pair(self, x=None, yc=None):
        x = self.x if x is None else x
        yc = self.yc if yc is None else yc
        return (x * 2 + lax.rem(yc, 2)) * 2 + yc // 2

    def enter(self):
        barrier = pltpu.get_barrier_semaphore()
        partners = [self.dev(k) for k in range(1, 8)]
        for k in range(1, PLANES):
            plane = lax.rem(self.z + k, PLANES)
            partners += [self.at(plane), self.at(plane, self.flip(1)[1])]
        for partner in partners:
            pl.semaphore_signal(barrier, inc=1, device_id=partner)
        pl.semaphore_wait(barrier, len(partners))


def remote(src, dst, send_sem, recv_sem, dev):
    return pltpu.make_async_remote_copy(src, dst, send_sem, recv_sem, device_id=dev)


def dot(left, right, left_dim=1, right_dim=0):
    return lax.dot_general(
        left, right, (((left_dim,), (right_dim,)), ((), ())), preferred_element_type=F32
    )


PAIRS = (((0, 1),), ((2, 4), (3, 5)), ((6, 7),))
OUT_PAIRS = ((3, 5), (7, 1), (2, 4), (6, 0))


class Parts:
    def __init__(self, count):
        self.count = count
        self.rows = 128 // count

    def __iter__(self):
        return iter(range(self.count))

    def of(self, part):
        return slice(part * self.rows, part * self.rows + self.rows)

    def take(self, ref, slots, part):
        return jnp.concatenate([ref[slot, self.of(part), :] for slot in slots], axis=0)

    def put(self, ref, slots, part, value):
        for index, slot in enumerate(slots):
            ref[slot, self.of(part), :] = value[index * self.rows : index * self.rows + self.rows]


class Gather:
    def __init__(self, place, blocks, sems):
        self.place, self.blocks = place, blocks
        self.send, self.recv = sems
        self.rows = place.parts.rows
        self.sent = []

    def at(self, slot, part, half=None):
        count = self.rows if half is None else self.rows // 2
        first = part * self.rows + (half or 0) * count
        return self.blocks.at[slot, pl.ds(first, count)]

    def copy(self, rows, to, part, sem):
        sem = part * 11 + sem
        return remote(rows, rows, self.send.at[sem], self.recv.at[sem], self.place.dev(to))

    def hand(self, rows, to, part, sem):
        copy = self.copy(rows, to, part, sem)
        copy.start()
        self.sent.append(copy)

    def push(self, part, value):
        own = self.place.slot(0)
        self.blocks[own, self.place.parts.of(part), :] = value
        for half in range(2):
            self.hand(self.at(own, part, 1 - half), 4, part, 4 + 5 * (half == 1))
            self.hand(self.at(own, part, half), 2, part, 2 + 8 * (half == 1))
        self.hand(self.at(own, part), 1, part, 1)

    def arrive(self, rows, part, sem):
        self.copy(rows, 1, part, sem).wait_recv()

    def fetch(self, ks, part):
        slots = {k: self.place.slot(k) for k in ks}
        if 2 in slots:
            self.arrive(self.at(slots[2], part, 0), part, 2)
            self.hand(self.at(slots[2], part, 0), 4, part, 6)
            self.arrive(self.at(slots[4], part, 1), part, 4)
            self.hand(self.at(slots[4], part, 1), 2, part, 8)
            self.arrive(self.at(slots[2], part, 1), part, 10)
            self.hand(self.at(slots[2], part), 1, part, 3)
            self.arrive(self.at(slots[4], part, 0), part, 9)
            self.hand(self.at(slots[4], part), 1, part, 5)
        if 6 in slots:
            self.arrive(self.at(slots[6], part, 0), part, 6)
            self.arrive(self.at(slots[6], part, 1), part, 8)
            self.hand(self.at(slots[6], part), 1, part, 7)
        for k in ks:
            if k % 2:
                self.arrive(self.at(slots[k], part), part, k)
        return slots

    def drain(self):
        for copy in self.sent:
            copy.wait_send()


class Scatter:
    def __init__(self, place, buffers, sems):
        self.place = place
        self.part, self.staged, self.sibling, self.reduced, self.received = buffers
        self.send, self.recv = sems
        self.sent = []

    @staticmethod
    def scratch(parts, rows, width):
        return [
            VMEM((parts, 4, rows, width), F32),
            VMEM((parts, 4, rows, width), BF16),
            VMEM((parts, 4, rows, width), BF16),
            VMEM((parts, 3, rows, width), BF16),
            VMEM((parts, 3, rows, width), BF16),
        ]

    def copy(self, src, dst, part, sem, k):
        sem = part * 8 + sem
        return remote(src, dst, self.send.at[sem], self.recv.at[sem], self.place.dev(k))

    def push(self, *what):
        copy = self.copy(*what)
        copy.start()
        self.sent.append(copy)

    def emit(self, k, part, value):
        index = k // 2
        if k % 2:
            self.staged[part, index] = value.astype(BF16)
            self.push(
                self.staged.at[part, index], self.sibling.at[part, index], part, index, 1
            )
        else:
            self.part[part, index] = value

    def emit_pair(self, pair, part, value):
        rows = value.shape[0] // len(pair)
        for index, k in enumerate(pair):
            self.emit(k, part, value[index * rows : index * rows + rows])

    def finish(self, k, part):
        index = k // 2
        into = self.sibling.at[part, index]
        self.copy(into, into, part, index, 1).wait_recv()
        total = self.part[part, index] + self.sibling[part, index].astype(F32)
        if k:
            self.reduced[part, index - 1] = total.astype(BF16)
            self.push(
                self.reduced.at[part, index - 1],
                self.received.at[part, index - 1],
                part,
                3 + index,
                k,
            )
        else:
            self.part[part, 0] = total

    def total(self, part):
        value = self.part[part, 0]
        for index in range(3):
            into = self.received.at[part, index]
            self.copy(into, into, part, 4 + index, 1).wait_recv()
            value = value + self.received[part, index].astype(F32)
        return value

    def drain(self):
        for copy in self.sent:
            copy.wait_send()


def gather_blocks(place, gather, process, scatter=None):
    for part in place.parts:
        for group in PAIRS:
            slots = gather.fetch([k for pair in group for k in pair], part)
            for pair in group:
                process(pair, [slots[k] for k in pair], part)
            if scatter and group == PAIRS[1]:
                scatter.finish(2, part)
                scatter.finish(4, part)
        if scatter:
            scatter.finish(6, part)
            scatter.finish(0, part)


def scatter_blocks(place, scatter, rows, weight, side=0):
    for part in place.parts:
        for pair in OUT_PAIRS:
            slots = [place.slot(k) for k in pair]
            scatter.emit_pair(pair, part, dot(rows(slots, part), flat(weight), 1, side))
        for k in (2, 4, 6, 0):
            scatter.finish(k, part)


def carry(place, scatter, gather, step):
    for part in place.parts:
        gather.push(part, step(part, scatter.total(part)))
    scatter.drain()


class Refs:
    pass


def kernel_call(body, collective, ins, outs, scratch):
    in_names = list(ins)
    out_names = list(outs)
    scratch_names = list(scratch)
    flat_scratch = []
    counts = []
    for name in scratch_names:
        item = scratch[name]
        counts.append(len(item) if isinstance(item, list) else 0)
        flat_scratch += item if isinstance(item, list) else [item]

    def kernel(*refs):
        held = Refs()
        at = 0
        for name in in_names + out_names:
            setattr(held, name, refs[at])
            at += 1
        for name, count in zip(scratch_names, counts):
            setattr(held, name, refs[at : at + count] if count else refs[at])
            at += max(count, 1)
        body(held)

    results = pl.pallas_call(
        kernel,
        out_shape=[jax.ShapeDtypeStruct(shape, dtype) for shape, dtype, unused in outs.values()],
        in_specs=[pl.BlockSpec(memory_space=space) for unused, space in ins.values()],
        out_specs=[pl.BlockSpec(memory_space=space) for unused, unused_type, space in outs.values()],
        scratch_shapes=flat_scratch,
        compiler_params=pltpu.CompilerParams(
            collective_id=collective, has_side_effects=True, vmem_limit_bytes=VMEM_LIMIT
        ),
    )(*[array for array, unused in ins.values()])
    return dict(zip(out_names, results))


class AlongZ:
    def __init__(self, place, sems, block):
        self.place = place
        self.send, self.recv = sems
        self.block = block
        self.sent = []

    def copy(self, source, owner, plane, sem):
        into = self.block(owner)
        return remote(
            source, into, self.send.at[sem], self.recv.at[owner], self.place.at(plane)
        )

    def arrive(self, owner):
        self.copy(self.block(owner), owner, owner, 0).wait_recv()

    def start(self, source):
        place = self.place
        self.sent = [
            self.copy(source, place.z, place.across, 0),
            self.copy(source, place.z, place.beside, 1),
        ]
        self.last = [
            self.copy(source, place.z, place.opposite, 2),
            self.copy(self.block(place.opposite), place.opposite, place.line(0), 3),
        ]
        for copy in self.sent:
            copy.start()

        @pl.when(place.middle)
        def start():
            self.last[0].start()

    def relay(self):
        @pl.when(self.place.middle)
        def hand_on():
            self.arrive(self.place.opposite)
            self.last[1].start()

    def finish(self):
        place = self.place
        self.arrive(place.beside)
        self.arrive(place.across)

        @pl.when(place.end)
        def last():
            self.arrive(place.opposite)

        for copy in self.sent:
            copy.wait_send()

        @pl.when(place.middle)
        def drain():
            for copy in self.last:
                copy.wait_send()


class GatherRows:
    def __init__(self, place, src, dst, sems, pieces):
        self.place, self.dst = place, dst
        self.send, self.recv, self.local = sems[:3]
        self.along = AlongZ(place, sems[3:], lambda plane: dst.at[pl.ds(plane * 4, 4)])
        mine = place.z * 4 + place.yc
        for k in (0, 2, 3, 1):
            x, to = place.flip(k)
            for index, column in enumerate(pieces(place, to)):
                source = src.at[:, pl.ds(pl.multiple_of(column * 128, 128), 128)]
                into = dst.at[mine, :, pl.ds(index * 128, 128)]
                if k:
                    remote(source, into, self.send.at[k], self.recv.at[k], place.dev(k)).start()
                else:
                    pltpu.make_async_copy(source, into, self.local).start()

    def along_z(self):
        place = self.place
        mine = self.dst.at[place.z * 4 + place.yc]
        pltpu.make_async_copy(mine, mine, self.local).wait()
        for k in (2, 3, 1):
            into = self.dst.at[place.z * 4 + place.flip(k)[1]]
            remote(into, into, self.send.at[k], self.recv.at[k], place.dev(k)).wait_recv()
        self.along.start(self.dst.at[pl.ds(place.z * 4, 4)])

    def relay(self):
        self.along.relay()

    def finish(self):
        place = self.place
        self.along.finish()
        mine = self.dst.at[place.z * 4 + place.yc]
        for k in (2, 3, 1):
            remote(mine, mine, self.send.at[k], self.recv.at[k], place.dev(k)).wait_send()

    @staticmethod
    def scratch():
        return [DMA((4,)), DMA((4,)), DMA, DMA((4,)), DMA((PLANES,))]


def ffn_pieces(place, yc):
    return [(plane * 4 + yc) * 2 + place.x for plane in range(PLANES)]


def head_pieces(place, yc):
    return [kind * 8 + place.pair(None, yc) for kind in range(3)]


def channel_pieces(place, yc):
    return [kind * 8 + place.pair(None, yc) for kind in range(2)]


class GatherBlocks:
    def __init__(self, place, src, dst, sems, columns=slice(0, 1024)):
        columns = pl.ds(columns.start, columns.stop - columns.start)
        src = src.at[pl.ds(place.x * 128, 128), columns]
        self.along = AlongZ(place, sems[1:], lambda plane: dst.at[plane, :, columns])
        self.own = pltpu.make_async_copy(src, dst.at[place.z, :, columns], sems[0])
        self.own.start()
        self.along.start(src)

    def relay(self):
        self.along.relay()

    def finish(self):
        self.own.wait()
        self.along.finish()

    @staticmethod
    def scratch():
        return [DMA, DMA((4,)), DMA((PLANES,))]


class PlaneSum:
    def __init__(self, place, refs):
        self.place = place
        self.own, self.staged, self.received, self.relayed, self.send, self.recv = refs

    @staticmethod
    def scratch(rows, width):
        return [
            VMEM((rows, width), F32),
            VMEM((3, rows, width), BF16),
            VMEM((3, rows, width), BF16),
            VMEM((rows, width), BF16),
            DMA((4,)),
            DMA((4,)),
        ]

    def term_copy(self, index, plane):
        slot = lax.rem(plane + 3 - self.place.z, PLANES)
        return remote(
            self.staged.at[index],
            self.received.at[slot],
            self.send.at[index],
            self.recv.at[slot],
            self.place.at(plane),
        )

    def relay_copy(self):
        return remote(
            self.staged.at[0],
            self.relayed,
            self.send.at[3],
            self.recv.at[3],
            self.place.at(self.place.beside),
        )

    def first(self, term):
        self.staged[0] = term(self.place.opposite).astype(BF16)

        @pl.when(self.place.end)
        def start():
            self.relay_copy().start()

    def rest(self, term):
        place = self.place
        self.staged[1] = term(place.across).astype(BF16)
        self.term_copy(1, place.across).start()
        self.staged[2] = term(place.beside).astype(BF16)
        self.term_copy(2, place.beside).start()
        self.own[...] = term(place.z)

    def relay(self):
        @pl.when(self.place.middle)
        def add():
            self.relay_copy().wait_recv()
            self.staged[0] = (
                self.staged[0].astype(F32) + self.relayed[...].astype(F32)
            ).astype(BF16)
            self.term_copy(0, self.place.opposite).start()

    def arrive(self, plane):
        slot = lax.rem(self.place.z + 3 - plane, PLANES)
        into = self.received.at[slot]
        remote(
            into, into, self.send.at[0], self.recv.at[slot], self.place.at(plane)
        ).wait_recv()

    def total(self):
        place = self.place
        self.arrive(place.beside)
        self.arrive(place.across)

        @pl.when(place.middle)
        def last():
            self.arrive(place.opposite)
            self.term_copy(0, place.opposite).wait_send()

        @pl.when(place.end)
        def nothing():
            self.received[lax.rem(place.z + 3 - place.opposite, PLANES)] = jnp.zeros(
                self.received.shape[1:], BF16
            )
            self.relay_copy().wait_send()

        self.term_copy(1, place.across).wait_send()
        self.term_copy(2, place.beside).wait_send()
        value = self.own[...]
        for index in range(3):
            value = value + self.received[index].astype(F32)
        return value


class Exchange:
    def __init__(self, place, blocks, sems, partners=tuple(range(1, 8)), slot=None):
        self.place = place
        self.blocks = blocks
        self.send, self.recv = sems
        self.partners = partners
        self.slot = slot or place.slot
        self.sent = []

    def start(self, source):
        own = self.slot(0)
        for k in self.partners:
            copy = remote(
                source(k), self.blocks.at[own], self.send.at[k], self.recv.at[k], self.place.dev(k)
            )
            copy.start()
            self.sent.append(copy)

    def wait(self):
        for k in self.partners:
            into = self.blocks.at[self.slot(k)]
            remote(into, into, self.send.at[k], self.recv.at[k], self.place.dev(k)).wait_recv()
        for copy in self.sent:
            copy.wait_send()


def flat(ref):
    value = ref[...]
    return value.reshape(value.shape[0] * value.shape[1], value.shape[2])


def ffn_forward(place, gather, hidden, w_in, w_out, scatter, ready):
    def process(pair, slots, part):
        if part == 0 and pair[0] == 0:
            ready()
        value = dot(place.parts.take(gather.blocks, slots, part), flat(w_in))
        place.parts.put(hidden, slots, part, value)
        scatter.emit_pair(pair, part, dot(sigmoid_linear(value).astype(BF16), flat(w_out)))

    gather_blocks(place, gather, process, scatter)


def ffn_backward(place, gather, hidden, hidden_grads, active, w_in, w_out, scatter, ready):
    def process(pair, slots, part):
        if part == 0 and pair[0] == 0:
            ready()
        value = place.parts.take(hidden, slots, part)
        sigma = jax.nn.sigmoid(value)
        place.parts.put(active, slots, part, (value * sigma).astype(BF16))
        back = dot(place.parts.take(gather.blocks, slots, part), flat(w_out), 1, 1)
        low = (back * (sigma * (1.0 + value * (1.0 - sigma)))).astype(BF16)
        place.parts.put(hidden_grads, slots, part, low)
        scatter.emit_pair(pair, part, dot(low, flat(w_in), 1, 1))

    gather_blocks(place, gather, process, scatter)


def token_dot(left, columns, right):
    count, rows, unused = left.shape
    taken = left[:, :, columns].reshape(count * rows, -1)
    return dot(taken, flat(right), 0, 0)


def columns_of(plane, width):
    return pl.ds(pl.multiple_of(plane * width, width), width)


class WeightGrads:
    def __init__(self, place, refs, name, sums, wide):
        self.place = place
        self.sum_in = PlaneSum(place, getattr(refs, sums + "_sum_in"))
        self.total_in = getattr(refs, name + "_total_in")
        self.share_in = Exchange(
            place, getattr(refs, name + "_grad_in"), getattr(refs, name + "_share_in")
        )
        self.wide = wide
        if wide:
            self.sum_out = PlaneSum(place, getattr(refs, sums + "_sum_out"))
            self.share_out = Exchange(
                place,
                getattr(refs, name + "_grad_out"),
                getattr(refs, name + "_share_out"),
                (4,),
                lambda k: place.flip(k)[0],
            )
        else:
            self.sum_out = HalfSum(
                place, getattr(refs, sums + "_sum_out"), getattr(refs, name + "_grad_out")
            )

    def put_out(self, active, grads):
        self.sum_out.put(dot(flat(active), flat(grads), 0, 0))

    def put_in(self, blocks, grads):
        def term(plane):
            return token_dot(blocks, columns_of(plane, 256), grads)

        self.sum_in.first(term)
        self.sum_in.rest(term)

    def put_both(self, active, grads, blocks, hidden_grads):
        def out(plane):
            return token_dot(active, columns_of(plane, 128), grads)

        def into(plane):
            return token_dot(blocks, columns_of(plane, 256), hidden_grads)

        self.sum_out.first(out)
        self.sum_in.first(into)
        self.sum_out.rest(out)
        self.sum_in.rest(into)

    def relay(self):
        self.sum_out.relay()
        self.sum_in.relay()

    def share(self):
        if self.wide:
            self.share_out.blocks[self.place.x] = self.sum_out.total().astype(BF16)
            self.share_out.start(lambda k: self.share_out.blocks.at[self.place.x])
        else:
            self.sum_out.add()
        self.total_in[...] = self.sum_in.total().astype(BF16).reshape(self.total_in.shape)
        self.share_in.blocks[self.place.slot(0)] = self.total_in[self.place.yc]
        self.share_in.start(lambda k: self.total_in.at[self.place.flip(k)[1]])

    def wait(self):
        (self.share_out if self.wide else self.sum_out).wait()
        self.share_in.wait()

    @staticmethod
    def sums(name, width, wide):
        return {
            name + "_sum_in": PlaneSum.scratch(256, width),
            name + "_sum_out": PlaneSum.scratch(128, 1024) if wide else HalfSum.scratch(1024),
        }

    @staticmethod
    def scratch(name, width, wide):
        held = {
            name + "_total_in": VMEM((4, 64, width), BF16),
            name + "_share_in": [DMA((8,)), DMA((8,))],
        }
        if wide:
            held[name + "_share_out"] = [DMA((8,)), DMA((8,))]
        return held

    @staticmethod
    def outs(name, width, wide):
        return {
            name + "_grad_in": ((8, 64, width), BF16, VMEM),
            name + "_grad_out": ((2, 128, 1024) if wide else (64, 1024), BF16, VMEM),
        }


AG_SEMS = [DMA((22,)), DMA((22,))]


def norm_rows(values, gain):
    normed, saved = norm_forward(values, gain)
    return normed.astype(BF16), saved


def norm_input_grad(grads, gain, saved):
    unit_part, inverse = saved
    scaled = grads * gain
    gain_grad = jnp.sum(grads * unit_part, axis=0, keepdims=True)
    input_part = inverse * (
        scaled
        - jnp.mean(scaled, axis=-1, keepdims=True)
        - unit_part * jnp.mean(scaled * unit_part, axis=-1, keepdims=True)
    )
    return input_part, gain_grad


class GatherHalf:
    def __init__(self, place, src, dst, sems):
        self.place, self.dst = place, dst
        self.send, self.recv, self.local = sems
        self.source = place.z // 2 == place.x
        self.first, self.last = 2 - place.x, 3 - 3 * place.x
        target = place.yc // 2 * 2 + lax.rem(place.z, 2)
        self.same = lax.rem(place.z, 2) == place.core
        self.own = pltpu.make_async_copy(src, dst.at[place.core], self.local)

        def copy(sem, plane):
            return remote(
                src,
                dst.at[place.core],
                self.send.at[sem],
                self.recv.at[place.core],
                place.at(plane, target),
            )

        self.far, self.near, self.sibling = (
            copy(0, self.first),
            copy(1, place.x * 2 + 1 - lax.rem(place.z, 2)),
            copy(2, place.z),
        )

        @pl.when(self.source)
        def start():
            self.far.start()
            self.near.start()

            @pl.when(self.same)
            def local():
                self.own.start()

            @pl.when(jnp.logical_not(self.same))
            def sibling():
                self.sibling.start()

    def on(self, half):
        rows = self.dst.at[half]
        return remote(
            rows, rows, self.send.at[half], self.recv.at[half], self.place.at(self.last)
        )

    def relay(self):
        @pl.when(self.place.z == self.first)
        def hand_on():
            for half in range(2):
                self.on(half).wait_recv()
                self.on(half).start()

    def finish(self):
        place = self.place
        at_home = place.z == place.x * 2 + place.core
        for half in range(2):
            here = jnp.logical_or(
                jnp.logical_and(at_home, place.core == half), place.z == self.first
            )

            @pl.when(jnp.logical_not(here))
            def arrive():
                self.on(half).wait_recv()

        @pl.when(self.source)
        def drain():
            self.far.wait_send()
            self.near.wait_send()

            @pl.when(self.same)
            def local():
                self.own.wait()

            @pl.when(jnp.logical_not(self.same))
            def sibling():
                self.sibling.wait_send()

        @pl.when(place.z == self.first)
        def drain_on():
            for half in range(2):
                self.on(half).wait_send()

    @staticmethod
    def scratch():
        return [DMA((3,)), DMA((2,)), DMA]


class HalfSum:
    def __init__(self, place, refs, result):
        self.place = place
        self.staged, self.received, self.relayed, self.send, self.recv, self.last = refs
        self.result = result
        self.near = place.z // 2 == place.x
        self.far_middle, self.far_end = 2 - place.x, 3 - 3 * place.x
        self.home = place.x * 2 + place.core

    @staticmethod
    def scratch(width):
        return [
            VMEM((2, 64, width), BF16),
            VMEM((3, 64, width), BF16),
            VMEM((2, 64, width), BF16),
            DMA((3,)),
            DMA((4,)),
            DMA((2,)),
        ]

    def term_copy(self, half, slot):
        place = self.place
        return remote(
            self.staged.at[half],
            self.received.at[slot],
            self.send.at[half],
            self.recv.at[slot],
            place.at(self.home, place.yc // 2 * 2 + half),
        )

    def relay_copy(self):
        return remote(
            self.staged,
            self.relayed,
            self.send.at[2],
            self.recv.at[3],
            self.place.at(self.far_middle),
        )

    def near_copies(self):
        place = self.place
        for half in range(2):
            here = jnp.logical_and(place.z == self.home, place.core == half)
            slot = lax.rem(place.z + self.home, 2)
            yield jnp.logical_and(self.near, jnp.logical_not(here)), self.term_copy(half, slot)

    def put(self, value):
        self.staged[...] = value.astype(BF16).reshape(self.staged.shape)

    def start(self):
        place = self.place

        @pl.when(place.z == self.far_end)
        def relay():
            self.relay_copy().start()

        for away, copy in self.near_copies():

            @pl.when(away)
            def start(copy=copy):
                copy.start()

    def relay(self):
        @pl.when(self.place.z == self.far_middle)
        def add():
            self.relay_copy().wait_recv()
            self.staged[...] = (
                self.staged[...].astype(F32) + self.relayed[...].astype(F32)
            ).astype(BF16)
            for half in range(2):
                self.term_copy(half, 2).start()

    def add(self):
        place = self.place
        at_home = jnp.logical_and(self.near, place.z == self.home)

        @pl.when(self.near)
        def reduce():
            @pl.when(at_home)
            def own():
                self.received[0] = self.staged[place.core]

            for slot in range(3):

                def arrive():
                    into = self.received.at[slot]
                    remote(
                        into, into, self.send.at[0], self.recv.at[slot], place.at(place.z)
                    ).wait_recv()

                if slot:
                    arrive()
                else:
                    pl.when(jnp.logical_not(at_home))(arrive)
            value = self.received[0].astype(F32)
            for slot in range(1, 3):
                value = value + self.received[slot].astype(F32)
            self.result[...] = value.astype(BF16)
            self.hand_over().start()

        for away, copy in self.near_copies():

            @pl.when(away)
            def drain(copy=copy):
                copy.wait_send()

        @pl.when(place.z == self.far_middle)
        def drain_sums():
            for half in range(2):
                self.term_copy(half, 2).wait_send()

        @pl.when(place.z == self.far_end)
        def drain_relay():
            self.relay_copy().wait_send()

    def hand_over(self):
        return remote(
            self.result, self.result, self.last.at[0], self.last.at[1], self.place.dev(4)
        )

    def wait(self):
        @pl.when(self.near)
        def sent():
            self.hand_over().wait_send()

        @pl.when(jnp.logical_not(self.near))
        def arrived():
            self.hand_over().wait_recv()


class Turn:
    def __init__(self, place, refs):
        self.place = place
        self.staged, self.received, self.send, self.recv = refs

    @staticmethod
    def scratch(rows):
        return [VMEM((PLANES, rows, 128), BF16), VMEM((PLANES, rows, 128), BF16), DMA((4,)), DMA((4,))]

    def copy(self, k):
        place = self.place
        return remote(
            self.staged.at[lax.rem(place.z + k, PLANES)],
            self.received.at[place.z],
            self.send.at[k],
            self.recv.at[k],
            place.zdev(k),
        )

    def start(self):
        for k in (2, 1, 3):
            self.copy(k).start()
        self.keep()

    def keep(self):
        self.received[self.place.z] = self.staged[self.place.z]

    def wait(self):
        for k in (1, 2, 3):
            into = self.received.at[lax.rem(self.place.z + 4 - k, PLANES)]
            remote(into, into, self.send.at[k], self.recv.at[k], self.place.zdev(k)).wait_recv()
        for k in (1, 2, 3):
            self.copy(k).wait_send()


def swap_halves(values):
    lane = lax.broadcasted_iota(jnp.int32, values.shape, 1)
    return jnp.where(lane % 64 < 32, pltpu.roll(values, 96, 1), pltpu.roll(values, 32, 1))


def head_part(values, head):
    return values[:, head * 64 : head * 64 + 64]


def pack_wide(turn, pair, left, right):
    row, head = divmod(pair, 2)
    for block in range(4):
        turn.staged[pair, block * 128 : block * 128 + 128, :] = jnp.concatenate(
            [head_part(left[row * 4 + block], head), head_part(right[row * 4 + block], head)], axis=1
        )


def pack_narrow(turn, pair, values):
    row, head = divmod(pair, 2)
    for block in range(2):
        turn.staged[pair, block * 128 : block * 128 + 128, :] = jnp.concatenate(
            [
                head_part(values[row * 4 + block], head),
                head_part(values[row * 4 + block + 2], head),
            ],
            axis=1,
        )


def unpack_narrow(turn, row, block):
    rows = slice((block % 2) * 128, (block % 2) * 128 + 128)
    return jnp.concatenate(
        [head_part(turn.received[row * 2 + head, rows, :], block // 2) for head in range(2)], axis=1
    )


def unpack_wide(turn, row, block, side):
    rows = slice(block * 128, block * 128 + 128)
    return jnp.concatenate(
        [head_part(turn.received[row * 2 + head, rows, :], side) for head in range(2)], axis=1
    )


QUERY_BLOCK = 256


def segment_ends(refs, row):
    lengths = refs.row_lengths[row]
    ends = [lengths[0:1, 0:1]]
    for index in range(1, 4):
        ends.append(ends[-1] + lengths[0:1, index : index + 1])
    return ends


def segment_features(refs, plane, row):
    frame = (plane * 512 + lax.broadcasted_iota(jnp.int32, (512, 64), 0)).astype(F32)
    lane = lax.broadcasted_iota(jnp.int32, (512, 64), 1).astype(F32)
    segment = jnp.zeros((512, 64), F32)
    for end in segment_ends(refs, row)[:3]:
        segment = segment + jnp.where(frame >= end, 1.0, 0.0)
    other = jnp.where(lane < 4.0, -MASKED, 0.0)
    return (
        jnp.where(lane == segment, 0.0, other).astype(BF16),
        jnp.where(lane == segment, -1.0, 0.0).astype(BF16),
    )


def segment_reach(place, refs, slot):
    row, block = slot // 4, slot % 4
    frame = place.z * 512 + block * 128 + lax.broadcasted_iota(jnp.int32, (128, 128), 0)
    frame = frame.astype(F32)
    ends = segment_ends(refs, row)
    first, last = jnp.zeros((128, 128), F32), ends[3]
    for end in ends[:3]:
        first = jnp.where(frame >= end, end, first)
    for end in ends[2::-1]:
        last = jnp.where(frame < end, end, last)
    return first - frame, last - frame


def open_heads(place, refs, turn_qk, turn_v):
    for plane in range(PLANES):
        seg_query, seg_key = segment_features(refs, plane, place.z // 2)
        rows = slice(plane * 512, plane * 512 + 512)
        pair = turn_qk.received[plane]
        scaled = (pair[:, :64].astype(F32) * HEAD_DIM ** (-0.5)).astype(BF16)
        refs.queries[rows, :] = jnp.concatenate([scaled, seg_query], axis=1)
        refs.keys[rows, :] = jnp.concatenate([pair[:, 64:], seg_key], axis=1)
        both = turn_v.received[plane]
        turned = jnp.transpose(both.astype(F32)).astype(BF16)
        refs.values[plane * 512 : plane * 512 + 256, :] = both[:, :64]
        refs.values[plane * 512 + 256 : plane * 512 + 512, :] = both[:, 64:]
        refs.values_t[:, plane * 512 : plane * 512 + 256] = turned[:64]
        refs.values_t[:, plane * 512 + 256 : plane * 512 + 512] = turned[64:]


def attend(place, refs, turn_mix):
    def plane_step(step, unused):
        k = lax.rem(step + 1, PLANES)
        plane = lax.rem(place.z + k, PLANES)
        parts = []
        for half in range(2):
            first = plane * 512 + half * 256
            query = refs.queries[pl.ds(pl.multiple_of(first, 256), QUERY_BLOCK), :]
            scores = dot(refs.keys[...], query, 1, 1)
            top = jnp.max(scores, axis=0, keepdims=True)
            weights = jnp.exp(scores - top)
            total = jnp.sum(weights, axis=0, keepdims=True)
            low = (weights * (1.0 / total)).astype(BF16)
            parts.append(jnp.transpose(dot(refs.values_t[...], low)))
            refs.log_total[plane * 2 + half] = jnp.broadcast_to(top + jnp.log(total), (8, 256))
        turn_mix.staged[plane] = jnp.concatenate(parts, axis=1).astype(BF16)

        @pl.when(step < PLANES - 1)
        def send():
            turn_mix.copy(k).start()

        return unused

    lax.fori_loop(0, PLANES, plane_step, 0)


def attention_forward(place, refs, gather, scatter):
    def process(pair, slots, part):
        if part == 0 and pair[0] == 0:
            refs.finish_qkv()
        value = dot(place.parts.take(gather.blocks, slots, part), flat(refs.w_qkv))

        def frames_of(slot, part):
            count = place.parts.rows
            first = lax.rem(slot, 4) * 128 + part * count
            return pl.ds(pl.multiple_of(first, count), count)

        def table(ref):
            return jnp.concatenate(
                [
                    ref[frames_of(slot, part), :]
                    for slot in slots
                ],
                axis=0,
            )

        cos, sin = table(refs.cos), table(refs.sin)
        query, key = value[:, :128], value[:, 128:256]
        place.parts.put(refs.q_rows, slots, part, (query * cos + swap_halves(query) * sin).astype(BF16))
        place.parts.put(refs.k_rows, slots, part, (key * cos + swap_halves(key) * sin).astype(BF16))
        place.parts.put(refs.v_rows, slots, part, value[:, 256:].astype(BF16))

    gather_blocks(place, gather, process)
    turn_qk, turn_v = Turn(place, refs.turn_qk), Turn(place, refs.turn_v)
    for pair in range(PLANES):
        pack_wide(turn_qk, pair, refs.q_rows, refs.k_rows)
        pack_narrow(turn_v, pair, refs.v_rows)
    turn_qk.start()
    turn_v.start()
    gather.drain()
    turn_qk.wait()
    turn_v.wait()
    refs.after_turn()
    open_heads(place, refs, turn_qk, turn_v)
    turn_mix = Turn(place, refs.turn_mix)
    attend(place, refs, turn_mix)
    turn_mix.keep()
    turn_mix.wait()
    refs.after_mix()
    for slot in range(8):
        refs.mixed[slot] = unpack_narrow(turn_mix, slot // 4, slot % 4)
    scatter_blocks(
        place, scatter, lambda slots, part: place.parts.take(refs.mixed, slots, part), refs.w_o
    )


def attention_kept():
    return dict(
        attn_blocks=((8, 128, 1024), BF16),
        w_qkv=((16, 64, 384), BF16),
        w_o=((2, 64, 1024), BF16),
        queries=((2048, 128), BF16),
        keys=((2048, 128), BF16),
        values=((2048, 64), BF16),
        log_total=((8, 8, 256), F32),
        mixed=((8, 128, 128), BF16),
    )


def attend_back(place, refs, turn_kv, turn_q):
    refs.key_grad[...] = jnp.zeros_like(refs.key_grad)
    refs.value_grad[...] = jnp.zeros_like(refs.value_grad)

    def plane_step(step, unused):
        k = lax.rem(step + 1, PLANES)
        plane = lax.rem(place.z + k, PLANES)
        parts = []
        for half in range(2):
            first = pl.multiple_of(plane * 512 + half * 256, 256)
            query = refs.queries[pl.ds(first, QUERY_BLOCK), :]
            grad = refs.mix_grads[pl.ds(first, QUERY_BLOCK), :]
            log_total = refs.log_total[plane * 2 + half][:1]
            probs = jnp.exp(dot(refs.keys[...], query, 1, 1) - log_total)
            prob_grads = dot(refs.values[...], grad, 1, 1)
            delta = jnp.sum(probs * prob_grads, axis=0, keepdims=True)
            low = (probs * (prob_grads - delta)).astype(BF16)
            refs.key_grad[...] += dot(low, query[:, :64])
            refs.value_grad[...] += dot(probs.astype(BF16), grad)
            parts.append(jnp.transpose(dot(refs.keys_t[...], low)) * HEAD_DIM ** (-0.5))
        turn_q.staged[plane] = jnp.concatenate(parts, axis=1).astype(BF16)

        @pl.when(step < PLANES - 1)
        def send():
            turn_q.copy(k).start()

        return unused

    lax.fori_loop(0, PLANES, plane_step, 0)
    turn_q.keep()
    for plane in range(PLANES):
        rows = slice(plane * 512, plane * 512 + 512)
        turn_kv.staged[plane] = jnp.concatenate(
            [refs.key_grad[rows, :], refs.value_grad[rows, :]], axis=1
        ).astype(BF16)


def attention_backward(place, refs, gather, scatter):
    def process(pair, slots, part):
        if part == 0 and pair[0] == 0:
            refs.finish_attn()
        rows = dot(place.parts.take(gather.blocks, slots, part), flat(refs.w_o), 1, 1)
        place.parts.put(refs.mix_rows, slots, part, rows.astype(BF16))

    gather_blocks(place, gather, process)
    turn_mix = Turn(place, refs.turn_mix)
    for pair in range(PLANES):
        pack_narrow(turn_mix, pair, refs.mix_rows)
    turn_mix.start()
    gather.drain()
    weights = WeightGrads(place, refs, "qkv", "qkv", False)
    weights.put_out(refs.mixed, gather.blocks)
    turned = jnp.transpose(refs.keys[...].astype(F32))
    refs.keys_t[...] = turned[:64].astype(BF16)
    turn_mix.wait()
    for plane in range(PLANES):
        both = turn_mix.received[plane]
        refs.mix_grads[plane * 512 : plane * 512 + 256, :] = both[:, :64]
        refs.mix_grads[plane * 512 + 256 : plane * 512 + 512, :] = both[:, 64:]
    weights.sum_out.start()
    refs.before_attend()
    turn_kv, turn_q = Turn(place, refs.turn_qk), Turn(place, refs.turn_v)
    attend_back(place, refs, turn_kv, turn_q)
    turn_kv.start()
    weights.sum_out.relay()
    refs.after_attend()
    turn_q.wait()
    turn_kv.wait()
    for slot in range(8):
        row, block = divmod(slot, 4)
        cos = refs.cos[block * 128 : block * 128 + 128, :]
        sin = refs.sin[block * 128 : block * 128 + 128, :]
        query = unpack_narrow(turn_q, row, block).astype(F32)
        key = unpack_wide(turn_kv, row, block, 0).astype(F32)
        refs.qkv_grads[slot] = jnp.concatenate(
            [
                (query * cos - swap_halves(query) * sin).astype(BF16),
                (key * cos - swap_halves(key) * sin).astype(BF16),
                unpack_wide(turn_kv, row, block, 1),
            ],
            axis=1,
        )
    scatter_blocks(
        place, scatter, lambda slots, part: place.parts.take(refs.qkv_grads, slots, part), refs.w_qkv, 1
    )
    return weights


def fill_tables(refs):
    cos, sin = refs.cos_rows[...], refs.sin_rows[...]
    refs.cos[...] = jnp.concatenate([cos] * 4, axis=1)
    refs.sin[...] = jnp.concatenate([-sin, sin] * 2, axis=1)


def fill_channels(place, refs):
    columns = columns_of(place.pair(), 128)
    refs.taps[0:KERNEL, :] = refs.all_taps[:, columns].astype(F32)
    refs.gain_inner[...] = refs.all_inner[:, columns]
    for slot in range(8):
        refs.before[slot], refs.after[slot] = segment_reach(place, refs, slot)


def table_scratch():
    return dict(
        cos=VMEM((512, 128), F32),
        sin=VMEM((512, 128), F32),
        taps=VMEM((32, 128), F32),
        gain_inner=VMEM((1, 128), F32),
        before=VMEM((8, 128, 128), F32),
        after=VMEM((8, 128, 128), F32),
    )


class Edges:
    def __init__(self, place, refs):
        self.place = place
        self.staged, self.received, self.send, self.recv = refs

    @staticmethod
    def scratch():
        return [VMEM((2, 2, 16, 128), BF16), VMEM((2, 2, 16, 128), BF16), DMA((2,)), DMA((2,))]

    def copies(self):
        place = self.place
        for side, inside, step in ((0, place.z < PLANES - 1, 1), (1, place.z > 0, -1)):
            plane = jnp.clip(place.z + step, 0, PLANES - 1)
            yield (
                side,
                inside,
                remote(
                    self.staged.at[side],
                    self.received.at[side],
                    self.send.at[side],
                    self.recv.at[side],
                    {"seq": plane * 4 + place.yc, "row": place.x},
                ),
            )

    def start(self, blocks):
        for row in range(2):
            self.staged[0, row] = blocks[row * 4 + 3, 112:128, :]
            self.staged[1, row] = blocks[row * 4, 0:16, :]
        for side, inside, copy in self.copies():

            @pl.when(inside)
            def start(copy=copy):
                copy.start()

    def wait(self, blocks, padded):
        for slot in range(8):
            row, block = divmod(slot, 4)
            padded[slot, 16:144, :] = blocks[slot].astype(F32)
            if block > 0:
                padded[slot, 0:16, :] = blocks[slot - 1, 112:128, :].astype(F32)
            if block < 3:
                padded[slot, 144:160, :] = blocks[slot + 1, 0:16, :].astype(F32)
        place = self.place
        for side, outside in ((0, place.z == 0), (1, place.z == PLANES - 1)):
            first, rows = ((0, slice(0, 16)), (3, slice(144, 160)))[side]
            into = self.received.at[side]

            @pl.when(outside)
            def nothing():
                for row in range(2):
                    padded[row * 4 + first, rows, :] = jnp.zeros((16, 128), F32)

            @pl.when(jnp.logical_not(outside))
            def arrive():
                remote(
                    into, into, self.send.at[side], self.recv.at[side], place.zdev(1)
                ).wait_recv()
                for row in range(2):
                    padded[row * 4 + first, rows, :] = self.received[side, row].astype(F32)

        for side, inside, copy in self.copies():

            @pl.when(inside)
            def drain(copy=copy):
                copy.wait_send()


def lane_is(index, rows=128):
    return lax.broadcasted_iota(jnp.int32, (rows, 128), 1) == index


def put_columns(tile, slot, first, second):
    return jnp.where(lane_is(slot), first, jnp.where(lane_is(slot + 8), second, tile))


def share_columns(place, refs, tile):
    share = Exchange(place, refs[0], refs[1:])
    own = place.slot(0)
    share.blocks[own] = jnp.transpose(tile)[:16]
    share.start(lambda k: share.blocks.at[own])
    return share


def back_to_columns(first, second):
    rows = jnp.concatenate([first, second, jnp.zeros((112, 128), F32)], axis=0)
    return jnp.transpose(rows)


def column(tile, slot):
    return jnp.sum(jnp.where(lane_is(slot, tile.shape[0]), tile, 0.0), axis=1, keepdims=True)


def kept_frames(value, offset, before, after):
    if offset < 0:
        return jnp.where(before <= offset, value, 0.0)
    if offset > 0:
        return jnp.where(after > offset, value, 0.0)
    return value


CHUNK = 64


def convolve(refs):
    taps = [refs.taps[j : j + 1, :] for j in range(KERNEL)]

    def step(slot, tile):
        for first in range(0, 128, CHUNK):
            rows = slice(first, first + CHUNK)
            before, after = refs.before[slot, rows, :], refs.after[slot, rows, :]
            total = jnp.zeros((CHUNK, 128), F32)
            for j in range(KERNEL):
                start = first + j + 1
                value = refs.glu_padded[slot, start : start + CHUNK, :]
                total = total + taps[j] * kept_frames(value, j - HALF, before, after)
            refs.conv[slot, rows, :] = total
        value = refs.conv[slot]
        mean = jnp.mean(value, axis=1, keepdims=True)
        center = value - mean
        return put_columns(tile, slot, mean, jnp.sum(center * center, axis=1, keepdims=True))

    return lax.fori_loop(0, 8, step, jnp.zeros((128, 128), F32))


def inner_norm(refs, slot, rows=slice(0, 128)):
    tile = refs.inner_stats[rows, :]
    mean, inverse = column(tile, slot), column(tile, slot + 8)
    return (refs.conv[slot, rows, :] - mean) * inverse, inverse


def conv_forward(place, refs, gather, scatter):
    def process(pair, slots, part):
        if part == 0 and pair[0] == 0:
            refs.finish_ci()
        value = dot(place.parts.take(gather.blocks, slots, part), flat(refs.w_ci))
        place.parts.put(refs.gate_up, slots, part, value)
        place.parts.put(
            refs.glu,
            slots,
            part,
            (value[:, :128] * jax.nn.sigmoid(value[:, 128:])).astype(BF16),
        )

    gather_blocks(place, gather, process)
    edges = Edges(place, refs.edges)
    edges.start(refs.glu)
    gather.drain()
    edges.wait(refs.glu, refs.glu_padded)
    share = share_columns(place, refs.stats, convolve(refs))
    refs.conv_middle()
    share.wait()
    stats = share.blocks[...]
    means, spreads = stats[:, :8], stats[:, 8:]
    mean = jnp.mean(means, axis=0)
    spread = jnp.sum(spreads + 128.0 * jnp.square(means - mean[None]), axis=0) / 1024.0
    refs.inner_stats[...] = back_to_columns(mean, lax.rsqrt(spread + EPSILON))
    refs.finish_co()

    def active_rows(slots, part):
        rows = place.parts.of(part)
        parts = []
        for slot in slots:
            unit_part, unused = inner_norm(refs, slot, rows)
            parts.append(sigmoid_linear(unit_part * refs.gain_inner[...]).astype(BF16))
        value = jnp.concatenate(parts, axis=0)
        place.parts.put(refs.conv_active, slots, part, value)
        return value

    scatter_blocks(place, scatter, active_rows, refs.w_co)


def conv_kept():
    return dict(
        conv_blocks=((8, 128, 1024), BF16),
        w_ci=((16, 64, 256), BF16),
        w_co=((2, 64, 1024), BF16),
        gate_up=((8, 128, 256), F32),
        glu_padded=((8, 160, 128), F32),
        conv=((8, 128, 128), F32),
        inner_stats=((128, 128), F32),
        conv_active=((8, 128, 128), BF16),
    )


STATS = [VMEM((8, 16, 128), F32), DMA((8,)), DMA((8,))]


def convolve_back(refs):
    taps = [refs.taps[j : j + 1, :] for j in range(KERNEL)]
    refs.tap_sums[...] = jnp.zeros_like(refs.tap_sums)

    def step(slot, unused):
        for first in range(0, 128, CHUNK):
            rows = slice(first, first + CHUNK)
            before, after = refs.before[slot, rows, :], refs.after[slot, rows, :]
            total = jnp.zeros((CHUNK, 128), F32)
            grad = refs.conv_grad_padded[slot, first + 16 : first + 16 + CHUNK, :]
            for j in range(KERNEL):
                offset = j - HALF
                start = first + 16 - offset
                value = refs.conv_grad_padded[slot, start : start + CHUNK, :]
                total = total + taps[j] * kept_frames(value, -offset, before, after)
                start = first + 16 + offset
                value = refs.glu_padded[slot, start : start + CHUNK, :]
                product = kept_frames(value * grad, offset, before, after)
                refs.tap_sums[j] += jnp.sum(product.reshape(CHUNK // 8, 8, 128), axis=0)
            refs.glu_grad[slot, rows, :] = total
        return unused

    lax.fori_loop(0, 8, step, 0)
    return jnp.sum(refs.tap_sums[...], axis=1)


def conv_backward(place, refs, gather, scatter):
    gain = refs.gain_inner[...]

    def process(pair, slots, part):
        if part == 0 and pair[0] == 0:
            refs.finish_conv()
        back = dot(place.parts.take(gather.blocks, slots, part), flat(refs.w_co), 1, 1)
        rows = place.parts.of(part)
        units = jnp.concatenate([inner_norm(refs, slot, rows)[0] for slot in slots], axis=0)
        place.parts.put(refs.inner_grad, slots, part, back * sigmoid_linear_grad(units * gain))

    gather_blocks(place, gather, process)

    def sums(slot, current):
        tile, gain_grad = current
        value = refs.inner_grad[slot]
        unit_part, unused = inner_norm(refs, slot)
        scaled = value * gain
        tile = put_columns(
            tile,
            slot,
            jnp.sum(scaled, axis=1, keepdims=True),
            jnp.sum(scaled * unit_part, axis=1, keepdims=True),
        )
        return tile, gain_grad + jnp.sum(value * unit_part, axis=0, keepdims=True)

    tile, inner_gain_grad = lax.fori_loop(
        0, 8, sums, (jnp.zeros((128, 128), F32), jnp.zeros((1, 128), F32))
    )
    share = share_columns(place, refs.stats, tile)
    weights = WeightGrads(place, refs, "conv", "conv", False)
    weights.put_out(refs.conv_active, gather.blocks)
    gather.drain()
    share.wait()
    means = jnp.sum(share.blocks[...], axis=0) / 1024.0
    refs.grad_stats[...] = back_to_columns(means[:8], means[8:])

    def input_grad(slot, unused):
        unit_part, inverse = inner_norm(refs, slot)
        tile = refs.grad_stats[...]
        refs.conv_grad[slot] = (
            inverse
            * (
                refs.inner_grad[slot] * gain
                - column(tile, slot)
                - unit_part * column(tile, slot + 8)
            )
        ).astype(BF16)
        return unused

    lax.fori_loop(0, 8, input_grad, 0)
    edges = Edges(place, refs.edges)
    edges.start(refs.conv_grad)
    refs.conv_begin()
    edges.wait(refs.conv_grad, refs.conv_grad_padded)
    weights.sum_out.start()
    tap_grads = convolve_back(refs)
    refs.conv_middle()

    def gate_rows(slots, part):
        value, glu_grad = place.parts.take(refs.gate_up, slots, part), place.parts.take(refs.glu_grad, slots, part)
        sigma = jax.nn.sigmoid(value[:, 128:])
        low = jnp.concatenate(
            [glu_grad * sigma, glu_grad * value[:, :128] * sigma * (1.0 - sigma)], axis=1
        ).astype(BF16)
        place.parts.put(refs.gate_grads, slots, part, low)
        return low

    scatter_blocks(place, scatter, gate_rows, refs.w_ci, 1)
    return inner_gain_grad, tap_grads, weights


class Traffic:
    def __init__(self, refs, sems):
        self.refs, self.sems = refs, sems
        self.count = 0

    def start(self, pairs):
        copies = []
        for source, target in pairs:
            copy = pltpu.make_async_copy(source, target, self.sems.at[self.count])
            copy.start()
            copies.append(copy)
            self.count += 1

        def finish():
            for copy in copies:
                copy.wait()

        return finish

    def save(self, names):
        return self.start(
            [(getattr(self.refs, name), getattr(self.refs, "keep_" + name)) for name in names]
        )

    def load(self, names):
        return self.start(
            [(getattr(self.refs, "keep_" + name), getattr(self.refs, name)) for name in names]
        )


def ffn_kept():
    return dict(
        blocks=((8, 128, 1024), BF16),
        hidden=((8, 128, 512), F32),
        w_in=((16, 64, 512), BF16),
        w_out=((4, 128, 1024), BF16),
    )


SCATTER_SEMS = [DMA((16,)), DMA((16,))]


def forward_body(refs):
    place = Place(FORWARD_PARTS)
    place.enter()
    traffic = Traffic(refs, refs.traffic)
    gather_in = GatherRows(place, refs.w_in_rows, refs.w_in, refs.gather_in, ffn_pieces)
    refs.row_lengths[place.x] = refs.own_lengths[...]
    lengths = remote(
        refs.own_lengths,
        refs.row_lengths.at[place.x],
        refs.length_sems.at[0],
        refs.length_sems.at[1],
        place.dev(4),
    )
    lengths.start()
    halves = (slice(0, 512), slice(512, 1024))
    gather_out = [
        GatherBlocks(place, refs.w_out_rows, refs.w_out, refs.gather_out, halves[0])
    ]
    gather = Gather(place, refs.blocks, refs.ffn_ag)
    for part in place.parts:
        frames = place.parts.of(part)
        gather.push(part, norm_rows(refs.stream[frames, :].astype(F32), refs.gain_ffn1[...])[0])
    gather_in.along_z()
    gather_out.append(
        GatherBlocks(place, refs.w_out_rows, refs.w_out, refs.gather_out_last, halves[1])
    )
    gather_qkv = GatherRows(place, refs.qkv_rows, refs.w_qkv, refs.gather_qkv, head_pieces)
    lengths.wait()
    fill_tables(refs)
    fill_channels(place, refs)
    held = Refs()
    gather_blocks(place, gather, lambda pair, slots, part: None)
    gather_out[0].relay()
    gather_in.relay()
    gather_in.finish()
    for part in place.parts:
        for group in PAIRS:
            for pair in group:
                slots = [place.slot(k) for k in pair]
                value = dot(place.parts.take(refs.blocks, slots, part), flat(refs.w_in))
                place.parts.put(refs.hidden, slots, part, value)
                place.parts.put(refs.active, slots, part, sigmoid_linear(value).astype(BF16))
    gather.drain()
    scatter = Scatter(place, refs.scatter_columns, refs.ffn_scatter)
    for half, columns in enumerate(halves):
        if half:
            gather_out[half].relay()
        gather_out[half].finish()
        if half:
            gather_qkv.along_z()
            gather_o = GatherHalf(place, refs.o_rows, refs.w_o, refs.gather_o)
        weight = refs.w_out[:, :, columns].reshape(512, 512)
        for pair in OUT_PAIRS:
            rows = jnp.concatenate([refs.active[place.slot(k)] for k in pair], axis=0)
            scatter.emit_pair(pair, half, dot(rows, weight))
        for k in (2, 4, 6, 0):
            scatter.finish(k, half)
    saved = [traffic.save(ffn_kept())]
    gather_ci = GatherRows(place, refs.ci_rows, refs.w_ci, refs.gather_ci, channel_pieces)
    gather_next = GatherRows(place, refs.next_in_rows, refs.next_in, refs.gather_next, ffn_pieces)

    def to_attention(part, total):
        frames = place.parts.of(part)
        value = refs.stream[frames, :].astype(F32) + 0.5 * total
        refs.stream_one[frames, :] = value
        return norm_rows(value, refs.gain_attn[...])[0]

    def to_conv(part, total):
        frames = place.parts.of(part)
        value = refs.stream_one[frames, :] + total
        refs.stream_two[frames, :] = value
        return norm_rows(value, refs.gain_conv[...])[0]

    gather = Gather(place, refs.attn_blocks, refs.attn_ag)
    total = jnp.concatenate([scatter.total(half) for half in range(2)], axis=1)
    for part in place.parts:
        gather.push(part, to_attention(part, total[place.parts.of(part)]))
    scatter.drain()
    gather_qkv.relay()
    gather_o.relay()

    def after_turn():
        gather_ci.along_z()
        held.co = GatherHalf(place, refs.co_rows, refs.w_co, refs.gather_co)

    def after_mix():
        gather_ci.relay()
        held.co.relay()
        gather_o.finish()
        gather_next.along_z()
        held.next_out = GatherBlocks(
            place, refs.next_out_rows, refs.next_out, refs.gather_next_out
        )

    def conv_middle():
        gather_next.relay()
        held.next_out.relay()

    refs.after_turn, refs.after_mix, refs.conv_middle = after_turn, after_mix, conv_middle
    refs.finish_qkv, refs.finish_ci, refs.finish_co = (
        gather_qkv.finish,
        gather_ci.finish,
        lambda: held.co.finish(),
    )
    scatter = Scatter(place, refs.scatter, refs.attn_scatter)
    attention_forward(place, refs, gather, scatter)
    saved.append(traffic.save(attention_kept()))
    gather = Gather(place, refs.conv_blocks, refs.conv_ag)
    carry(place, scatter, gather, to_conv)
    scatter = Scatter(place, refs.scatter, refs.conv_scatter)
    conv_forward(place, refs, gather, scatter)
    saved.append(traffic.save(conv_kept()))
    for part in place.parts:
        frames = place.parts.of(part)
        refs.stream_three[frames, :] = refs.stream_two[frames, :] + scatter.total(part)
    scatter.drain()
    gather_next.finish()
    held.next_out.finish()
    for finish in saved:
        finish()


def scratch_of(kept):
    return {name: VMEM(shape, dtype) for name, (shape, dtype) in kept.items()}


def forward_call(ins):
    kept = {**ffn_kept(), **attention_kept(), **conv_kept()}
    outs = dict(
        stream_one=((128, 1024), F32, VMEM),
        stream_two=((128, 1024), F32, VMEM),
        stream_three=((128, 1024), F32, VMEM),
        next_in=((16, 64, 512), BF16, pl.ANY),
        next_out=((4, 128, 1024), BF16, pl.ANY),
    )
    outs["row_lengths"] = ((2, 8, 128), F32, VMEM)
    for name, (shape, dtype) in kept.items():
        outs["keep_" + name] = (shape, dtype, pl.ANY)
    scratch = dict(
        scratch_of(kept),
        active=VMEM((8, 128, 512), BF16),
        gather_in=GatherRows.scratch(),
        gather_out=GatherBlocks.scratch(),
        gather_out_last=GatherBlocks.scratch(),
        gather_qkv=GatherRows.scratch(),
        gather_o=GatherHalf.scratch(),
        gather_ci=GatherRows.scratch(),
        gather_co=GatherHalf.scratch(),
        gather_next=GatherRows.scratch(),
        gather_next_out=GatherBlocks.scratch(),
        length_sems=DMA((2,)),
        **table_scratch(),
        traffic=DMA((len(kept),)),
        scatter=Scatter.scratch(FORWARD_PARTS, 128 // FORWARD_PARTS, 1024),
        scatter_columns=Scatter.scratch(2, 128, 512),
        ffn_ag=AG_SEMS,
        attn_ag=AG_SEMS,
        conv_ag=AG_SEMS,
        ffn_scatter=SCATTER_SEMS,
        attn_scatter=SCATTER_SEMS,
        conv_scatter=SCATTER_SEMS,
        q_rows=VMEM((8, 128, 128), BF16),
        k_rows=VMEM((8, 128, 128), BF16),
        v_rows=VMEM((8, 128, 128), BF16),
        turn_qk=Turn.scratch(512),
        turn_v=Turn.scratch(256),
        turn_mix=Turn.scratch(256),
        values_t=VMEM((64, 2048), BF16),
        glu=VMEM((8, 128, 128), BF16),
        edges=Edges.scratch(),
        stats=STATS,
    )
    return kernel_call(forward_body, 1, ins, outs, scratch)


class SmallSum:
    def __init__(self, place, refs):
        self.place, self.refs = place, refs
        self.first = Exchange(place, refs.small_first, refs.small_first_sems)
        self.last = Exchange(place, refs.small, refs.small_last_sems)
        self.sent = []

    def start(self):
        refs, place = self.refs, self.place

        def part(slot):
            return refs.gain_grads.at[:, columns_of(slot, 128)]

        self.first.blocks[place.slot(0)] = refs.gain_grads[:, columns_of(place.slot(0), 128)]
        self.first.start(lambda k: part(place.slot(k)))

    def along_z(self):
        refs, place = self.refs, self.place
        self.first.wait()
        refs.small_planes[place.z, 0:8, :] = jnp.sum(self.first.blocks[...], axis=0)
        refs.small_planes[place.z, 8:48, :] = refs.channel_grads[...]
        send, recv = refs.small_z_sems
        rows = refs.small_planes.at[place.z]
        for k in (1, 2, 3):
            copy = remote(rows, rows, send.at[k], recv.at[k], place.zdev(k))
            copy.start()
            self.sent.append(copy)

    def spread(self):
        refs, place = self.refs, self.place
        send, recv = refs.small_z_sems
        for k in (1, 2, 3):
            into = refs.small_planes.at[lax.rem(place.z + 4 - k, PLANES)]
            remote(into, into, send.at[k], recv.at[k], place.zdev(k)).wait_recv()
        for copy in self.sent:
            copy.wait_send()
        own = place.slot(0)
        self.last.blocks[own] = jnp.sum(refs.small_planes[...], axis=0)
        self.last.start(lambda k: self.last.blocks.at[own])

    def wait(self):
        self.last.wait()


def backward_step(place, refs, stream, gain, row, scale):
    saved = [
        norm_forward(stream[place.parts.of(part), :].astype(F32), gain)[1] for part in place.parts
    ]

    def step(part, total):
        frames = place.parts.of(part)
        input_part, gain_grad = norm_input_grad(total, gain, saved[part])
        value = refs.grad_stream[frames, :] + input_part
        refs.grad_stream[frames, :] = value
        refs.gain_grads[row : row + 1, :] += gain_grad
        return (scale * value).astype(BF16)

    return step


def backward_body(refs):
    place = Place(BACKWARD_PARTS)
    place.enter()
    traffic = Traffic(refs, refs.traffic)
    ready = traffic.start([(refs.next_in, refs.w_in), (refs.next_out, refs.w_out)])
    gather = Gather(place, refs.blocks, refs.ffn2_ag)
    for part in place.parts:
        frames = place.parts.of(part)
        gather.push(part, norm_rows(refs.stream_three[frames, :], refs.gain_ffn2[...])[0])
    refs.finish_conv = traffic.load(conv_kept())
    refs.finish_attn = traffic.load(attention_kept())
    fill_tables(refs)
    fill_channels(place, refs)
    refs.gain_grads[...] = jnp.zeros_like(refs.gain_grads)
    refs.channel_grads[...] = jnp.zeros_like(refs.channel_grads)
    scatter = Scatter(place, refs.scatter, refs.ffn2_scatter)
    ffn_forward(place, gather, refs.hidden, refs.w_in, refs.w_out, scatter, ready)
    gather.drain()

    def turn_round(part, total):
        frames = place.parts.of(part)
        final, saved = norm_forward(refs.stream_three[frames, :] + 0.5 * total, refs.gain_out[...])
        refs.output[frames, :] = final.astype(BF16)
        grad, gain_grad = norm_input_grad(
            refs.cotangent[frames, :].astype(F32), refs.gain_out[...], saved
        )
        refs.grad_stream[frames, :] = grad
        refs.gain_grads[4:5, :] += gain_grad
        return (0.5 * grad).astype(BF16)

    gather = Gather(place, refs.grads_even, refs.ffn2_ag_back)
    carry(place, scatter, gather, turn_round)
    scatter = Scatter(place, refs.scatter, refs.ffn2_scatter_back)
    ffn_backward(
        place,
        gather,
        refs.hidden,
        refs.hidden_grads,
        refs.active,
        refs.w_in,
        refs.w_out,
        scatter,
        lambda: None,
    )
    gather.drain()
    step = backward_step(place, refs, refs.stream_three, refs.gain_ffn2[...], 3, 1.0)
    weights_two = WeightGrads(place, refs, "ffn2", "ffn", True)
    weights_two.put_both(refs.active, refs.grads_even, refs.blocks, refs.hidden_grads)
    gather = Gather(place, refs.grads_odd, refs.conv_ag)
    carry(place, scatter, gather, step)
    load_first = traffic.load(ffn_kept())
    refs.conv_begin, refs.conv_middle = weights_two.sum_out.relay, weights_two.sum_in.relay
    scatter = Scatter(place, refs.scatter, refs.conv_scatter)
    inner, taps, weights_three = conv_backward(place, refs, gather, scatter)
    step = backward_step(place, refs, refs.stream_two, refs.gain_conv[...], 2, 1.0)
    refs.channel_grads[0:32, :] = taps
    refs.channel_grads[32:33, :] = inner
    weights_three.put_in(refs.conv_blocks, refs.gate_grads)
    gather = Gather(place, refs.grads_even, refs.attn_ag)
    carry(place, scatter, gather, step)

    def before_attend():
        weights_two.share()
        weights_three.relay()

    refs.before_attend, refs.after_attend = before_attend, weights_three.share
    scatter = Scatter(place, refs.scatter, refs.attn_scatter)
    weights_four = attention_backward(place, refs, gather, scatter)
    step = backward_step(place, refs, refs.stream_one, refs.gain_attn[...], 1, 0.5)
    weights_four.put_in(refs.attn_blocks, refs.qkv_grads)
    gather = Gather(place, refs.grads_odd, refs.ffn1_ag)
    carry(place, scatter, gather, step)
    weights_two.wait()
    weights_three.wait()
    scatter = Scatter(place, refs.scatter, refs.ffn1_scatter)
    ffn_backward(
        place,
        gather,
        refs.hidden,
        refs.hidden_grads,
        refs.active,
        refs.w_in,
        refs.w_out,
        scatter,
        load_first,
    )
    gather.drain()
    weights_one = WeightGrads(place, refs, "ffn1", "ffn", True)
    weights_one.put_both(refs.active, refs.grads_odd, refs.blocks, refs.hidden_grads)
    weights_four.sum_in.relay()
    weights_four.share()
    weights_one.sum_out.relay()
    step = backward_step(place, refs, refs.stream, refs.gain_ffn1[...], 0, 1.0)
    for part in place.parts:
        step(part, scatter.total(part))
    scatter.drain()
    small = SmallSum(place, refs)
    small.start()
    weights_one.sum_in.relay()
    small.along_z()
    small.spread()
    weights_four.wait()
    weights_one.share()
    small.wait()
    weights_one.wait()


MODULES = (("ffn1", 512, True), ("qkv", 384, False), ("conv", 256, False), ("ffn2", 512, True))


def backward_call(ins):
    kept = {**ffn_kept(), **attention_kept(), **conv_kept()}
    outs = dict(
        output=((128, 1024), BF16, VMEM),
        grad_stream=((128, 1024), F32, VMEM),
        small=((8, 48, 128), F32, VMEM),
    )
    scratch = dict(
        scratch_of(kept),
        active=VMEM((8, 128, 512), BF16),
        hidden_grads=VMEM((8, 128, 512), BF16),
        grads_even=VMEM((8, 128, 1024), BF16),
        grads_odd=VMEM((8, 128, 1024), BF16),
        traffic=DMA((2 + len(kept),)),
        scatter=Scatter.scratch(BACKWARD_PARTS, 128 // BACKWARD_PARTS, 1024),
        ffn2_ag=AG_SEMS,
        ffn2_ag_back=AG_SEMS,
        conv_ag=AG_SEMS,
        attn_ag=AG_SEMS,
        ffn1_ag=AG_SEMS,
        ffn2_scatter=SCATTER_SEMS,
        ffn2_scatter_back=SCATTER_SEMS,
        conv_scatter=SCATTER_SEMS,
        attn_scatter=SCATTER_SEMS,
        ffn1_scatter=SCATTER_SEMS,
        mix_rows=VMEM((8, 128, 128), BF16),
        mix_grads=VMEM((2048, 64), BF16),
        keys_t=VMEM((64, 2048), BF16),
        turn_qk=Turn.scratch(512),
        turn_v=Turn.scratch(256),
        turn_mix=Turn.scratch(256),
        key_grad=VMEM((2048, 64), F32),
        value_grad=VMEM((2048, 64), F32),
        qkv_grads=VMEM((8, 128, 384), BF16),
        **table_scratch(),
        inner_grad=VMEM((8, 128, 128), F32),
        grad_stats=VMEM((128, 128), F32),
        conv_grad=VMEM((8, 128, 128), BF16),
        conv_grad_padded=VMEM((8, 160, 128), F32),
        glu_grad=VMEM((8, 128, 128), F32),
        gate_grads=VMEM((8, 128, 256), BF16),
        tap_sums=VMEM((32, 8, 128), F32),
        edges=Edges.scratch(),
        stats=STATS,
        gain_grads=VMEM((8, 1024), F32),
        channel_grads=VMEM((40, 128), F32),
        small_first=VMEM((8, 8, 128), F32),
        small_planes=VMEM((PLANES, 48, 128), F32),
        small_first_sems=[DMA((8,)), DMA((8,))],
        small_z_sems=[DMA((4,)), DMA((4,))],
        small_last_sems=[DMA((8,)), DMA((8,))],
        **WeightGrads.sums("ffn", 512, True),
        **WeightGrads.sums("qkv", 384, False),
        **WeightGrads.sums("conv", 256, False),
    )
    for name, width, wide in MODULES:
        outs.update(WeightGrads.outs(name, width, wide))
        scratch.update(WeightGrads.scratch(name, width, wide))
    return kernel_call(backward_body, 2, ins, outs, scratch)


def unpack_body(count, *refs):
    sources, outs = refs[:count], refs[count : 2 * count + 8]
    (
        output,
        grad_stream,
        small,
        ffn1_in,
        ffn1_out,
        qkv_in,
        qkv_out,
        conv_in,
        conv_out,
        ffn2_in,
        ffn2_out,
    ) = sources
    outs[0][...] = output[...]
    outs[1][...] = grad_stream[...]
    for slot in range(8):
        x, yc = divmod(slot, 4)
        pair = ((x * 2 + yc % 2) * 2 + yc // 2) * 128
        for index, row in enumerate((0, 1, 2, None, 3, 4)):
            if row is not None:
                outs[2 + index][:, slot * 128 : slot * 128 + 128] = small[slot, row : row + 1, :]
        outs[5][:, pair : pair + 128] = small[slot, 40:41, :]
        outs[8][:, pair : pair + 128] = small[slot, 8 : 8 + KERNEL, :]
        for source, out in ((ffn1_in, outs[9]), (ffn2_in, outs[15])):
            for plane in range(PLANES):
                column = ((plane * 4 + yc) * 2 + x) * 128
                out[:, column : column + 128] = source[
                    slot, :, plane * 128 : plane * 128 + 128
                ].astype(F32)
        for source, out, kinds in ((qkv_in, outs[11], 3), (conv_in, outs[13], 2)):
            for kind in range(kinds):
                column = kind * 1024 + pair
                out[:, column : column + 128] = source[slot, :, kind * 128 : kind * 128 + 128].astype(
                    F32
                )
    for source, out in ((ffn1_out, outs[10]), (ffn2_out, outs[16])):
        out[0:128, :] = source[0].astype(F32)
        out[128:256, :] = source[1].astype(F32)
    outs[12][...] = qkv_out[...].astype(F32)
    outs[14][...] = conv_out[...].astype(F32)


def unpack_call(backward):
    arrays = list(backward.values())
    gain = jax.ShapeDtypeStruct((1, 1024), F32)
    shapes = [
        jax.ShapeDtypeStruct((128, 1024), BF16),
        jax.ShapeDtypeStruct((128, 1024), F32),
        *[gain] * 6,
        jax.ShapeDtypeStruct((KERNEL, 1024), F32),
    ] + [
        jax.ShapeDtypeStruct(shape, F32)
        for shape in (
            (64, 4096),
            (256, 1024),
            (64, 3072),
            (64, 1024),
            (64, 2048),
            (64, 1024),
            (64, 4096),
            (256, 1024),
        )
    ]
    whole = pl.BlockSpec(memory_space=VMEM)
    return pl.pallas_call(
        functools.partial(unpack_body, len(arrays)),
        out_shape=shapes,
        in_specs=[whole] * len(arrays),
        out_specs=[whole] * len(shapes),
        compiler_params=pltpu.CompilerParams(vmem_limit_bytes=VMEM_LIMIT),
    )(*arrays)


def local_planes(
    inputs,
    lengths,
    gain_ffn1,
    gain_attn,
    gain_conv,
    gain_inner,
    gain_ffn2,
    gain_out,
    conv_kernel,
    ffn1_in,
    ffn1_out,
    attn_qkv,
    attn_out,
    conv_in,
    conv_out,
    ffn2_in,
    ffn2_out,
    cotangent,
):
    plane = lax.axis_index("seq") // 4
    cos, sin = rotary_tables(plane * 512 + jnp.arange(512, dtype=jnp.int32))
    shared = dict(
        stream=(inputs[0], VMEM),
        gain_ffn1=(gain_ffn1[None], VMEM),
        gain_attn=(gain_attn[None], VMEM),
        gain_conv=(gain_conv[None], VMEM),
        all_inner=(gain_inner[None], VMEM),
        all_taps=(conv_kernel, VMEM),
        cos_rows=(cos, VMEM),
        sin_rows=(sin, VMEM),
    )
    forward = forward_call(
        dict(
            shared,
            own_lengths=(jnp.pad(lengths.astype(F32), ((0, 7), (0, 124))), VMEM),
            w_in_rows=(ffn1_in, pl.ANY),
            w_out_rows=(ffn1_out, pl.ANY),
            qkv_rows=(attn_qkv, pl.ANY),
            o_rows=(attn_out, pl.ANY),
            ci_rows=(conv_in, pl.ANY),
            co_rows=(conv_out, pl.ANY),
            next_in_rows=(ffn2_in, pl.ANY),
            next_out_rows=(ffn2_out, pl.ANY),
        )
    )
    ins = dict(
        shared,
        cotangent=(cotangent[0], VMEM),
        gain_ffn2=(gain_ffn2[None], VMEM),
        gain_out=(gain_out[None], VMEM),
    )
    for name, array in forward.items():
        held = name.startswith("stream") or name == "row_lengths"
        ins[name] = (array, VMEM if held else pl.ANY)
    results = unpack_call(backward_call(ins))
    return (
        results[0][None],
        results[1][None],
        *[gain[0] for gain in results[2:8]],
        *results[8:],
    )


def solution(mesh):
    return jax.shard_map(
        local_planes if mesh.shape["seq"] == 16 and mesh.shape["row"] == 2 else local,
        mesh=mesh,
        in_specs=(
            P("row", "seq", None),
            P("row", None),
            P(),
            P(),
            P(),
            P(),
            P(),
            P(),
            P(),
            P("seq", None),
            P("seq", None),
            P("seq", None),
            P("seq", None),
            P("seq", None),
            P("seq", None),
            P("seq", None),
            P("seq", None),
            P("row", "seq", None),
        ),
        out_specs=(
            P("row", "seq", None),
            P("row", "seq", None),
            P(),
            P(),
            P(),
            P(),
            P(),
            P(),
            P(),
            P("seq", None),
            P("seq", None),
            P("seq", None),
            P("seq", None),
            P("seq", None),
            P("seq", None),
            P("seq", None),
            P("seq", None),
        ),
        check_vma=False,
    )
```

```python
import functools
import math

import jax
import jax.numpy as jnp
from jax import lax
from jax.experimental import pallas as pl
from jax.experimental.pallas import tpu as pltpu
from jax.sharding import PartitionSpec as P

HEADS = 16
HEAD_DIM = 64
KERNEL = 31
HALF = 15


EPSILON = 1e-05
MASKED = -1e30


def with_halo(block, sides, width):
    for axis, dim in sides:
        count = lax.axis_size(axis)
        forward = [(i, i + 1) for i in range(count - 1)]
        backward = [(target, source) for source, target in forward]
        low = lax.ppermute(
            lax.slice_in_dim(block, block.shape[dim] - width, None, axis=dim), axis, forward
        )
        high = lax.ppermute(lax.slice_in_dim(block, 0, width, axis=dim), axis, backward)
        block = jnp.concatenate([low, block, high], axis=dim)
    return block


def shifted(array, axis, by):
    size = lax.axis_size(axis)
    return lax.ppermute(array, axis, [(i, (i + by) % size) for i in range(size)])


def segment_of(positions, seg_lengths):
    boundary = jnp.cumsum(seg_lengths)[:-1]
    return jnp.sum((positions[:, None] >= boundary[None, :]).astype(jnp.int32), axis=1)


def rotary_tables(positions):
    half_dim = HEAD_DIM // 2
    inverse = jnp.exp(-jnp.log(10000.0) * jnp.arange(half_dim, dtype=jnp.float32) / half_dim)
    angles = positions.astype(jnp.float32)[:, None] * inverse[None, :]
    return (jnp.cos(angles), jnp.sin(angles))


def split_heads(values):
    return values.reshape(values.shape[0], HEADS, HEAD_DIM)


def rotate(values, cos_table, sin_table):
    half_dim = HEAD_DIM // 2
    shaped = split_heads(values)
    first_half = shaped[..., :half_dim]
    second_half = shaped[..., half_dim:]
    cos_heads = cos_table[:, None, :]
    sin_heads = sin_table[:, None, :]
    turned = jnp.concatenate(
        [
            first_half * cos_heads - second_half * sin_heads,
            second_half * cos_heads + first_half * sin_heads,
        ],
        axis=-1,
    )
    return turned.reshape(values.shape)


def unrotate(grads, cos_table, sin_table):
    half_dim = HEAD_DIM // 2
    shaped = split_heads(grads)
    first_half = shaped[..., :half_dim]
    second_half = shaped[..., half_dim:]
    cos_heads = cos_table[:, None, :]
    sin_heads = sin_table[:, None, :]
    turned = jnp.concatenate(
        [
            first_half * cos_heads + second_half * sin_heads,
            second_half * cos_heads - first_half * sin_heads,
        ],
        axis=-1,
    )
    return turned.reshape(grads.shape)


def norm_forward(values, gain):
    center = values - jnp.mean(values, axis=-1, keepdims=True)
    spread = jnp.mean(center * center, axis=-1, keepdims=True)
    inverse = lax.rsqrt(spread + EPSILON)
    unit_part = center * inverse
    return (unit_part * gain, (unit_part, inverse))


def norm_backward(grads, gain, saved):
    unit_part, inverse = saved
    scaled = grads * gain
    gain_grad = jnp.sum(grads * unit_part, axis=0)
    input_part = inverse * (
        scaled
        - jnp.mean(scaled, axis=-1, keepdims=True)
        - unit_part * jnp.mean(scaled * unit_part, axis=-1, keepdims=True)
    )
    return (input_part, gain_grad)


def sigmoid_linear(values):
    return values * jax.nn.sigmoid(values)


def sigmoid_linear_grad(values):
    sigma = jax.nn.sigmoid(values)
    return sigma * (1.0 + values * (1.0 - sigma))


def project(left_side, weight):
    return (
        jnp.dot(
            left_side,
            lax.all_gather(weight, "seq", axis=0, tiled=True),
            preferred_element_type=jnp.float32,
        ),
        weight,
    )


def project_back(grad_side, weight):
    return lax.dot_general(
        grad_side,
        lax.all_gather(weight, "seq", axis=0, tiled=True),
        (((1,), (1,)), ((), ())),
        preferred_element_type=jnp.float32,
    )


def weight_grad(left_side, grad_side):
    return lax.psum_scatter(
        lax.dot_general(
            left_side, grad_side, (((0,), (0,)), ((), ())), preferred_element_type=jnp.float32
        ).astype(jnp.bfloat16),
        "seq",
        scatter_dimension=0,
        tiled=True,
    ).astype(jnp.float32)


def over_blocks(advance, running, pieces):
    total_rows = pieces[0].shape[0]
    block_size = math.gcd(total_rows, 512)
    number = total_rows // block_size
    stacked = tuple((piece.reshape((number, block_size) + piece.shape[1:]) for piece in pieces))

    def scan_step(current, block_item):
        block_index, blocks = block_item
        return (advance(current, blocks, block_index * block_size), None)

    running, unused = lax.scan(scan_step, running, (jnp.arange(number, dtype=jnp.int32), stacked))
    return running


def block_scores(query_heads, key_heads, query_segments, key_segments):
    scale = HEAD_DIM ** (-0.5)
    raw_scores = (
        jnp.einsum("qhd,khd->hqk", query_heads, key_heads, preferred_element_type=jnp.float32)
        * scale
    )
    return jnp.where((query_segments[:, None] == key_segments[None, :])[None], raw_scores, MASKED)


def pair_grads(
    query_rows, grad_rows, log_total, delta, query_segments, key_rows, value_rows, key_segments
):
    scale = HEAD_DIM ** (-0.5)
    query_heads = split_heads(query_rows)
    grad_heads = split_heads(grad_rows)
    key_heads = split_heads(key_rows)
    value_heads = split_heads(value_rows)
    probs = jnp.exp(
        block_scores(query_heads, key_heads, query_segments, key_segments) - log_total[:, :, None]
    )
    prob_grads = jnp.einsum(
        "qhd,khd->hqk", grad_heads, value_heads, preferred_element_type=jnp.float32
    )
    score_grads = (probs * (prob_grads - delta[:, :, None])).astype(jnp.bfloat16)
    query_grad = (
        jnp.einsum("hqk,khd->qhd", score_grads, key_heads, preferred_element_type=jnp.float32)
        * scale
    )
    key_grad = (
        jnp.einsum("hqk,qhd->khd", score_grads, query_heads, preferred_element_type=jnp.float32)
        * scale
    )
    value_grad = jnp.einsum(
        "hqk,qhd->khd", probs.astype(jnp.bfloat16), grad_heads, preferred_element_type=jnp.float32
    )
    return (
        query_grad.reshape(query_rows.shape),
        key_grad.reshape(key_rows.shape),
        value_grad.reshape(value_rows.shape),
    )


def local(
    inputs,
    lengths,
    gain_ffn1,
    gain_attn,
    gain_conv,
    gain_inner,
    gain_ffn2,
    gain_out,
    conv_kernel,
    ffn1_in,
    ffn1_out,
    attn_qkv,
    attn_out,
    conv_in,
    conv_out,
    ffn2_in,
    ffn2_out,
    cotangent,
):
    frame_count = inputs.shape[1]
    model_width = inputs.shape[2]
    device_count = lax.axis_size("seq")
    position_index = lax.axis_index("seq")
    seg_lengths = lengths[0]
    first_frame = position_index * frame_count
    local_frames = jnp.arange(frame_count, dtype=jnp.int32)
    positions = first_frame + local_frames
    query_segments = segment_of(positions, seg_lengths)
    cos_table, sin_table = rotary_tables(positions)
    stream = inputs[0].astype(jnp.float32)
    normed_one, saved_one = norm_forward(stream, gain_ffn1)
    normed_one_low = normed_one.astype(jnp.bfloat16)
    hidden_one, kept_ffn1_in = project(normed_one_low, ffn1_in)
    active_one = sigmoid_linear(hidden_one).astype(jnp.bfloat16)
    branch_one, kept_ffn1_out = project(active_one, ffn1_out)
    stream_one = stream + 0.5 * branch_one
    normed_two, saved_two = norm_forward(stream_one, gain_attn)
    normed_two_low = normed_two.astype(jnp.bfloat16)
    projected, kept_qkv = project(normed_two_low, attn_qkv)
    query_low = rotate(projected[:, :model_width], cos_table, sin_table).astype(jnp.bfloat16)
    key_low = rotate(projected[:, model_width : 2 * model_width], cos_table, sin_table).astype(
        jnp.bfloat16
    )
    value_low = projected[:, 2 * model_width :].astype(jnp.bfloat16)
    query_heads = split_heads(query_low)

    def stats_step(current, blocks, first_row):
        top_score, denominator = current
        key_block = blocks[0]
        key_segments = segment_of(
            first_row + jnp.arange(key_block.shape[0], dtype=jnp.int32), seg_lengths
        )
        masked = block_scores(query_heads, split_heads(key_block), query_segments, key_segments)
        new_top = jnp.maximum(top_score, jnp.max(masked, axis=-1))
        denominator = denominator * jnp.exp(top_score - new_top) + jnp.sum(
            jnp.exp(masked - new_top[:, :, None]), axis=-1
        )
        return (new_top, denominator)

    top_init = jnp.full((HEADS, frame_count), MASKED, jnp.float32)
    total_init = jnp.zeros((HEADS, frame_count), jnp.float32)
    top_score, denominator = over_blocks(
        stats_step, (top_init, total_init), (lax.all_gather(key_low, "seq", axis=0, tiled=True),)
    )
    log_total = top_score + jnp.log(denominator)

    def value_step(current, blocks, first_row):
        mixed_sum, rest_sum = current
        key_block, value_block = blocks
        key_segments = segment_of(
            first_row + jnp.arange(key_block.shape[0], dtype=jnp.int32), seg_lengths
        )
        probs = jnp.exp(
            block_scores(query_heads, split_heads(key_block), query_segments, key_segments)
            - log_total[:, :, None]
        )
        probs_high = probs.astype(jnp.bfloat16)
        probs_rest = (probs - probs_high.astype(jnp.float32)).astype(jnp.bfloat16)
        value_heads = split_heads(value_block)
        mixed_sum = mixed_sum + jnp.einsum(
            "hqk,khd->qhd", probs_high, value_heads, preferred_element_type=jnp.float32
        )
        rest_sum = rest_sum + jnp.einsum(
            "hqk,khd->qhd", probs_rest, value_heads, preferred_element_type=jnp.float32
        )
        return (mixed_sum, rest_sum)

    zero_heads = jnp.zeros((frame_count, HEADS, HEAD_DIM), jnp.float32)
    mixed_sum, rest_sum = over_blocks(
        value_step,
        (zero_heads, zero_heads),
        (
            lax.all_gather(key_low, "seq", axis=0, tiled=True),
            lax.all_gather(value_low, "seq", axis=0, tiled=True),
        ),
    )
    exact_sum = mixed_sum + rest_sum
    mixed_low = mixed_sum.reshape(frame_count, model_width).astype(jnp.bfloat16)
    branch_two, kept_attn_out = project(mixed_low, attn_out)
    stream_two = stream_one + branch_two
    normed_three, saved_three = norm_forward(stream_two, gain_conv)
    normed_three_low = normed_three.astype(jnp.bfloat16)
    gate_up, kept_conv_in = project(normed_three_low, conv_in)
    first_part = gate_up[:, :model_width]
    gate_sigma = jax.nn.sigmoid(gate_up[:, model_width:])
    glu_low = (first_part * gate_sigma).astype(jnp.bfloat16)
    padded = with_halo(glu_low, (("seq", 0),), HALF).astype(jnp.float32)
    padded_segments = segment_of(
        first_frame - HALF + jnp.arange(frame_count + 2 * HALF, dtype=jnp.int32), seg_lengths
    )
    kernel_taps = conv_kernel.astype(jnp.float32)
    conv_values = jnp.zeros((frame_count, model_width), jnp.float32)
    for offset in range(KERNEL):
        same_segment = (padded_segments[offset : offset + frame_count] == query_segments).astype(
            jnp.float32
        )
        conv_values = (
            conv_values
            + kernel_taps[offset] * padded[offset : offset + frame_count] * same_segment[:, None]
        )
    normed_four, saved_four = norm_forward(conv_values, gain_inner)
    active_four = sigmoid_linear(normed_four).astype(jnp.bfloat16)
    branch_three, kept_conv_out = project(active_four, conv_out)
    stream_three = stream_two + branch_three
    normed_five, saved_five = norm_forward(stream_three, gain_ffn2)
    normed_five_low = normed_five.astype(jnp.bfloat16)
    hidden_two, kept_ffn2_in = project(normed_five_low, ffn2_in)
    active_two = sigmoid_linear(hidden_two).astype(jnp.bfloat16)
    branch_four, kept_ffn2_out = project(active_two, ffn2_out)
    stream_four = stream_three + 0.5 * branch_four
    final_norm, saved_six = norm_forward(stream_four, gain_out)
    output = final_norm.astype(jnp.bfloat16)[None]
    grad_four, grad_gain_six = norm_backward(cotangent[0].astype(jnp.float32), gain_out, saved_six)
    out_two_low = (0.5 * grad_four).astype(jnp.bfloat16)
    grad_ffn_two_out = weight_grad(active_two, out_two_low)
    hidden_two_low = (project_back(out_two_low, ffn2_out) * sigmoid_linear_grad(hidden_two)).astype(
        jnp.bfloat16
    )
    grad_ffn_two_in = weight_grad(normed_five_low, hidden_two_low)
    input_part, grad_gain_five = norm_backward(
        project_back(hidden_two_low, ffn2_in), gain_ffn2, saved_five
    )
    grad_three = grad_four + input_part
    conv_out_low = grad_three.astype(jnp.bfloat16)
    grad_conv_weight_out = weight_grad(active_four, conv_out_low)
    active_grad = project_back(conv_out_low, conv_out) * sigmoid_linear_grad(normed_four)
    conv_grad, grad_gain_four = norm_backward(active_grad, gain_inner, saved_four)
    conv_grad_low = conv_grad.astype(jnp.bfloat16)
    conv_grad_value = conv_grad_low.astype(jnp.float32)
    rim_grad = with_halo(conv_grad_low, (("seq", 0),), HALF).astype(jnp.float32)
    tap_grads = []
    glu_grad = jnp.zeros((frame_count, model_width), jnp.float32)
    for offset in range(KERNEL):
        same_segment = (padded_segments[offset : offset + frame_count] == query_segments).astype(
            jnp.float32
        )
        tap_grads.append(
            jnp.sum(
                padded[offset : offset + frame_count] * same_segment[:, None] * conv_grad_value,
                axis=0,
            )
        )
        back_start = 2 * HALF - offset
        back_segment = (
            padded_segments[back_start : back_start + frame_count] == query_segments
        ).astype(jnp.float32)
        glu_grad = (
            glu_grad
            + kernel_taps[offset]
            * rim_grad[back_start : back_start + frame_count]
            * back_segment[:, None]
        )
    kernel_grad = jnp.stack(tap_grads, axis=0)
    gate_up_low = jnp.concatenate(
        [glu_grad * gate_sigma, glu_grad * first_part * gate_sigma * (1.0 - gate_sigma)], axis=1
    ).astype(jnp.bfloat16)
    grad_conv_weight_in = weight_grad(normed_three_low, gate_up_low)
    input_part, grad_gain_three = norm_backward(
        project_back(gate_up_low, conv_in), gain_conv, saved_three
    )
    grad_two = grad_three + input_part
    attn_grad_low = grad_two.astype(jnp.bfloat16)
    grad_attn_weight = weight_grad(mixed_low, attn_grad_low)
    mixed_grad_low = project_back(attn_grad_low, attn_out).astype(jnp.bfloat16)
    delta = jnp.transpose(
        jnp.sum(split_heads(mixed_grad_low).astype(jnp.float32) * exact_sum, axis=-1)
    )

    def key_turn(turn_index, current):
        key_rows, value_rows, key_acc, value_acc, query_acc = current
        owner = (position_index - turn_index) % device_count
        key_segments = segment_of(owner * frame_count + local_frames, seg_lengths)
        query_part, key_part, value_part = pair_grads(
            query_low,
            mixed_grad_low,
            log_total,
            delta,
            query_segments,
            key_rows,
            value_rows,
            key_segments,
        )
        key_rows, value_rows = shifted((key_rows, value_rows), "seq", 1)
        key_acc, value_acc = (
            shifted((key_acc + key_part).astype(jnp.bfloat16), "seq", 1).astype(jnp.float32),
            shifted((value_acc + value_part).astype(jnp.bfloat16), "seq", 1).astype(jnp.float32),
        )
        return (key_rows, value_rows, key_acc, value_acc, query_acc + query_part)

    zero_rows = jnp.zeros((frame_count, model_width), jnp.float32)
    unused_keys, unused_values, key_grad, value_grad, query_grad = lax.fori_loop(
        0, device_count, key_turn, (key_low, value_low, zero_rows, zero_rows, zero_rows)
    )
    projected_grad_low = jnp.concatenate(
        [
            unrotate(query_grad, cos_table, sin_table),
            unrotate(key_grad, cos_table, sin_table),
            value_grad,
        ],
        axis=1,
    ).astype(jnp.bfloat16)
    grad_qkv_weight = weight_grad(normed_two_low, projected_grad_low)
    input_part, grad_gain_two = norm_backward(
        project_back(projected_grad_low, attn_qkv), gain_attn, saved_two
    )
    grad_one = grad_two + input_part
    out_one_low = (0.5 * grad_one).astype(jnp.bfloat16)
    grad_ffn_one_out = weight_grad(active_one, out_one_low)
    hidden_one_low = (project_back(out_one_low, ffn1_out) * sigmoid_linear_grad(hidden_one)).astype(
        jnp.bfloat16
    )
    grad_ffn_one_in = weight_grad(normed_one_low, hidden_one_low)
    input_part, grad_gain_one = norm_backward(
        project_back(hidden_one_low, ffn1_in), gain_ffn1, saved_one
    )
    input_grad = (grad_one + input_part)[None]
    small_grads = lax.psum(
        (
            grad_gain_one,
            grad_gain_two,
            grad_gain_three,
            grad_gain_four,
            grad_gain_five,
            grad_gain_six,
            kernel_grad,
        ),
        ("seq", "row"),
    )
    large_grads = (
        grad_ffn_one_in,
        grad_ffn_one_out,
        grad_qkv_weight,
        grad_attn_weight,
        grad_conv_weight_in,
        grad_conv_weight_out,
        grad_ffn_two_in,
        grad_ffn_two_out,
    )
    large_grads = (
        lax.psum(grad_ffn_one_in.astype(jnp.bfloat16), "row").astype(jnp.float32),
        lax.psum(grad_ffn_one_out.astype(jnp.bfloat16), "row").astype(jnp.float32),
        lax.psum(grad_qkv_weight.astype(jnp.bfloat16), "row").astype(jnp.float32),
        lax.psum(grad_attn_weight.astype(jnp.bfloat16), "row").astype(jnp.float32),
        lax.psum(grad_conv_weight_in.astype(jnp.bfloat16), "row").astype(jnp.float32),
        lax.psum(grad_conv_weight_out.astype(jnp.bfloat16), "row").astype(jnp.float32),
        lax.psum(grad_ffn_two_in.astype(jnp.bfloat16), "row").astype(jnp.float32),
        lax.psum(grad_ffn_two_out.astype(jnp.bfloat16), "row").astype(jnp.float32),
    )
    return (
        output,
        input_grad,
        small_grads[0],
        small_grads[1],
        small_grads[2],
        small_grads[3],
        small_grads[4],
        small_grads[5],
        small_grads[6],
        large_grads[0],
        large_grads[1],
        large_grads[2],
        large_grads[3],
        large_grads[4],
        large_grads[5],
        large_grads[6],
        large_grads[7],
    )


BF16 = jnp.bfloat16
F32 = jnp.float32
PLANES = 4
VMEM = pltpu.VMEM
DMA = pltpu.SemaphoreType.DMA
VMEM_LIMIT = 60 * 1024 * 1024
FORWARD_PARTS = 1
BACKWARD_PARTS = 1


class Place:
    def __init__(self, parts):
        self.parts = Parts(parts)
        seq = lax.axis_index("seq")
        self.x = lax.axis_index("row")
        self.z = seq // 4
        self.yc = lax.rem(seq, 4)
        self.core = lax.rem(self.yc, 2)
        inside = lax.rem(self.z + self.z // 2, 2)
        self.end, self.middle = inside == 0, inside == 1
        self.beside, self.across, self.opposite = self.line(1 - inside), self.line(2), self.line(3)

    def flip(self, k):
        y, c, x = self.yc // 2, lax.rem(self.yc, 2), self.x
        c = 1 - c if k & 1 else c
        y = 1 - y if k & 2 else y
        x = 1 - x if k & 4 else x
        return x, y * 2 + c

    def dev(self, k):
        x, yc = self.flip(k)
        return {"seq": self.z * 4 + yc, "row": x}

    def slot(self, k):
        x, yc = self.flip(k)
        return x * 4 + yc

    def zdev(self, k):
        return self.at(lax.rem(self.z + k, PLANES))

    def at(self, plane, yc=None):
        return {"seq": plane * 4 + (self.yc if yc is None else yc), "row": self.x}

    def line(self, index):
        return index + self.z // 2 * (3 - 2 * index)

    def pair(self, x=None, yc=None):
        x = self.x if x is None else x
        yc = self.yc if yc is None else yc
        return (x * 2 + lax.rem(yc, 2)) * 2 + yc // 2

    def enter(self):
        barrier = pltpu.get_barrier_semaphore()
        partners = [self.dev(k) for k in range(1, 8)]
        for k in range(1, PLANES):
            plane = lax.rem(self.z + k, PLANES)
            partners += [self.at(plane), self.at(plane, self.flip(1)[1])]
        for partner in partners:
            pl.semaphore_signal(barrier, inc=1, device_id=partner)
        pl.semaphore_wait(barrier, len(partners))


def remote(src, dst, send_sem, recv_sem, dev):
    return pltpu.make_async_remote_copy(src, dst, send_sem, recv_sem, device_id=dev)


def dot(left, right, left_dim=1, right_dim=0):
    return lax.dot_general(
        left, right, (((left_dim,), (right_dim,)), ((), ())), preferred_element_type=F32
    )


PAIRS = (((0, 1),), ((2, 4), (3, 5)), ((6, 7),))
OUT_PAIRS = ((7, 3), (5, 1), (6, 2), (4, 0))


class Parts:
    def __init__(self, count):
        self.count = count
        self.rows = 128 // count

    def __iter__(self):
        return iter(range(self.count))

    def of(self, part):
        return slice(part * self.rows, part * self.rows + self.rows)

    def take(self, ref, slots, part):
        return jnp.concatenate([ref[slot, self.of(part), :] for slot in slots], axis=0)

    def put(self, ref, slots, part, value):
        for index, slot in enumerate(slots):
            ref[slot, self.of(part), :] = value[index * self.rows : index * self.rows + self.rows]


class Gather:
    def __init__(self, place, blocks, sems):
        self.place, self.blocks = place, blocks
        self.send, self.recv = sems
        self.rows = place.parts.rows
        self.sent = []

    def at(self, slot, part, half=None):
        count = self.rows if half is None else self.rows // 2
        first = part * self.rows + (half or 0) * count
        return self.blocks.at[slot, pl.ds(first, count)]

    def copy(self, rows, to, part, sem):
        sem = part * 11 + sem
        return remote(rows, rows, self.send.at[sem], self.recv.at[sem], self.place.dev(to))

    def hand(self, rows, to, part, sem):
        copy = self.copy(rows, to, part, sem)
        copy.start()
        self.sent.append(copy)

    def push(self, part, value):
        own = self.place.slot(0)
        self.blocks[own, self.place.parts.of(part), :] = value
        for half in range(2):
            self.hand(self.at(own, part, 1 - half), 4, part, 4 + 5 * (half == 1))
            self.hand(self.at(own, part, half), 2, part, 2 + 8 * (half == 1))
        self.hand(self.at(own, part), 1, part, 1)

    def arrive(self, rows, part, sem):
        self.copy(rows, 1, part, sem).wait_recv()

    def fetch(self, ks, part):
        slots = {k: self.place.slot(k) for k in ks}
        if 2 in slots:
            self.arrive(self.at(slots[2], part, 0), part, 2)
            self.hand(self.at(slots[2], part, 0), 4, part, 6)
            self.arrive(self.at(slots[4], part, 1), part, 4)
            self.hand(self.at(slots[4], part, 1), 2, part, 8)
            self.arrive(self.at(slots[2], part, 1), part, 10)
            self.hand(self.at(slots[2], part), 1, part, 3)
            self.arrive(self.at(slots[4], part, 0), part, 9)
            self.hand(self.at(slots[4], part), 1, part, 5)
        if 6 in slots:
            self.arrive(self.at(slots[6], part, 0), part, 6)
            self.arrive(self.at(slots[6], part, 1), part, 8)
            self.hand(self.at(slots[6], part), 1, part, 7)
        for k in ks:
            if k % 2:
                self.arrive(self.at(slots[k], part), part, k)
        return slots

    def drain(self):
        for copy in self.sent:
            copy.wait_send()


class Scatter:
    def __init__(self, place, buffers, sems):
        self.place = place
        self.part, self.staged, self.sibling, self.reduced, self.received, self.relayed = buffers
        self.relays = False
        self.send, self.recv = sems
        self.sent = []

    @staticmethod
    def scratch(parts, rows, width):
        return [
            VMEM((parts, 4, rows, width), F32),
            VMEM((parts, 4, rows, width), BF16),
            VMEM((parts, 4, rows, width), BF16),
            VMEM((parts, 3, rows, width), BF16),
            VMEM((parts, 3, rows, width), BF16),
            VMEM((parts, 2, rows // 2, width), BF16),
        ]

    def copy(self, src, dst, part, sem, k):
        sem = part * 11 + sem
        return remote(src, dst, self.send.at[sem], self.recv.at[sem], self.place.dev(k))

    def push(self, *what):
        copy = self.copy(*what)
        copy.start()
        self.sent.append(copy)

    def emit(self, k, part, value):
        index = k // 2
        if k % 2:
            self.staged[part, index] = value.astype(BF16)
            self.push(
                self.staged.at[part, index], self.sibling.at[part, index], part, index, 1
            )
        else:
            self.part[part, index] = value

    def emit_pair(self, pair, part, value):
        rows = value.shape[0] // len(pair)
        for index, k in enumerate(pair):
            self.emit(k, part, value[index * rows : index * rows + rows])

    def of_chip(self, index, part):
        into = self.sibling.at[part, index]
        self.copy(into, into, part, index, 1).wait_recv()
        return self.part[part, index] + self.sibling[part, index].astype(F32)

    def finish_all(self, part):
        self.relays = True
        count = self.relayed.shape[2]
        halves = (pl.ds(0, count), pl.ds(count, count))
        self.reduced[part, 2] = self.of_chip(3, part).astype(BF16)
        for half, k in ((0, 4), (1, 2)):
            self.push(
                self.reduced.at[part, 2, halves[half]], self.relayed.at[part, half], part, 7 + half, k
            )
        sums = [self.of_chip(1, part), self.of_chip(2, part)]

        def send(index, half, value, sem):
            self.reduced[part, index, halves[half], :] = value.astype(BF16)
            self.push(
                self.reduced.at[part, index, halves[half]],
                self.received.at[part, index, halves[half]],
                part,
                sem,
                2 + 2 * index,
            )

        send(0, 1, sums[0][count:], 4)
        send(1, 0, sums[1][:count], 5)
        self.part[part, 0] = self.of_chip(0, part)
        for index, rows in ((0, slice(0, count)), (1, slice(count, 2 * count))):
            into = self.relayed.at[part, index]
            self.copy(into, into, part, 7 + index, 1).wait_recv()
            send(index, index, sums[index][rows] + self.relayed[part, index].astype(F32), 9 + index)

    def finish(self, k, part):
        index = k // 2
        total = self.of_chip(index, part)
        if k:
            self.reduced[part, index - 1] = total.astype(BF16)
            self.push(
                self.reduced.at[part, index - 1],
                self.received.at[part, index - 1],
                part,
                3 + index,
                k,
            )
        else:
            self.part[part, 0] = total

    def total(self, part):
        value = self.part[part, 0]
        if self.relays:
            count = self.relayed.shape[2]
            for index in range(2):
                for half in range(2):
                    into = self.received.at[part, index, pl.ds(half * count, count)]
                    sem = 9 + index if half == index else 4 + index
                    self.copy(into, into, part, sem, 1).wait_recv()
                value = value + self.received[part, index].astype(F32)
            return value
        for index in range(3):
            into = self.received.at[part, index]
            self.copy(into, into, part, 4 + index, 1).wait_recv()
            value = value + self.received[part, index].astype(F32)
        return value

    def drain(self):
        for copy in self.sent:
            copy.wait_send()


def gather_blocks(place, gather, process, scatter=None):
    for part in place.parts:
        for group in PAIRS:
            slots = gather.fetch([k for pair in group for k in pair], part)
            for pair in group:
                process(pair, [slots[k] for k in pair], part)
            if scatter and group == PAIRS[1]:
                scatter.finish(2, part)
                scatter.finish(4, part)
        if scatter:
            scatter.finish(6, part)
            scatter.finish(0, part)


def scatter_blocks(place, scatter, rows, weight, side=0):
    for part in place.parts:
        for pair in OUT_PAIRS:
            slots = [place.slot(k) for k in pair]
            scatter.emit_pair(pair, part, dot(rows(slots, part), flat(weight), 1, side))
        scatter.finish_all(part)


def carry(place, scatter, gather, step):
    for part in place.parts:
        gather.push(part, step(part, scatter.total(part)))
    scatter.drain()


class Refs:
    pass


def kernel_call(body, collective, ins, outs, scratch):
    in_names = list(ins)
    out_names = list(outs)
    scratch_names = list(scratch)
    flat_scratch = []
    counts = []
    for name in scratch_names:
        item = scratch[name]
        counts.append(len(item) if isinstance(item, list) else 0)
        flat_scratch += item if isinstance(item, list) else [item]

    def kernel(*refs):
        held = Refs()
        at = 0
        for name in in_names + out_names:
            setattr(held, name, refs[at])
            at += 1
        for name, count in zip(scratch_names, counts):
            setattr(held, name, refs[at : at + count] if count else refs[at])
            at += max(count, 1)
        body(held)

    results = pl.pallas_call(
        kernel,
        out_shape=[jax.ShapeDtypeStruct(shape, dtype) for shape, dtype, unused in outs.values()],
        in_specs=[pl.BlockSpec(memory_space=space) for unused, space in ins.values()],
        out_specs=[pl.BlockSpec(memory_space=space) for unused, unused_type, space in outs.values()],
        scratch_shapes=flat_scratch,
        compiler_params=pltpu.CompilerParams(
            collective_id=collective, has_side_effects=True, vmem_limit_bytes=VMEM_LIMIT
        ),
    )(*[array for array, unused in ins.values()])
    return dict(zip(out_names, results))


class AlongZ:
    def __init__(self, place, sems, block):
        self.place = place
        self.send, self.recv = sems
        self.block = block
        self.sent = []

    def copy(self, source, owner, plane, sem):
        into = self.block(owner)
        return remote(
            source, into, self.send.at[sem], self.recv.at[owner], self.place.at(plane)
        )

    def arrive(self, owner):
        self.copy(self.block(owner), owner, owner, 0).wait_recv()

    def start(self, source):
        place = self.place
        self.sent = [
            self.copy(source, place.z, place.across, 0),
            self.copy(source, place.z, place.beside, 1),
        ]
        self.last = [
            self.copy(source, place.z, place.opposite, 2),
            self.copy(self.block(place.opposite), place.opposite, place.line(0), 3),
        ]
        for copy in self.sent:
            copy.start()

        @pl.when(place.middle)
        def start():
            self.last[0].start()

    def relay(self):
        @pl.when(self.place.middle)
        def hand_on():
            self.arrive(self.place.opposite)
            self.last[1].start()

    def finish(self):
        place = self.place
        self.arrive(place.beside)
        self.arrive(place.across)

        @pl.when(place.end)
        def last():
            self.arrive(place.opposite)

        for copy in self.sent:
            copy.wait_send()

        @pl.when(place.middle)
        def drain():
            for copy in self.last:
                copy.wait_send()


class GatherRows:
    def __init__(self, place, src, dst, sems, pieces):
        self.place, self.dst = place, dst
        self.send, self.recv, self.local = sems[:3]
        self.along = AlongZ(place, sems[3:], lambda plane: dst.at[pl.ds(plane * 4, 4)])
        mine = place.z * 4 + place.yc
        for k in (0, 2, 3, 1):
            x, to = place.flip(k)
            for index, column in enumerate(pieces(place, to)):
                source = src.at[:, pl.ds(pl.multiple_of(column * 128, 128), 128)]
                into = dst.at[mine, :, pl.ds(index * 128, 128)]
                if k:
                    remote(source, into, self.send.at[k], self.recv.at[k], place.dev(k)).start()
                else:
                    pltpu.make_async_copy(source, into, self.local).start()

    def along_z(self):
        place = self.place
        mine = self.dst.at[place.z * 4 + place.yc]
        pltpu.make_async_copy(mine, mine, self.local).wait()
        for k in (2, 3, 1):
            into = self.dst.at[place.z * 4 + place.flip(k)[1]]
            remote(into, into, self.send.at[k], self.recv.at[k], place.dev(k)).wait_recv()
        self.along.start(self.dst.at[pl.ds(place.z * 4, 4)])

    def relay(self):
        self.along.relay()

    def finish(self):
        place = self.place
        self.along.finish()
        mine = self.dst.at[place.z * 4 + place.yc]
        for k in (2, 3, 1):
            remote(mine, mine, self.send.at[k], self.recv.at[k], place.dev(k)).wait_send()

    @staticmethod
    def scratch():
        return [DMA((4,)), DMA((4,)), DMA, DMA((4,)), DMA((PLANES,))]


def ffn_pieces(place, yc):
    return [(plane * 4 + yc) * 2 + place.x for plane in range(PLANES)]


def head_pieces(place, yc):
    return [kind * 8 + place.pair(None, yc) for kind in range(3)]


def channel_pieces(place, yc):
    return [kind * 8 + place.pair(None, yc) for kind in range(2)]


class GatherBlocks:
    def __init__(self, place, src, dst, sems, columns=slice(0, 1024)):
        columns = pl.ds(columns.start, columns.stop - columns.start)
        src = src.at[pl.ds(place.x * 128, 128), columns]
        self.along = AlongZ(place, sems[1:], lambda plane: dst.at[plane, :, columns])
        self.own = pltpu.make_async_copy(src, dst.at[place.z, :, columns], sems[0])
        self.own.start()
        self.along.start(src)

    def relay(self):
        self.along.relay()

    def finish(self):
        self.own.wait()
        self.along.finish()

    @staticmethod
    def scratch():
        return [DMA, DMA((4,)), DMA((PLANES,))]


class PlaneSum:
    def __init__(self, place, refs):
        self.place = place
        self.own, self.staged, self.received, self.relayed, self.send, self.recv = refs

    @staticmethod
    def scratch(rows, width):
        return [
            VMEM((rows, width), F32),
            VMEM((3, rows, width), BF16),
            VMEM((3, rows, width), BF16),
            VMEM((rows, width), BF16),
            DMA((4,)),
            DMA((4,)),
        ]

    def term_copy(self, index, plane):
        slot = lax.rem(plane + 3 - self.place.z, PLANES)
        return remote(
            self.staged.at[index],
            self.received.at[slot],
            self.send.at[index],
            self.recv.at[slot],
            self.place.at(plane),
        )

    def relay_copy(self):
        return remote(
            self.staged.at[0],
            self.relayed,
            self.send.at[3],
            self.recv.at[3],
            self.place.at(self.place.beside),
        )

    def first(self, term):
        self.staged[0] = term(self.place.opposite).astype(BF16)

        @pl.when(self.place.end)
        def start():
            self.relay_copy().start()

    def rest(self, term):
        place = self.place
        self.staged[1] = term(place.across).astype(BF16)
        self.term_copy(1, place.across).start()
        self.staged[2] = term(place.beside).astype(BF16)
        self.term_copy(2, place.beside).start()
        self.own[...] = term(place.z)

    def relay(self):
        @pl.when(self.place.middle)
        def add():
            self.relay_copy().wait_recv()
            self.staged[0] = (
                self.staged[0].astype(F32) + self.relayed[...].astype(F32)
            ).astype(BF16)
            self.term_copy(0, self.place.opposite).start()

    def arrive(self, plane):
        slot = lax.rem(self.place.z + 3 - plane, PLANES)
        into = self.received.at[slot]
        remote(
            into, into, self.send.at[0], self.recv.at[slot], self.place.at(plane)
        ).wait_recv()

    def total(self):
        place = self.place
        self.arrive(place.beside)
        self.arrive(place.across)

        @pl.when(place.middle)
        def last():
            self.arrive(place.opposite)
            self.term_copy(0, place.opposite).wait_send()

        @pl.when(place.end)
        def nothing():
            self.received[lax.rem(place.z + 3 - place.opposite, PLANES)] = jnp.zeros(
                self.received.shape[1:], BF16
            )
            self.relay_copy().wait_send()

        self.term_copy(1, place.across).wait_send()
        self.term_copy(2, place.beside).wait_send()
        value = self.own[...]
        for index in range(3):
            value = value + self.received[index].astype(F32)
        return value


class Exchange:
    def __init__(self, place, blocks, sems, partners=tuple(range(1, 8)), slot=None):
        self.place = place
        self.blocks = blocks
        self.send, self.recv = sems
        self.partners = partners
        self.slot = slot or place.slot
        self.sent = []

    def start(self, source):
        own = self.slot(0)
        for k in self.partners:
            copy = remote(
                source(k), self.blocks.at[own], self.send.at[k], self.recv.at[k], self.place.dev(k)
            )
            copy.start()
            self.sent.append(copy)

    def wait(self):
        for k in self.partners:
            into = self.blocks.at[self.slot(k)]
            remote(into, into, self.send.at[k], self.recv.at[k], self.place.dev(k)).wait_recv()
        for copy in self.sent:
            copy.wait_send()


def flat(ref):
    value = ref[...]
    return value.reshape(value.shape[0] * value.shape[1], value.shape[2])


def ffn_forward(place, gather, hidden, w_in, w_out, scatter, ready):
    def process(pair, slots, part):
        if part == 0 and pair[0] == 0:
            ready()
        value = dot(place.parts.take(gather.blocks, slots, part), flat(w_in))
        place.parts.put(hidden, slots, part, value)
        scatter.emit_pair(pair, part, dot(sigmoid_linear(value).astype(BF16), flat(w_out)))

    gather_blocks(place, gather, process, scatter)


def ffn_backward(place, gather, hidden, hidden_grads, active, w_in, w_out, scatter, ready):
    def process(pair, slots, part):
        if part == 0 and pair[0] == 0:
            ready()
        value = place.parts.take(hidden, slots, part)
        sigma = jax.nn.sigmoid(value)
        place.parts.put(active, slots, part, (value * sigma).astype(BF16))
        back = dot(place.parts.take(gather.blocks, slots, part), flat(w_out), 1, 1)
        low = (back * (sigma * (1.0 + value * (1.0 - sigma)))).astype(BF16)
        place.parts.put(hidden_grads, slots, part, low)
        scatter.emit_pair(pair, part, dot(low, flat(w_in), 1, 1))

    gather_blocks(place, gather, process, scatter)


def token_dot(left, columns, right):
    count, rows, unused = left.shape
    taken = left[:, :, columns].reshape(count * rows, -1)
    return dot(taken, flat(right), 0, 0)


def columns_of(plane, width):
    return pl.ds(pl.multiple_of(plane * width, width), width)


class WeightGrads:
    def __init__(self, place, refs, name, sums, wide):
        self.place = place
        self.sum_in = PlaneSum(place, getattr(refs, sums + "_sum_in"))
        self.total_in = getattr(refs, name + "_total_in")
        self.share_in = Exchange(
            place, getattr(refs, name + "_grad_in"), getattr(refs, name + "_share_in")
        )
        self.wide = wide
        if wide:
            self.sum_out = PlaneSum(place, getattr(refs, sums + "_sum_out"))
            self.share_out = Exchange(
                place,
                getattr(refs, name + "_grad_out"),
                getattr(refs, name + "_share_out"),
                (4,),
                lambda k: place.flip(k)[0],
            )
        else:
            self.sum_out = HalfSum(
                place, getattr(refs, sums + "_sum_out"), getattr(refs, name + "_grad_out")
            )

    def put_out(self, active, grads):
        self.sum_out.put(dot(flat(active), flat(grads), 0, 0))

    def put_in(self, blocks, grads):
        def term(plane):
            return token_dot(blocks, columns_of(plane, 256), grads)

        self.sum_in.first(term)
        self.sum_in.rest(term)

    def put_both(self, active, grads, blocks, hidden_grads):
        def out(plane):
            return token_dot(active, columns_of(plane, 128), grads)

        def into(plane):
            return token_dot(blocks, columns_of(plane, 256), hidden_grads)

        self.sum_out.first(out)
        self.sum_in.first(into)
        self.sum_out.rest(out)
        self.sum_in.rest(into)

    def relay(self):
        self.sum_out.relay()
        self.sum_in.relay()

    def share(self):
        if self.wide:
            self.share_out.blocks[self.place.x] = self.sum_out.total().astype(BF16)
            self.share_out.start(lambda k: self.share_out.blocks.at[self.place.x])
        else:
            self.sum_out.add()
        self.total_in[...] = self.sum_in.total().astype(BF16).reshape(self.total_in.shape)
        self.share_in.blocks[self.place.slot(0)] = self.total_in[self.place.yc]
        self.share_in.start(lambda k: self.total_in.at[self.place.flip(k)[1]])

    def wait(self):
        (self.share_out if self.wide else self.sum_out).wait()
        self.share_in.wait()

    @staticmethod
    def sums(name, width, wide):
        return {
            name + "_sum_in": PlaneSum.scratch(256, width),
            name + "_sum_out": PlaneSum.scratch(128, 1024) if wide else HalfSum.scratch(1024),
        }

    @staticmethod
    def scratch(name, width, wide):
        held = {
            name + "_total_in": VMEM((4, 64, width), BF16),
            name + "_share_in": [DMA((8,)), DMA((8,))],
        }
        if wide:
            held[name + "_share_out"] = [DMA((8,)), DMA((8,))]
        return held

    @staticmethod
    def outs(name, width, wide):
        return {
            name + "_grad_in": ((8, 64, width), BF16, VMEM),
            name + "_grad_out": ((2, 128, 1024) if wide else (64, 1024), BF16, VMEM),
        }


AG_SEMS = [DMA((22,)), DMA((22,))]


def norm_rows(values, gain):
    normed, saved = norm_forward(values, gain)
    return normed.astype(BF16), saved


def norm_input_grad(grads, gain, saved):
    unit_part, inverse = saved
    scaled = grads * gain
    gain_grad = jnp.sum(grads * unit_part, axis=0, keepdims=True)
    input_part = inverse * (
        scaled
        - jnp.mean(scaled, axis=-1, keepdims=True)
        - unit_part * jnp.mean(scaled * unit_part, axis=-1, keepdims=True)
    )
    return input_part, gain_grad


class GatherHalf:
    def __init__(self, place, src, dst, sems):
        self.place, self.dst = place, dst
        self.send, self.recv, self.local = sems
        self.source = place.z // 2 == place.x
        self.first, self.last = 2 - place.x, 3 - 3 * place.x
        target = place.yc // 2 * 2 + lax.rem(place.z, 2)
        self.same = lax.rem(place.z, 2) == place.core
        self.own = pltpu.make_async_copy(src, dst.at[place.core], self.local)

        def copy(sem, plane):
            return remote(
                src,
                dst.at[place.core],
                self.send.at[sem],
                self.recv.at[place.core],
                place.at(plane, target),
            )

        self.far, self.near, self.sibling = (
            copy(0, self.first),
            copy(1, place.x * 2 + 1 - lax.rem(place.z, 2)),
            copy(2, place.z),
        )

        @pl.when(self.source)
        def start():
            self.far.start()
            self.near.start()

            @pl.when(self.same)
            def local():
                self.own.start()

            @pl.when(jnp.logical_not(self.same))
            def sibling():
                self.sibling.start()

    def on(self, half):
        rows = self.dst.at[half]
        return remote(
            rows, rows, self.send.at[half], self.recv.at[half], self.place.at(self.last)
        )

    def relay(self):
        @pl.when(self.place.z == self.first)
        def hand_on():
            for half in range(2):
                self.on(half).wait_recv()
                self.on(half).start()

    def finish(self):
        place = self.place
        at_home = place.z == place.x * 2 + place.core
        for half in range(2):
            here = jnp.logical_or(
                jnp.logical_and(at_home, place.core == half), place.z == self.first
            )

            @pl.when(jnp.logical_not(here))
            def arrive():
                self.on(half).wait_recv()

        @pl.when(self.source)
        def drain():
            self.far.wait_send()
            self.near.wait_send()

            @pl.when(self.same)
            def local():
                self.own.wait()

            @pl.when(jnp.logical_not(self.same))
            def sibling():
                self.sibling.wait_send()

        @pl.when(place.z == self.first)
        def drain_on():
            for half in range(2):
                self.on(half).wait_send()

    @staticmethod
    def scratch():
        return [DMA((3,)), DMA((2,)), DMA]


class HalfSum:
    def __init__(self, place, refs, result):
        self.place = place
        self.staged, self.received, self.relayed, self.send, self.recv, self.last = refs
        self.result = result
        self.near = place.z // 2 == place.x
        self.far_middle, self.far_end = 2 - place.x, 3 - 3 * place.x
        self.home = place.x * 2 + place.core

    @staticmethod
    def scratch(width):
        return [
            VMEM((2, 64, width), BF16),
            VMEM((3, 64, width), BF16),
            VMEM((2, 64, width), BF16),
            DMA((3,)),
            DMA((4,)),
            DMA((2,)),
        ]

    def term_copy(self, half, slot):
        place = self.place
        return remote(
            self.staged.at[half],
            self.received.at[slot],
            self.send.at[half],
            self.recv.at[slot],
            place.at(self.home, place.yc // 2 * 2 + half),
        )

    def relay_copy(self):
        return remote(
            self.staged,
            self.relayed,
            self.send.at[2],
            self.recv.at[3],
            self.place.at(self.far_middle),
        )

    def near_copies(self):
        place = self.place
        for half in range(2):
            here = jnp.logical_and(place.z == self.home, place.core == half)
            slot = lax.rem(place.z + self.home, 2)
            yield jnp.logical_and(self.near, jnp.logical_not(here)), self.term_copy(half, slot)

    def put(self, value):
        self.staged[...] = value.astype(BF16).reshape(self.staged.shape)

    def start(self):
        place = self.place

        @pl.when(place.z == self.far_end)
        def relay():
            self.relay_copy().start()

        for away, copy in self.near_copies():

            @pl.when(away)
            def start(copy=copy):
                copy.start()

    def relay(self):
        @pl.when(self.place.z == self.far_middle)
        def add():
            self.relay_copy().wait_recv()
            self.staged[...] = (
                self.staged[...].astype(F32) + self.relayed[...].astype(F32)
            ).astype(BF16)
            for half in range(2):
                self.term_copy(half, 2).start()

    def add(self):
        place = self.place
        at_home = jnp.logical_and(self.near, place.z == self.home)

        @pl.when(self.near)
        def reduce():
            @pl.when(at_home)
            def own():
                self.received[0] = self.staged[place.core]

            for slot in range(3):

                def arrive():
                    into = self.received.at[slot]
                    remote(
                        into, into, self.send.at[0], self.recv.at[slot], place.at(place.z)
                    ).wait_recv()

                if slot:
                    arrive()
                else:
                    pl.when(jnp.logical_not(at_home))(arrive)
            value = self.received[0].astype(F32)
            for slot in range(1, 3):
                value = value + self.received[slot].astype(F32)
            self.result[...] = value.astype(BF16)
            self.hand_over().start()

        for away, copy in self.near_copies():

            @pl.when(away)
            def drain(copy=copy):
                copy.wait_send()

        @pl.when(place.z == self.far_middle)
        def drain_sums():
            for half in range(2):
                self.term_copy(half, 2).wait_send()

        @pl.when(place.z == self.far_end)
        def drain_relay():
            self.relay_copy().wait_send()

    def hand_over(self):
        return remote(
            self.result, self.result, self.last.at[0], self.last.at[1], self.place.dev(4)
        )

    def wait(self):
        @pl.when(self.near)
        def sent():
            self.hand_over().wait_send()

        @pl.when(jnp.logical_not(self.near))
        def arrived():
            self.hand_over().wait_recv()


class Turn:
    def __init__(self, place, refs):
        self.place = place
        self.staged, self.received, self.send, self.recv = refs

    @staticmethod
    def scratch(rows):
        return [VMEM((PLANES, rows, 128), BF16), VMEM((PLANES, rows, 128), BF16), DMA((4,)), DMA((4,))]

    def copy(self, k):
        place = self.place
        return remote(
            self.staged.at[lax.rem(place.z + k, PLANES)],
            self.received.at[place.z],
            self.send.at[k],
            self.recv.at[k],
            place.zdev(k),
        )

    def start(self):
        for k in (2, 1, 3):
            self.copy(k).start()
        self.keep()

    def keep(self):
        self.received[self.place.z] = self.staged[self.place.z]

    def wait(self):
        for k in (1, 2, 3):
            into = self.received.at[lax.rem(self.place.z + 4 - k, PLANES)]
            remote(into, into, self.send.at[k], self.recv.at[k], self.place.zdev(k)).wait_recv()
        for k in (1, 2, 3):
            self.copy(k).wait_send()


def swap_halves(values):
    lane = lax.broadcasted_iota(jnp.int32, values.shape, 1)
    return jnp.where(lane % 64 < 32, pltpu.roll(values, 96, 1), pltpu.roll(values, 32, 1))


def head_part(values, head):
    return values[:, head * 64 : head * 64 + 64]


def pack_wide(turn, pair, left, right):
    row, head = divmod(pair, 2)
    for block in range(4):
        turn.staged[pair, block * 128 : block * 128 + 128, :] = jnp.concatenate(
            [head_part(left[row * 4 + block], head), head_part(right[row * 4 + block], head)], axis=1
        )


def pack_narrow(turn, pair, values):
    row, head = divmod(pair, 2)
    for block in range(2):
        turn.staged[pair, block * 128 : block * 128 + 128, :] = jnp.concatenate(
            [
                head_part(values[row * 4 + block], head),
                head_part(values[row * 4 + block + 2], head),
            ],
            axis=1,
        )


def unpack_narrow(turn, row, block):
    rows = slice((block % 2) * 128, (block % 2) * 128 + 128)
    return jnp.concatenate(
        [head_part(turn.received[row * 2 + head, rows, :], block // 2) for head in range(2)], axis=1
    )


def unpack_wide(turn, row, block, side):
    rows = slice(block * 128, block * 128 + 128)
    return jnp.concatenate(
        [head_part(turn.received[row * 2 + head, rows, :], side) for head in range(2)], axis=1
    )


QUERY_BLOCK = 256


def segment_ends(refs, row):
    lengths = refs.row_lengths[row]
    ends = [lengths[0:1, 0:1]]
    for index in range(1, 4):
        ends.append(ends[-1] + lengths[0:1, index : index + 1])
    return ends


def segment_features(refs, plane, row):
    frame = (plane * 512 + lax.broadcasted_iota(jnp.int32, (512, 64), 0)).astype(F32)
    lane = lax.broadcasted_iota(jnp.int32, (512, 64), 1).astype(F32)
    segment = jnp.zeros((512, 64), F32)
    for end in segment_ends(refs, row)[:3]:
        segment = segment + jnp.where(frame >= end, 1.0, 0.0)
    other = jnp.where(lane < 4.0, -MASKED, 0.0)
    return (
        jnp.where(lane == segment, 0.0, other).astype(BF16),
        jnp.where(lane == segment, -1.0, 0.0).astype(BF16),
    )


def segment_reach(place, refs, slot):
    row, block = slot // 4, slot % 4
    frame = place.z * 512 + block * 128 + lax.broadcasted_iota(jnp.int32, (128, 128), 0)
    frame = frame.astype(F32)
    ends = segment_ends(refs, row)
    first, last = jnp.zeros((128, 128), F32), ends[3]
    for end in ends[:3]:
        first = jnp.where(frame >= end, end, first)
    for end in ends[2::-1]:
        last = jnp.where(frame < end, end, last)
    return first - frame, last - frame


def open_heads(place, refs, turn_qk, turn_v):
    for plane in range(PLANES):
        seg_query, seg_key = segment_features(refs, plane, place.z // 2)
        rows = slice(plane * 512, plane * 512 + 512)
        pair = turn_qk.received[plane]
        scaled = (pair[:, :64].astype(F32) * HEAD_DIM ** (-0.5)).astype(BF16)
        refs.queries[rows, :] = jnp.concatenate([scaled, seg_query], axis=1)
        refs.keys[rows, :] = jnp.concatenate([pair[:, 64:], seg_key], axis=1)
        both = turn_v.received[plane]
        turned = jnp.transpose(both.astype(F32)).astype(BF16)
        refs.values[plane * 512 : plane * 512 + 256, :] = both[:, :64]
        refs.values[plane * 512 + 256 : plane * 512 + 512, :] = both[:, 64:]
        refs.values_t[:, plane * 512 : plane * 512 + 256] = turned[:64]
        refs.values_t[:, plane * 512 + 256 : plane * 512 + 512] = turned[64:]


def attend(place, refs, turn_mix):
    def plane_step(step, unused):
        k = lax.rem(step + 1, PLANES)
        plane = lax.rem(place.z + k, PLANES)
        parts = []
        for half in range(2):
            first = plane * 512 + half * 256
            query = refs.queries[pl.ds(pl.multiple_of(first, 256), QUERY_BLOCK), :]
            scores = dot(refs.keys[...], query, 1, 1)
            top = jnp.max(scores, axis=0, keepdims=True)
            weights = jnp.exp(scores - top)
            total = jnp.sum(weights, axis=0, keepdims=True)
            low = (weights * (1.0 / total)).astype(BF16)
            parts.append(jnp.transpose(dot(refs.values_t[...], low)))
            refs.log_total[plane * 2 + half] = jnp.broadcast_to(top + jnp.log(total), (8, 256))
        turn_mix.staged[plane] = jnp.concatenate(parts, axis=1).astype(BF16)

        @pl.when(step < PLANES - 1)
        def send():
            turn_mix.copy(k).start()

        return unused

    lax.fori_loop(0, PLANES, plane_step, 0)


def attention_forward(place, refs, gather, scatter):
    def process(pair, slots, part):
        if part == 0 and pair[0] == 0:
            refs.finish_qkv()
        value = dot(place.parts.take(gather.blocks, slots, part), flat(refs.w_qkv))

        def frames_of(slot, part):
            count = place.parts.rows
            first = lax.rem(slot, 4) * 128 + part * count
            return pl.ds(pl.multiple_of(first, count), count)

        def table(ref):
            return jnp.concatenate(
                [
                    ref[frames_of(slot, part), :]
                    for slot in slots
                ],
                axis=0,
            )

        cos, sin = table(refs.cos), table(refs.sin)
        query, key = value[:, :128], value[:, 128:256]
        place.parts.put(refs.q_rows, slots, part, (query * cos + swap_halves(query) * sin).astype(BF16))
        place.parts.put(refs.k_rows, slots, part, (key * cos + swap_halves(key) * sin).astype(BF16))
        place.parts.put(refs.v_rows, slots, part, value[:, 256:].astype(BF16))

    gather_blocks(place, gather, process)
    turn_qk, turn_v = Turn(place, refs.turn_qk), Turn(place, refs.turn_v)
    for pair in range(PLANES):
        pack_wide(turn_qk, pair, refs.q_rows, refs.k_rows)
        pack_narrow(turn_v, pair, refs.v_rows)
    turn_qk.start()
    turn_v.start()
    gather.drain()
    turn_qk.wait()
    turn_v.wait()
    refs.after_turn()
    open_heads(place, refs, turn_qk, turn_v)
    turn_mix = Turn(place, refs.turn_mix)
    attend(place, refs, turn_mix)
    turn_mix.keep()
    turn_mix.wait()
    refs.after_mix()
    for slot in range(8):
        refs.mixed[slot] = unpack_narrow(turn_mix, slot // 4, slot % 4)
    scatter_blocks(
        place, scatter, lambda slots, part: place.parts.take(refs.mixed, slots, part), refs.w_o
    )


def attention_kept():
    return dict(
        attn_blocks=((8, 128, 1024), BF16),
        w_qkv=((16, 64, 384), BF16),
        w_o=((2, 64, 1024), BF16),
        queries=((2048, 128), BF16),
        keys=((2048, 128), BF16),
        values=((2048, 64), BF16),
        log_total=((8, 8, 256), F32),
        mixed=((8, 128, 128), BF16),
    )


def attend_back(place, refs, turn_kv, turn_q):
    refs.key_grad[...] = jnp.zeros_like(refs.key_grad)
    refs.value_grad[...] = jnp.zeros_like(refs.value_grad)

    def plane_step(step, unused):
        k = lax.rem(step + 1, PLANES)
        plane = lax.rem(place.z + k, PLANES)
        parts = []
        for half in range(2):
            first = pl.multiple_of(plane * 512 + half * 256, 256)
            query = refs.queries[pl.ds(first, QUERY_BLOCK), :]
            grad = refs.mix_grads[pl.ds(first, QUERY_BLOCK), :]
            log_total = refs.log_total[plane * 2 + half][:1]
            probs = jnp.exp(dot(refs.keys[...], query, 1, 1) - log_total)
            prob_grads = dot(refs.values[...], grad, 1, 1)
            delta = jnp.sum(probs * prob_grads, axis=0, keepdims=True)
            low = (probs * (prob_grads - delta)).astype(BF16)
            refs.key_grad[...] += dot(low, query[:, :64])
            refs.value_grad[...] += dot(probs.astype(BF16), grad)
            parts.append(jnp.transpose(dot(refs.keys_t[...], low)) * HEAD_DIM ** (-0.5))
        turn_q.staged[plane] = jnp.concatenate(parts, axis=1).astype(BF16)

        @pl.when(step < PLANES - 1)
        def send():
            turn_q.copy(k).start()

        return unused

    lax.fori_loop(0, PLANES, plane_step, 0)
    turn_q.keep()
    for plane in range(PLANES):
        rows = slice(plane * 512, plane * 512 + 512)
        turn_kv.staged[plane] = jnp.concatenate(
            [refs.key_grad[rows, :], refs.value_grad[rows, :]], axis=1
        ).astype(BF16)


def attention_backward(place, refs, gather, scatter):
    def process(pair, slots, part):
        if part == 0 and pair[0] == 0:
            refs.finish_attn()
        rows = dot(place.parts.take(gather.blocks, slots, part), flat(refs.w_o), 1, 1)
        place.parts.put(refs.mix_rows, slots, part, rows.astype(BF16))

    gather_blocks(place, gather, process)
    turn_mix = Turn(place, refs.turn_mix)
    for pair in range(PLANES):
        pack_narrow(turn_mix, pair, refs.mix_rows)
    turn_mix.start()
    gather.drain()
    weights = WeightGrads(place, refs, "qkv", "qkv", False)
    weights.put_out(refs.mixed, gather.blocks)
    turned = jnp.transpose(refs.keys[...].astype(F32))
    refs.keys_t[...] = turned[:64].astype(BF16)
    refs.before_mix()
    turn_mix.wait()
    for plane in range(PLANES):
        both = turn_mix.received[plane]
        refs.mix_grads[plane * 512 : plane * 512 + 256, :] = both[:, :64]
        refs.mix_grads[plane * 512 + 256 : plane * 512 + 512, :] = both[:, 64:]
    weights.sum_out.start()
    refs.before_attend()
    turn_kv, turn_q = Turn(place, refs.turn_qk), Turn(place, refs.turn_v)
    attend_back(place, refs, turn_kv, turn_q)
    turn_kv.start()
    weights.sum_out.relay()
    refs.after_attend()
    turn_q.wait()
    turn_kv.wait()
    for slot in range(8):
        row, block = divmod(slot, 4)
        cos = refs.cos[block * 128 : block * 128 + 128, :]
        sin = refs.sin[block * 128 : block * 128 + 128, :]
        query = unpack_narrow(turn_q, row, block).astype(F32)
        key = unpack_wide(turn_kv, row, block, 0).astype(F32)
        refs.qkv_grads[slot] = jnp.concatenate(
            [
                (query * cos - swap_halves(query) * sin).astype(BF16),
                (key * cos - swap_halves(key) * sin).astype(BF16),
                unpack_wide(turn_kv, row, block, 1),
            ],
            axis=1,
        )
    scatter_blocks(
        place, scatter, lambda slots, part: place.parts.take(refs.qkv_grads, slots, part), refs.w_qkv, 1
    )
    return weights


def fill_tables(refs):
    cos, sin = refs.cos_rows[...], refs.sin_rows[...]
    refs.cos[...] = jnp.concatenate([cos] * 4, axis=1)
    refs.sin[...] = jnp.concatenate([-sin, sin] * 2, axis=1)


def fill_channels(place, refs):
    columns = columns_of(place.pair(), 128)
    refs.taps[0:KERNEL, :] = refs.all_taps[:, columns].astype(F32)
    refs.gain_inner[...] = refs.all_inner[:, columns]
    for slot in range(8):
        refs.before[slot], refs.after[slot] = segment_reach(place, refs, slot)


def table_scratch():
    return dict(
        cos=VMEM((512, 128), F32),
        sin=VMEM((512, 128), F32),
        taps=VMEM((32, 128), F32),
        gain_inner=VMEM((1, 128), F32),
        before=VMEM((8, 128, 128), F32),
        after=VMEM((8, 128, 128), F32),
    )


class Edges:
    def __init__(self, place, refs):
        self.place = place
        self.staged, self.received, self.send, self.recv = refs

    @staticmethod
    def scratch():
        return [VMEM((2, 2, 16, 128), BF16), VMEM((2, 2, 16, 128), BF16), DMA((2,)), DMA((2,))]

    def copies(self):
        place = self.place
        for side, inside, step in ((0, place.z < PLANES - 1, 1), (1, place.z > 0, -1)):
            plane = jnp.clip(place.z + step, 0, PLANES - 1)
            yield (
                side,
                inside,
                remote(
                    self.staged.at[side],
                    self.received.at[side],
                    self.send.at[side],
                    self.recv.at[side],
                    {"seq": plane * 4 + place.yc, "row": place.x},
                ),
            )

    def start(self, blocks):
        for row in range(2):
            self.staged[0, row] = blocks[row * 4 + 3, 112:128, :]
            self.staged[1, row] = blocks[row * 4, 0:16, :]
        for side, inside, copy in self.copies():

            @pl.when(inside)
            def start(copy=copy):
                copy.start()

    def wait(self, blocks, padded):
        for slot in range(8):
            row, block = divmod(slot, 4)
            padded[slot, 16:144, :] = blocks[slot].astype(F32)
            if block > 0:
                padded[slot, 0:16, :] = blocks[slot - 1, 112:128, :].astype(F32)
            if block < 3:
                padded[slot, 144:160, :] = blocks[slot + 1, 0:16, :].astype(F32)
        place = self.place
        for side, outside in ((0, place.z == 0), (1, place.z == PLANES - 1)):
            first, rows = ((0, slice(0, 16)), (3, slice(144, 160)))[side]
            into = self.received.at[side]

            @pl.when(outside)
            def nothing():
                for row in range(2):
                    padded[row * 4 + first, rows, :] = jnp.zeros((16, 128), F32)

            @pl.when(jnp.logical_not(outside))
            def arrive():
                remote(
                    into, into, self.send.at[side], self.recv.at[side], place.zdev(1)
                ).wait_recv()
                for row in range(2):
                    padded[row * 4 + first, rows, :] = self.received[side, row].astype(F32)

        for side, inside, copy in self.copies():

            @pl.when(inside)
            def drain(copy=copy):
                copy.wait_send()


def lane_is(index, rows=128):
    return lax.broadcasted_iota(jnp.int32, (rows, 128), 1) == index


def put_columns(tile, slot, first, second):
    return jnp.where(lane_is(slot), first, jnp.where(lane_is(slot + 8), second, tile))


def share_columns(place, refs, tile):
    share = Exchange(place, refs[0], refs[1:])
    own = place.slot(0)
    share.blocks[own] = jnp.transpose(tile)[:16]
    share.start(lambda k: share.blocks.at[own])
    return share


def back_to_columns(first, second):
    rows = jnp.concatenate([first, second, jnp.zeros((112, 128), F32)], axis=0)
    return jnp.transpose(rows)


def column(tile, slot):
    return jnp.sum(jnp.where(lane_is(slot, tile.shape[0]), tile, 0.0), axis=1, keepdims=True)


def kept_frames(value, offset, before, after):
    if offset < 0:
        return jnp.where(before <= offset, value, 0.0)
    if offset > 0:
        return jnp.where(after > offset, value, 0.0)
    return value


CHUNK = 64


def convolve(refs):
    taps = [refs.taps[j : j + 1, :] for j in range(KERNEL)]

    def step(slot, tile):
        for first in range(0, 128, CHUNK):
            rows = slice(first, first + CHUNK)
            before, after = refs.before[slot, rows, :], refs.after[slot, rows, :]
            total = jnp.zeros((CHUNK, 128), F32)
            for j in range(KERNEL):
                start = first + j + 1
                value = refs.glu_padded[slot, start : start + CHUNK, :]
                total = total + taps[j] * kept_frames(value, j - HALF, before, after)
            refs.conv[slot, rows, :] = total
        value = refs.conv[slot]
        mean = jnp.mean(value, axis=1, keepdims=True)
        center = value - mean
        return put_columns(tile, slot, mean, jnp.sum(center * center, axis=1, keepdims=True))

    return lax.fori_loop(0, 8, step, jnp.zeros((128, 128), F32))


def inner_norm(refs, slot, rows=slice(0, 128)):
    tile = refs.inner_stats[rows, :]
    mean, inverse = column(tile, slot), column(tile, slot + 8)
    return (refs.conv[slot, rows, :] - mean) * inverse, inverse


def conv_forward(place, refs, gather, scatter):
    def process(pair, slots, part):
        if part == 0 and pair[0] == 0:
            refs.finish_ci()
        value = dot(place.parts.take(gather.blocks, slots, part), flat(refs.w_ci))
        place.parts.put(refs.gate_up, slots, part, value)
        place.parts.put(
            refs.glu,
            slots,
            part,
            (value[:, :128] * jax.nn.sigmoid(value[:, 128:])).astype(BF16),
        )

    gather_blocks(place, gather, process)
    edges = Edges(place, refs.edges)
    edges.start(refs.glu)
    gather.drain()
    edges.wait(refs.glu, refs.glu_padded)
    share = share_columns(place, refs.stats, convolve(refs))
    refs.conv_middle()
    share.wait()
    stats = share.blocks[...]
    means, spreads = stats[:, :8], stats[:, 8:]
    mean = jnp.mean(means, axis=0)
    spread = jnp.sum(spreads + 128.0 * jnp.square(means - mean[None]), axis=0) / 1024.0
    refs.inner_stats[...] = back_to_columns(mean, lax.rsqrt(spread + EPSILON))
    refs.finish_co()

    def active_rows(slots, part):
        rows = place.parts.of(part)
        parts = []
        for slot in slots:
            unit_part, unused = inner_norm(refs, slot, rows)
            parts.append(sigmoid_linear(unit_part * refs.gain_inner[...]).astype(BF16))
        value = jnp.concatenate(parts, axis=0)
        place.parts.put(refs.conv_active, slots, part, value)
        return value

    scatter_blocks(place, scatter, active_rows, refs.w_co)


def conv_kept():
    return dict(
        conv_blocks=((8, 128, 1024), BF16),
        w_ci=((16, 64, 256), BF16),
        w_co=((2, 64, 1024), BF16),
        gate_up=((8, 128, 256), F32),
        glu_padded=((8, 160, 128), F32),
        conv=((8, 128, 128), F32),
        inner_stats=((128, 128), F32),
        conv_active=((8, 128, 128), BF16),
    )


STATS = [VMEM((8, 16, 128), F32), DMA((8,)), DMA((8,))]


def convolve_back(refs):
    taps = [refs.taps[j : j + 1, :] for j in range(KERNEL)]
    refs.tap_sums[...] = jnp.zeros_like(refs.tap_sums)

    def step(slot, unused):
        for first in range(0, 128, CHUNK):
            rows = slice(first, first + CHUNK)
            before, after = refs.before[slot, rows, :], refs.after[slot, rows, :]
            total = jnp.zeros((CHUNK, 128), F32)
            grad = refs.conv_grad_padded[slot, first + 16 : first + 16 + CHUNK, :]
            for j in range(KERNEL):
                offset = j - HALF
                start = first + 16 - offset
                value = refs.conv_grad_padded[slot, start : start + CHUNK, :]
                total = total + taps[j] * kept_frames(value, -offset, before, after)
                start = first + 16 + offset
                value = refs.glu_padded[slot, start : start + CHUNK, :]
                product = kept_frames(value * grad, offset, before, after)
                refs.tap_sums[j] += jnp.sum(product.reshape(CHUNK // 8, 8, 128), axis=0)
            refs.glu_grad[slot, rows, :] = total
        return unused

    lax.fori_loop(0, 8, step, 0)
    return jnp.sum(refs.tap_sums[...], axis=1)


def conv_backward(place, refs, gather, scatter):
    gain = refs.gain_inner[...]

    def process(pair, slots, part):
        if part == 0 and pair[0] == 0:
            refs.finish_conv()
        back = dot(place.parts.take(gather.blocks, slots, part), flat(refs.w_co), 1, 1)
        rows = place.parts.of(part)
        units = jnp.concatenate([inner_norm(refs, slot, rows)[0] for slot in slots], axis=0)
        place.parts.put(refs.inner_grad, slots, part, back * sigmoid_linear_grad(units * gain))

    gather_blocks(place, gather, process)

    def sums(slot, current):
        tile, gain_grad = current
        value = refs.inner_grad[slot]
        unit_part, unused = inner_norm(refs, slot)
        scaled = value * gain
        tile = put_columns(
            tile,
            slot,
            jnp.sum(scaled, axis=1, keepdims=True),
            jnp.sum(scaled * unit_part, axis=1, keepdims=True),
        )
        return tile, gain_grad + jnp.sum(value * unit_part, axis=0, keepdims=True)

    tile, inner_gain_grad = lax.fori_loop(
        0, 8, sums, (jnp.zeros((128, 128), F32), jnp.zeros((1, 128), F32))
    )
    share = share_columns(place, refs.stats, tile)
    weights = WeightGrads(place, refs, "conv", "conv", False)
    weights.put_out(refs.conv_active, gather.blocks)
    gather.drain()
    share.wait()
    means = jnp.sum(share.blocks[...], axis=0) / 1024.0
    refs.grad_stats[...] = back_to_columns(means[:8], means[8:])

    def input_grad(slot, unused):
        unit_part, inverse = inner_norm(refs, slot)
        tile = refs.grad_stats[...]
        refs.conv_grad[slot] = (
            inverse
            * (
                refs.inner_grad[slot] * gain
                - column(tile, slot)
                - unit_part * column(tile, slot + 8)
            )
        ).astype(BF16)
        return unused

    lax.fori_loop(0, 8, input_grad, 0)
    edges = Edges(place, refs.edges)
    edges.start(refs.conv_grad)
    refs.conv_begin()
    edges.wait(refs.conv_grad, refs.conv_grad_padded)
    weights.sum_out.start()
    tap_grads = convolve_back(refs)
    refs.conv_middle()

    def gate_rows(slots, part):
        value, glu_grad = place.parts.take(refs.gate_up, slots, part), place.parts.take(refs.glu_grad, slots, part)
        sigma = jax.nn.sigmoid(value[:, 128:])
        low = jnp.concatenate(
            [glu_grad * sigma, glu_grad * value[:, :128] * sigma * (1.0 - sigma)], axis=1
        ).astype(BF16)
        place.parts.put(refs.gate_grads, slots, part, low)
        return low

    scatter_blocks(place, scatter, gate_rows, refs.w_ci, 1)
    return inner_gain_grad, tap_grads, weights


class Traffic:
    def __init__(self, refs, sems):
        self.refs, self.sems = refs, sems
        self.count = 0

    def start(self, pairs):
        copies = []
        for source, target in pairs:
            copy = pltpu.make_async_copy(source, target, self.sems.at[self.count])
            copy.start()
            copies.append(copy)
            self.count += 1

        def finish():
            for copy in copies:
                copy.wait()

        return finish

    def save(self, names):
        return self.start(
            [(getattr(self.refs, name), getattr(self.refs, "keep_" + name)) for name in names]
        )

    def load(self, names):
        return self.start(
            [(getattr(self.refs, "keep_" + name), getattr(self.refs, name)) for name in names]
        )


def ffn_kept():
    return dict(
        blocks=((8, 128, 1024), BF16),
        hidden=((8, 128, 512), F32),
        w_in=((16, 64, 512), BF16),
        w_out=((4, 128, 1024), BF16),
    )


SCATTER_SEMS = [DMA((22,)), DMA((22,))]


def forward_body(refs):
    place = Place(FORWARD_PARTS)
    place.enter()
    traffic = Traffic(refs, refs.traffic)
    gather_in = GatherRows(place, refs.w_in_rows, refs.w_in, refs.gather_in, ffn_pieces)
    refs.row_lengths[place.x] = refs.own_lengths[...]
    lengths = remote(
        refs.own_lengths,
        refs.row_lengths.at[place.x],
        refs.length_sems.at[0],
        refs.length_sems.at[1],
        place.dev(4),
    )
    lengths.start()
    halves = (slice(0, 512), slice(512, 1024))
    gather_out = [
        GatherBlocks(place, refs.w_out_rows, refs.w_out, refs.gather_out, halves[0])
    ]
    gather = Gather(place, refs.blocks, refs.ffn_ag)
    for part in place.parts:
        frames = place.parts.of(part)
        gather.push(part, norm_rows(refs.stream[frames, :].astype(F32), refs.gain_ffn1[...])[0])
    gather_in.along_z()
    gather_out.append(
        GatherBlocks(place, refs.w_out_rows, refs.w_out, refs.gather_out_last, halves[1])
    )
    gather_qkv = GatherRows(place, refs.qkv_rows, refs.w_qkv, refs.gather_qkv, head_pieces)
    lengths.wait()
    fill_tables(refs)
    fill_channels(place, refs)
    held = Refs()
    gather_blocks(place, gather, lambda pair, slots, part: None)
    gather_out[0].relay()
    gather_in.relay()
    gather_in.finish()
    for part in place.parts:
        for group in PAIRS:
            for pair in group:
                slots = [place.slot(k) for k in pair]
                value = dot(place.parts.take(refs.blocks, slots, part), flat(refs.w_in))
                place.parts.put(refs.hidden, slots, part, value)
                place.parts.put(refs.active, slots, part, sigmoid_linear(value).astype(BF16))
    gather.drain()
    scatter = Scatter(place, refs.scatter_columns, refs.ffn_scatter)
    for half, columns in enumerate(halves):
        if half:
            gather_out[half].relay()
        gather_out[half].finish()
        if half:
            gather_qkv.along_z()
            gather_o = GatherHalf(place, refs.o_rows, refs.w_o, refs.gather_o)
        weight = refs.w_out[:, :, columns].reshape(512, 512)
        for pair in OUT_PAIRS:
            rows = jnp.concatenate([refs.active[place.slot(k)] for k in pair], axis=0)
            scatter.emit_pair(pair, half, dot(rows, weight))
        for k in (2, 4, 6, 0):
            scatter.finish(k, half)
    saved = [traffic.save(ffn_kept())]
    gather_ci = GatherRows(place, refs.ci_rows, refs.w_ci, refs.gather_ci, channel_pieces)
    gather_next = GatherRows(place, refs.next_in_rows, refs.next_in, refs.gather_next, ffn_pieces)

    def to_attention(part, total):
        frames = place.parts.of(part)
        value = refs.stream[frames, :].astype(F32) + 0.5 * total
        refs.stream_one[frames, :] = value
        return norm_rows(value, refs.gain_attn[...])[0]

    def to_conv(part, total):
        frames = place.parts.of(part)
        value = refs.stream_one[frames, :] + total
        refs.stream_two[frames, :] = value
        return norm_rows(value, refs.gain_conv[...])[0]

    gather = Gather(place, refs.attn_blocks, refs.attn_ag)
    total = jnp.concatenate([scatter.total(half) for half in range(2)], axis=1)
    for part in place.parts:
        gather.push(part, to_attention(part, total[place.parts.of(part)]))
    scatter.drain()
    gather_qkv.relay()
    gather_o.relay()

    def after_turn():
        gather_ci.along_z()
        held.co = GatherHalf(place, refs.co_rows, refs.w_co, refs.gather_co)

    def after_mix():
        gather_ci.relay()
        held.co.relay()
        gather_o.finish()
        gather_next.along_z()
        held.next_out = GatherBlocks(
            place, refs.next_out_rows, refs.next_out, refs.gather_next_out
        )

    def conv_middle():
        gather_next.relay()

    refs.after_turn, refs.after_mix, refs.conv_middle = after_turn, after_mix, conv_middle
    refs.finish_qkv, refs.finish_ci, refs.finish_co = (
        gather_qkv.finish,
        gather_ci.finish,
        lambda: held.co.finish(),
    )
    scatter = Scatter(place, refs.scatter, refs.attn_scatter)
    attention_forward(place, refs, gather, scatter)
    saved.append(traffic.save(attention_kept()))
    gather = Gather(place, refs.conv_blocks, refs.conv_ag)
    carry(place, scatter, gather, to_conv)
    scatter = Scatter(place, refs.scatter, refs.conv_scatter)
    conv_forward(place, refs, gather, scatter)
    held.next_out.relay()
    saved.append(traffic.save(conv_kept()))
    for part in place.parts:
        frames = place.parts.of(part)
        refs.stream_three[frames, :] = refs.stream_two[frames, :] + scatter.total(part)
    scatter.drain()
    gather_next.finish()
    held.next_out.finish()
    for finish in saved:
        finish()


def scratch_of(kept):
    return {name: VMEM(shape, dtype) for name, (shape, dtype) in kept.items()}


def forward_call(ins):
    kept = {**ffn_kept(), **attention_kept(), **conv_kept()}
    outs = dict(
        stream_one=((128, 1024), F32, VMEM),
        stream_two=((128, 1024), F32, VMEM),
        stream_three=((128, 1024), F32, VMEM),
        next_in=((16, 64, 512), BF16, pl.ANY),
        next_out=((4, 128, 1024), BF16, pl.ANY),
    )
    outs["row_lengths"] = ((2, 8, 128), F32, VMEM)
    for name, (shape, dtype) in kept.items():
        outs["keep_" + name] = (shape, dtype, pl.ANY)
    scratch = dict(
        scratch_of(kept),
        active=VMEM((8, 128, 512), BF16),
        gather_in=GatherRows.scratch(),
        gather_out=GatherBlocks.scratch(),
        gather_out_last=GatherBlocks.scratch(),
        gather_qkv=GatherRows.scratch(),
        gather_o=GatherHalf.scratch(),
        gather_ci=GatherRows.scratch(),
        gather_co=GatherHalf.scratch(),
        gather_next=GatherRows.scratch(),
        gather_next_out=GatherBlocks.scratch(),
        length_sems=DMA((2,)),
        **table_scratch(),
        traffic=DMA((len(kept),)),
        scatter=Scatter.scratch(FORWARD_PARTS, 128 // FORWARD_PARTS, 1024),
        scatter_columns=Scatter.scratch(2, 128, 512),
        ffn_ag=AG_SEMS,
        attn_ag=AG_SEMS,
        conv_ag=AG_SEMS,
        ffn_scatter=SCATTER_SEMS,
        attn_scatter=SCATTER_SEMS,
        conv_scatter=SCATTER_SEMS,
        q_rows=VMEM((8, 128, 128), BF16),
        k_rows=VMEM((8, 128, 128), BF16),
        v_rows=VMEM((8, 128, 128), BF16),
        turn_qk=Turn.scratch(512),
        turn_v=Turn.scratch(256),
        turn_mix=Turn.scratch(256),
        values_t=VMEM((64, 2048), BF16),
        glu=VMEM((8, 128, 128), BF16),
        edges=Edges.scratch(),
        stats=STATS,
    )
    return kernel_call(forward_body, 1, ins, outs, scratch)


class SmallSum:
    def __init__(self, place, refs):
        self.place, self.refs = place, refs
        self.first = Exchange(place, refs.small_first, refs.small_first_sems)
        self.last = Exchange(place, refs.small, refs.small_last_sems)
        self.sent = []

    def start(self):
        refs, place = self.refs, self.place

        def part(slot):
            return refs.gain_grads.at[:, columns_of(slot, 128)]

        self.first.blocks[place.slot(0)] = refs.gain_grads[:, columns_of(place.slot(0), 128)]
        self.first.start(lambda k: part(place.slot(k)))

    def along_z(self):
        refs, place = self.refs, self.place
        self.first.wait()
        refs.small_planes[place.z, 0:8, :] = jnp.sum(self.first.blocks[...], axis=0)
        refs.small_planes[place.z, 8:48, :] = refs.channel_grads[...]
        send, recv = refs.small_z_sems
        rows = refs.small_planes.at[place.z]
        for k in (1, 2, 3):
            copy = remote(rows, rows, send.at[k], recv.at[k], place.zdev(k))
            copy.start()
            self.sent.append(copy)

    def spread(self):
        refs, place = self.refs, self.place
        send, recv = refs.small_z_sems
        for k in (1, 2, 3):
            into = refs.small_planes.at[lax.rem(place.z + 4 - k, PLANES)]
            remote(into, into, send.at[k], recv.at[k], place.zdev(k)).wait_recv()
        for copy in self.sent:
            copy.wait_send()
        own = place.slot(0)
        self.last.blocks[own] = jnp.sum(refs.small_planes[...], axis=0)
        self.last.start(lambda k: self.last.blocks.at[own])

    def wait(self):
        self.last.wait()


def backward_step(place, refs, stream, gain, row, scale):
    saved = [
        norm_forward(stream[place.parts.of(part), :].astype(F32), gain)[1] for part in place.parts
    ]

    def step(part, total):
        frames = place.parts.of(part)
        input_part, gain_grad = norm_input_grad(total, gain, saved[part])
        value = refs.grad_stream[frames, :] + input_part
        refs.grad_stream[frames, :] = value
        refs.gain_grads[row : row + 1, :] += gain_grad
        return (scale * value).astype(BF16)

    return step


def backward_body(refs):
    place = Place(BACKWARD_PARTS)
    place.enter()
    traffic = Traffic(refs, refs.traffic)
    ready = traffic.start([(refs.next_in, refs.w_in), (refs.next_out, refs.w_out)])
    gather = Gather(place, refs.blocks, refs.ffn2_ag)
    for part in place.parts:
        frames = place.parts.of(part)
        gather.push(part, norm_rows(refs.stream_three[frames, :], refs.gain_ffn2[...])[0])
    refs.finish_conv = traffic.load(conv_kept())
    refs.finish_attn = traffic.load(attention_kept())
    fill_tables(refs)
    fill_channels(place, refs)
    refs.gain_grads[...] = jnp.zeros_like(refs.gain_grads)
    refs.channel_grads[...] = jnp.zeros_like(refs.channel_grads)
    scatter = Scatter(place, refs.scatter, refs.ffn2_scatter)
    ffn_forward(place, gather, refs.hidden, refs.w_in, refs.w_out, scatter, ready)
    gather.drain()

    def turn_round(part, total):
        frames = place.parts.of(part)
        final, saved = norm_forward(refs.stream_three[frames, :] + 0.5 * total, refs.gain_out[...])
        refs.output[frames, :] = final.astype(BF16)
        grad, gain_grad = norm_input_grad(
            refs.cotangent[frames, :].astype(F32), refs.gain_out[...], saved
        )
        refs.grad_stream[frames, :] = grad
        refs.gain_grads[4:5, :] += gain_grad
        return (0.5 * grad).astype(BF16)

    gather = Gather(place, refs.grads_even, refs.ffn2_ag_back)
    carry(place, scatter, gather, turn_round)
    scatter = Scatter(place, refs.scatter, refs.ffn2_scatter_back)
    ffn_backward(
        place,
        gather,
        refs.hidden,
        refs.hidden_grads,
        refs.active,
        refs.w_in,
        refs.w_out,
        scatter,
        lambda: None,
    )
    gather.drain()
    step = backward_step(place, refs, refs.stream_three, refs.gain_ffn2[...], 3, 1.0)
    weights_two = WeightGrads(place, refs, "ffn2", "ffn", True)
    weights_two.put_both(refs.active, refs.grads_even, refs.blocks, refs.hidden_grads)
    gather = Gather(place, refs.grads_odd, refs.conv_ag)
    carry(place, scatter, gather, step)
    load_first = traffic.load(ffn_kept())
    refs.conv_begin, refs.conv_middle = weights_two.sum_out.relay, weights_two.sum_in.relay
    scatter = Scatter(place, refs.scatter, refs.conv_scatter)
    inner, taps, weights_three = conv_backward(place, refs, gather, scatter)
    step = backward_step(place, refs, refs.stream_two, refs.gain_conv[...], 2, 1.0)
    refs.channel_grads[0:32, :] = taps
    refs.channel_grads[32:33, :] = inner
    weights_three.put_in(refs.conv_blocks, refs.gate_grads)
    gather = Gather(place, refs.grads_even, refs.attn_ag)
    carry(place, scatter, gather, step)

    refs.before_mix = weights_two.share
    refs.before_attend, refs.after_attend = weights_three.relay, weights_three.share
    scatter = Scatter(place, refs.scatter, refs.attn_scatter)
    weights_four = attention_backward(place, refs, gather, scatter)
    step = backward_step(place, refs, refs.stream_one, refs.gain_attn[...], 1, 0.5)
    weights_four.put_in(refs.attn_blocks, refs.qkv_grads)
    gather = Gather(place, refs.grads_odd, refs.ffn1_ag)
    carry(place, scatter, gather, step)
    weights_two.wait()
    weights_three.wait()
    scatter = Scatter(place, refs.scatter, refs.ffn1_scatter)
    ffn_backward(
        place,
        gather,
        refs.hidden,
        refs.hidden_grads,
        refs.active,
        refs.w_in,
        refs.w_out,
        scatter,
        load_first,
    )
    gather.drain()
    weights_one = WeightGrads(place, refs, "ffn1", "ffn", True)
    weights_one.put_both(refs.active, refs.grads_odd, refs.blocks, refs.hidden_grads)
    weights_four.sum_in.relay()
    weights_four.share()
    weights_one.sum_out.relay()
    step = backward_step(place, refs, refs.stream, refs.gain_ffn1[...], 0, 1.0)
    for part in place.parts:
        step(part, scatter.total(part))
    scatter.drain()
    small = SmallSum(place, refs)
    small.start()
    weights_one.sum_in.relay()
    small.along_z()
    small.spread()
    weights_four.wait()
    weights_one.share()
    small.wait()
    weights_one.wait()


MODULES = (("ffn1", 512, True), ("qkv", 384, False), ("conv", 256, False), ("ffn2", 512, True))


def backward_call(ins):
    kept = {**ffn_kept(), **attention_kept(), **conv_kept()}
    outs = dict(
        output=((128, 1024), BF16, VMEM),
        grad_stream=((128, 1024), F32, VMEM),
        small=((8, 48, 128), F32, VMEM),
    )
    scratch = dict(
        scratch_of(kept),
        active=VMEM((8, 128, 512), BF16),
        hidden_grads=VMEM((8, 128, 512), BF16),
        grads_even=VMEM((8, 128, 1024), BF16),
        grads_odd=VMEM((8, 128, 1024), BF16),
        traffic=DMA((2 + len(kept),)),
        scatter=Scatter.scratch(BACKWARD_PARTS, 128 // BACKWARD_PARTS, 1024),
        ffn2_ag=AG_SEMS,
        ffn2_ag_back=AG_SEMS,
        conv_ag=AG_SEMS,
        attn_ag=AG_SEMS,
        ffn1_ag=AG_SEMS,
        ffn2_scatter=SCATTER_SEMS,
        ffn2_scatter_back=SCATTER_SEMS,
        conv_scatter=SCATTER_SEMS,
        attn_scatter=SCATTER_SEMS,
        ffn1_scatter=SCATTER_SEMS,
        mix_rows=VMEM((8, 128, 128), BF16),
        mix_grads=VMEM((2048, 64), BF16),
        keys_t=VMEM((64, 2048), BF16),
        turn_qk=Turn.scratch(512),
        turn_v=Turn.scratch(256),
        turn_mix=Turn.scratch(256),
        key_grad=VMEM((2048, 64), F32),
        value_grad=VMEM((2048, 64), F32),
        qkv_grads=VMEM((8, 128, 384), BF16),
        **table_scratch(),
        inner_grad=VMEM((8, 128, 128), F32),
        grad_stats=VMEM((128, 128), F32),
        conv_grad=VMEM((8, 128, 128), BF16),
        conv_grad_padded=VMEM((8, 160, 128), F32),
        glu_grad=VMEM((8, 128, 128), F32),
        gate_grads=VMEM((8, 128, 256), BF16),
        tap_sums=VMEM((32, 8, 128), F32),
        edges=Edges.scratch(),
        stats=STATS,
        gain_grads=VMEM((8, 1024), F32),
        channel_grads=VMEM((40, 128), F32),
        small_first=VMEM((8, 8, 128), F32),
        small_planes=VMEM((PLANES, 48, 128), F32),
        small_first_sems=[DMA((8,)), DMA((8,))],
        small_z_sems=[DMA((4,)), DMA((4,))],
        small_last_sems=[DMA((8,)), DMA((8,))],
        **WeightGrads.sums("ffn", 512, True),
        **WeightGrads.sums("qkv", 384, False),
        **WeightGrads.sums("conv", 256, False),
    )
    for name, width, wide in MODULES:
        outs.update(WeightGrads.outs(name, width, wide))
        scratch.update(WeightGrads.scratch(name, width, wide))
    return kernel_call(backward_body, 2, ins, outs, scratch)


def unpack_body(count, *refs):
    sources, outs = refs[:count], refs[count : 2 * count + 8]
    (
        output,
        grad_stream,
        small,
        ffn1_in,
        ffn1_out,
        qkv_in,
        qkv_out,
        conv_in,
        conv_out,
        ffn2_in,
        ffn2_out,
    ) = sources
    outs[0][...] = output[...]
    outs[1][...] = grad_stream[...]
    for slot in range(8):
        x, yc = divmod(slot, 4)
        pair = ((x * 2 + yc % 2) * 2 + yc // 2) * 128
        for index, row in enumerate((0, 1, 2, None, 3, 4)):
            if row is not None:
                outs[2 + index][:, slot * 128 : slot * 128 + 128] = small[slot, row : row + 1, :]
        outs[5][:, pair : pair + 128] = small[slot, 40:41, :]
        outs[8][:, pair : pair + 128] = small[slot, 8 : 8 + KERNEL, :]
        for source, out in ((ffn1_in, outs[9]), (ffn2_in, outs[15])):
            for plane in range(PLANES):
                column = ((plane * 4 + yc) * 2 + x) * 128
                out[:, column : column + 128] = source[
                    slot, :, plane * 128 : plane * 128 + 128
                ].astype(F32)
        for source, out, kinds in ((qkv_in, outs[11], 3), (conv_in, outs[13], 2)):
            for kind in range(kinds):
                column = kind * 1024 + pair
                out[:, column : column + 128] = source[slot, :, kind * 128 : kind * 128 + 128].astype(
                    F32
                )
    for source, out in ((ffn1_out, outs[10]), (ffn2_out, outs[16])):
        out[0:128, :] = source[0].astype(F32)
        out[128:256, :] = source[1].astype(F32)
    outs[12][...] = qkv_out[...].astype(F32)
    outs[14][...] = conv_out[...].astype(F32)


def unpack_call(backward):
    arrays = list(backward.values())
    gain = jax.ShapeDtypeStruct((1, 1024), F32)
    shapes = [
        jax.ShapeDtypeStruct((128, 1024), BF16),
        jax.ShapeDtypeStruct((128, 1024), F32),
        *[gain] * 6,
        jax.ShapeDtypeStruct((KERNEL, 1024), F32),
    ] + [
        jax.ShapeDtypeStruct(shape, F32)
        for shape in (
            (64, 4096),
            (256, 1024),
            (64, 3072),
            (64, 1024),
            (64, 2048),
            (64, 1024),
            (64, 4096),
            (256, 1024),
        )
    ]
    whole = pl.BlockSpec(memory_space=VMEM)
    return pl.pallas_call(
        functools.partial(unpack_body, len(arrays)),
        out_shape=shapes,
        in_specs=[whole] * len(arrays),
        out_specs=[whole] * len(shapes),
        compiler_params=pltpu.CompilerParams(vmem_limit_bytes=VMEM_LIMIT),
    )(*arrays)


def local_planes(
    inputs,
    lengths,
    gain_ffn1,
    gain_attn,
    gain_conv,
    gain_inner,
    gain_ffn2,
    gain_out,
    conv_kernel,
    ffn1_in,
    ffn1_out,
    attn_qkv,
    attn_out,
    conv_in,
    conv_out,
    ffn2_in,
    ffn2_out,
    cotangent,
):
    plane = lax.axis_index("seq") // 4
    cos, sin = rotary_tables(plane * 512 + jnp.arange(512, dtype=jnp.int32))
    shared = dict(
        stream=(inputs[0], VMEM),
        gain_ffn1=(gain_ffn1[None], VMEM),
        gain_attn=(gain_attn[None], VMEM),
        gain_conv=(gain_conv[None], VMEM),
        all_inner=(gain_inner[None], VMEM),
        all_taps=(conv_kernel, VMEM),
        cos_rows=(cos, VMEM),
        sin_rows=(sin, VMEM),
    )
    forward = forward_call(
        dict(
            shared,
            own_lengths=(jnp.pad(lengths.astype(F32), ((0, 7), (0, 124))), VMEM),
            w_in_rows=(ffn1_in, pl.ANY),
            w_out_rows=(ffn1_out, pl.ANY),
            qkv_rows=(attn_qkv, pl.ANY),
            o_rows=(attn_out, pl.ANY),
            ci_rows=(conv_in, pl.ANY),
            co_rows=(conv_out, pl.ANY),
            next_in_rows=(ffn2_in, pl.ANY),
            next_out_rows=(ffn2_out, pl.ANY),
        )
    )
    ins = dict(
        shared,
        cotangent=(cotangent[0], VMEM),
        gain_ffn2=(gain_ffn2[None], VMEM),
        gain_out=(gain_out[None], VMEM),
    )
    for name, array in forward.items():
        held = name.startswith("stream") or name == "row_lengths"
        ins[name] = (array, VMEM if held else pl.ANY)
    results = unpack_call(backward_call(ins))
    return (
        results[0][None],
        results[1][None],
        *[gain[0] for gain in results[2:8]],
        *results[8:],
    )


def solution(mesh):
    return jax.shard_map(
        local_planes if mesh.shape["seq"] == 16 and mesh.shape["row"] == 2 else local,
        mesh=mesh,
        in_specs=(
            P("row", "seq", None),
            P("row", None),
            P(),
            P(),
            P(),
            P(),
            P(),
            P(),
            P(),
            P("seq", None),
            P("seq", None),
            P("seq", None),
            P("seq", None),
            P("seq", None),
            P("seq", None),
            P("seq", None),
            P("seq", None),
            P("row", "seq", None),
        ),
        out_specs=(
            P("row", "seq", None),
            P("row", "seq", None),
            P(),
            P(),
            P(),
            P(),
            P(),
            P(),
            P(),
            P("seq", None),
            P("seq", None),
            P("seq", None),
            P("seq", None),
            P("seq", None),
            P("seq", None),
            P("seq", None),
            P("seq", None),
        ),
        check_vma=False,
    )
```

```python
import functools
import math

import jax
import jax.numpy as jnp
from jax import lax
from jax.experimental import pallas as pl
from jax.experimental.pallas import tpu as pltpu
from jax.sharding import PartitionSpec as P

HEADS = 16
HEAD_DIM = 64
KERNEL = 31
HALF = 15


EPSILON = 1e-05
MASKED = -1e30


def with_halo(block, sides, width):
    for axis, dim in sides:
        count = lax.axis_size(axis)
        forward = [(i, i + 1) for i in range(count - 1)]
        backward = [(target, source) for source, target in forward]
        low = lax.ppermute(
            lax.slice_in_dim(block, block.shape[dim] - width, None, axis=dim), axis, forward
        )
        high = lax.ppermute(lax.slice_in_dim(block, 0, width, axis=dim), axis, backward)
        block = jnp.concatenate([low, block, high], axis=dim)
    return block


def shifted(array, axis, by):
    size = lax.axis_size(axis)
    return lax.ppermute(array, axis, [(i, (i + by) % size) for i in range(size)])


def segment_of(positions, seg_lengths):
    boundary = jnp.cumsum(seg_lengths)[:-1]
    return jnp.sum((positions[:, None] >= boundary[None, :]).astype(jnp.int32), axis=1)


def rotary_tables(positions):
    half_dim = HEAD_DIM // 2
    inverse = jnp.exp(-jnp.log(10000.0) * jnp.arange(half_dim, dtype=jnp.float32) / half_dim)
    angles = positions.astype(jnp.float32)[:, None] * inverse[None, :]
    return (jnp.cos(angles), jnp.sin(angles))


def split_heads(values):
    return values.reshape(values.shape[0], HEADS, HEAD_DIM)


def rotate(values, cos_table, sin_table):
    half_dim = HEAD_DIM // 2
    shaped = split_heads(values)
    first_half = shaped[..., :half_dim]
    second_half = shaped[..., half_dim:]
    cos_heads = cos_table[:, None, :]
    sin_heads = sin_table[:, None, :]
    turned = jnp.concatenate(
        [
            first_half * cos_heads - second_half * sin_heads,
            second_half * cos_heads + first_half * sin_heads,
        ],
        axis=-1,
    )
    return turned.reshape(values.shape)


def unrotate(grads, cos_table, sin_table):
    half_dim = HEAD_DIM // 2
    shaped = split_heads(grads)
    first_half = shaped[..., :half_dim]
    second_half = shaped[..., half_dim:]
    cos_heads = cos_table[:, None, :]
    sin_heads = sin_table[:, None, :]
    turned = jnp.concatenate(
        [
            first_half * cos_heads + second_half * sin_heads,
            second_half * cos_heads - first_half * sin_heads,
        ],
        axis=-1,
    )
    return turned.reshape(grads.shape)


def norm_forward(values, gain):
    center = values - jnp.mean(values, axis=-1, keepdims=True)
    spread = jnp.mean(center * center, axis=-1, keepdims=True)
    inverse = lax.rsqrt(spread + EPSILON)
    unit_part = center * inverse
    return (unit_part * gain, (unit_part, inverse))


def norm_backward(grads, gain, saved):
    unit_part, inverse = saved
    scaled = grads * gain
    gain_grad = jnp.sum(grads * unit_part, axis=0)
    input_part = inverse * (
        scaled
        - jnp.mean(scaled, axis=-1, keepdims=True)
        - unit_part * jnp.mean(scaled * unit_part, axis=-1, keepdims=True)
    )
    return (input_part, gain_grad)


def sigmoid_linear(values):
    return values * jax.nn.sigmoid(values)


def sigmoid_linear_grad(values):
    sigma = jax.nn.sigmoid(values)
    return sigma * (1.0 + values * (1.0 - sigma))


def project(left_side, weight):
    return (
        jnp.dot(
            left_side,
            lax.all_gather(weight, "seq", axis=0, tiled=True),
            preferred_element_type=jnp.float32,
        ),
        weight,
    )


def project_back(grad_side, weight):
    return lax.dot_general(
        grad_side,
        lax.all_gather(weight, "seq", axis=0, tiled=True),
        (((1,), (1,)), ((), ())),
        preferred_element_type=jnp.float32,
    )


def weight_grad(left_side, grad_side):
    return lax.psum_scatter(
        lax.dot_general(
            left_side, grad_side, (((0,), (0,)), ((), ())), preferred_element_type=jnp.float32
        ).astype(jnp.bfloat16),
        "seq",
        scatter_dimension=0,
        tiled=True,
    ).astype(jnp.float32)


def over_blocks(advance, running, pieces):
    total_rows = pieces[0].shape[0]
    block_size = math.gcd(total_rows, 512)
    number = total_rows // block_size
    stacked = tuple((piece.reshape((number, block_size) + piece.shape[1:]) for piece in pieces))

    def scan_step(current, block_item):
        block_index, blocks = block_item
        return (advance(current, blocks, block_index * block_size), None)

    running, unused = lax.scan(scan_step, running, (jnp.arange(number, dtype=jnp.int32), stacked))
    return running


def block_scores(query_heads, key_heads, query_segments, key_segments):
    scale = HEAD_DIM ** (-0.5)
    raw_scores = (
        jnp.einsum("qhd,khd->hqk", query_heads, key_heads, preferred_element_type=jnp.float32)
        * scale
    )
    return jnp.where((query_segments[:, None] == key_segments[None, :])[None], raw_scores, MASKED)


def pair_grads(
    query_rows, grad_rows, log_total, delta, query_segments, key_rows, value_rows, key_segments
):
    scale = HEAD_DIM ** (-0.5)
    query_heads = split_heads(query_rows)
    grad_heads = split_heads(grad_rows)
    key_heads = split_heads(key_rows)
    value_heads = split_heads(value_rows)
    probs = jnp.exp(
        block_scores(query_heads, key_heads, query_segments, key_segments) - log_total[:, :, None]
    )
    prob_grads = jnp.einsum(
        "qhd,khd->hqk", grad_heads, value_heads, preferred_element_type=jnp.float32
    )
    score_grads = (probs * (prob_grads - delta[:, :, None])).astype(jnp.bfloat16)
    query_grad = (
        jnp.einsum("hqk,khd->qhd", score_grads, key_heads, preferred_element_type=jnp.float32)
        * scale
    )
    key_grad = (
        jnp.einsum("hqk,qhd->khd", score_grads, query_heads, preferred_element_type=jnp.float32)
        * scale
    )
    value_grad = jnp.einsum(
        "hqk,qhd->khd", probs.astype(jnp.bfloat16), grad_heads, preferred_element_type=jnp.float32
    )
    return (
        query_grad.reshape(query_rows.shape),
        key_grad.reshape(key_rows.shape),
        value_grad.reshape(value_rows.shape),
    )


def local(
    inputs,
    lengths,
    gain_ffn1,
    gain_attn,
    gain_conv,
    gain_inner,
    gain_ffn2,
    gain_out,
    conv_kernel,
    ffn1_in,
    ffn1_out,
    attn_qkv,
    attn_out,
    conv_in,
    conv_out,
    ffn2_in,
    ffn2_out,
    cotangent,
):
    frame_count = inputs.shape[1]
    model_width = inputs.shape[2]
    device_count = lax.axis_size("seq")
    position_index = lax.axis_index("seq")
    seg_lengths = lengths[0]
    first_frame = position_index * frame_count
    local_frames = jnp.arange(frame_count, dtype=jnp.int32)
    positions = first_frame + local_frames
    query_segments = segment_of(positions, seg_lengths)
    cos_table, sin_table = rotary_tables(positions)
    stream = inputs[0].astype(jnp.float32)
    normed_one, saved_one = norm_forward(stream, gain_ffn1)
    normed_one_low = normed_one.astype(jnp.bfloat16)
    hidden_one, kept_ffn1_in = project(normed_one_low, ffn1_in)
    active_one = sigmoid_linear(hidden_one).astype(jnp.bfloat16)
    branch_one, kept_ffn1_out = project(active_one, ffn1_out)
    stream_one = stream + 0.5 * branch_one
    normed_two, saved_two = norm_forward(stream_one, gain_attn)
    normed_two_low = normed_two.astype(jnp.bfloat16)
    projected, kept_qkv = project(normed_two_low, attn_qkv)
    query_low = rotate(projected[:, :model_width], cos_table, sin_table).astype(jnp.bfloat16)
    key_low = rotate(projected[:, model_width : 2 * model_width], cos_table, sin_table).astype(
        jnp.bfloat16
    )
    value_low = projected[:, 2 * model_width :].astype(jnp.bfloat16)
    query_heads = split_heads(query_low)

    def stats_step(current, blocks, first_row):
        top_score, denominator = current
        key_block = blocks[0]
        key_segments = segment_of(
            first_row + jnp.arange(key_block.shape[0], dtype=jnp.int32), seg_lengths
        )
        masked = block_scores(query_heads, split_heads(key_block), query_segments, key_segments)
        new_top = jnp.maximum(top_score, jnp.max(masked, axis=-1))
        denominator = denominator * jnp.exp(top_score - new_top) + jnp.sum(
            jnp.exp(masked - new_top[:, :, None]), axis=-1
        )
        return (new_top, denominator)

    top_init = jnp.full((HEADS, frame_count), MASKED, jnp.float32)
    total_init = jnp.zeros((HEADS, frame_count), jnp.float32)
    top_score, denominator = over_blocks(
        stats_step, (top_init, total_init), (lax.all_gather(key_low, "seq", axis=0, tiled=True),)
    )
    log_total = top_score + jnp.log(denominator)

    def value_step(current, blocks, first_row):
        mixed_sum, rest_sum = current
        key_block, value_block = blocks
        key_segments = segment_of(
            first_row + jnp.arange(key_block.shape[0], dtype=jnp.int32), seg_lengths
        )
        probs = jnp.exp(
            block_scores(query_heads, split_heads(key_block), query_segments, key_segments)
            - log_total[:, :, None]
        )
        probs_high = probs.astype(jnp.bfloat16)
        probs_rest = (probs - probs_high.astype(jnp.float32)).astype(jnp.bfloat16)
        value_heads = split_heads(value_block)
        mixed_sum = mixed_sum + jnp.einsum(
            "hqk,khd->qhd", probs_high, value_heads, preferred_element_type=jnp.float32
        )
        rest_sum = rest_sum + jnp.einsum(
            "hqk,khd->qhd", probs_rest, value_heads, preferred_element_type=jnp.float32
        )
        return (mixed_sum, rest_sum)

    zero_heads = jnp.zeros((frame_count, HEADS, HEAD_DIM), jnp.float32)
    mixed_sum, rest_sum = over_blocks(
        value_step,
        (zero_heads, zero_heads),
        (
            lax.all_gather(key_low, "seq", axis=0, tiled=True),
            lax.all_gather(value_low, "seq", axis=0, tiled=True),
        ),
    )
    exact_sum = mixed_sum + rest_sum
    mixed_low = mixed_sum.reshape(frame_count, model_width).astype(jnp.bfloat16)
    branch_two, kept_attn_out = project(mixed_low, attn_out)
    stream_two = stream_one + branch_two
    normed_three, saved_three = norm_forward(stream_two, gain_conv)
    normed_three_low = normed_three.astype(jnp.bfloat16)
    gate_up, kept_conv_in = project(normed_three_low, conv_in)
    first_part = gate_up[:, :model_width]
    gate_sigma = jax.nn.sigmoid(gate_up[:, model_width:])
    glu_low = (first_part * gate_sigma).astype(jnp.bfloat16)
    padded = with_halo(glu_low, (("seq", 0),), HALF).astype(jnp.float32)
    padded_segments = segment_of(
        first_frame - HALF + jnp.arange(frame_count + 2 * HALF, dtype=jnp.int32), seg_lengths
    )
    kernel_taps = conv_kernel.astype(jnp.float32)
    conv_values = jnp.zeros((frame_count, model_width), jnp.float32)
    for offset in range(KERNEL):
        same_segment = (padded_segments[offset : offset + frame_count] == query_segments).astype(
            jnp.float32
        )
        conv_values = (
            conv_values
            + kernel_taps[offset] * padded[offset : offset + frame_count] * same_segment[:, None]
        )
    normed_four, saved_four = norm_forward(conv_values, gain_inner)
    active_four = sigmoid_linear(normed_four).astype(jnp.bfloat16)
    branch_three, kept_conv_out = project(active_four, conv_out)
    stream_three = stream_two + branch_three
    normed_five, saved_five = norm_forward(stream_three, gain_ffn2)
    normed_five_low = normed_five.astype(jnp.bfloat16)
    hidden_two, kept_ffn2_in = project(normed_five_low, ffn2_in)
    active_two = sigmoid_linear(hidden_two).astype(jnp.bfloat16)
    branch_four, kept_ffn2_out = project(active_two, ffn2_out)
    stream_four = stream_three + 0.5 * branch_four
    final_norm, saved_six = norm_forward(stream_four, gain_out)
    output = final_norm.astype(jnp.bfloat16)[None]
    grad_four, grad_gain_six = norm_backward(cotangent[0].astype(jnp.float32), gain_out, saved_six)
    out_two_low = (0.5 * grad_four).astype(jnp.bfloat16)
    grad_ffn_two_out = weight_grad(active_two, out_two_low)
    hidden_two_low = (project_back(out_two_low, ffn2_out) * sigmoid_linear_grad(hidden_two)).astype(
        jnp.bfloat16
    )
    grad_ffn_two_in = weight_grad(normed_five_low, hidden_two_low)
    input_part, grad_gain_five = norm_backward(
        project_back(hidden_two_low, ffn2_in), gain_ffn2, saved_five
    )
    grad_three = grad_four + input_part
    conv_out_low = grad_three.astype(jnp.bfloat16)
    grad_conv_weight_out = weight_grad(active_four, conv_out_low)
    active_grad = project_back(conv_out_low, conv_out) * sigmoid_linear_grad(normed_four)
    conv_grad, grad_gain_four = norm_backward(active_grad, gain_inner, saved_four)
    conv_grad_low = conv_grad.astype(jnp.bfloat16)
    conv_grad_value = conv_grad_low.astype(jnp.float32)
    rim_grad = with_halo(conv_grad_low, (("seq", 0),), HALF).astype(jnp.float32)
    tap_grads = []
    glu_grad = jnp.zeros((frame_count, model_width), jnp.float32)
    for offset in range(KERNEL):
        same_segment = (padded_segments[offset : offset + frame_count] == query_segments).astype(
            jnp.float32
        )
        tap_grads.append(
            jnp.sum(
                padded[offset : offset + frame_count] * same_segment[:, None] * conv_grad_value,
                axis=0,
            )
        )
        back_start = 2 * HALF - offset
        back_segment = (
            padded_segments[back_start : back_start + frame_count] == query_segments
        ).astype(jnp.float32)
        glu_grad = (
            glu_grad
            + kernel_taps[offset]
            * rim_grad[back_start : back_start + frame_count]
            * back_segment[:, None]
        )
    kernel_grad = jnp.stack(tap_grads, axis=0)
    gate_up_low = jnp.concatenate(
        [glu_grad * gate_sigma, glu_grad * first_part * gate_sigma * (1.0 - gate_sigma)], axis=1
    ).astype(jnp.bfloat16)
    grad_conv_weight_in = weight_grad(normed_three_low, gate_up_low)
    input_part, grad_gain_three = norm_backward(
        project_back(gate_up_low, conv_in), gain_conv, saved_three
    )
    grad_two = grad_three + input_part
    attn_grad_low = grad_two.astype(jnp.bfloat16)
    grad_attn_weight = weight_grad(mixed_low, attn_grad_low)
    mixed_grad_low = project_back(attn_grad_low, attn_out).astype(jnp.bfloat16)
    delta = jnp.transpose(
        jnp.sum(split_heads(mixed_grad_low).astype(jnp.float32) * exact_sum, axis=-1)
    )

    def key_turn(turn_index, current):
        key_rows, value_rows, key_acc, value_acc, query_acc = current
        owner = (position_index - turn_index) % device_count
        key_segments = segment_of(owner * frame_count + local_frames, seg_lengths)
        query_part, key_part, value_part = pair_grads(
            query_low,
            mixed_grad_low,
            log_total,
            delta,
            query_segments,
            key_rows,
            value_rows,
            key_segments,
        )
        key_rows, value_rows = shifted((key_rows, value_rows), "seq", 1)
        key_acc, value_acc = (
            shifted((key_acc + key_part).astype(jnp.bfloat16), "seq", 1).astype(jnp.float32),
            shifted((value_acc + value_part).astype(jnp.bfloat16), "seq", 1).astype(jnp.float32),
        )
        return (key_rows, value_rows, key_acc, value_acc, query_acc + query_part)

    zero_rows = jnp.zeros((frame_count, model_width), jnp.float32)
    unused_keys, unused_values, key_grad, value_grad, query_grad = lax.fori_loop(
        0, device_count, key_turn, (key_low, value_low, zero_rows, zero_rows, zero_rows)
    )
    projected_grad_low = jnp.concatenate(
        [
            unrotate(query_grad, cos_table, sin_table),
            unrotate(key_grad, cos_table, sin_table),
            value_grad,
        ],
        axis=1,
    ).astype(jnp.bfloat16)
    grad_qkv_weight = weight_grad(normed_two_low, projected_grad_low)
    input_part, grad_gain_two = norm_backward(
        project_back(projected_grad_low, attn_qkv), gain_attn, saved_two
    )
    grad_one = grad_two + input_part
    out_one_low = (0.5 * grad_one).astype(jnp.bfloat16)
    grad_ffn_one_out = weight_grad(active_one, out_one_low)
    hidden_one_low = (project_back(out_one_low, ffn1_out) * sigmoid_linear_grad(hidden_one)).astype(
        jnp.bfloat16
    )
    grad_ffn_one_in = weight_grad(normed_one_low, hidden_one_low)
    input_part, grad_gain_one = norm_backward(
        project_back(hidden_one_low, ffn1_in), gain_ffn1, saved_one
    )
    input_grad = (grad_one + input_part)[None]
    small_grads = lax.psum(
        (
            grad_gain_one,
            grad_gain_two,
            grad_gain_three,
            grad_gain_four,
            grad_gain_five,
            grad_gain_six,
            kernel_grad,
        ),
        ("seq", "row"),
    )
    large_grads = (
        grad_ffn_one_in,
        grad_ffn_one_out,
        grad_qkv_weight,
        grad_attn_weight,
        grad_conv_weight_in,
        grad_conv_weight_out,
        grad_ffn_two_in,
        grad_ffn_two_out,
    )
    large_grads = (
        lax.psum(grad_ffn_one_in.astype(jnp.bfloat16), "row").astype(jnp.float32),
        lax.psum(grad_ffn_one_out.astype(jnp.bfloat16), "row").astype(jnp.float32),
        lax.psum(grad_qkv_weight.astype(jnp.bfloat16), "row").astype(jnp.float32),
        lax.psum(grad_attn_weight.astype(jnp.bfloat16), "row").astype(jnp.float32),
        lax.psum(grad_conv_weight_in.astype(jnp.bfloat16), "row").astype(jnp.float32),
        lax.psum(grad_conv_weight_out.astype(jnp.bfloat16), "row").astype(jnp.float32),
        lax.psum(grad_ffn_two_in.astype(jnp.bfloat16), "row").astype(jnp.float32),
        lax.psum(grad_ffn_two_out.astype(jnp.bfloat16), "row").astype(jnp.float32),
    )
    return (
        output,
        input_grad,
        small_grads[0],
        small_grads[1],
        small_grads[2],
        small_grads[3],
        small_grads[4],
        small_grads[5],
        small_grads[6],
        large_grads[0],
        large_grads[1],
        large_grads[2],
        large_grads[3],
        large_grads[4],
        large_grads[5],
        large_grads[6],
        large_grads[7],
    )


BF16 = jnp.bfloat16
F32 = jnp.float32
PLANES = 4
VMEM = pltpu.VMEM
DMA = pltpu.SemaphoreType.DMA
VMEM_LIMIT = 60 * 1024 * 1024
FORWARD_PARTS = 1
BACKWARD_PARTS = 1


class Place:
    def __init__(self, parts):
        self.parts = Parts(parts)
        seq = lax.axis_index("seq")
        self.x = lax.axis_index("row")
        self.z = seq // 4
        self.yc = lax.rem(seq, 4)
        self.core = lax.rem(self.yc, 2)
        inside = lax.rem(self.z + self.z // 2, 2)
        self.end, self.middle = inside == 0, inside == 1
        self.beside, self.across, self.opposite = self.line(1 - inside), self.line(2), self.line(3)

    def flip(self, k):
        y, c, x = self.yc // 2, lax.rem(self.yc, 2), self.x
        c = 1 - c if k & 1 else c
        y = 1 - y if k & 2 else y
        x = 1 - x if k & 4 else x
        return x, y * 2 + c

    def dev(self, k):
        x, yc = self.flip(k)
        return {"seq": self.z * 4 + yc, "row": x}

    def slot(self, k):
        x, yc = self.flip(k)
        return x * 4 + yc

    def row(self, k):
        return self.flip(k)[0]

    def zdev(self, k):
        return self.at(lax.rem(self.z + k, PLANES))

    def at(self, plane, yc=None):
        return {"seq": plane * 4 + (self.yc if yc is None else yc), "row": self.x}

    def line(self, index):
        return index + self.z // 2 * (3 - 2 * index)

    def pair(self, x=None, yc=None):
        x = self.x if x is None else x
        yc = self.yc if yc is None else yc
        return (x * 2 + lax.rem(yc, 2)) * 2 + yc // 2

    def enter(self):
        barrier = pltpu.get_barrier_semaphore()
        partners = [self.dev(k) for k in range(1, 8)]
        for k in range(1, PLANES):
            plane = lax.rem(self.z + k, PLANES)
            partners += [self.at(plane), self.at(plane, self.flip(1)[1])]
        for partner in partners:
            pl.semaphore_signal(barrier, inc=1, device_id=partner)
        pl.semaphore_wait(barrier, len(partners))


def remote(src, dst, send_sem, recv_sem, dev):
    return pltpu.make_async_remote_copy(src, dst, send_sem, recv_sem, device_id=dev)


def dot(left, right, left_dim=1, right_dim=0):
    return lax.dot_general(
        left, right, (((left_dim,), (right_dim,)), ((), ())), preferred_element_type=F32
    )


PAIRS = (((0, 1),), ((2, 4), (3, 5)), ((6, 7),))
LAST_OF_ROW = {(3, 5): 0, (6, 7): 4}
OUT_PAIRS = ((7, 3), (5, 1), (6, 2), (4, 0))


class Parts:
    def __init__(self, count):
        self.count = count
        self.rows = 128 // count

    def __iter__(self):
        return iter(range(self.count))

    def of(self, part):
        return slice(part * self.rows, part * self.rows + self.rows)

    def take(self, ref, slots, part):
        return jnp.concatenate([ref[slot, self.of(part), :] for slot in slots], axis=0)

    def put(self, ref, slots, part, value):
        for index, slot in enumerate(slots):
            ref[slot, self.of(part), :] = value[index * self.rows : index * self.rows + self.rows]


class Gather:
    def __init__(self, place, blocks, sems):
        self.place, self.blocks = place, blocks
        self.send, self.recv = sems
        self.rows = place.parts.rows
        self.sent = []

    def at(self, slot, part, half=None):
        count = self.rows if half is None else self.rows // 2
        first = part * self.rows + (half or 0) * count
        return self.blocks.at[slot, pl.ds(first, count)]

    def copy(self, rows, to, part, sem):
        sem = part * 11 + sem
        return remote(rows, rows, self.send.at[sem], self.recv.at[sem], self.place.dev(to))

    def hand(self, rows, to, part, sem):
        copy = self.copy(rows, to, part, sem)
        copy.start()
        self.sent.append(copy)

    def push(self, part, value):
        own = self.place.slot(0)
        self.blocks[own, self.place.parts.of(part), :] = value
        for half in range(2):
            self.hand(self.at(own, part, 1 - half), 4, part, 4 + 5 * (half == 1))
            self.hand(self.at(own, part, half), 2, part, 2 + 8 * (half == 1))
        self.hand(self.at(own, part), 1, part, 1)

    def arrive(self, rows, part, sem):
        self.copy(rows, 1, part, sem).wait_recv()

    def fetch(self, ks, part):
        slots = {k: self.place.slot(k) for k in ks}
        if 2 in slots:
            self.arrive(self.at(slots[2], part, 0), part, 2)
            self.hand(self.at(slots[2], part, 0), 4, part, 6)
            self.arrive(self.at(slots[4], part, 1), part, 4)
            self.hand(self.at(slots[4], part, 1), 2, part, 8)
            self.arrive(self.at(slots[2], part, 1), part, 10)
            self.hand(self.at(slots[2], part), 1, part, 3)
            self.arrive(self.at(slots[4], part, 0), part, 9)
            self.hand(self.at(slots[4], part), 1, part, 5)
        if 6 in slots:
            self.arrive(self.at(slots[6], part, 0), part, 6)
            self.arrive(self.at(slots[6], part, 1), part, 8)
            self.hand(self.at(slots[6], part), 1, part, 7)
        for k in ks:
            if k % 2:
                self.arrive(self.at(slots[k], part), part, k)
        return slots

    def drain(self):
        for copy in self.sent:
            copy.wait_send()


class Scatter:
    def __init__(self, place, buffers, sems):
        self.place = place
        self.part, self.staged, self.sibling, self.reduced, self.received, self.relayed = buffers
        self.relays = False
        self.send, self.recv = sems
        self.sent = []

    @staticmethod
    def scratch(parts, rows, width):
        return [
            VMEM((parts, 4, rows, width), F32),
            VMEM((parts, 4, rows, width), BF16),
            VMEM((parts, 4, rows, width), BF16),
            VMEM((parts, 3, rows, width), BF16),
            VMEM((parts, 3, rows, width), BF16),
            VMEM((parts, 2, rows // 2, width), BF16),
        ]

    def copy(self, src, dst, part, sem, k):
        sem = part * 11 + sem
        return remote(src, dst, self.send.at[sem], self.recv.at[sem], self.place.dev(k))

    def push(self, *what):
        copy = self.copy(*what)
        copy.start()
        self.sent.append(copy)

    def emit(self, k, part, value):
        index = k // 2
        if k % 2:
            self.staged[part, index] = value.astype(BF16)
            self.push(
                self.staged.at[part, index], self.sibling.at[part, index], part, index, 1
            )
        else:
            self.part[part, index] = value

    def emit_pair(self, pair, part, value):
        rows = value.shape[0] // len(pair)
        for index, k in enumerate(pair):
            self.emit(k, part, value[index * rows : index * rows + rows])

    def of_chip(self, index, part):
        into = self.sibling.at[part, index]
        self.copy(into, into, part, index, 1).wait_recv()
        return self.part[part, index] + self.sibling[part, index].astype(F32)

    def finish_all(self, part):
        self.relays = True
        count = self.relayed.shape[2]
        halves = (pl.ds(0, count), pl.ds(count, count))
        self.reduced[part, 2] = self.of_chip(3, part).astype(BF16)
        for half, k in ((0, 4), (1, 2)):
            self.push(
                self.reduced.at[part, 2, halves[half]], self.relayed.at[part, half], part, 7 + half, k
            )
        sums = [self.of_chip(1, part), self.of_chip(2, part)]

        def send(index, half, value, sem):
            self.reduced[part, index, halves[half], :] = value.astype(BF16)
            self.push(
                self.reduced.at[part, index, halves[half]],
                self.received.at[part, index, halves[half]],
                part,
                sem,
                2 + 2 * index,
            )

        send(0, 1, sums[0][count:], 4)
        send(1, 0, sums[1][:count], 5)
        self.part[part, 0] = self.of_chip(0, part)
        for index, rows in ((0, slice(0, count)), (1, slice(count, 2 * count))):
            into = self.relayed.at[part, index]
            self.copy(into, into, part, 7 + index, 1).wait_recv()
            send(index, index, sums[index][rows] + self.relayed[part, index].astype(F32), 9 + index)

    def finish(self, k, part):
        index = k // 2
        total = self.of_chip(index, part)
        if k:
            self.reduced[part, index - 1] = total.astype(BF16)
            self.push(
                self.reduced.at[part, index - 1],
                self.received.at[part, index - 1],
                part,
                3 + index,
                k,
            )
        else:
            self.part[part, 0] = total

    def total(self, part):
        value = self.part[part, 0]
        if self.relays:
            count = self.relayed.shape[2]
            for index in range(2):
                for half in range(2):
                    into = self.received.at[part, index, pl.ds(half * count, count)]
                    sem = 9 + index if half == index else 4 + index
                    self.copy(into, into, part, sem, 1).wait_recv()
                value = value + self.received[part, index].astype(F32)
            return value
        for index in range(3):
            into = self.received.at[part, index]
            self.copy(into, into, part, 4 + index, 1).wait_recv()
            value = value + self.received[part, index].astype(F32)
        return value

    def drain(self):
        for copy in self.sent:
            copy.wait_send()


def gather_blocks(place, gather, process, scatter=None):
    for part in place.parts:
        for group in PAIRS:
            slots = gather.fetch([k for pair in group for k in pair], part)
            for pair in group:
                process(pair, [slots[k] for k in pair], part)
            if scatter and group == PAIRS[1]:
                scatter.finish(2, part)
                scatter.finish(4, part)
        if scatter:
            scatter.finish(6, part)
            scatter.finish(0, part)


def scatter_blocks(place, scatter, rows, weight, side=0):
    for part in place.parts:
        for pair in OUT_PAIRS:
            slots = [place.slot(k) for k in pair]
            scatter.emit_pair(pair, part, dot(rows(slots, part), flat(weight), 1, side))
        scatter.finish_all(part)


def carry(place, scatter, gather, step):
    for part in place.parts:
        gather.push(part, step(part, scatter.total(part)))
    scatter.drain()


class Refs:
    pass


def kernel_call(body, collective, ins, outs, scratch):
    in_names = list(ins)
    out_names = list(outs)
    scratch_names = list(scratch)
    flat_scratch = []
    counts = []
    for name in scratch_names:
        item = scratch[name]
        counts.append(len(item) if isinstance(item, list) else 0)
        flat_scratch += item if isinstance(item, list) else [item]

    def kernel(*refs):
        held = Refs()
        at = 0
        for name in in_names + out_names:
            setattr(held, name, refs[at])
            at += 1
        for name, count in zip(scratch_names, counts):
            setattr(held, name, refs[at : at + count] if count else refs[at])
            at += max(count, 1)
        body(held)

    results = pl.pallas_call(
        kernel,
        out_shape=[jax.ShapeDtypeStruct(shape, dtype) for shape, dtype, unused in outs.values()],
        in_specs=[pl.BlockSpec(memory_space=space) for unused, space in ins.values()],
        out_specs=[pl.BlockSpec(memory_space=space) for unused, unused_type, space in outs.values()],
        scratch_shapes=flat_scratch,
        compiler_params=pltpu.CompilerParams(
            collective_id=collective, has_side_effects=True, vmem_limit_bytes=VMEM_LIMIT
        ),
    )(*[array for array, unused in ins.values()])
    return dict(zip(out_names, results))


class AlongZ:
    def __init__(self, place, sems, block):
        self.place = place
        self.send, self.recv = sems
        self.block = block
        self.sent = []

    def copy(self, source, owner, plane, sem):
        into = self.block(owner)
        return remote(
            source, into, self.send.at[sem], self.recv.at[owner], self.place.at(plane)
        )

    def arrive(self, owner):
        self.copy(self.block(owner), owner, owner, 0).wait_recv()

    def start(self, source):
        place = self.place
        self.sent = [
            self.copy(source, place.z, place.across, 0),
            self.copy(source, place.z, place.beside, 1),
        ]
        self.last = [
            self.copy(source, place.z, place.opposite, 2),
            self.copy(self.block(place.opposite), place.opposite, place.line(0), 3),
        ]
        for copy in self.sent:
            copy.start()

        @pl.when(place.middle)
        def start():
            self.last[0].start()

    def relay(self):
        @pl.when(self.place.middle)
        def hand_on():
            self.arrive(self.place.opposite)
            self.last[1].start()

    def finish(self):
        place = self.place
        self.arrive(place.beside)
        self.arrive(place.across)

        @pl.when(place.end)
        def last():
            self.arrive(place.opposite)

        for copy in self.sent:
            copy.wait_send()

        @pl.when(place.middle)
        def drain():
            for copy in self.last:
                copy.wait_send()


class GatherRows:
    def __init__(self, place, src, dst, sems, pieces):
        self.place, self.dst = place, dst
        self.send, self.recv, self.local = sems[:3]
        self.along = AlongZ(place, sems[3:], lambda plane: dst.at[pl.ds(plane * 4, 4)])
        mine = place.z * 4 + place.yc
        for k in (0, 2, 3, 1):
            x, to = place.flip(k)
            for index, column in enumerate(pieces(place, to)):
                source = src.at[:, pl.ds(pl.multiple_of(column * 128, 128), 128)]
                into = dst.at[mine, :, pl.ds(index * 128, 128)]
                if k:
                    remote(source, into, self.send.at[k], self.recv.at[k], place.dev(k)).start()
                else:
                    pltpu.make_async_copy(source, into, self.local).start()

    def along_z(self):
        place = self.place
        mine = self.dst.at[place.z * 4 + place.yc]
        pltpu.make_async_copy(mine, mine, self.local).wait()
        for k in (2, 3, 1):
            into = self.dst.at[place.z * 4 + place.flip(k)[1]]
            remote(into, into, self.send.at[k], self.recv.at[k], place.dev(k)).wait_recv()
        self.along.start(self.dst.at[pl.ds(place.z * 4, 4)])

    def relay(self):
        self.along.relay()

    def finish(self):
        place = self.place
        self.along.finish()
        mine = self.dst.at[place.z * 4 + place.yc]
        for k in (2, 3, 1):
            remote(mine, mine, self.send.at[k], self.recv.at[k], place.dev(k)).wait_send()

    @staticmethod
    def scratch():
        return [DMA((4,)), DMA((4,)), DMA, DMA((4,)), DMA((PLANES,))]


def ffn_pieces(place, yc):
    return [(plane * 4 + yc) * 2 + place.x for plane in range(PLANES)]


def head_pieces(place, yc):
    return [kind * 8 + place.pair(None, yc) for kind in range(3)]


def channel_pieces(place, yc):
    return [kind * 8 + place.pair(None, yc) for kind in range(2)]


class GatherBlocks:
    def __init__(self, place, src, dst, sems, columns=slice(0, 1024)):
        columns = pl.ds(columns.start, columns.stop - columns.start)
        src = src.at[pl.ds(place.x * 128, 128), columns]
        self.along = AlongZ(place, sems[1:], lambda plane: dst.at[plane, :, columns])
        self.own = pltpu.make_async_copy(src, dst.at[place.z, :, columns], sems[0])
        self.own.start()
        self.along.start(src)

    def relay(self):
        self.along.relay()

    def finish(self):
        self.own.wait()
        self.along.finish()

    @staticmethod
    def scratch():
        return [DMA, DMA((4,)), DMA((PLANES,))]


class PlaneSum:
    def __init__(self, place, refs):
        self.place = place
        self.own, self.staged, self.received, self.relayed, self.send, self.recv = refs

    @staticmethod
    def scratch(rows, width):
        return [
            VMEM((rows, width), F32),
            VMEM((3, rows, width), BF16),
            VMEM((3, rows, width), BF16),
            VMEM((rows, width), BF16),
            DMA((4,)),
            DMA((4,)),
        ]

    def term_copy(self, index, plane):
        slot = lax.rem(plane + 3 - self.place.z, PLANES)
        return remote(
            self.staged.at[index],
            self.received.at[slot],
            self.send.at[index],
            self.recv.at[slot],
            self.place.at(plane),
        )

    def relay_copy(self):
        return remote(
            self.staged.at[0],
            self.relayed,
            self.send.at[3],
            self.recv.at[3],
            self.place.at(self.place.beside),
        )

    def first(self, term):
        self.staged[0] = term(self.place.opposite).astype(BF16)

        @pl.when(self.place.end)
        def start():
            self.relay_copy().start()

    def rest(self, term):
        place = self.place
        self.staged[1] = term(place.across).astype(BF16)
        self.term_copy(1, place.across).start()
        self.staged[2] = term(place.beside).astype(BF16)
        self.term_copy(2, place.beside).start()
        self.own[...] = term(place.z)

    def relay(self):
        @pl.when(self.place.middle)
        def add():
            self.relay_copy().wait_recv()
            self.staged[0] = (
                self.staged[0].astype(F32) + self.relayed[...].astype(F32)
            ).astype(BF16)
            self.term_copy(0, self.place.opposite).start()

    def arrive(self, plane):
        slot = lax.rem(self.place.z + 3 - plane, PLANES)
        into = self.received.at[slot]
        remote(
            into, into, self.send.at[0], self.recv.at[slot], self.place.at(plane)
        ).wait_recv()

    def total(self):
        place = self.place
        self.arrive(place.beside)
        self.arrive(place.across)

        @pl.when(place.middle)
        def last():
            self.arrive(place.opposite)
            self.term_copy(0, place.opposite).wait_send()

        @pl.when(place.end)
        def nothing():
            self.received[lax.rem(place.z + 3 - place.opposite, PLANES)] = jnp.zeros(
                self.received.shape[1:], BF16
            )
            self.relay_copy().wait_send()

        self.term_copy(1, place.across).wait_send()
        self.term_copy(2, place.beside).wait_send()
        value = self.own[...]
        for index in range(3):
            value = value + self.received[index].astype(F32)
        return value


class Exchange:
    def __init__(self, place, blocks, sems, partners=tuple(range(1, 8)), slot=None):
        self.place = place
        self.blocks = blocks
        self.send, self.recv = sems
        self.partners = partners
        self.slot = slot or place.slot
        self.sent = []

    def start(self, source):
        own = self.slot(0)
        for k in self.partners:
            copy = remote(
                source(k), self.blocks.at[own], self.send.at[k], self.recv.at[k], self.place.dev(k)
            )
            copy.start()
            self.sent.append(copy)

    def wait(self):
        for k in self.partners:
            into = self.blocks.at[self.slot(k)]
            remote(into, into, self.send.at[k], self.recv.at[k], self.place.dev(k)).wait_recv()
        for copy in self.sent:
            copy.wait_send()


def flat(ref):
    value = ref[...]
    return value.reshape(value.shape[0] * value.shape[1], value.shape[2])


def ffn_forward(place, gather, hidden, w_in, w_out, scatter, ready):
    def process(pair, slots, part):
        if part == 0 and pair[0] == 0:
            ready()
        value = dot(place.parts.take(gather.blocks, slots, part), flat(w_in))
        place.parts.put(hidden, slots, part, value)
        scatter.emit_pair(pair, part, dot(sigmoid_linear(value).astype(BF16), flat(w_out)))

    gather_blocks(place, gather, process, scatter)


def ffn_backward(place, gather, hidden, hidden_grads, active, w_in, w_out, scatter, ready):
    def process(pair, slots, part):
        if part == 0 and pair[0] == 0:
            ready()
        value = place.parts.take(hidden, slots, part)
        sigma = jax.nn.sigmoid(value)
        place.parts.put(active, slots, part, (value * sigma).astype(BF16))
        back = dot(place.parts.take(gather.blocks, slots, part), flat(w_out), 1, 1)
        low = (back * (sigma * (1.0 + value * (1.0 - sigma)))).astype(BF16)
        place.parts.put(hidden_grads, slots, part, low)
        scatter.emit_pair(pair, part, dot(low, flat(w_in), 1, 1))

    gather_blocks(place, gather, process, scatter)


def token_dot(left, columns, right):
    count, rows, unused = left.shape
    taken = left[:, :, columns].reshape(count * rows, -1)
    return dot(taken, flat(right), 0, 0)


def columns_of(plane, width):
    return pl.ds(pl.multiple_of(plane * width, width), width)


class WeightGrads:
    def __init__(self, place, refs, name, sums, wide):
        self.place = place
        self.sum_in = PlaneSum(place, getattr(refs, sums + "_sum_in"))
        self.total_in = getattr(refs, name + "_total_in")
        self.share_in = Exchange(
            place, getattr(refs, name + "_grad_in"), getattr(refs, name + "_share_in")
        )
        self.wide = wide
        if wide:
            self.sum_out = PlaneSum(place, getattr(refs, sums + "_sum_out"))
            self.share_out = Exchange(
                place,
                getattr(refs, name + "_grad_out"),
                getattr(refs, name + "_share_out"),
                (4,),
                lambda k: place.flip(k)[0],
            )
        else:
            self.sum_out = HalfSum(
                place, getattr(refs, sums + "_sum_out"), getattr(refs, name + "_grad_out")
            )

    def put_out(self, active, grads):
        self.sum_out.put(dot(flat(active), flat(grads), 0, 0))

    def put_in(self, blocks, grads):
        def term(plane):
            return token_dot(blocks, columns_of(plane, 256), grads)

        self.sum_in.first(term)
        self.sum_in.rest(term)

    def put_both(self, active, grads, blocks, hidden_grads):
        def out(plane):
            return token_dot(active, columns_of(plane, 128), grads)

        def into(plane):
            return token_dot(blocks, columns_of(plane, 256), hidden_grads)

        self.sum_out.first(out)
        self.sum_in.first(into)
        self.sum_out.rest(out)
        self.sum_in.rest(into)

    def relay(self):
        self.sum_out.relay()
        self.sum_in.relay()

    def share(self):
        if self.wide:
            self.share_out.blocks[self.place.x] = self.sum_out.total().astype(BF16)
            self.share_out.start(lambda k: self.share_out.blocks.at[self.place.x])
        else:
            self.sum_out.add()
        self.total_in[...] = self.sum_in.total().astype(BF16).reshape(self.total_in.shape)
        self.share_in.blocks[self.place.slot(0)] = self.total_in[self.place.yc]
        self.share_in.start(lambda k: self.total_in.at[self.place.flip(k)[1]])

    def wait(self):
        (self.share_out if self.wide else self.sum_out).wait()
        self.share_in.wait()

    @staticmethod
    def sums(name, width, wide):
        return {
            name + "_sum_in": PlaneSum.scratch(256, width),
            name + "_sum_out": PlaneSum.scratch(128, 1024) if wide else HalfSum.scratch(1024),
        }

    @staticmethod
    def scratch(name, width, wide):
        held = {
            name + "_total_in": VMEM((4, 64, width), BF16),
            name + "_share_in": [DMA((8,)), DMA((8,))],
        }
        if wide:
            held[name + "_share_out"] = [DMA((8,)), DMA((8,))]
        return held

    @staticmethod
    def outs(name, width, wide):
        return {
            name + "_grad_in": ((8, 64, width), BF16, VMEM),
            name + "_grad_out": ((2, 128, 1024) if wide else (64, 1024), BF16, VMEM),
        }


AG_SEMS = [DMA((22,)), DMA((22,))]


def norm_rows(values, gain):
    normed, saved = norm_forward(values, gain)
    return normed.astype(BF16), saved


def norm_input_grad(grads, gain, saved):
    unit_part, inverse = saved
    scaled = grads * gain
    gain_grad = jnp.sum(grads * unit_part, axis=0, keepdims=True)
    input_part = inverse * (
        scaled
        - jnp.mean(scaled, axis=-1, keepdims=True)
        - unit_part * jnp.mean(scaled * unit_part, axis=-1, keepdims=True)
    )
    return input_part, gain_grad


class GatherHalf:
    def __init__(self, place, src, dst, sems):
        self.place, self.dst = place, dst
        self.send, self.recv, self.local = sems
        self.source = place.z // 2 == place.x
        self.first, self.last = 2 - place.x, 3 - 3 * place.x
        target = place.yc // 2 * 2 + lax.rem(place.z, 2)
        self.same = lax.rem(place.z, 2) == place.core
        self.own = pltpu.make_async_copy(src, dst.at[place.core], self.local)

        def copy(sem, plane):
            return remote(
                src,
                dst.at[place.core],
                self.send.at[sem],
                self.recv.at[place.core],
                place.at(plane, target),
            )

        self.far, self.near, self.sibling = (
            copy(0, self.first),
            copy(1, place.x * 2 + 1 - lax.rem(place.z, 2)),
            copy(2, place.z),
        )

        @pl.when(self.source)
        def start():
            self.far.start()
            self.near.start()

            @pl.when(self.same)
            def local():
                self.own.start()

            @pl.when(jnp.logical_not(self.same))
            def sibling():
                self.sibling.start()

    def on(self, half):
        rows = self.dst.at[half]
        return remote(
            rows, rows, self.send.at[half], self.recv.at[half], self.place.at(self.last)
        )

    def relay(self):
        @pl.when(self.place.z == self.first)
        def hand_on():
            for half in range(2):
                self.on(half).wait_recv()
                self.on(half).start()

    def finish(self):
        place = self.place
        at_home = place.z == place.x * 2 + place.core
        for half in range(2):
            here = jnp.logical_or(
                jnp.logical_and(at_home, place.core == half), place.z == self.first
            )

            @pl.when(jnp.logical_not(here))
            def arrive():
                self.on(half).wait_recv()

        @pl.when(self.source)
        def drain():
            self.far.wait_send()
            self.near.wait_send()

            @pl.when(self.same)
            def local():
                self.own.wait()

            @pl.when(jnp.logical_not(self.same))
            def sibling():
                self.sibling.wait_send()

        @pl.when(place.z == self.first)
        def drain_on():
            for half in range(2):
                self.on(half).wait_send()

    @staticmethod
    def scratch():
        return [DMA((3,)), DMA((2,)), DMA]


class HalfSum:
    def __init__(self, place, refs, result):
        self.place = place
        self.staged, self.received, self.relayed, self.send, self.recv, self.last = refs
        self.result = result
        self.near = place.z // 2 == place.x
        self.far_middle, self.far_end = 2 - place.x, 3 - 3 * place.x
        self.home = place.x * 2 + place.core

    @staticmethod
    def scratch(width):
        return [
            VMEM((2, 64, width), BF16),
            VMEM((3, 64, width), BF16),
            VMEM((2, 64, width), BF16),
            DMA((3,)),
            DMA((4,)),
            DMA((2,)),
        ]

    def term_copy(self, half, slot):
        place = self.place
        return remote(
            self.staged.at[half],
            self.received.at[slot],
            self.send.at[half],
            self.recv.at[slot],
            place.at(self.home, place.yc // 2 * 2 + half),
        )

    def relay_copy(self):
        return remote(
            self.staged,
            self.relayed,
            self.send.at[2],
            self.recv.at[3],
            self.place.at(self.far_middle),
        )

    def near_copies(self):
        place = self.place
        for half in range(2):
            here = jnp.logical_and(place.z == self.home, place.core == half)
            slot = lax.rem(place.z + self.home, 2)
            yield jnp.logical_and(self.near, jnp.logical_not(here)), self.term_copy(half, slot)

    def put(self, value):
        self.staged[...] = value.astype(BF16).reshape(self.staged.shape)

    def start(self):
        place = self.place

        @pl.when(place.z == self.far_end)
        def relay():
            self.relay_copy().start()

        for away, copy in self.near_copies():

            @pl.when(away)
            def start(copy=copy):
                copy.start()

    def relay(self):
        @pl.when(self.place.z == self.far_middle)
        def add():
            self.relay_copy().wait_recv()
            self.staged[...] = (
                self.staged[...].astype(F32) + self.relayed[...].astype(F32)
            ).astype(BF16)
            for half in range(2):
                self.term_copy(half, 2).start()

    def add(self):
        place = self.place
        at_home = jnp.logical_and(self.near, place.z == self.home)

        @pl.when(self.near)
        def reduce():
            @pl.when(at_home)
            def own():
                self.received[0] = self.staged[place.core]

            for slot in range(3):

                def arrive():
                    into = self.received.at[slot]
                    remote(
                        into, into, self.send.at[0], self.recv.at[slot], place.at(place.z)
                    ).wait_recv()

                if slot:
                    arrive()
                else:
                    pl.when(jnp.logical_not(at_home))(arrive)
            value = self.received[0].astype(F32)
            for slot in range(1, 3):
                value = value + self.received[slot].astype(F32)
            self.result[...] = value.astype(BF16)
            self.hand_over().start()

        for away, copy in self.near_copies():

            @pl.when(away)
            def drain(copy=copy):
                copy.wait_send()

        @pl.when(place.z == self.far_middle)
        def drain_sums():
            for half in range(2):
                self.term_copy(half, 2).wait_send()

        @pl.when(place.z == self.far_end)
        def drain_relay():
            self.relay_copy().wait_send()

    def hand_over(self):
        return remote(
            self.result, self.result, self.last.at[0], self.last.at[1], self.place.dev(4)
        )

    def wait(self):
        @pl.when(self.near)
        def sent():
            self.hand_over().wait_send()

        @pl.when(jnp.logical_not(self.near))
        def arrived():
            self.hand_over().wait_recv()


class Turn:
    def __init__(self, place, refs):
        self.place = place
        self.staged, self.received, self.send, self.recv = refs

    @staticmethod
    def scratch(rows):
        return [VMEM((PLANES, rows, 128), BF16), VMEM((PLANES, rows, 128), BF16), DMA((4,)), DMA((4,))]

    def copy(self, k):
        place = self.place
        return remote(
            self.staged.at[lax.rem(place.z + k, PLANES)],
            self.received.at[place.z],
            self.send.at[k],
            self.recv.at[k],
            place.zdev(k),
        )

    def start(self):
        for k in (2, 1, 3):
            self.copy(k).start()
        self.keep()

    def dispatch(self, pair):
        k = lax.rem(pair + PLANES - self.place.z, PLANES)

        @pl.when(k > 0)
        def start():
            self.copy(k).start()

        @pl.when(k == 0)
        def own():
            self.keep()

    def keep(self):
        self.received[self.place.z] = self.staged[self.place.z]

    def wait(self):
        for k in (1, 2, 3):
            into = self.received.at[lax.rem(self.place.z + 4 - k, PLANES)]
            remote(into, into, self.send.at[k], self.recv.at[k], self.place.zdev(k)).wait_recv()
        for k in (1, 2, 3):
            self.copy(k).wait_send()


def swap_halves(values):
    lane = lax.broadcasted_iota(jnp.int32, values.shape, 1)
    return jnp.where(lane % 64 < 32, pltpu.roll(values, 96, 1), pltpu.roll(values, 32, 1))


def head_part(values, head):
    return values[:, head * 64 : head * 64 + 64]


def pack_wide(turn, row, head, left, right):
    pair = row * 2 + head
    for block in range(4):
        turn.staged[pair, block * 128 : block * 128 + 128, :] = jnp.concatenate(
            [head_part(left[row * 4 + block], head), head_part(right[row * 4 + block], head)], axis=1
        )


def pack_narrow(turn, row, head, values):
    pair = row * 2 + head
    for block in range(2):
        turn.staged[pair, block * 128 : block * 128 + 128, :] = jnp.concatenate(
            [
                head_part(values[row * 4 + block], head),
                head_part(values[row * 4 + block + 2], head),
            ],
            axis=1,
        )


def unpack_narrow(turn, row, block):
    rows = slice((block % 2) * 128, (block % 2) * 128 + 128)
    return jnp.concatenate(
        [head_part(turn.received[row * 2 + head, rows, :], block // 2) for head in range(2)], axis=1
    )


def unpack_wide(turn, row, block, side):
    rows = slice(block * 128, block * 128 + 128)
    return jnp.concatenate(
        [head_part(turn.received[row * 2 + head, rows, :], side) for head in range(2)], axis=1
    )


QUERY_BLOCK = 256


def segment_ends(refs, row):
    lengths = refs.row_lengths[row]
    ends = [lengths[0:1, 0:1]]
    for index in range(1, 4):
        ends.append(ends[-1] + lengths[0:1, index : index + 1])
    return ends


def segment_features(refs, plane, row):
    frame = (plane * 512 + lax.broadcasted_iota(jnp.int32, (512, 64), 0)).astype(F32)
    lane = lax.broadcasted_iota(jnp.int32, (512, 64), 1).astype(F32)
    segment = jnp.zeros((512, 64), F32)
    for end in segment_ends(refs, row)[:3]:
        segment = segment + jnp.where(frame >= end, 1.0, 0.0)
    other = jnp.where(lane < 4.0, -MASKED, 0.0)
    return (
        jnp.where(lane == segment, 0.0, other).astype(BF16),
        jnp.where(lane == segment, -1.0, 0.0).astype(BF16),
    )


def segment_reach(place, refs, slot):
    row, block = slot // 4, slot % 4
    frame = place.z * 512 + block * 128 + lax.broadcasted_iota(jnp.int32, (128, 128), 0)
    frame = frame.astype(F32)
    ends = segment_ends(refs, row)
    first, last = jnp.zeros((128, 128), F32), ends[3]
    for end in ends[:3]:
        first = jnp.where(frame >= end, end, first)
    for end in ends[2::-1]:
        last = jnp.where(frame < end, end, last)
    return first - frame, last - frame


def open_heads(place, refs, turn_qk, turn_v):
    for plane in range(PLANES):
        seg_query, seg_key = segment_features(refs, plane, place.z // 2)
        rows = slice(plane * 512, plane * 512 + 512)
        pair = turn_qk.received[plane]
        scaled = (pair[:, :64].astype(F32) * HEAD_DIM ** (-0.5)).astype(BF16)
        refs.queries[rows, :] = jnp.concatenate([scaled, seg_query], axis=1)
        refs.keys[rows, :] = jnp.concatenate([pair[:, 64:], seg_key], axis=1)
        both = turn_v.received[plane]
        turned = jnp.transpose(both.astype(F32)).astype(BF16)
        refs.values[plane * 512 : plane * 512 + 256, :] = both[:, :64]
        refs.values[plane * 512 + 256 : plane * 512 + 512, :] = both[:, 64:]
        refs.values_t[:, plane * 512 : plane * 512 + 256] = turned[:64]
        refs.values_t[:, plane * 512 + 256 : plane * 512 + 512] = turned[64:]


def attend(place, refs, turn_mix):
    def plane_step(step, unused):
        k = lax.rem(step + 1, PLANES)
        plane = lax.rem(place.z + k, PLANES)
        parts = []
        for half in range(2):
            first = plane * 512 + half * 256
            query = refs.queries[pl.ds(pl.multiple_of(first, 256), QUERY_BLOCK), :]
            scores = dot(refs.keys[...], query, 1, 1)
            top = jnp.max(scores, axis=0, keepdims=True)
            weights = jnp.exp(scores - top)
            total = jnp.sum(weights, axis=0, keepdims=True)
            low = (weights * (1.0 / total)).astype(BF16)
            parts.append(jnp.transpose(dot(refs.values_t[...], low)))
            refs.log_total[plane * 2 + half] = jnp.broadcast_to(top + jnp.log(total), (8, 256))
        turn_mix.staged[plane] = jnp.concatenate(parts, axis=1).astype(BF16)

        @pl.when(step < PLANES - 1)
        def send():
            turn_mix.copy(k).start()

        return unused

    lax.fori_loop(0, PLANES, plane_step, 0)


def attention_forward(place, refs, gather, scatter):
    def process(pair, slots, part):
        if part == 0 and pair[0] == 0:
            refs.finish_qkv()
        value = dot(place.parts.take(gather.blocks, slots, part), flat(refs.w_qkv))

        def frames_of(slot, part):
            count = place.parts.rows
            first = lax.rem(slot, 4) * 128 + part * count
            return pl.ds(pl.multiple_of(first, count), count)

        def table(ref):
            return jnp.concatenate(
                [
                    ref[frames_of(slot, part), :]
                    for slot in slots
                ],
                axis=0,
            )

        cos, sin = table(refs.cos), table(refs.sin)
        query, key = value[:, :128], value[:, 128:256]
        place.parts.put(refs.q_rows, slots, part, (query * cos + swap_halves(query) * sin).astype(BF16))
        place.parts.put(refs.k_rows, slots, part, (key * cos + swap_halves(key) * sin).astype(BF16))
        place.parts.put(refs.v_rows, slots, part, value[:, 256:].astype(BF16))
        if part == place.parts.count - 1 and pair in LAST_OF_ROW:
            row = place.row(LAST_OF_ROW[pair])
            for head in range(2):
                pack_wide(turn_qk, row, head, refs.q_rows, refs.k_rows)
                turn_qk.dispatch(row * 2 + head)
            for head in range(2):
                pack_narrow(turn_v, row, head, refs.v_rows)
                turn_v.dispatch(row * 2 + head)

    turn_qk, turn_v = Turn(place, refs.turn_qk), Turn(place, refs.turn_v)
    gather_blocks(place, gather, process)
    gather.drain()
    turn_qk.wait()
    turn_v.wait()
    refs.after_turn()
    open_heads(place, refs, turn_qk, turn_v)
    turn_mix = Turn(place, refs.turn_mix)
    attend(place, refs, turn_mix)
    turn_mix.keep()
    turn_mix.wait()
    refs.after_mix()
    for slot in range(8):
        refs.mixed[slot] = unpack_narrow(turn_mix, slot // 4, slot % 4)
    scatter_blocks(
        place, scatter, lambda slots, part: place.parts.take(refs.mixed, slots, part), refs.w_o
    )


def attention_kept():
    return dict(
        attn_blocks=((8, 128, 1024), BF16),
        w_qkv=((16, 64, 384), BF16),
        w_o=((2, 64, 1024), BF16),
        queries=((2048, 128), BF16),
        keys=((2048, 128), BF16),
        values=((2048, 64), BF16),
        log_total=((8, 8, 256), F32),
        mixed=((8, 128, 128), BF16),
    )


def attend_back(place, refs, turn_kv, turn_q):
    refs.key_grad[...] = jnp.zeros_like(refs.key_grad)
    refs.value_grad[...] = jnp.zeros_like(refs.value_grad)

    def plane_step(step, unused):
        k = lax.rem(step + 1, PLANES)
        plane = lax.rem(place.z + k, PLANES)
        parts = []
        for half in range(2):
            first = pl.multiple_of(plane * 512 + half * 256, 256)
            query = refs.queries[pl.ds(first, QUERY_BLOCK), :]
            grad = refs.mix_grads[pl.ds(first, QUERY_BLOCK), :]
            log_total = refs.log_total[plane * 2 + half][:1]
            probs = jnp.exp(dot(refs.keys[...], query, 1, 1) - log_total)
            prob_grads = dot(refs.values[...], grad, 1, 1)
            delta = jnp.sum(probs * prob_grads, axis=0, keepdims=True)
            low = (probs * (prob_grads - delta)).astype(BF16)
            refs.key_grad[...] += dot(low, query[:, :64])
            refs.value_grad[...] += dot(probs.astype(BF16), grad)
            parts.append(jnp.transpose(dot(refs.keys_t[...], low)) * HEAD_DIM ** (-0.5))
        turn_q.staged[plane] = jnp.concatenate(parts, axis=1).astype(BF16)

        @pl.when(step < PLANES - 1)
        def send():
            turn_q.copy(k).start()

        return unused

    lax.fori_loop(0, PLANES, plane_step, 0)
    turn_q.keep()
    for plane in range(PLANES):
        rows = slice(plane * 512, plane * 512 + 512)
        turn_kv.staged[plane] = jnp.concatenate(
            [refs.key_grad[rows, :], refs.value_grad[rows, :]], axis=1
        ).astype(BF16)


def attention_backward(place, refs, gather, scatter):
    def process(pair, slots, part):
        if part == 0 and pair[0] == 0:
            refs.finish_attn()
        rows = dot(place.parts.take(gather.blocks, slots, part), flat(refs.w_o), 1, 1)
        place.parts.put(refs.mix_rows, slots, part, rows.astype(BF16))
        if part == place.parts.count - 1 and pair in LAST_OF_ROW:
            row = place.row(LAST_OF_ROW[pair])
            for head in range(2):
                pack_narrow(turn_mix, row, head, refs.mix_rows)
                turn_mix.dispatch(row * 2 + head)

    turn_mix = Turn(place, refs.turn_mix)
    gather_blocks(place, gather, process)
    gather.drain()
    weights = WeightGrads(place, refs, "qkv", "qkv", False)
    weights.put_out(refs.mixed, gather.blocks)
    turned = jnp.transpose(refs.keys[...].astype(F32))
    refs.keys_t[...] = turned[:64].astype(BF16)
    refs.before_mix()
    turn_mix.wait()
    for plane in range(PLANES):
        both = turn_mix.received[plane]
        refs.mix_grads[plane * 512 : plane * 512 + 256, :] = both[:, :64]
        refs.mix_grads[plane * 512 + 256 : plane * 512 + 512, :] = both[:, 64:]
    weights.sum_out.start()
    refs.before_attend()
    turn_kv, turn_q = Turn(place, refs.turn_qk), Turn(place, refs.turn_v)
    attend_back(place, refs, turn_kv, turn_q)
    turn_kv.start()
    weights.sum_out.relay()
    refs.after_attend()
    turn_q.wait()
    turn_kv.wait()
    for slot in range(8):
        row, block = divmod(slot, 4)
        cos = refs.cos[block * 128 : block * 128 + 128, :]
        sin = refs.sin[block * 128 : block * 128 + 128, :]
        query = unpack_narrow(turn_q, row, block).astype(F32)
        key = unpack_wide(turn_kv, row, block, 0).astype(F32)
        refs.qkv_grads[slot] = jnp.concatenate(
            [
                (query * cos - swap_halves(query) * sin).astype(BF16),
                (key * cos - swap_halves(key) * sin).astype(BF16),
                unpack_wide(turn_kv, row, block, 1),
            ],
            axis=1,
        )
    scatter_blocks(
        place, scatter, lambda slots, part: place.parts.take(refs.qkv_grads, slots, part), refs.w_qkv, 1
    )
    return weights


def fill_tables(refs):
    cos, sin = refs.cos_rows[...], refs.sin_rows[...]
    refs.cos[...] = jnp.concatenate([cos] * 4, axis=1)
    refs.sin[...] = jnp.concatenate([-sin, sin] * 2, axis=1)


def fill_channels(place, refs):
    columns = columns_of(place.pair(), 128)
    refs.taps[0:KERNEL, :] = refs.all_taps[:, columns].astype(F32)
    refs.gain_inner[...] = refs.all_inner[:, columns]
    for slot in range(8):
        refs.before[slot], refs.after[slot] = segment_reach(place, refs, slot)


def table_scratch():
    return dict(
        cos=VMEM((512, 128), F32),
        sin=VMEM((512, 128), F32),
        taps=VMEM((32, 128), F32),
        gain_inner=VMEM((1, 128), F32),
        before=VMEM((8, 128, 128), F32),
        after=VMEM((8, 128, 128), F32),
    )


class Edges:
    def __init__(self, place, refs):
        self.place = place
        self.staged, self.received, self.send, self.recv = refs

    @staticmethod
    def scratch():
        return [VMEM((2, 2, 16, 128), BF16), VMEM((2, 2, 16, 128), BF16), DMA((2,)), DMA((2,))]

    def copies(self):
        place = self.place
        for side, inside, step in ((0, place.z < PLANES - 1, 1), (1, place.z > 0, -1)):
            plane = jnp.clip(place.z + step, 0, PLANES - 1)
            yield (
                side,
                inside,
                remote(
                    self.staged.at[side],
                    self.received.at[side],
                    self.send.at[side],
                    self.recv.at[side],
                    {"seq": plane * 4 + place.yc, "row": place.x},
                ),
            )

    def start(self, blocks):
        for row in range(2):
            self.staged[0, row] = blocks[row * 4 + 3, 112:128, :]
            self.staged[1, row] = blocks[row * 4, 0:16, :]
        for side, inside, copy in self.copies():

            @pl.when(inside)
            def start(copy=copy):
                copy.start()

    def wait(self, blocks, padded):
        for slot in range(8):
            row, block = divmod(slot, 4)
            padded[slot, 16:144, :] = blocks[slot].astype(F32)
            if block > 0:
                padded[slot, 0:16, :] = blocks[slot - 1, 112:128, :].astype(F32)
            if block < 3:
                padded[slot, 144:160, :] = blocks[slot + 1, 0:16, :].astype(F32)
        place = self.place
        for side, outside in ((0, place.z == 0), (1, place.z == PLANES - 1)):
            first, rows = ((0, slice(0, 16)), (3, slice(144, 160)))[side]
            into = self.received.at[side]

            @pl.when(outside)
            def nothing():
                for row in range(2):
                    padded[row * 4 + first, rows, :] = jnp.zeros((16, 128), F32)

            @pl.when(jnp.logical_not(outside))
            def arrive():
                remote(
                    into, into, self.send.at[side], self.recv.at[side], place.zdev(1)
                ).wait_recv()
                for row in range(2):
                    padded[row * 4 + first, rows, :] = self.received[side, row].astype(F32)

        for side, inside, copy in self.copies():

            @pl.when(inside)
            def drain(copy=copy):
                copy.wait_send()


def lane_is(index, rows=128):
    return lax.broadcasted_iota(jnp.int32, (rows, 128), 1) == index


def put_columns(tile, slot, first, second):
    return jnp.where(lane_is(slot), first, jnp.where(lane_is(slot + 8), second, tile))


def share_columns(place, refs, tile):
    share = Exchange(place, refs[0], refs[1:])
    own = place.slot(0)
    share.blocks[own] = jnp.transpose(tile)[:16]
    share.start(lambda k: share.blocks.at[own])
    return share


def back_to_columns(first, second):
    rows = jnp.concatenate([first, second, jnp.zeros((112, 128), F32)], axis=0)
    return jnp.transpose(rows)


def column(tile, slot):
    return jnp.sum(jnp.where(lane_is(slot, tile.shape[0]), tile, 0.0), axis=1, keepdims=True)


def kept_frames(value, offset, before, after):
    if offset < 0:
        return jnp.where(before <= offset, value, 0.0)
    if offset > 0:
        return jnp.where(after > offset, value, 0.0)
    return value


CHUNK = 64


def convolve(refs):
    taps = [refs.taps[j : j + 1, :] for j in range(KERNEL)]

    def step(slot, tile):
        for first in range(0, 128, CHUNK):
            rows = slice(first, first + CHUNK)
            before, after = refs.before[slot, rows, :], refs.after[slot, rows, :]
            total = jnp.zeros((CHUNK, 128), F32)
            for j in range(KERNEL):
                start = first + j + 1
                value = refs.glu_padded[slot, start : start + CHUNK, :]
                total = total + taps[j] * kept_frames(value, j - HALF, before, after)
            refs.conv[slot, rows, :] = total
        value = refs.conv[slot]
        mean = jnp.mean(value, axis=1, keepdims=True)
        center = value - mean
        return put_columns(tile, slot, mean, jnp.sum(center * center, axis=1, keepdims=True))

    return lax.fori_loop(0, 8, step, jnp.zeros((128, 128), F32))


def inner_norm(refs, slot, rows=slice(0, 128)):
    tile = refs.inner_stats[rows, :]
    mean, inverse = column(tile, slot), column(tile, slot + 8)
    return (refs.conv[slot, rows, :] - mean) * inverse, inverse


def conv_forward(place, refs, gather, scatter):
    def process(pair, slots, part):
        if part == 0 and pair[0] == 0:
            refs.finish_ci()
        value = dot(place.parts.take(gather.blocks, slots, part), flat(refs.w_ci))
        place.parts.put(refs.gate_up, slots, part, value)
        place.parts.put(
            refs.glu,
            slots,
            part,
            (value[:, :128] * jax.nn.sigmoid(value[:, 128:])).astype(BF16),
        )

    gather_blocks(place, gather, process)
    edges = Edges(place, refs.edges)
    edges.start(refs.glu)
    gather.drain()
    edges.wait(refs.glu, refs.glu_padded)
    share = share_columns(place, refs.stats, convolve(refs))
    refs.conv_middle()
    share.wait()
    stats = share.blocks[...]
    means, spreads = stats[:, :8], stats[:, 8:]
    mean = jnp.mean(means, axis=0)
    spread = jnp.sum(spreads + 128.0 * jnp.square(means - mean[None]), axis=0) / 1024.0
    refs.inner_stats[...] = back_to_columns(mean, lax.rsqrt(spread + EPSILON))
    refs.finish_co()

    def active_rows(slots, part):
        rows = place.parts.of(part)
        parts = []
        for slot in slots:
            unit_part, unused = inner_norm(refs, slot, rows)
            parts.append(sigmoid_linear(unit_part * refs.gain_inner[...]).astype(BF16))
        value = jnp.concatenate(parts, axis=0)
        place.parts.put(refs.conv_active, slots, part, value)
        return value

    scatter_blocks(place, scatter, active_rows, refs.w_co)


def conv_kept():
    return dict(
        conv_blocks=((8, 128, 1024), BF16),
        w_ci=((16, 64, 256), BF16),
        w_co=((2, 64, 1024), BF16),
        gate_up=((8, 128, 256), F32),
        glu_padded=((8, 160, 128), F32),
        conv=((8, 128, 128), F32),
        inner_stats=((128, 128), F32),
        conv_active=((8, 128, 128), BF16),
    )


STATS = [VMEM((8, 16, 128), F32), DMA((8,)), DMA((8,))]


def convolve_back(refs):
    taps = [refs.taps[j : j + 1, :] for j in range(KERNEL)]
    refs.tap_sums[...] = jnp.zeros_like(refs.tap_sums)

    def step(slot, unused):
        for first in range(0, 128, CHUNK):
            rows = slice(first, first + CHUNK)
            before, after = refs.before[slot, rows, :], refs.after[slot, rows, :]
            total = jnp.zeros((CHUNK, 128), F32)
            grad = refs.conv_grad_padded[slot, first + 16 : first + 16 + CHUNK, :]
            for j in range(KERNEL):
                offset = j - HALF
                start = first + 16 - offset
                value = refs.conv_grad_padded[slot, start : start + CHUNK, :]
                total = total + taps[j] * kept_frames(value, -offset, before, after)
                start = first + 16 + offset
                value = refs.glu_padded[slot, start : start + CHUNK, :]
                product = kept_frames(value * grad, offset, before, after)
                refs.tap_sums[j] += jnp.sum(product.reshape(CHUNK // 8, 8, 128), axis=0)
            refs.glu_grad[slot, rows, :] = total
        return unused

    lax.fori_loop(0, 8, step, 0)
    return jnp.sum(refs.tap_sums[...], axis=1)


def conv_backward(place, refs, gather, scatter):
    gain = refs.gain_inner[...]

    def process(pair, slots, part):
        if part == 0 and pair[0] == 0:
            refs.finish_conv()
        back = dot(place.parts.take(gather.blocks, slots, part), flat(refs.w_co), 1, 1)
        rows = place.parts.of(part)
        units = jnp.concatenate([inner_norm(refs, slot, rows)[0] for slot in slots], axis=0)
        place.parts.put(refs.inner_grad, slots, part, back * sigmoid_linear_grad(units * gain))

    gather_blocks(place, gather, process)

    def sums(slot, current):
        tile, gain_grad = current
        value = refs.inner_grad[slot]
        unit_part, unused = inner_norm(refs, slot)
        scaled = value * gain
        tile = put_columns(
            tile,
            slot,
            jnp.sum(scaled, axis=1, keepdims=True),
            jnp.sum(scaled * unit_part, axis=1, keepdims=True),
        )
        return tile, gain_grad + jnp.sum(value * unit_part, axis=0, keepdims=True)

    tile, inner_gain_grad = lax.fori_loop(
        0, 8, sums, (jnp.zeros((128, 128), F32), jnp.zeros((1, 128), F32))
    )
    share = share_columns(place, refs.stats, tile)
    weights = WeightGrads(place, refs, "conv", "conv", False)
    weights.put_out(refs.conv_active, gather.blocks)
    gather.drain()
    share.wait()
    means = jnp.sum(share.blocks[...], axis=0) / 1024.0
    refs.grad_stats[...] = back_to_columns(means[:8], means[8:])

    def input_grad(slot, unused):
        unit_part, inverse = inner_norm(refs, slot)
        tile = refs.grad_stats[...]
        refs.conv_grad[slot] = (
            inverse
            * (
                refs.inner_grad[slot] * gain
                - column(tile, slot)
                - unit_part * column(tile, slot + 8)
            )
        ).astype(BF16)
        return unused

    lax.fori_loop(0, 8, input_grad, 0)
    edges = Edges(place, refs.edges)
    edges.start(refs.conv_grad)
    refs.conv_begin()
    edges.wait(refs.conv_grad, refs.conv_grad_padded)
    weights.sum_out.start()
    tap_grads = convolve_back(refs)
    refs.conv_middle()

    def gate_rows(slots, part):
        value, glu_grad = place.parts.take(refs.gate_up, slots, part), place.parts.take(refs.glu_grad, slots, part)
        sigma = jax.nn.sigmoid(value[:, 128:])
        low = jnp.concatenate(
            [glu_grad * sigma, glu_grad * value[:, :128] * sigma * (1.0 - sigma)], axis=1
        ).astype(BF16)
        place.parts.put(refs.gate_grads, slots, part, low)
        return low

    scatter_blocks(place, scatter, gate_rows, refs.w_ci, 1)
    return inner_gain_grad, tap_grads, weights


class Traffic:
    def __init__(self, refs, sems):
        self.refs, self.sems = refs, sems
        self.count = 0

    def start(self, pairs):
        copies = []
        for source, target in pairs:
            copy = pltpu.make_async_copy(source, target, self.sems.at[self.count])
            copy.start()
            copies.append(copy)
            self.count += 1

        def finish():
            for copy in copies:
                copy.wait()

        return finish

    def save(self, names):
        return self.start(
            [(getattr(self.refs, name), getattr(self.refs, "keep_" + name)) for name in names]
        )

    def load(self, names):
        return self.start(
            [(getattr(self.refs, "keep_" + name), getattr(self.refs, name)) for name in names]
        )


def ffn_kept():
    return dict(
        blocks=((8, 128, 1024), BF16),
        hidden=((8, 128, 512), F32),
        w_in=((16, 64, 512), BF16),
        w_out=((4, 128, 1024), BF16),
    )


SCATTER_SEMS = [DMA((22,)), DMA((22,))]


def forward_body(refs):
    place = Place(FORWARD_PARTS)
    place.enter()
    traffic = Traffic(refs, refs.traffic)
    gather_in = GatherRows(place, refs.w_in_rows, refs.w_in, refs.gather_in, ffn_pieces)
    refs.row_lengths[place.x] = refs.own_lengths[...]
    lengths = remote(
        refs.own_lengths,
        refs.row_lengths.at[place.x],
        refs.length_sems.at[0],
        refs.length_sems.at[1],
        place.dev(4),
    )
    lengths.start()
    halves = (slice(0, 512), slice(512, 1024))
    gather_out = [
        GatherBlocks(place, refs.w_out_rows, refs.w_out, refs.gather_out, halves[0])
    ]
    gather = Gather(place, refs.blocks, refs.ffn_ag)
    for part in place.parts:
        frames = place.parts.of(part)
        gather.push(part, norm_rows(refs.stream[frames, :].astype(F32), refs.gain_ffn1[...])[0])
    gather_in.along_z()
    gather_out.append(
        GatherBlocks(place, refs.w_out_rows, refs.w_out, refs.gather_out_last, halves[1])
    )
    gather_qkv = GatherRows(place, refs.qkv_rows, refs.w_qkv, refs.gather_qkv, head_pieces)
    held = Refs()
    gather_out[0].relay()
    gather_blocks(place, gather, lambda pair, slots, part: None)
    gather_in.relay()
    lengths.wait()
    fill_tables(refs)
    fill_channels(place, refs)
    gather_in.finish()
    for part in place.parts:
        for group in PAIRS:
            for pair in group:
                slots = [place.slot(k) for k in pair]
                value = dot(place.parts.take(refs.blocks, slots, part), flat(refs.w_in))
                place.parts.put(refs.hidden, slots, part, value)
                place.parts.put(refs.active, slots, part, sigmoid_linear(value).astype(BF16))
    gather.drain()
    scatter = Scatter(place, refs.scatter_columns, refs.ffn_scatter)
    for half, columns in enumerate(halves):
        if half:
            gather_out[half].relay()
        gather_out[half].finish()
        if half:
            gather_qkv.along_z()
            gather_o = GatherHalf(place, refs.o_rows, refs.w_o, refs.gather_o)
        weight = refs.w_out[:, :, columns].reshape(512, 512)
        for pair in OUT_PAIRS:
            rows = jnp.concatenate([refs.active[place.slot(k)] for k in pair], axis=0)
            scatter.emit_pair(pair, half, dot(rows, weight))
        for k in (2, 4, 6, 0):
            scatter.finish(k, half)
    saved = [traffic.save(ffn_kept())]
    gather_ci = GatherRows(place, refs.ci_rows, refs.w_ci, refs.gather_ci, channel_pieces)
    gather_next = GatherRows(place, refs.next_in_rows, refs.next_in, refs.gather_next, ffn_pieces)

    def to_attention(part, total):
        frames = place.parts.of(part)
        value = refs.stream[frames, :].astype(F32) + 0.5 * total
        refs.stream_one[frames, :] = value
        return norm_rows(value, refs.gain_attn[...])[0]

    def to_conv(part, total):
        frames = place.parts.of(part)
        value = refs.stream_one[frames, :] + total
        refs.stream_two[frames, :] = value
        return norm_rows(value, refs.gain_conv[...])[0]

    gather = Gather(place, refs.attn_blocks, refs.attn_ag)
    total = jnp.concatenate([scatter.total(half) for half in range(2)], axis=1)
    for part in place.parts:
        gather.push(part, to_attention(part, total[place.parts.of(part)]))
    scatter.drain()
    gather_qkv.relay()
    gather_o.relay()

    def after_turn():
        gather_ci.along_z()
        held.co = GatherHalf(place, refs.co_rows, refs.w_co, refs.gather_co)

    def after_mix():
        gather_ci.relay()
        held.co.relay()
        gather_o.finish()
        gather_next.along_z()
        held.next_out = GatherBlocks(
            place, refs.next_out_rows, refs.next_out, refs.gather_next_out
        )

    def conv_middle():
        gather_next.relay()

    refs.after_turn, refs.after_mix, refs.conv_middle = after_turn, after_mix, conv_middle
    refs.finish_qkv, refs.finish_ci, refs.finish_co = (
        gather_qkv.finish,
        gather_ci.finish,
        lambda: held.co.finish(),
    )
    scatter = Scatter(place, refs.scatter, refs.attn_scatter)
    attention_forward(place, refs, gather, scatter)
    saved.append(traffic.save(attention_kept()))
    gather = Gather(place, refs.conv_blocks, refs.conv_ag)
    carry(place, scatter, gather, to_conv)
    scatter = Scatter(place, refs.scatter, refs.conv_scatter)
    conv_forward(place, refs, gather, scatter)
    held.next_out.relay()
    saved.append(traffic.save(conv_kept()))
    for part in place.parts:
        frames = place.parts.of(part)
        refs.stream_three[frames, :] = refs.stream_two[frames, :] + scatter.total(part)
    scatter.drain()
    gather_next.finish()
    held.next_out.finish()
    for finish in saved:
        finish()


def scratch_of(kept):
    return {name: VMEM(shape, dtype) for name, (shape, dtype) in kept.items()}


def forward_call(ins):
    kept = {**ffn_kept(), **attention_kept(), **conv_kept()}
    outs = dict(
        stream_one=((128, 1024), F32, VMEM),
        stream_two=((128, 1024), F32, VMEM),
        stream_three=((128, 1024), F32, VMEM),
        next_in=((16, 64, 512), BF16, pl.ANY),
        next_out=((4, 128, 1024), BF16, pl.ANY),
    )
    outs["row_lengths"] = ((2, 8, 128), F32, VMEM)
    for name, (shape, dtype) in kept.items():
        outs["keep_" + name] = (shape, dtype, pl.ANY)
    scratch = dict(
        scratch_of(kept),
        active=VMEM((8, 128, 512), BF16),
        gather_in=GatherRows.scratch(),
        gather_out=GatherBlocks.scratch(),
        gather_out_last=GatherBlocks.scratch(),
        gather_qkv=GatherRows.scratch(),
        gather_o=GatherHalf.scratch(),
        gather_ci=GatherRows.scratch(),
        gather_co=GatherHalf.scratch(),
        gather_next=GatherRows.scratch(),
        gather_next_out=GatherBlocks.scratch(),
        length_sems=DMA((2,)),
        **table_scratch(),
        traffic=DMA((len(kept),)),
        scatter=Scatter.scratch(FORWARD_PARTS, 128 // FORWARD_PARTS, 1024),
        scatter_columns=Scatter.scratch(2, 128, 512),
        ffn_ag=AG_SEMS,
        attn_ag=AG_SEMS,
        conv_ag=AG_SEMS,
        ffn_scatter=SCATTER_SEMS,
        attn_scatter=SCATTER_SEMS,
        conv_scatter=SCATTER_SEMS,
        q_rows=VMEM((8, 128, 128), BF16),
        k_rows=VMEM((8, 128, 128), BF16),
        v_rows=VMEM((8, 128, 128), BF16),
        turn_qk=Turn.scratch(512),
        turn_v=Turn.scratch(256),
        turn_mix=Turn.scratch(256),
        values_t=VMEM((64, 2048), BF16),
        glu=VMEM((8, 128, 128), BF16),
        edges=Edges.scratch(),
        stats=STATS,
    )
    return kernel_call(forward_body, 1, ins, outs, scratch)


class SmallSum:
    def __init__(self, place, refs):
        self.place, self.refs = place, refs
        self.first = Exchange(place, refs.small_first, refs.small_first_sems)
        self.last = Exchange(place, refs.small, refs.small_last_sems)
        self.sent = []

    def start(self):
        refs, place = self.refs, self.place

        def part(slot):
            return refs.gain_grads.at[:, columns_of(slot, 128)]

        self.first.blocks[place.slot(0)] = refs.gain_grads[:, columns_of(place.slot(0), 128)]
        self.first.start(lambda k: part(place.slot(k)))

    def along_z(self):
        refs, place = self.refs, self.place
        self.first.wait()
        refs.small_planes[place.z, 0:8, :] = jnp.sum(self.first.blocks[...], axis=0)
        refs.small_planes[place.z, 8:48, :] = refs.channel_grads[...]
        send, recv = refs.small_z_sems
        rows = refs.small_planes.at[place.z]
        for k in (1, 2, 3):
            copy = remote(rows, rows, send.at[k], recv.at[k], place.zdev(k))
            copy.start()
            self.sent.append(copy)

    def spread(self):
        refs, place = self.refs, self.place
        send, recv = refs.small_z_sems
        for k in (1, 2, 3):
            into = refs.small_planes.at[lax.rem(place.z + 4 - k, PLANES)]
            remote(into, into, send.at[k], recv.at[k], place.zdev(k)).wait_recv()
        for copy in self.sent:
            copy.wait_send()
        own = place.slot(0)
        self.last.blocks[own] = jnp.sum(refs.small_planes[...], axis=0)
        self.last.start(lambda k: self.last.blocks.at[own])

    def wait(self):
        self.last.wait()


def backward_step(place, refs, stream, gain, row, scale):
    saved = [
        norm_forward(stream[place.parts.of(part), :].astype(F32), gain)[1] for part in place.parts
    ]

    def step(part, total):
        frames = place.parts.of(part)
        input_part, gain_grad = norm_input_grad(total, gain, saved[part])
        value = refs.grad_stream[frames, :] + input_part
        refs.grad_stream[frames, :] = value
        refs.gain_grads[row : row + 1, :] += gain_grad
        return (scale * value).astype(BF16)

    return step


def backward_body(refs):
    place = Place(BACKWARD_PARTS)
    place.enter()
    traffic = Traffic(refs, refs.traffic)
    ready = traffic.start([(refs.next_in, refs.w_in), (refs.next_out, refs.w_out)])
    gather = Gather(place, refs.blocks, refs.ffn2_ag)
    for part in place.parts:
        frames = place.parts.of(part)
        gather.push(part, norm_rows(refs.stream_three[frames, :], refs.gain_ffn2[...])[0])
    refs.finish_conv = traffic.load(conv_kept())
    refs.finish_attn = traffic.load(attention_kept())
    refs.gain_grads[...] = jnp.zeros_like(refs.gain_grads)
    refs.channel_grads[...] = jnp.zeros_like(refs.channel_grads)
    scatter = Scatter(place, refs.scatter, refs.ffn2_scatter)
    ffn_forward(place, gather, refs.hidden, refs.w_in, refs.w_out, scatter, ready)
    gather.drain()
    fill_tables(refs)
    fill_channels(place, refs)

    def turn_round(part, total):
        frames = place.parts.of(part)
        final, saved = norm_forward(refs.stream_three[frames, :] + 0.5 * total, refs.gain_out[...])
        refs.output[frames, :] = final.astype(BF16)
        grad, gain_grad = norm_input_grad(
            refs.cotangent[frames, :].astype(F32), refs.gain_out[...], saved
        )
        refs.grad_stream[frames, :] = grad
        refs.gain_grads[4:5, :] += gain_grad
        return (0.5 * grad).astype(BF16)

    gather = Gather(place, refs.grads_even, refs.ffn2_ag_back)
    carry(place, scatter, gather, turn_round)
    scatter = Scatter(place, refs.scatter, refs.ffn2_scatter_back)
    ffn_backward(
        place,
        gather,
        refs.hidden,
        refs.hidden_grads,
        refs.active,
        refs.w_in,
        refs.w_out,
        scatter,
        lambda: None,
    )
    gather.drain()
    step = backward_step(place, refs, refs.stream_three, refs.gain_ffn2[...], 3, 1.0)
    weights_two = WeightGrads(place, refs, "ffn2", "ffn", True)
    weights_two.put_both(refs.active, refs.grads_even, refs.blocks, refs.hidden_grads)
    gather = Gather(place, refs.grads_odd, refs.conv_ag)
    carry(place, scatter, gather, step)
    load_first = traffic.load(ffn_kept())
    refs.conv_begin, refs.conv_middle = weights_two.sum_out.relay, weights_two.sum_in.relay
    scatter = Scatter(place, refs.scatter, refs.conv_scatter)
    inner, taps, weights_three = conv_backward(place, refs, gather, scatter)
    step = backward_step(place, refs, refs.stream_two, refs.gain_conv[...], 2, 1.0)
    refs.channel_grads[0:32, :] = taps
    refs.channel_grads[32:33, :] = inner
    weights_three.put_in(refs.conv_blocks, refs.gate_grads)
    gather = Gather(place, refs.grads_even, refs.attn_ag)
    carry(place, scatter, gather, step)

    refs.before_mix = weights_two.share
    refs.before_attend, refs.after_attend = weights_three.relay, weights_three.share
    scatter = Scatter(place, refs.scatter, refs.attn_scatter)
    weights_four = attention_backward(place, refs, gather, scatter)
    step = backward_step(place, refs, refs.stream_one, refs.gain_attn[...], 1, 0.5)
    weights_four.put_in(refs.attn_blocks, refs.qkv_grads)
    gather = Gather(place, refs.grads_odd, refs.ffn1_ag)
    carry(place, scatter, gather, step)
    weights_two.wait()
    weights_three.wait()
    scatter = Scatter(place, refs.scatter, refs.ffn1_scatter)
    ffn_backward(
        place,
        gather,
        refs.hidden,
        refs.hidden_grads,
        refs.active,
        refs.w_in,
        refs.w_out,
        scatter,
        load_first,
    )
    gather.drain()
    weights_one = WeightGrads(place, refs, "ffn1", "ffn", True)
    weights_one.put_both(refs.active, refs.grads_odd, refs.blocks, refs.hidden_grads)
    weights_four.sum_in.relay()
    weights_four.share()
    weights_one.sum_out.relay()
    step = backward_step(place, refs, refs.stream, refs.gain_ffn1[...], 0, 1.0)
    for part in place.parts:
        step(part, scatter.total(part))
    scatter.drain()
    small = SmallSum(place, refs)
    small.start()
    weights_one.sum_in.relay()
    small.along_z()
    small.spread()
    weights_four.wait()
    weights_one.share()
    small.wait()
    weights_one.wait()


MODULES = (("ffn1", 512, True), ("qkv", 384, False), ("conv", 256, False), ("ffn2", 512, True))


def backward_call(ins):
    kept = {**ffn_kept(), **attention_kept(), **conv_kept()}
    outs = dict(
        output=((128, 1024), BF16, VMEM),
        grad_stream=((128, 1024), F32, VMEM),
        small=((8, 48, 128), F32, VMEM),
    )
    scratch = dict(
        scratch_of(kept),
        active=VMEM((8, 128, 512), BF16),
        hidden_grads=VMEM((8, 128, 512), BF16),
        grads_even=VMEM((8, 128, 1024), BF16),
        grads_odd=VMEM((8, 128, 1024), BF16),
        traffic=DMA((2 + len(kept),)),
        scatter=Scatter.scratch(BACKWARD_PARTS, 128 // BACKWARD_PARTS, 1024),
        ffn2_ag=AG_SEMS,
        ffn2_ag_back=AG_SEMS,
        conv_ag=AG_SEMS,
        attn_ag=AG_SEMS,
        ffn1_ag=AG_SEMS,
        ffn2_scatter=SCATTER_SEMS,
        ffn2_scatter_back=SCATTER_SEMS,
        conv_scatter=SCATTER_SEMS,
        attn_scatter=SCATTER_SEMS,
        ffn1_scatter=SCATTER_SEMS,
        mix_rows=VMEM((8, 128, 128), BF16),
        mix_grads=VMEM((2048, 64), BF16),
        keys_t=VMEM((64, 2048), BF16),
        turn_qk=Turn.scratch(512),
        turn_v=Turn.scratch(256),
        turn_mix=Turn.scratch(256),
        key_grad=VMEM((2048, 64), F32),
        value_grad=VMEM((2048, 64), F32),
        qkv_grads=VMEM((8, 128, 384), BF16),
        **table_scratch(),
        inner_grad=VMEM((8, 128, 128), F32),
        grad_stats=VMEM((128, 128), F32),
        conv_grad=VMEM((8, 128, 128), BF16),
        conv_grad_padded=VMEM((8, 160, 128), F32),
        glu_grad=VMEM((8, 128, 128), F32),
        gate_grads=VMEM((8, 128, 256), BF16),
        tap_sums=VMEM((32, 8, 128), F32),
        edges=Edges.scratch(),
        stats=STATS,
        gain_grads=VMEM((8, 1024), F32),
        channel_grads=VMEM((40, 128), F32),
        small_first=VMEM((8, 8, 128), F32),
        small_planes=VMEM((PLANES, 48, 128), F32),
        small_first_sems=[DMA((8,)), DMA((8,))],
        small_z_sems=[DMA((4,)), DMA((4,))],
        small_last_sems=[DMA((8,)), DMA((8,))],
        **WeightGrads.sums("ffn", 512, True),
        **WeightGrads.sums("qkv", 384, False),
        **WeightGrads.sums("conv", 256, False),
    )
    for name, width, wide in MODULES:
        outs.update(WeightGrads.outs(name, width, wide))
        scratch.update(WeightGrads.scratch(name, width, wide))
    return kernel_call(backward_body, 2, ins, outs, scratch)


def unpack_body(count, *refs):
    sources, outs = refs[:count], refs[count : 2 * count + 8]
    (
        output,
        grad_stream,
        small,
        ffn1_in,
        ffn1_out,
        qkv_in,
        qkv_out,
        conv_in,
        conv_out,
        ffn2_in,
        ffn2_out,
    ) = sources
    outs[0][...] = output[...]
    outs[1][...] = grad_stream[...]
    for slot in range(8):
        x, yc = divmod(slot, 4)
        pair = ((x * 2 + yc % 2) * 2 + yc // 2) * 128
        for index, row in enumerate((0, 1, 2, None, 3, 4)):
            if row is not None:
                outs[2 + index][:, slot * 128 : slot * 128 + 128] = small[slot, row : row + 1, :]
        outs[5][:, pair : pair + 128] = small[slot, 40:41, :]
        outs[8][:, pair : pair + 128] = small[slot, 8 : 8 + KERNEL, :]
        for source, out in ((ffn1_in, outs[9]), (ffn2_in, outs[15])):
            for plane in range(PLANES):
                column = ((plane * 4 + yc) * 2 + x) * 128
                out[:, column : column + 128] = source[
                    slot, :, plane * 128 : plane * 128 + 128
                ].astype(F32)
        for source, out, kinds in ((qkv_in, outs[11], 3), (conv_in, outs[13], 2)):
            for kind in range(kinds):
                column = kind * 1024 + pair
                out[:, column : column + 128] = source[slot, :, kind * 128 : kind * 128 + 128].astype(
                    F32
                )
    for source, out in ((ffn1_out, outs[10]), (ffn2_out, outs[16])):
        out[0:128, :] = source[0].astype(F32)
        out[128:256, :] = source[1].astype(F32)
    outs[12][...] = qkv_out[...].astype(F32)
    outs[14][...] = conv_out[...].astype(F32)


def unpack_call(backward):
    arrays = list(backward.values())
    gain = jax.ShapeDtypeStruct((1, 1024), F32)
    shapes = [
        jax.ShapeDtypeStruct((128, 1024), BF16),
        jax.ShapeDtypeStruct((128, 1024), F32),
        *[gain] * 6,
        jax.ShapeDtypeStruct((KERNEL, 1024), F32),
    ] + [
        jax.ShapeDtypeStruct(shape, F32)
        for shape in (
            (64, 4096),
            (256, 1024),
            (64, 3072),
            (64, 1024),
            (64, 2048),
            (64, 1024),
            (64, 4096),
            (256, 1024),
        )
    ]
    whole = pl.BlockSpec(memory_space=VMEM)
    return pl.pallas_call(
        functools.partial(unpack_body, len(arrays)),
        out_shape=shapes,
        in_specs=[whole] * len(arrays),
        out_specs=[whole] * len(shapes),
        compiler_params=pltpu.CompilerParams(vmem_limit_bytes=VMEM_LIMIT),
    )(*arrays)


def local_planes(
    inputs,
    lengths,
    gain_ffn1,
    gain_attn,
    gain_conv,
    gain_inner,
    gain_ffn2,
    gain_out,
    conv_kernel,
    ffn1_in,
    ffn1_out,
    attn_qkv,
    attn_out,
    conv_in,
    conv_out,
    ffn2_in,
    ffn2_out,
    cotangent,
):
    plane = lax.axis_index("seq") // 4
    cos, sin = rotary_tables(plane * 512 + jnp.arange(512, dtype=jnp.int32))
    shared = dict(
        stream=(inputs[0], VMEM),
        gain_ffn1=(gain_ffn1[None], VMEM),
        gain_attn=(gain_attn[None], VMEM),
        gain_conv=(gain_conv[None], VMEM),
        all_inner=(gain_inner[None], VMEM),
        all_taps=(conv_kernel, VMEM),
        cos_rows=(cos, VMEM),
        sin_rows=(sin, VMEM),
    )
    forward = forward_call(
        dict(
            shared,
            own_lengths=(jnp.pad(lengths.astype(F32), ((0, 7), (0, 124))), VMEM),
            w_in_rows=(ffn1_in, pl.ANY),
            w_out_rows=(ffn1_out, pl.ANY),
            qkv_rows=(attn_qkv, pl.ANY),
            o_rows=(attn_out, pl.ANY),
            ci_rows=(conv_in, pl.ANY),
            co_rows=(conv_out, pl.ANY),
            next_in_rows=(ffn2_in, pl.ANY),
            next_out_rows=(ffn2_out, pl.ANY),
        )
    )
    ins = dict(
        shared,
        cotangent=(cotangent[0], VMEM),
        gain_ffn2=(gain_ffn2[None], VMEM),
        gain_out=(gain_out[None], VMEM),
    )
    for name, array in forward.items():
        held = name.startswith("stream") or name == "row_lengths"
        ins[name] = (array, VMEM if held else pl.ANY)
    results = unpack_call(backward_call(ins))
    return (
        results[0][None],
        results[1][None],
        *[gain[0] for gain in results[2:8]],
        *results[8:],
    )


def solution(mesh):
    return jax.shard_map(
        local_planes if mesh.shape["seq"] == 16 and mesh.shape["row"] == 2 else local,
        mesh=mesh,
        in_specs=(
            P("row", "seq", None),
            P("row", None),
            P(),
            P(),
            P(),
            P(),
            P(),
            P(),
            P(),
            P("seq", None),
            P("seq", None),
            P("seq", None),
            P("seq", None),
            P("seq", None),
            P("seq", None),
            P("seq", None),
            P("seq", None),
            P("row", "seq", None),
        ),
        out_specs=(
            P("row", "seq", None),
            P("row", "seq", None),
            P(),
            P(),
            P(),
            P(),
            P(),
            P(),
            P(),
            P("seq", None),
            P("seq", None),
            P("seq", None),
            P("seq", None),
            P("seq", None),
            P("seq", None),
            P("seq", None),
            P("seq", None),
        ),
        check_vma=False,
    )
```

```python
import functools
import math

import jax
import jax.numpy as jnp
from jax import lax
from jax.experimental import pallas as pl
from jax.experimental.pallas import tpu as pltpu
from jax.sharding import PartitionSpec as P

HEADS = 16
HEAD_DIM = 64
KERNEL = 31
HALF = 15


EPSILON = 1e-05
MASKED = -1e30


def with_halo(block, sides, width):
    for axis, dim in sides:
        count = lax.axis_size(axis)
        forward = [(i, i + 1) for i in range(count - 1)]
        backward = [(target, source) for source, target in forward]
        low = lax.ppermute(
            lax.slice_in_dim(block, block.shape[dim] - width, None, axis=dim), axis, forward
        )
        high = lax.ppermute(lax.slice_in_dim(block, 0, width, axis=dim), axis, backward)
        block = jnp.concatenate([low, block, high], axis=dim)
    return block


def shifted(array, axis, by):
    size = lax.axis_size(axis)
    return lax.ppermute(array, axis, [(i, (i + by) % size) for i in range(size)])


def segment_of(positions, seg_lengths):
    boundary = jnp.cumsum(seg_lengths)[:-1]
    return jnp.sum((positions[:, None] >= boundary[None, :]).astype(jnp.int32), axis=1)


def rotary_tables(positions):
    half_dim = HEAD_DIM // 2
    inverse = jnp.exp(-jnp.log(10000.0) * jnp.arange(half_dim, dtype=jnp.float32) / half_dim)
    angles = positions.astype(jnp.float32)[:, None] * inverse[None, :]
    return (jnp.cos(angles), jnp.sin(angles))


def split_heads(values):
    return values.reshape(values.shape[0], HEADS, HEAD_DIM)


def rotate(values, cos_table, sin_table):
    half_dim = HEAD_DIM // 2
    shaped = split_heads(values)
    first_half = shaped[..., :half_dim]
    second_half = shaped[..., half_dim:]
    cos_heads = cos_table[:, None, :]
    sin_heads = sin_table[:, None, :]
    turned = jnp.concatenate(
        [
            first_half * cos_heads - second_half * sin_heads,
            second_half * cos_heads + first_half * sin_heads,
        ],
        axis=-1,
    )
    return turned.reshape(values.shape)


def unrotate(grads, cos_table, sin_table):
    half_dim = HEAD_DIM // 2
    shaped = split_heads(grads)
    first_half = shaped[..., :half_dim]
    second_half = shaped[..., half_dim:]
    cos_heads = cos_table[:, None, :]
    sin_heads = sin_table[:, None, :]
    turned = jnp.concatenate(
        [
            first_half * cos_heads + second_half * sin_heads,
            second_half * cos_heads - first_half * sin_heads,
        ],
        axis=-1,
    )
    return turned.reshape(grads.shape)


def norm_forward(values, gain):
    center = values - jnp.mean(values, axis=-1, keepdims=True)
    spread = jnp.mean(center * center, axis=-1, keepdims=True)
    inverse = lax.rsqrt(spread + EPSILON)
    unit_part = center * inverse
    return (unit_part * gain, (unit_part, inverse))


def norm_backward(grads, gain, saved):
    unit_part, inverse = saved
    scaled = grads * gain
    gain_grad = jnp.sum(grads * unit_part, axis=0)
    input_part = inverse * (
        scaled
        - jnp.mean(scaled, axis=-1, keepdims=True)
        - unit_part * jnp.mean(scaled * unit_part, axis=-1, keepdims=True)
    )
    return (input_part, gain_grad)


def sigmoid_linear(values):
    return values * jax.nn.sigmoid(values)


def sigmoid_linear_grad(values):
    sigma = jax.nn.sigmoid(values)
    return sigma * (1.0 + values * (1.0 - sigma))


def project(left_side, weight):
    return (
        jnp.dot(
            left_side,
            lax.all_gather(weight, "seq", axis=0, tiled=True),
            preferred_element_type=jnp.float32,
        ),
        weight,
    )


def project_back(grad_side, weight):
    return lax.dot_general(
        grad_side,
        lax.all_gather(weight, "seq", axis=0, tiled=True),
        (((1,), (1,)), ((), ())),
        preferred_element_type=jnp.float32,
    )


def weight_grad(left_side, grad_side):
    return lax.psum_scatter(
        lax.dot_general(
            left_side, grad_side, (((0,), (0,)), ((), ())), preferred_element_type=jnp.float32
        ).astype(jnp.bfloat16),
        "seq",
        scatter_dimension=0,
        tiled=True,
    ).astype(jnp.float32)


def over_blocks(advance, running, pieces):
    total_rows = pieces[0].shape[0]
    block_size = math.gcd(total_rows, 512)
    number = total_rows // block_size
    stacked = tuple((piece.reshape((number, block_size) + piece.shape[1:]) for piece in pieces))

    def scan_step(current, block_item):
        block_index, blocks = block_item
        return (advance(current, blocks, block_index * block_size), None)

    running, unused = lax.scan(scan_step, running, (jnp.arange(number, dtype=jnp.int32), stacked))
    return running


def block_scores(query_heads, key_heads, query_segments, key_segments):
    scale = HEAD_DIM ** (-0.5)
    raw_scores = (
        jnp.einsum("qhd,khd->hqk", query_heads, key_heads, preferred_element_type=jnp.float32)
        * scale
    )
    return jnp.where((query_segments[:, None] == key_segments[None, :])[None], raw_scores, MASKED)


def pair_grads(
    query_rows, grad_rows, log_total, delta, query_segments, key_rows, value_rows, key_segments
):
    scale = HEAD_DIM ** (-0.5)
    query_heads = split_heads(query_rows)
    grad_heads = split_heads(grad_rows)
    key_heads = split_heads(key_rows)
    value_heads = split_heads(value_rows)
    probs = jnp.exp(
        block_scores(query_heads, key_heads, query_segments, key_segments) - log_total[:, :, None]
    )
    prob_grads = jnp.einsum(
        "qhd,khd->hqk", grad_heads, value_heads, preferred_element_type=jnp.float32
    )
    score_grads = (probs * (prob_grads - delta[:, :, None])).astype(jnp.bfloat16)
    query_grad = (
        jnp.einsum("hqk,khd->qhd", score_grads, key_heads, preferred_element_type=jnp.float32)
        * scale
    )
    key_grad = (
        jnp.einsum("hqk,qhd->khd", score_grads, query_heads, preferred_element_type=jnp.float32)
        * scale
    )
    value_grad = jnp.einsum(
        "hqk,qhd->khd", probs.astype(jnp.bfloat16), grad_heads, preferred_element_type=jnp.float32
    )
    return (
        query_grad.reshape(query_rows.shape),
        key_grad.reshape(key_rows.shape),
        value_grad.reshape(value_rows.shape),
    )


def local(
    inputs,
    lengths,
    gain_ffn1,
    gain_attn,
    gain_conv,
    gain_inner,
    gain_ffn2,
    gain_out,
    conv_kernel,
    ffn1_in,
    ffn1_out,
    attn_qkv,
    attn_out,
    conv_in,
    conv_out,
    ffn2_in,
    ffn2_out,
    cotangent,
):
    frame_count = inputs.shape[1]
    model_width = inputs.shape[2]
    device_count = lax.axis_size("seq")
    position_index = lax.axis_index("seq")
    seg_lengths = lengths[0]
    first_frame = position_index * frame_count
    local_frames = jnp.arange(frame_count, dtype=jnp.int32)
    positions = first_frame + local_frames
    query_segments = segment_of(positions, seg_lengths)
    cos_table, sin_table = rotary_tables(positions)
    stream = inputs[0].astype(jnp.float32)
    normed_one, saved_one = norm_forward(stream, gain_ffn1)
    normed_one_low = normed_one.astype(jnp.bfloat16)
    hidden_one, kept_ffn1_in = project(normed_one_low, ffn1_in)
    active_one = sigmoid_linear(hidden_one).astype(jnp.bfloat16)
    branch_one, kept_ffn1_out = project(active_one, ffn1_out)
    stream_one = stream + 0.5 * branch_one
    normed_two, saved_two = norm_forward(stream_one, gain_attn)
    normed_two_low = normed_two.astype(jnp.bfloat16)
    projected, kept_qkv = project(normed_two_low, attn_qkv)
    query_low = rotate(projected[:, :model_width], cos_table, sin_table).astype(jnp.bfloat16)
    key_low = rotate(projected[:, model_width : 2 * model_width], cos_table, sin_table).astype(
        jnp.bfloat16
    )
    value_low = projected[:, 2 * model_width :].astype(jnp.bfloat16)
    query_heads = split_heads(query_low)

    def stats_step(current, blocks, first_row):
        top_score, denominator = current
        key_block = blocks[0]
        key_segments = segment_of(
            first_row + jnp.arange(key_block.shape[0], dtype=jnp.int32), seg_lengths
        )
        masked = block_scores(query_heads, split_heads(key_block), query_segments, key_segments)
        new_top = jnp.maximum(top_score, jnp.max(masked, axis=-1))
        denominator = denominator * jnp.exp(top_score - new_top) + jnp.sum(
            jnp.exp(masked - new_top[:, :, None]), axis=-1
        )
        return (new_top, denominator)

    top_init = jnp.full((HEADS, frame_count), MASKED, jnp.float32)
    total_init = jnp.zeros((HEADS, frame_count), jnp.float32)
    top_score, denominator = over_blocks(
        stats_step, (top_init, total_init), (lax.all_gather(key_low, "seq", axis=0, tiled=True),)
    )
    log_total = top_score + jnp.log(denominator)

    def value_step(current, blocks, first_row):
        mixed_sum, rest_sum = current
        key_block, value_block = blocks
        key_segments = segment_of(
            first_row + jnp.arange(key_block.shape[0], dtype=jnp.int32), seg_lengths
        )
        probs = jnp.exp(
            block_scores(query_heads, split_heads(key_block), query_segments, key_segments)
            - log_total[:, :, None]
        )
        probs_high = probs.astype(jnp.bfloat16)
        probs_rest = (probs - probs_high.astype(jnp.float32)).astype(jnp.bfloat16)
        value_heads = split_heads(value_block)
        mixed_sum = mixed_sum + jnp.einsum(
            "hqk,khd->qhd", probs_high, value_heads, preferred_element_type=jnp.float32
        )
        rest_sum = rest_sum + jnp.einsum(
            "hqk,khd->qhd", probs_rest, value_heads, preferred_element_type=jnp.float32
        )
        return (mixed_sum, rest_sum)

    zero_heads = jnp.zeros((frame_count, HEADS, HEAD_DIM), jnp.float32)
    mixed_sum, rest_sum = over_blocks(
        value_step,
        (zero_heads, zero_heads),
        (
            lax.all_gather(key_low, "seq", axis=0, tiled=True),
            lax.all_gather(value_low, "seq", axis=0, tiled=True),
        ),
    )
    exact_sum = mixed_sum + rest_sum
    mixed_low = mixed_sum.reshape(frame_count, model_width).astype(jnp.bfloat16)
    branch_two, kept_attn_out = project(mixed_low, attn_out)
    stream_two = stream_one + branch_two
    normed_three, saved_three = norm_forward(stream_two, gain_conv)
    normed_three_low = normed_three.astype(jnp.bfloat16)
    gate_up, kept_conv_in = project(normed_three_low, conv_in)
    first_part = gate_up[:, :model_width]
    gate_sigma = jax.nn.sigmoid(gate_up[:, model_width:])
    glu_low = (first_part * gate_sigma).astype(jnp.bfloat16)
    padded = with_halo(glu_low, (("seq", 0),), HALF).astype(jnp.float32)
    padded_segments = segment_of(
        first_frame - HALF + jnp.arange(frame_count + 2 * HALF, dtype=jnp.int32), seg_lengths
    )
    kernel_taps = conv_kernel.astype(jnp.float32)
    conv_values = jnp.zeros((frame_count, model_width), jnp.float32)
    for offset in range(KERNEL):
        same_segment = (padded_segments[offset : offset + frame_count] == query_segments).astype(
            jnp.float32
        )
        conv_values = (
            conv_values
            + kernel_taps[offset] * padded[offset : offset + frame_count] * same_segment[:, None]
        )
    normed_four, saved_four = norm_forward(conv_values, gain_inner)
    active_four = sigmoid_linear(normed_four).astype(jnp.bfloat16)
    branch_three, kept_conv_out = project(active_four, conv_out)
    stream_three = stream_two + branch_three
    normed_five, saved_five = norm_forward(stream_three, gain_ffn2)
    normed_five_low = normed_five.astype(jnp.bfloat16)
    hidden_two, kept_ffn2_in = project(normed_five_low, ffn2_in)
    active_two = sigmoid_linear(hidden_two).astype(jnp.bfloat16)
    branch_four, kept_ffn2_out = project(active_two, ffn2_out)
    stream_four = stream_three + 0.5 * branch_four
    final_norm, saved_six = norm_forward(stream_four, gain_out)
    output = final_norm.astype(jnp.bfloat16)[None]
    grad_four, grad_gain_six = norm_backward(cotangent[0].astype(jnp.float32), gain_out, saved_six)
    out_two_low = (0.5 * grad_four).astype(jnp.bfloat16)
    grad_ffn_two_out = weight_grad(active_two, out_two_low)
    hidden_two_low = (project_back(out_two_low, ffn2_out) * sigmoid_linear_grad(hidden_two)).astype(
        jnp.bfloat16
    )
    grad_ffn_two_in = weight_grad(normed_five_low, hidden_two_low)
    input_part, grad_gain_five = norm_backward(
        project_back(hidden_two_low, ffn2_in), gain_ffn2, saved_five
    )
    grad_three = grad_four + input_part
    conv_out_low = grad_three.astype(jnp.bfloat16)
    grad_conv_weight_out = weight_grad(active_four, conv_out_low)
    active_grad = project_back(conv_out_low, conv_out) * sigmoid_linear_grad(normed_four)
    conv_grad, grad_gain_four = norm_backward(active_grad, gain_inner, saved_four)
    conv_grad_low = conv_grad.astype(jnp.bfloat16)
    conv_grad_value = conv_grad_low.astype(jnp.float32)
    rim_grad = with_halo(conv_grad_low, (("seq", 0),), HALF).astype(jnp.float32)
    tap_grads = []
    glu_grad = jnp.zeros((frame_count, model_width), jnp.float32)
    for offset in range(KERNEL):
        same_segment = (padded_segments[offset : offset + frame_count] == query_segments).astype(
            jnp.float32
        )
        tap_grads.append(
            jnp.sum(
                padded[offset : offset + frame_count] * same_segment[:, None] * conv_grad_value,
                axis=0,
            )
        )
        back_start = 2 * HALF - offset
        back_segment = (
            padded_segments[back_start : back_start + frame_count] == query_segments
        ).astype(jnp.float32)
        glu_grad = (
            glu_grad
            + kernel_taps[offset]
            * rim_grad[back_start : back_start + frame_count]
            * back_segment[:, None]
        )
    kernel_grad = jnp.stack(tap_grads, axis=0)
    gate_up_low = jnp.concatenate(
        [glu_grad * gate_sigma, glu_grad * first_part * gate_sigma * (1.0 - gate_sigma)], axis=1
    ).astype(jnp.bfloat16)
    grad_conv_weight_in = weight_grad(normed_three_low, gate_up_low)
    input_part, grad_gain_three = norm_backward(
        project_back(gate_up_low, conv_in), gain_conv, saved_three
    )
    grad_two = grad_three + input_part
    attn_grad_low = grad_two.astype(jnp.bfloat16)
    grad_attn_weight = weight_grad(mixed_low, attn_grad_low)
    mixed_grad_low = project_back(attn_grad_low, attn_out).astype(jnp.bfloat16)
    delta = jnp.transpose(
        jnp.sum(split_heads(mixed_grad_low).astype(jnp.float32) * exact_sum, axis=-1)
    )

    def key_turn(turn_index, current):
        key_rows, value_rows, key_acc, value_acc, query_acc = current
        owner = (position_index - turn_index) % device_count
        key_segments = segment_of(owner * frame_count + local_frames, seg_lengths)
        query_part, key_part, value_part = pair_grads(
            query_low,
            mixed_grad_low,
            log_total,
            delta,
            query_segments,
            key_rows,
            value_rows,
            key_segments,
        )
        key_rows, value_rows = shifted((key_rows, value_rows), "seq", 1)
        key_acc, value_acc = (
            shifted((key_acc + key_part).astype(jnp.bfloat16), "seq", 1).astype(jnp.float32),
            shifted((value_acc + value_part).astype(jnp.bfloat16), "seq", 1).astype(jnp.float32),
        )
        return (key_rows, value_rows, key_acc, value_acc, query_acc + query_part)

    zero_rows = jnp.zeros((frame_count, model_width), jnp.float32)
    unused_keys, unused_values, key_grad, value_grad, query_grad = lax.fori_loop(
        0, device_count, key_turn, (key_low, value_low, zero_rows, zero_rows, zero_rows)
    )
    projected_grad_low = jnp.concatenate(
        [
            unrotate(query_grad, cos_table, sin_table),
            unrotate(key_grad, cos_table, sin_table),
            value_grad,
        ],
        axis=1,
    ).astype(jnp.bfloat16)
    grad_qkv_weight = weight_grad(normed_two_low, projected_grad_low)
    input_part, grad_gain_two = norm_backward(
        project_back(projected_grad_low, attn_qkv), gain_attn, saved_two
    )
    grad_one = grad_two + input_part
    out_one_low = (0.5 * grad_one).astype(jnp.bfloat16)
    grad_ffn_one_out = weight_grad(active_one, out_one_low)
    hidden_one_low = (project_back(out_one_low, ffn1_out) * sigmoid_linear_grad(hidden_one)).astype(
        jnp.bfloat16
    )
    grad_ffn_one_in = weight_grad(normed_one_low, hidden_one_low)
    input_part, grad_gain_one = norm_backward(
        project_back(hidden_one_low, ffn1_in), gain_ffn1, saved_one
    )
    input_grad = (grad_one + input_part)[None]
    small_grads = lax.psum(
        (
            grad_gain_one,
            grad_gain_two,
            grad_gain_three,
            grad_gain_four,
            grad_gain_five,
            grad_gain_six,
            kernel_grad,
        ),
        ("seq", "row"),
    )
    large_grads = (
        grad_ffn_one_in,
        grad_ffn_one_out,
        grad_qkv_weight,
        grad_attn_weight,
        grad_conv_weight_in,
        grad_conv_weight_out,
        grad_ffn_two_in,
        grad_ffn_two_out,
    )
    large_grads = (
        lax.psum(grad_ffn_one_in.astype(jnp.bfloat16), "row").astype(jnp.float32),
        lax.psum(grad_ffn_one_out.astype(jnp.bfloat16), "row").astype(jnp.float32),
        lax.psum(grad_qkv_weight.astype(jnp.bfloat16), "row").astype(jnp.float32),
        lax.psum(grad_attn_weight.astype(jnp.bfloat16), "row").astype(jnp.float32),
        lax.psum(grad_conv_weight_in.astype(jnp.bfloat16), "row").astype(jnp.float32),
        lax.psum(grad_conv_weight_out.astype(jnp.bfloat16), "row").astype(jnp.float32),
        lax.psum(grad_ffn_two_in.astype(jnp.bfloat16), "row").astype(jnp.float32),
        lax.psum(grad_ffn_two_out.astype(jnp.bfloat16), "row").astype(jnp.float32),
    )
    return (
        output,
        input_grad,
        small_grads[0],
        small_grads[1],
        small_grads[2],
        small_grads[3],
        small_grads[4],
        small_grads[5],
        small_grads[6],
        large_grads[0],
        large_grads[1],
        large_grads[2],
        large_grads[3],
        large_grads[4],
        large_grads[5],
        large_grads[6],
        large_grads[7],
    )


BF16 = jnp.bfloat16
F32 = jnp.float32
PLANES = 4
VMEM = pltpu.VMEM
DMA = pltpu.SemaphoreType.DMA
VMEM_LIMIT = 60 * 1024 * 1024
FORWARD_PARTS = 1
BACKWARD_PARTS = 1


class Place:
    def __init__(self, parts):
        self.parts = Parts(parts)
        seq = lax.axis_index("seq")
        self.x = lax.axis_index("row")
        self.z = seq // 4
        self.yc = lax.rem(seq, 4)
        self.core = lax.rem(self.yc, 2)
        inside = lax.rem(self.z + self.z // 2, 2)
        self.end, self.middle = inside == 0, inside == 1
        self.beside, self.across, self.opposite = self.line(1 - inside), self.line(2), self.line(3)

    def flip(self, k):
        y, c, x = self.yc // 2, lax.rem(self.yc, 2), self.x
        c = 1 - c if k & 1 else c
        y = 1 - y if k & 2 else y
        x = 1 - x if k & 4 else x
        return x, y * 2 + c

    def dev(self, k):
        x, yc = self.flip(k)
        return {"seq": self.z * 4 + yc, "row": x}

    def slot(self, k):
        x, yc = self.flip(k)
        return x * 4 + yc

    def row(self, k):
        return self.flip(k)[0]

    def zdev(self, k):
        return self.at(lax.rem(self.z + k, PLANES))

    def at(self, plane, yc=None):
        return {"seq": plane * 4 + (self.yc if yc is None else yc), "row": self.x}

    def line(self, index):
        return index + self.z // 2 * (3 - 2 * index)

    def pair(self, x=None, yc=None):
        x = self.x if x is None else x
        yc = self.yc if yc is None else yc
        return (x * 2 + lax.rem(yc, 2)) * 2 + yc // 2

    def enter(self):
        barrier = pltpu.get_barrier_semaphore()
        partners = [self.dev(k) for k in range(1, 8)]
        for k in range(1, PLANES):
            plane = lax.rem(self.z + k, PLANES)
            partners += [self.at(plane), self.at(plane, self.flip(1)[1])]
        for partner in partners:
            pl.semaphore_signal(barrier, inc=1, device_id=partner)
        pl.semaphore_wait(barrier, len(partners))


def remote(src, dst, send_sem, recv_sem, dev):
    return pltpu.make_async_remote_copy(src, dst, send_sem, recv_sem, device_id=dev)


def dot(left, right, left_dim=1, right_dim=0):
    return lax.dot_general(
        left, right, (((left_dim,), (right_dim,)), ((), ())), preferred_element_type=F32
    )


PAIRS = (((0, 1),), ((2, 4), (3, 5)), ((6, 7),))
LAST_OF_ROW = {(3, 5): 0, (6, 7): 4}
OUT_PAIRS = ((7, 3), (5, 1), (6, 2), (4, 0))


class Parts:
    def __init__(self, count):
        self.count = count
        self.rows = 128 // count

    def __iter__(self):
        return iter(range(self.count))

    def of(self, part):
        return slice(part * self.rows, part * self.rows + self.rows)

    def take(self, ref, slots, part):
        return jnp.concatenate([ref[slot, self.of(part), :] for slot in slots], axis=0)

    def put(self, ref, slots, part, value):
        for index, slot in enumerate(slots):
            ref[slot, self.of(part), :] = value[index * self.rows : index * self.rows + self.rows]


class Gather:
    def __init__(self, place, blocks, sems):
        self.place, self.blocks = place, blocks
        self.send, self.recv = sems
        self.rows = place.parts.rows
        self.sent = []

    def at(self, slot, part, half=None):
        count = self.rows if half is None else self.rows // 2
        first = part * self.rows + (half or 0) * count
        return self.blocks.at[slot, pl.ds(first, count)]

    def copy(self, rows, to, part, sem):
        sem = part * 11 + sem
        return remote(rows, rows, self.send.at[sem], self.recv.at[sem], self.place.dev(to))

    def hand(self, rows, to, part, sem):
        copy = self.copy(rows, to, part, sem)
        copy.start()
        self.sent.append(copy)

    def push(self, part, value):
        own = self.place.slot(0)
        self.blocks[own, self.place.parts.of(part), :] = value
        for half in range(2):
            self.hand(self.at(own, part, 1 - half), 4, part, 4 + 5 * (half == 1))
            self.hand(self.at(own, part, half), 2, part, 2 + 8 * (half == 1))
        self.hand(self.at(own, part), 1, part, 1)

    def arrive(self, rows, part, sem):
        self.copy(rows, 1, part, sem).wait_recv()

    def fetch(self, ks, part):
        slots = {k: self.place.slot(k) for k in ks}
        if 2 in slots:
            self.arrive(self.at(slots[2], part, 0), part, 2)
            self.hand(self.at(slots[2], part, 0), 4, part, 6)
            self.arrive(self.at(slots[4], part, 1), part, 4)
            self.hand(self.at(slots[4], part, 1), 2, part, 8)
            self.arrive(self.at(slots[2], part, 1), part, 10)
            self.hand(self.at(slots[2], part), 1, part, 3)
            self.arrive(self.at(slots[4], part, 0), part, 9)
            self.hand(self.at(slots[4], part), 1, part, 5)
        if 6 in slots:
            self.arrive(self.at(slots[6], part, 0), part, 6)
            self.arrive(self.at(slots[6], part, 1), part, 8)
            self.hand(self.at(slots[6], part), 1, part, 7)
        for k in ks:
            if k % 2:
                self.arrive(self.at(slots[k], part), part, k)
        return slots

    def drain(self):
        for copy in self.sent:
            copy.wait_send()


class Scatter:
    def __init__(self, place, buffers, sems):
        self.place = place
        self.part, self.staged, self.sibling, self.reduced, self.received, self.relayed = buffers
        self.relays = False
        self.send, self.recv = sems
        self.sent = []

    @staticmethod
    def scratch(parts, rows, width):
        return [
            VMEM((parts, 4, rows, width), F32),
            VMEM((parts, 4, rows, width), BF16),
            VMEM((parts, 4, rows, width), BF16),
            VMEM((parts, 3, rows, width), BF16),
            VMEM((parts, 3, rows, width), BF16),
            VMEM((parts, 2, rows // 2, width), BF16),
        ]

    def copy(self, src, dst, part, sem, k):
        sem = part * 11 + sem
        return remote(src, dst, self.send.at[sem], self.recv.at[sem], self.place.dev(k))

    def push(self, *what):
        copy = self.copy(*what)
        copy.start()
        self.sent.append(copy)

    def emit(self, k, part, value):
        index = k // 2
        if k % 2:
            self.staged[part, index] = value.astype(BF16)
            self.push(
                self.staged.at[part, index], self.sibling.at[part, index], part, index, 1
            )
        else:
            self.part[part, index] = value

    def emit_pair(self, pair, part, value):
        rows = value.shape[0] // len(pair)
        for index, k in enumerate(pair):
            self.emit(k, part, value[index * rows : index * rows + rows])

    def of_chip(self, index, part):
        into = self.sibling.at[part, index]
        self.copy(into, into, part, index, 1).wait_recv()
        return self.part[part, index] + self.sibling[part, index].astype(F32)

    def finish_all(self, part):
        self.relays = True
        count = self.relayed.shape[2]
        halves = (pl.ds(0, count), pl.ds(count, count))
        self.reduced[part, 2] = self.of_chip(3, part).astype(BF16)
        for half, k in ((0, 4), (1, 2)):
            self.push(
                self.reduced.at[part, 2, halves[half]], self.relayed.at[part, half], part, 7 + half, k
            )
        sums = [self.of_chip(1, part), self.of_chip(2, part)]

        def send(index, half, value, sem):
            self.reduced[part, index, halves[half], :] = value.astype(BF16)
            self.push(
                self.reduced.at[part, index, halves[half]],
                self.received.at[part, index, halves[half]],
                part,
                sem,
                2 + 2 * index,
            )

        send(0, 1, sums[0][count:], 4)
        send(1, 0, sums[1][:count], 5)
        self.part[part, 0] = self.of_chip(0, part)
        for index, rows in ((0, slice(0, count)), (1, slice(count, 2 * count))):
            into = self.relayed.at[part, index]
            self.copy(into, into, part, 7 + index, 1).wait_recv()
            send(index, index, sums[index][rows] + self.relayed[part, index].astype(F32), 9 + index)

    def finish(self, k, part):
        index = k // 2
        total = self.of_chip(index, part)
        if k:
            self.reduced[part, index - 1] = total.astype(BF16)
            self.push(
                self.reduced.at[part, index - 1],
                self.received.at[part, index - 1],
                part,
                3 + index,
                k,
            )
        else:
            self.part[part, 0] = total

    def total(self, part):
        value = self.part[part, 0]
        if self.relays:
            count = self.relayed.shape[2]
            for index in range(2):
                for half in range(2):
                    into = self.received.at[part, index, pl.ds(half * count, count)]
                    sem = 9 + index if half == index else 4 + index
                    self.copy(into, into, part, sem, 1).wait_recv()
                value = value + self.received[part, index].astype(F32)
            return value
        for index in range(3):
            into = self.received.at[part, index]
            self.copy(into, into, part, 4 + index, 1).wait_recv()
            value = value + self.received[part, index].astype(F32)
        return value

    def drain(self):
        for copy in self.sent:
            copy.wait_send()


def gather_blocks(place, gather, process, scatter=None, before_last=None):
    for part in place.parts:
        for group in PAIRS:
            slots = gather.fetch([k for pair in group for k in pair], part)
            for pair in group:
                process(pair, [slots[k] for k in pair], part)
            if scatter and group == PAIRS[1]:
                scatter.finish(2, part)
                scatter.finish(4, part)
        if before_last and part == place.parts.count - 1:
            before_last()
        if scatter:
            scatter.finish(6, part)
            scatter.finish(0, part)


def scatter_blocks(place, scatter, rows, weight, side=0):
    for part in place.parts:
        for pair in OUT_PAIRS:
            slots = [place.slot(k) for k in pair]
            scatter.emit_pair(pair, part, dot(rows(slots, part), flat(weight), 1, side))
        scatter.finish_all(part)


def carry(place, scatter, gather, step):
    for part in place.parts:
        gather.push(part, step(part, scatter.total(part)))
    scatter.drain()


class Refs:
    pass


def kernel_call(body, collective, ins, outs, scratch):
    in_names = list(ins)
    out_names = list(outs)
    scratch_names = list(scratch)
    flat_scratch = []
    counts = []
    for name in scratch_names:
        item = scratch[name]
        counts.append(len(item) if isinstance(item, list) else 0)
        flat_scratch += item if isinstance(item, list) else [item]

    def kernel(*refs):
        held = Refs()
        at = 0
        for name in in_names + out_names:
            setattr(held, name, refs[at])
            at += 1
        for name, count in zip(scratch_names, counts):
            setattr(held, name, refs[at : at + count] if count else refs[at])
            at += max(count, 1)
        body(held)

    results = pl.pallas_call(
        kernel,
        out_shape=[jax.ShapeDtypeStruct(shape, dtype) for shape, dtype, unused in outs.values()],
        in_specs=[pl.BlockSpec(memory_space=space) for unused, space in ins.values()],
        out_specs=[pl.BlockSpec(memory_space=space) for unused, unused_type, space in outs.values()],
        scratch_shapes=flat_scratch,
        compiler_params=pltpu.CompilerParams(
            collective_id=collective, has_side_effects=True, vmem_limit_bytes=VMEM_LIMIT
        ),
    )(*[array for array, unused in ins.values()])
    return dict(zip(out_names, results))


class AlongZ:
    def __init__(self, place, sems, block):
        self.place = place
        self.send, self.recv = sems
        self.block = block
        self.sent = []

    def copy(self, source, owner, plane, sem):
        into = self.block(owner)
        return remote(
            source, into, self.send.at[sem], self.recv.at[owner], self.place.at(plane)
        )

    def arrive(self, owner):
        self.copy(self.block(owner), owner, owner, 0).wait_recv()

    def start(self, source):
        place = self.place
        self.sent = [
            self.copy(source, place.z, place.across, 0),
            self.copy(source, place.z, place.beside, 1),
        ]
        self.last = [
            self.copy(source, place.z, place.opposite, 2),
            self.copy(self.block(place.opposite), place.opposite, place.line(0), 3),
        ]
        for copy in self.sent:
            copy.start()

        @pl.when(place.middle)
        def start():
            self.last[0].start()

    def relay(self):
        @pl.when(self.place.middle)
        def hand_on():
            self.arrive(self.place.opposite)
            self.last[1].start()

    def finish(self):
        place = self.place
        self.arrive(place.beside)
        self.arrive(place.across)

        @pl.when(place.end)
        def last():
            self.arrive(place.opposite)

        for copy in self.sent:
            copy.wait_send()

        @pl.when(place.middle)
        def drain():
            for copy in self.last:
                copy.wait_send()


class GatherRows:
    def __init__(self, place, src, dst, sems, pieces):
        self.place, self.dst = place, dst
        self.send, self.recv, self.local = sems[:3]
        self.along = AlongZ(place, sems[3:], lambda plane: dst.at[pl.ds(plane * 4, 4)])
        mine = place.z * 4 + place.yc
        for k in (0, 2, 3, 1):
            x, to = place.flip(k)
            for index, column in enumerate(pieces(place, to)):
                source = src.at[:, pl.ds(pl.multiple_of(column * 128, 128), 128)]
                into = dst.at[mine, :, pl.ds(index * 128, 128)]
                if k:
                    remote(source, into, self.send.at[k], self.recv.at[k], place.dev(k)).start()
                else:
                    pltpu.make_async_copy(source, into, self.local).start()

    def along_z(self):
        place = self.place
        mine = self.dst.at[place.z * 4 + place.yc]
        pltpu.make_async_copy(mine, mine, self.local).wait()
        for k in (2, 3, 1):
            into = self.dst.at[place.z * 4 + place.flip(k)[1]]
            remote(into, into, self.send.at[k], self.recv.at[k], place.dev(k)).wait_recv()
        self.along.start(self.dst.at[pl.ds(place.z * 4, 4)])

    def relay(self):
        self.along.relay()

    def finish(self):
        place = self.place
        self.along.finish()
        mine = self.dst.at[place.z * 4 + place.yc]
        for k in (2, 3, 1):
            remote(mine, mine, self.send.at[k], self.recv.at[k], place.dev(k)).wait_send()

    @staticmethod
    def scratch():
        return [DMA((4,)), DMA((4,)), DMA, DMA((4,)), DMA((PLANES,))]


def ffn_pieces(place, yc):
    return [(plane * 4 + yc) * 2 + place.x for plane in range(PLANES)]


def head_pieces(place, yc):
    return [kind * 8 + place.pair(None, yc) for kind in range(3)]


def channel_pieces(place, yc):
    return [kind * 8 + place.pair(None, yc) for kind in range(2)]


class GatherBlocks:
    def __init__(self, place, src, dst, sems, columns=slice(0, 1024)):
        columns = pl.ds(columns.start, columns.stop - columns.start)
        src = src.at[pl.ds(place.x * 128, 128), columns]
        self.along = AlongZ(place, sems[1:], lambda plane: dst.at[plane, :, columns])
        self.own = pltpu.make_async_copy(src, dst.at[place.z, :, columns], sems[0])
        self.own.start()
        self.along.start(src)

    def relay(self):
        self.along.relay()

    def finish(self):
        self.own.wait()
        self.along.finish()

    @staticmethod
    def scratch():
        return [DMA, DMA((4,)), DMA((PLANES,))]


class PlaneSum:
    def __init__(self, place, refs):
        self.place = place
        self.own, self.staged, self.received, self.relayed, self.send, self.recv = refs

    @staticmethod
    def scratch(rows, width):
        return [
            VMEM((rows, width), F32),
            VMEM((3, rows, width), BF16),
            VMEM((3, rows, width), BF16),
            VMEM((rows, width), BF16),
            DMA((4,)),
            DMA((4,)),
        ]

    def term_copy(self, index, plane):
        slot = lax.rem(plane + 3 - self.place.z, PLANES)
        return remote(
            self.staged.at[index],
            self.received.at[slot],
            self.send.at[index],
            self.recv.at[slot],
            self.place.at(plane),
        )

    def relay_copy(self):
        return remote(
            self.staged.at[0],
            self.relayed,
            self.send.at[3],
            self.recv.at[3],
            self.place.at(self.place.beside),
        )

    def first(self, term):
        self.staged[0] = term(self.place.opposite).astype(BF16)

        @pl.when(self.place.end)
        def start():
            self.relay_copy().start()

    def rest(self, term):
        place = self.place
        self.staged[1] = term(place.across).astype(BF16)
        self.term_copy(1, place.across).start()
        self.staged[2] = term(place.beside).astype(BF16)
        self.term_copy(2, place.beside).start()
        self.own[...] = term(place.z)

    def relay(self):
        @pl.when(self.place.middle)
        def add():
            self.relay_copy().wait_recv()
            self.staged[0] = (
                self.staged[0].astype(F32) + self.relayed[...].astype(F32)
            ).astype(BF16)
            self.term_copy(0, self.place.opposite).start()

    def arrive(self, plane):
        slot = lax.rem(self.place.z + 3 - plane, PLANES)
        into = self.received.at[slot]
        remote(
            into, into, self.send.at[0], self.recv.at[slot], self.place.at(plane)
        ).wait_recv()

    def total(self):
        place = self.place
        self.arrive(place.beside)
        self.arrive(place.across)

        @pl.when(place.middle)
        def last():
            self.arrive(place.opposite)
            self.term_copy(0, place.opposite).wait_send()

        @pl.when(place.end)
        def nothing():
            self.received[lax.rem(place.z + 3 - place.opposite, PLANES)] = jnp.zeros(
                self.received.shape[1:], BF16
            )
            self.relay_copy().wait_send()

        self.term_copy(1, place.across).wait_send()
        self.term_copy(2, place.beside).wait_send()
        value = self.own[...]
        for index in range(3):
            value = value + self.received[index].astype(F32)
        return value


class Exchange:
    def __init__(self, place, blocks, sems, partners=tuple(range(1, 8)), slot=None):
        self.place = place
        self.blocks = blocks
        self.send, self.recv = sems
        self.partners = partners
        self.slot = slot or place.slot
        self.sent = []

    def start(self, source):
        own = self.slot(0)
        for k in self.partners:
            copy = remote(
                source(k), self.blocks.at[own], self.send.at[k], self.recv.at[k], self.place.dev(k)
            )
            copy.start()
            self.sent.append(copy)

    def wait(self):
        for k in self.partners:
            into = self.blocks.at[self.slot(k)]
            remote(into, into, self.send.at[k], self.recv.at[k], self.place.dev(k)).wait_recv()
        for copy in self.sent:
            copy.wait_send()


def flat(ref):
    value = ref[...]
    return value.reshape(value.shape[0] * value.shape[1], value.shape[2])


def ffn_forward(place, gather, hidden, w_in, w_out, scatter, ready):
    def process(pair, slots, part):
        if part == 0 and pair[0] == 0:
            ready()
        value = dot(place.parts.take(gather.blocks, slots, part), flat(w_in))
        place.parts.put(hidden, slots, part, value)
        scatter.emit_pair(pair, part, dot(sigmoid_linear(value).astype(BF16), flat(w_out)))

    gather_blocks(place, gather, process, scatter)


def ffn_backward(place, gather, hidden, hidden_grads, active, w_in, w_out, scatter, ready, before_last=None):
    def process(pair, slots, part):
        if part == 0 and pair[0] == 0:
            ready()
        value = place.parts.take(hidden, slots, part)
        sigma = jax.nn.sigmoid(value)
        place.parts.put(active, slots, part, (value * sigma).astype(BF16))
        back = dot(place.parts.take(gather.blocks, slots, part), flat(w_out), 1, 1)
        low = (back * (sigma * (1.0 + value * (1.0 - sigma)))).astype(BF16)
        place.parts.put(hidden_grads, slots, part, low)
        scatter.emit_pair(pair, part, dot(low, flat(w_in), 1, 1))

    gather_blocks(place, gather, process, scatter, before_last)


def token_dot(left, columns, right):
    count, rows, unused = left.shape
    taken = left[:, :, columns].reshape(count * rows, -1)
    return dot(taken, flat(right), 0, 0)


def columns_of(plane, width):
    return pl.ds(pl.multiple_of(plane * width, width), width)


class WeightGrads:
    def __init__(self, place, refs, name, sums, wide):
        self.place = place
        self.sum_in = PlaneSum(place, getattr(refs, sums + "_sum_in"))
        self.total_in = getattr(refs, name + "_total_in")
        self.share_in = Exchange(
            place, getattr(refs, name + "_grad_in"), getattr(refs, name + "_share_in")
        )
        self.wide = wide
        if wide:
            self.sum_out = PlaneSum(place, getattr(refs, sums + "_sum_out"))
            self.share_out = Exchange(
                place,
                getattr(refs, name + "_grad_out"),
                getattr(refs, name + "_share_out"),
                (4,),
                lambda k: place.flip(k)[0],
            )
        else:
            self.sum_out = HalfSum(
                place, getattr(refs, sums + "_sum_out"), getattr(refs, name + "_grad_out")
            )

    def put_out(self, active, grads):
        self.sum_out.put(dot(flat(active), flat(grads), 0, 0))

    def put_in(self, blocks, grads):
        def term(plane):
            return token_dot(blocks, columns_of(plane, 256), grads)

        self.sum_in.first(term)
        self.sum_in.rest(term)

    def put_both(self, active, grads, blocks, hidden_grads):
        def out(plane):
            return token_dot(active, columns_of(plane, 128), grads)

        def into(plane):
            return token_dot(blocks, columns_of(plane, 256), hidden_grads)

        self.sum_out.first(out)
        self.sum_in.first(into)
        self.sum_out.rest(out)
        self.sum_in.rest(into)

    def relay(self):
        self.sum_out.relay()
        self.sum_in.relay()

    def share(self):
        self.share_rows()
        self.share_columns()

    def share_rows(self):
        if self.wide:
            self.share_out.blocks[self.place.x] = self.sum_out.total().astype(BF16)
            self.share_out.start(lambda k: self.share_out.blocks.at[self.place.x])
        else:
            self.sum_out.add()

    def share_columns(self):
        self.total_in[...] = self.sum_in.total().astype(BF16).reshape(self.total_in.shape)
        self.share_in.blocks[self.place.slot(0)] = self.total_in[self.place.yc]
        self.share_in.start(lambda k: self.total_in.at[self.place.flip(k)[1]])

    def wait(self):
        (self.share_out if self.wide else self.sum_out).wait()
        self.share_in.wait()

    @staticmethod
    def sums(name, width, wide):
        return {
            name + "_sum_in": PlaneSum.scratch(256, width),
            name + "_sum_out": PlaneSum.scratch(128, 1024) if wide else HalfSum.scratch(1024),
        }

    @staticmethod
    def scratch(name, width, wide):
        held = {
            name + "_total_in": VMEM((4, 64, width), BF16),
            name + "_share_in": [DMA((8,)), DMA((8,))],
        }
        if wide:
            held[name + "_share_out"] = [DMA((8,)), DMA((8,))]
        return held

    @staticmethod
    def outs(name, width, wide):
        return {
            name + "_grad_in": ((8, 64, width), BF16, VMEM),
            name + "_grad_out": ((2, 128, 1024) if wide else (64, 1024), BF16, VMEM),
        }


AG_SEMS = [DMA((22,)), DMA((22,))]


def norm_rows(values, gain):
    normed, saved = norm_forward(values, gain)
    return normed.astype(BF16), saved


def norm_input_grad(grads, gain, saved):
    unit_part, inverse = saved
    scaled = grads * gain
    gain_grad = jnp.sum(grads * unit_part, axis=0, keepdims=True)
    input_part = inverse * (
        scaled
        - jnp.mean(scaled, axis=-1, keepdims=True)
        - unit_part * jnp.mean(scaled * unit_part, axis=-1, keepdims=True)
    )
    return input_part, gain_grad


class GatherHalf:
    def __init__(self, place, src, dst, sems):
        self.place, self.dst = place, dst
        self.send, self.recv, self.local = sems
        self.source = place.z // 2 == place.x
        self.first, self.last = 2 - place.x, 3 - 3 * place.x
        target = place.yc // 2 * 2 + lax.rem(place.z, 2)
        self.same = lax.rem(place.z, 2) == place.core
        self.own = pltpu.make_async_copy(src, dst.at[place.core], self.local)

        def copy(sem, plane):
            return remote(
                src,
                dst.at[place.core],
                self.send.at[sem],
                self.recv.at[place.core],
                place.at(plane, target),
            )

        self.far, self.near, self.sibling = (
            copy(0, self.first),
            copy(1, place.x * 2 + 1 - lax.rem(place.z, 2)),
            copy(2, place.z),
        )

        @pl.when(self.source)
        def start():
            self.far.start()
            self.near.start()

            @pl.when(self.same)
            def local():
                self.own.start()

            @pl.when(jnp.logical_not(self.same))
            def sibling():
                self.sibling.start()

    def on(self, half):
        rows = self.dst.at[half]
        return remote(
            rows, rows, self.send.at[half], self.recv.at[half], self.place.at(self.last)
        )

    def relay(self):
        @pl.when(self.place.z == self.first)
        def hand_on():
            for half in range(2):
                self.on(half).wait_recv()
                self.on(half).start()

    def finish(self):
        place = self.place
        at_home = place.z == place.x * 2 + place.core
        for half in range(2):
            here = jnp.logical_or(
                jnp.logical_and(at_home, place.core == half), place.z == self.first
            )

            @pl.when(jnp.logical_not(here))
            def arrive():
                self.on(half).wait_recv()

        @pl.when(self.source)
        def drain():
            self.far.wait_send()
            self.near.wait_send()

            @pl.when(self.same)
            def local():
                self.own.wait()

            @pl.when(jnp.logical_not(self.same))
            def sibling():
                self.sibling.wait_send()

        @pl.when(place.z == self.first)
        def drain_on():
            for half in range(2):
                self.on(half).wait_send()

    @staticmethod
    def scratch():
        return [DMA((3,)), DMA((2,)), DMA]


class HalfSum:
    def __init__(self, place, refs, result):
        self.place = place
        self.staged, self.received, self.relayed, self.send, self.recv, self.last = refs
        self.result = result
        self.near = place.z // 2 == place.x
        self.far_middle, self.far_end = 2 - place.x, 3 - 3 * place.x
        self.home = place.x * 2 + place.core

    @staticmethod
    def scratch(width):
        return [
            VMEM((2, 64, width), BF16),
            VMEM((3, 64, width), BF16),
            VMEM((2, 64, width), BF16),
            DMA((3,)),
            DMA((4,)),
            DMA((2,)),
        ]

    def term_copy(self, half, slot):
        place = self.place
        return remote(
            self.staged.at[half],
            self.received.at[slot],
            self.send.at[half],
            self.recv.at[slot],
            place.at(self.home, place.yc // 2 * 2 + half),
        )

    def relay_copy(self):
        return remote(
            self.staged,
            self.relayed,
            self.send.at[2],
            self.recv.at[3],
            self.place.at(self.far_middle),
        )

    def near_copies(self):
        place = self.place
        for half in range(2):
            here = jnp.logical_and(place.z == self.home, place.core == half)
            slot = lax.rem(place.z + self.home, 2)
            yield jnp.logical_and(self.near, jnp.logical_not(here)), self.term_copy(half, slot)

    def put(self, value):
        self.staged[...] = value.astype(BF16).reshape(self.staged.shape)

    def start(self):
        place = self.place

        @pl.when(place.z == self.far_end)
        def relay():
            self.relay_copy().start()

        for away, copy in self.near_copies():

            @pl.when(away)
            def start(copy=copy):
                copy.start()

    def relay(self):
        @pl.when(self.place.z == self.far_middle)
        def add():
            self.relay_copy().wait_recv()
            self.staged[...] = (
                self.staged[...].astype(F32) + self.relayed[...].astype(F32)
            ).astype(BF16)
            for half in range(2):
                self.term_copy(half, 2).start()

    def add(self):
        place = self.place
        at_home = jnp.logical_and(self.near, place.z == self.home)

        @pl.when(self.near)
        def reduce():
            @pl.when(at_home)
            def own():
                self.received[0] = self.staged[place.core]

            for slot in range(3):

                def arrive():
                    into = self.received.at[slot]
                    remote(
                        into, into, self.send.at[0], self.recv.at[slot], place.at(place.z)
                    ).wait_recv()

                if slot:
                    arrive()
                else:
                    pl.when(jnp.logical_not(at_home))(arrive)
            value = self.received[0].astype(F32)
            for slot in range(1, 3):
                value = value + self.received[slot].astype(F32)
            self.result[...] = value.astype(BF16)
            self.hand_over().start()

        for away, copy in self.near_copies():

            @pl.when(away)
            def drain(copy=copy):
                copy.wait_send()

        @pl.when(place.z == self.far_middle)
        def drain_sums():
            for half in range(2):
                self.term_copy(half, 2).wait_send()

        @pl.when(place.z == self.far_end)
        def drain_relay():
            self.relay_copy().wait_send()

    def hand_over(self):
        return remote(
            self.result, self.result, self.last.at[0], self.last.at[1], self.place.dev(4)
        )

    def wait(self):
        @pl.when(self.near)
        def sent():
            self.hand_over().wait_send()

        @pl.when(jnp.logical_not(self.near))
        def arrived():
            self.hand_over().wait_recv()


class Turn:
    def __init__(self, place, refs):
        self.place = place
        self.staged, self.received, self.send, self.recv = refs

    @staticmethod
    def scratch(rows):
        return [VMEM((PLANES, rows, 128), BF16), VMEM((PLANES, rows, 128), BF16), DMA((4,)), DMA((4,))]

    def copy(self, k):
        place = self.place
        return remote(
            self.staged.at[lax.rem(place.z + k, PLANES)],
            self.received.at[place.z],
            self.send.at[k],
            self.recv.at[k],
            place.zdev(k),
        )

    def start(self):
        for k in (2, 1, 3):
            self.copy(k).start()
        self.keep()

    def dispatch(self, pair):
        k = lax.rem(pair + PLANES - self.place.z, PLANES)

        @pl.when(k > 0)
        def start():
            self.copy(k).start()

        @pl.when(k == 0)
        def own():
            self.keep()

    def keep(self):
        self.received[self.place.z] = self.staged[self.place.z]

    def wait(self):
        for k in (1, 2, 3):
            into = self.received.at[lax.rem(self.place.z + 4 - k, PLANES)]
            remote(into, into, self.send.at[k], self.recv.at[k], self.place.zdev(k)).wait_recv()
        for k in (1, 2, 3):
            self.copy(k).wait_send()


def swap_halves(values):
    lane = lax.broadcasted_iota(jnp.int32, values.shape, 1)
    return jnp.where(lane % 64 < 32, pltpu.roll(values, 96, 1), pltpu.roll(values, 32, 1))


def head_part(values, head):
    return values[:, head * 64 : head * 64 + 64]


def pack_wide(turn, row, head, left, right):
    pair = row * 2 + head
    for block in range(4):
        turn.staged[pair, block * 128 : block * 128 + 128, :] = jnp.concatenate(
            [head_part(left[row * 4 + block], head), head_part(right[row * 4 + block], head)], axis=1
        )


def pack_narrow(turn, row, head, values):
    pair = row * 2 + head
    for block in range(2):
        turn.staged[pair, block * 128 : block * 128 + 128, :] = jnp.concatenate(
            [
                head_part(values[row * 4 + block], head),
                head_part(values[row * 4 + block + 2], head),
            ],
            axis=1,
        )


def unpack_narrow(turn, row, block):
    rows = slice((block % 2) * 128, (block % 2) * 128 + 128)
    return jnp.concatenate(
        [head_part(turn.received[row * 2 + head, rows, :], block // 2) for head in range(2)], axis=1
    )


def unpack_wide(turn, row, block, side):
    rows = slice(block * 128, block * 128 + 128)
    return jnp.concatenate(
        [head_part(turn.received[row * 2 + head, rows, :], side) for head in range(2)], axis=1
    )


QUERY_BLOCK = 256


def segment_ends(refs, row):
    lengths = refs.row_lengths[row]
    ends = [lengths[0:1, 0:1]]
    for index in range(1, 4):
        ends.append(ends[-1] + lengths[0:1, index : index + 1])
    return ends


def segment_features(refs, plane, row):
    frame = (plane * 512 + lax.broadcasted_iota(jnp.int32, (512, 64), 0)).astype(F32)
    lane = lax.broadcasted_iota(jnp.int32, (512, 64), 1).astype(F32)
    segment = jnp.zeros((512, 64), F32)
    for end in segment_ends(refs, row)[:3]:
        segment = segment + jnp.where(frame >= end, 1.0, 0.0)
    other = jnp.where(lane < 4.0, -MASKED, 0.0)
    return (
        jnp.where(lane == segment, 0.0, other).astype(BF16),
        jnp.where(lane == segment, -1.0, 0.0).astype(BF16),
    )


def segment_reach(place, refs, slot):
    row, block = slot // 4, slot % 4
    frame = place.z * 512 + block * 128 + lax.broadcasted_iota(jnp.int32, (128, 128), 0)
    frame = frame.astype(F32)
    ends = segment_ends(refs, row)
    first, last = jnp.zeros((128, 128), F32), ends[3]
    for end in ends[:3]:
        first = jnp.where(frame >= end, end, first)
    for end in ends[2::-1]:
        last = jnp.where(frame < end, end, last)
    return first - frame, last - frame


def open_heads(place, refs, turn_qk, turn_v):
    for plane in range(PLANES):
        seg_query, seg_key = segment_features(refs, plane, place.z // 2)
        rows = slice(plane * 512, plane * 512 + 512)
        pair = turn_qk.received[plane]
        scaled = (pair[:, :64].astype(F32) * HEAD_DIM ** (-0.5)).astype(BF16)
        refs.queries[rows, :] = jnp.concatenate([scaled, seg_query], axis=1)
        refs.keys[rows, :] = jnp.concatenate([pair[:, 64:], seg_key], axis=1)
        both = turn_v.received[plane]
        turned = jnp.transpose(both.astype(F32)).astype(BF16)
        refs.values[plane * 512 : plane * 512 + 256, :] = both[:, :64]
        refs.values[plane * 512 + 256 : plane * 512 + 512, :] = both[:, 64:]
        refs.values_t[:, plane * 512 : plane * 512 + 256] = turned[:64]
        refs.values_t[:, plane * 512 + 256 : plane * 512 + 512] = turned[64:]


def attend(place, refs, turn_mix):
    def plane_step(step, unused):
        k = lax.rem(step + 1, PLANES)
        plane = lax.rem(place.z + k, PLANES)
        parts = []
        for half in range(2):
            first = plane * 512 + half * 256
            query = refs.queries[pl.ds(pl.multiple_of(first, 256), QUERY_BLOCK), :]
            scores = dot(refs.keys[...], query, 1, 1)
            top = jnp.max(scores, axis=0, keepdims=True)
            weights = jnp.exp(scores - top)
            total = jnp.sum(weights, axis=0, keepdims=True)
            low = (weights * (1.0 / total)).astype(BF16)
            parts.append(jnp.transpose(dot(refs.values_t[...], low)))
            refs.log_total[plane * 2 + half] = jnp.broadcast_to(top + jnp.log(total), (8, 256))
        turn_mix.staged[plane] = jnp.concatenate(parts, axis=1).astype(BF16)

        @pl.when(step < PLANES - 1)
        def send():
            turn_mix.copy(k).start()

        return unused

    lax.fori_loop(0, PLANES, plane_step, 0)


def attention_forward(place, refs, gather, scatter):
    def process(pair, slots, part):
        if part == 0 and pair[0] == 0:
            refs.finish_qkv()
        value = dot(place.parts.take(gather.blocks, slots, part), flat(refs.w_qkv))

        def frames_of(slot, part):
            count = place.parts.rows
            first = lax.rem(slot, 4) * 128 + part * count
            return pl.ds(pl.multiple_of(first, count), count)

        def table(ref):
            return jnp.concatenate(
                [
                    ref[frames_of(slot, part), :]
                    for slot in slots
                ],
                axis=0,
            )

        cos, sin = table(refs.cos), table(refs.sin)
        query, key = value[:, :128], value[:, 128:256]
        place.parts.put(refs.q_rows, slots, part, (query * cos + swap_halves(query) * sin).astype(BF16))
        place.parts.put(refs.k_rows, slots, part, (key * cos + swap_halves(key) * sin).astype(BF16))
        place.parts.put(refs.v_rows, slots, part, value[:, 256:].astype(BF16))
        if part == place.parts.count - 1 and pair in LAST_OF_ROW:
            row = place.row(LAST_OF_ROW[pair])
            for head in range(2):
                pack_wide(turn_qk, row, head, refs.q_rows, refs.k_rows)
                turn_qk.dispatch(row * 2 + head)
            for head in range(2):
                pack_narrow(turn_v, row, head, refs.v_rows)
                turn_v.dispatch(row * 2 + head)

    turn_qk, turn_v = Turn(place, refs.turn_qk), Turn(place, refs.turn_v)
    gather_blocks(place, gather, process)
    gather.drain()
    turn_qk.wait()
    turn_v.wait()
    refs.after_turn()
    open_heads(place, refs, turn_qk, turn_v)
    turn_mix = Turn(place, refs.turn_mix)
    attend(place, refs, turn_mix)
    turn_mix.keep()
    turn_mix.wait()
    refs.after_mix()
    for slot in range(8):
        refs.mixed[slot] = unpack_narrow(turn_mix, slot // 4, slot % 4)
    scatter_blocks(
        place, scatter, lambda slots, part: place.parts.take(refs.mixed, slots, part), refs.w_o
    )


def attention_kept():
    return dict(
        attn_blocks=((8, 128, 1024), BF16),
        w_qkv=((16, 64, 384), BF16),
        w_o=((2, 64, 1024), BF16),
        queries=((2048, 128), BF16),
        keys=((2048, 128), BF16),
        values=((2048, 64), BF16),
        log_total=((8, 8, 256), F32),
        mixed=((8, 128, 128), BF16),
    )


def attend_back(place, refs, turn_kv, turn_q):
    refs.key_grad[...] = jnp.zeros_like(refs.key_grad)
    refs.value_grad[...] = jnp.zeros_like(refs.value_grad)

    def plane_step(step, unused):
        k = lax.rem(step + 1, PLANES)
        plane = lax.rem(place.z + k, PLANES)
        parts = []
        for half in range(2):
            first = pl.multiple_of(plane * 512 + half * 256, 256)
            query = refs.queries[pl.ds(first, QUERY_BLOCK), :]
            grad = refs.mix_grads[pl.ds(first, QUERY_BLOCK), :]
            log_total = refs.log_total[plane * 2 + half][:1]
            probs = jnp.exp(dot(refs.keys[...], query, 1, 1) - log_total)
            prob_grads = dot(refs.values[...], grad, 1, 1)
            delta = jnp.sum(probs * prob_grads, axis=0, keepdims=True)
            low = (probs * (prob_grads - delta)).astype(BF16)
            refs.key_grad[...] += dot(low, query[:, :64])
            refs.value_grad[...] += dot(probs.astype(BF16), grad)
            parts.append(jnp.transpose(dot(refs.keys_t[...], low)) * HEAD_DIM ** (-0.5))
        turn_q.staged[plane] = jnp.concatenate(parts, axis=1).astype(BF16)

        @pl.when(step < PLANES - 1)
        def send():
            turn_q.copy(k).start()

        return unused

    lax.fori_loop(0, PLANES, plane_step, 0)
    turn_q.keep()
    for plane in range(PLANES):
        rows = slice(plane * 512, plane * 512 + 512)
        turn_kv.staged[plane] = jnp.concatenate(
            [refs.key_grad[rows, :], refs.value_grad[rows, :]], axis=1
        ).astype(BF16)


def attention_backward(place, refs, gather, scatter):
    def process(pair, slots, part):
        if part == 0 and pair[0] == 0:
            refs.finish_attn()
        rows = dot(place.parts.take(gather.blocks, slots, part), flat(refs.w_o), 1, 1)
        place.parts.put(refs.mix_rows, slots, part, rows.astype(BF16))
        if part == place.parts.count - 1 and pair in LAST_OF_ROW:
            row = place.row(LAST_OF_ROW[pair])
            for head in range(2):
                pack_narrow(turn_mix, row, head, refs.mix_rows)
                turn_mix.dispatch(row * 2 + head)

    turn_mix = Turn(place, refs.turn_mix)
    gather_blocks(place, gather, process)
    gather.drain()
    weights = WeightGrads(place, refs, "qkv", "qkv", False)
    weights.put_out(refs.mixed, gather.blocks)
    turned = jnp.transpose(refs.keys[...].astype(F32))
    refs.keys_t[...] = turned[:64].astype(BF16)
    refs.before_mix()
    turn_mix.wait()
    for plane in range(PLANES):
        both = turn_mix.received[plane]
        refs.mix_grads[plane * 512 : plane * 512 + 256, :] = both[:, :64]
        refs.mix_grads[plane * 512 + 256 : plane * 512 + 512, :] = both[:, 64:]
    weights.sum_out.start()
    refs.before_attend()
    turn_kv, turn_q = Turn(place, refs.turn_qk), Turn(place, refs.turn_v)
    attend_back(place, refs, turn_kv, turn_q)
    turn_kv.start()
    weights.sum_out.relay()
    refs.after_attend()
    turn_q.wait()
    turn_kv.wait()
    for slot in range(8):
        row, block = divmod(slot, 4)
        cos = refs.cos[block * 128 : block * 128 + 128, :]
        sin = refs.sin[block * 128 : block * 128 + 128, :]
        query = unpack_narrow(turn_q, row, block).astype(F32)
        key = unpack_wide(turn_kv, row, block, 0).astype(F32)
        refs.qkv_grads[slot] = jnp.concatenate(
            [
                (query * cos - swap_halves(query) * sin).astype(BF16),
                (key * cos - swap_halves(key) * sin).astype(BF16),
                unpack_wide(turn_kv, row, block, 1),
            ],
            axis=1,
        )
    scatter_blocks(
        place, scatter, lambda slots, part: place.parts.take(refs.qkv_grads, slots, part), refs.w_qkv, 1
    )
    return weights


def fill_tables(refs):
    cos, sin = refs.cos_rows[...], refs.sin_rows[...]
    refs.cos[...] = jnp.concatenate([cos] * 4, axis=1)
    refs.sin[...] = jnp.concatenate([-sin, sin] * 2, axis=1)


def fill_channels(place, refs):
    columns = columns_of(place.pair(), 128)
    refs.taps[0:KERNEL, :] = refs.all_taps[:, columns].astype(F32)
    refs.gain_inner[...] = refs.all_inner[:, columns]
    for slot in range(8):
        refs.before[slot], refs.after[slot] = segment_reach(place, refs, slot)


def table_scratch():
    return dict(
        cos=VMEM((512, 128), F32),
        sin=VMEM((512, 128), F32),
        taps=VMEM((32, 128), F32),
        gain_inner=VMEM((1, 128), F32),
        before=VMEM((8, 128, 128), F32),
        after=VMEM((8, 128, 128), F32),
    )


class Edges:
    def __init__(self, place, refs):
        self.place = place
        self.staged, self.received, self.send, self.recv = refs

    @staticmethod
    def scratch():
        return [VMEM((2, 2, 16, 128), BF16), VMEM((2, 2, 16, 128), BF16), DMA((2,)), DMA((2,))]

    def copies(self):
        place = self.place
        for side, inside, step in ((0, place.z < PLANES - 1, 1), (1, place.z > 0, -1)):
            plane = jnp.clip(place.z + step, 0, PLANES - 1)
            yield (
                side,
                inside,
                remote(
                    self.staged.at[side],
                    self.received.at[side],
                    self.send.at[side],
                    self.recv.at[side],
                    {"seq": plane * 4 + place.yc, "row": place.x},
                ),
            )

    def start(self, blocks):
        for row in range(2):
            self.staged[0, row] = blocks[row * 4 + 3, 112:128, :]
            self.staged[1, row] = blocks[row * 4, 0:16, :]
        for side, inside, copy in self.copies():

            @pl.when(inside)
            def start(copy=copy):
                copy.start()

    def wait(self, blocks, padded):
        for slot in range(8):
            row, block = divmod(slot, 4)
            padded[slot, 16:144, :] = blocks[slot].astype(F32)
            if block > 0:
                padded[slot, 0:16, :] = blocks[slot - 1, 112:128, :].astype(F32)
            if block < 3:
                padded[slot, 144:160, :] = blocks[slot + 1, 0:16, :].astype(F32)
        place = self.place
        for side, outside in ((0, place.z == 0), (1, place.z == PLANES - 1)):
            first, rows = ((0, slice(0, 16)), (3, slice(144, 160)))[side]
            into = self.received.at[side]

            @pl.when(outside)
            def nothing():
                for row in range(2):
                    padded[row * 4 + first, rows, :] = jnp.zeros((16, 128), F32)

            @pl.when(jnp.logical_not(outside))
            def arrive():
                remote(
                    into, into, self.send.at[side], self.recv.at[side], place.zdev(1)
                ).wait_recv()
                for row in range(2):
                    padded[row * 4 + first, rows, :] = self.received[side, row].astype(F32)

        for side, inside, copy in self.copies():

            @pl.when(inside)
            def drain(copy=copy):
                copy.wait_send()


def lane_is(index, rows=128):
    return lax.broadcasted_iota(jnp.int32, (rows, 128), 1) == index


def put_columns(tile, slot, first, second):
    return jnp.where(lane_is(slot), first, jnp.where(lane_is(slot + 8), second, tile))


def share_columns(place, refs, tile):
    share = Exchange(place, refs[0], refs[1:])
    own = place.slot(0)
    share.blocks[own] = jnp.transpose(tile)[:16]
    share.start(lambda k: share.blocks.at[own])
    return share


def back_to_columns(first, second):
    rows = jnp.concatenate([first, second, jnp.zeros((112, 128), F32)], axis=0)
    return jnp.transpose(rows)


def column(tile, slot):
    return jnp.sum(jnp.where(lane_is(slot, tile.shape[0]), tile, 0.0), axis=1, keepdims=True)


def kept_frames(value, offset, before, after):
    if offset < 0:
        return jnp.where(before <= offset, value, 0.0)
    if offset > 0:
        return jnp.where(after > offset, value, 0.0)
    return value


CHUNK = 64


def convolve(refs):
    taps = [refs.taps[j : j + 1, :] for j in range(KERNEL)]

    def step(slot, tile):
        for first in range(0, 128, CHUNK):
            rows = slice(first, first + CHUNK)
            before, after = refs.before[slot, rows, :], refs.after[slot, rows, :]
            total = jnp.zeros((CHUNK, 128), F32)
            for j in range(KERNEL):
                start = first + j + 1
                value = refs.glu_padded[slot, start : start + CHUNK, :]
                total = total + taps[j] * kept_frames(value, j - HALF, before, after)
            refs.conv[slot, rows, :] = total
        value = refs.conv[slot]
        mean = jnp.mean(value, axis=1, keepdims=True)
        center = value - mean
        return put_columns(tile, slot, mean, jnp.sum(center * center, axis=1, keepdims=True))

    return lax.fori_loop(0, 8, step, jnp.zeros((128, 128), F32))


def inner_norm(refs, slot, rows=slice(0, 128)):
    tile = refs.inner_stats[rows, :]
    mean, inverse = column(tile, slot), column(tile, slot + 8)
    return (refs.conv[slot, rows, :] - mean) * inverse, inverse


def conv_forward(place, refs, gather, scatter):
    def process(pair, slots, part):
        if part == 0 and pair[0] == 0:
            refs.finish_ci()
        value = dot(place.parts.take(gather.blocks, slots, part), flat(refs.w_ci))
        place.parts.put(refs.gate_up, slots, part, value)
        place.parts.put(
            refs.glu,
            slots,
            part,
            (value[:, :128] * jax.nn.sigmoid(value[:, 128:])).astype(BF16),
        )

    gather_blocks(place, gather, process)
    edges = Edges(place, refs.edges)
    edges.start(refs.glu)
    gather.drain()
    edges.wait(refs.glu, refs.glu_padded)
    share = share_columns(place, refs.stats, convolve(refs))
    refs.conv_middle()
    share.wait()
    stats = share.blocks[...]
    means, spreads = stats[:, :8], stats[:, 8:]
    mean = jnp.mean(means, axis=0)
    spread = jnp.sum(spreads + 128.0 * jnp.square(means - mean[None]), axis=0) / 1024.0
    refs.inner_stats[...] = back_to_columns(mean, lax.rsqrt(spread + EPSILON))
    refs.finish_co()

    def active_rows(slots, part):
        rows = place.parts.of(part)
        parts = []
        for slot in slots:
            unit_part, unused = inner_norm(refs, slot, rows)
            parts.append(sigmoid_linear(unit_part * refs.gain_inner[...]).astype(BF16))
        value = jnp.concatenate(parts, axis=0)
        place.parts.put(refs.conv_active, slots, part, value)
        return value

    scatter_blocks(place, scatter, active_rows, refs.w_co)


def conv_kept():
    return dict(
        conv_blocks=((8, 128, 1024), BF16),
        w_ci=((16, 64, 256), BF16),
        w_co=((2, 64, 1024), BF16),
        gate_up=((8, 128, 256), F32),
        glu_padded=((8, 160, 128), F32),
        conv=((8, 128, 128), F32),
        inner_stats=((128, 128), F32),
        conv_active=((8, 128, 128), BF16),
    )


STATS = [VMEM((8, 16, 128), F32), DMA((8,)), DMA((8,))]


def convolve_back(refs):
    taps = [refs.taps[j : j + 1, :] for j in range(KERNEL)]
    refs.tap_sums[...] = jnp.zeros_like(refs.tap_sums)

    def step(slot, unused):
        for first in range(0, 128, CHUNK):
            rows = slice(first, first + CHUNK)
            before, after = refs.before[slot, rows, :], refs.after[slot, rows, :]
            total = jnp.zeros((CHUNK, 128), F32)
            grad = refs.conv_grad_padded[slot, first + 16 : first + 16 + CHUNK, :]
            for j in range(KERNEL):
                offset = j - HALF
                start = first + 16 - offset
                value = refs.conv_grad_padded[slot, start : start + CHUNK, :]
                total = total + taps[j] * kept_frames(value, -offset, before, after)
                start = first + 16 + offset
                value = refs.glu_padded[slot, start : start + CHUNK, :]
                product = kept_frames(value * grad, offset, before, after)
                refs.tap_sums[j] += jnp.sum(product.reshape(CHUNK // 8, 8, 128), axis=0)
            refs.glu_grad[slot, rows, :] = total
        return unused

    lax.fori_loop(0, 8, step, 0)
    return jnp.sum(refs.tap_sums[...], axis=1)


def conv_backward(place, refs, gather, scatter):
    gain = refs.gain_inner[...]

    def process(pair, slots, part):
        if part == 0 and pair[0] == 0:
            refs.finish_conv()
        back = dot(place.parts.take(gather.blocks, slots, part), flat(refs.w_co), 1, 1)
        rows = place.parts.of(part)
        units = jnp.concatenate([inner_norm(refs, slot, rows)[0] for slot in slots], axis=0)
        place.parts.put(refs.inner_grad, slots, part, back * sigmoid_linear_grad(units * gain))

    gather_blocks(place, gather, process)

    def sums(slot, current):
        tile, gain_grad = current
        value = refs.inner_grad[slot]
        unit_part, unused = inner_norm(refs, slot)
        scaled = value * gain
        tile = put_columns(
            tile,
            slot,
            jnp.sum(scaled, axis=1, keepdims=True),
            jnp.sum(scaled * unit_part, axis=1, keepdims=True),
        )
        return tile, gain_grad + jnp.sum(value * unit_part, axis=0, keepdims=True)

    tile, inner_gain_grad = lax.fori_loop(
        0, 8, sums, (jnp.zeros((128, 128), F32), jnp.zeros((1, 128), F32))
    )
    share = share_columns(place, refs.stats, tile)
    weights = WeightGrads(place, refs, "conv", "conv", False)
    weights.put_out(refs.conv_active, gather.blocks)
    gather.drain()
    share.wait()
    means = jnp.sum(share.blocks[...], axis=0) / 1024.0
    refs.grad_stats[...] = back_to_columns(means[:8], means[8:])

    def input_grad(slot, unused):
        unit_part, inverse = inner_norm(refs, slot)
        tile = refs.grad_stats[...]
        refs.conv_grad[slot] = (
            inverse
            * (
                refs.inner_grad[slot] * gain
                - column(tile, slot)
                - unit_part * column(tile, slot + 8)
            )
        ).astype(BF16)
        return unused

    lax.fori_loop(0, 8, input_grad, 0)
    edges = Edges(place, refs.edges)
    edges.start(refs.conv_grad)
    refs.conv_begin()
    edges.wait(refs.conv_grad, refs.conv_grad_padded)
    weights.sum_out.start()
    tap_grads = convolve_back(refs)
    refs.conv_middle()

    def gate_rows(slots, part):
        value, glu_grad = place.parts.take(refs.gate_up, slots, part), place.parts.take(refs.glu_grad, slots, part)
        sigma = jax.nn.sigmoid(value[:, 128:])
        low = jnp.concatenate(
            [glu_grad * sigma, glu_grad * value[:, :128] * sigma * (1.0 - sigma)], axis=1
        ).astype(BF16)
        place.parts.put(refs.gate_grads, slots, part, low)
        return low

    scatter_blocks(place, scatter, gate_rows, refs.w_ci, 1)
    return inner_gain_grad, tap_grads, weights


class Traffic:
    def __init__(self, refs, sems):
        self.refs, self.sems = refs, sems
        self.count = 0

    def start(self, pairs):
        copies = []
        for source, target in pairs:
            copy = pltpu.make_async_copy(source, target, self.sems.at[self.count])
            copy.start()
            copies.append(copy)
            self.count += 1

        def finish():
            for copy in copies:
                copy.wait()

        return finish

    def save(self, names):
        return self.start(
            [(getattr(self.refs, name), getattr(self.refs, "keep_" + name)) for name in names]
        )

    def load(self, names):
        return self.start(
            [(getattr(self.refs, "keep_" + name), getattr(self.refs, name)) for name in names]
        )


def ffn_kept():
    return dict(
        blocks=((8, 128, 1024), BF16),
        hidden=((8, 128, 512), F32),
        w_in=((16, 64, 512), BF16),
        w_out=((4, 128, 1024), BF16),
    )


SCATTER_SEMS = [DMA((22,)), DMA((22,))]


def forward_body(refs):
    place = Place(FORWARD_PARTS)
    place.enter()
    traffic = Traffic(refs, refs.traffic)
    gather_in = GatherRows(place, refs.w_in_rows, refs.w_in, refs.gather_in, ffn_pieces)
    refs.row_lengths[place.x] = refs.own_lengths[...]
    lengths = remote(
        refs.own_lengths,
        refs.row_lengths.at[place.x],
        refs.length_sems.at[0],
        refs.length_sems.at[1],
        place.dev(4),
    )
    lengths.start()
    halves = (slice(0, 512), slice(512, 1024))
    gather_out = [
        GatherBlocks(place, refs.w_out_rows, refs.w_out, refs.gather_out, halves[0])
    ]
    gather = Gather(place, refs.blocks, refs.ffn_ag)
    for part in place.parts:
        frames = place.parts.of(part)
        gather.push(part, norm_rows(refs.stream[frames, :].astype(F32), refs.gain_ffn1[...])[0])
    gather_in.along_z()
    gather_out.append(
        GatherBlocks(place, refs.w_out_rows, refs.w_out, refs.gather_out_last, halves[1])
    )
    gather_qkv = GatherRows(place, refs.qkv_rows, refs.w_qkv, refs.gather_qkv, head_pieces)
    held = Refs()
    gather_out[0].relay()
    gather_blocks(place, gather, lambda pair, slots, part: None)
    gather_in.relay()
    lengths.wait()
    fill_tables(refs)
    fill_channels(place, refs)
    gather_in.finish()
    for part in place.parts:
        for group in PAIRS:
            for pair in group:
                slots = [place.slot(k) for k in pair]
                value = dot(place.parts.take(refs.blocks, slots, part), flat(refs.w_in))
                place.parts.put(refs.hidden, slots, part, value)
                place.parts.put(refs.active, slots, part, sigmoid_linear(value).astype(BF16))
    gather.drain()
    scatter = Scatter(place, refs.scatter_columns, refs.ffn_scatter)
    for half, columns in enumerate(halves):
        if half:
            gather_out[half].relay()
        gather_out[half].finish()
        if half:
            gather_qkv.along_z()
            gather_o = GatherHalf(place, refs.o_rows, refs.w_o, refs.gather_o)
        weight = refs.w_out[:, :, columns].reshape(512, 512)
        for pair in OUT_PAIRS:
            rows = jnp.concatenate([refs.active[place.slot(k)] for k in pair], axis=0)
            scatter.emit_pair(pair, half, dot(rows, weight))
        for k in (2, 4, 6, 0):
            scatter.finish(k, half)
    saved = [traffic.save(ffn_kept())]
    gather_ci = GatherRows(place, refs.ci_rows, refs.w_ci, refs.gather_ci, channel_pieces)
    gather_next = GatherRows(place, refs.next_in_rows, refs.next_in, refs.gather_next, ffn_pieces)

    def to_attention(part, total):
        frames = place.parts.of(part)
        value = refs.stream[frames, :].astype(F32) + 0.5 * total
        refs.stream_one[frames, :] = value
        return norm_rows(value, refs.gain_attn[...])[0]

    def to_conv(part, total):
        frames = place.parts.of(part)
        value = refs.stream_one[frames, :] + total
        refs.stream_two[frames, :] = value
        return norm_rows(value, refs.gain_conv[...])[0]

    gather = Gather(place, refs.attn_blocks, refs.attn_ag)
    total = jnp.concatenate([scatter.total(half) for half in range(2)], axis=1)
    for part in place.parts:
        gather.push(part, to_attention(part, total[place.parts.of(part)]))
    scatter.drain()
    gather_qkv.relay()
    gather_o.relay()

    def after_turn():
        gather_ci.along_z()
        held.co = GatherHalf(place, refs.co_rows, refs.w_co, refs.gather_co)

    def after_mix():
        gather_ci.relay()
        held.co.relay()
        gather_o.finish()
        gather_next.along_z()
        held.next_out = GatherBlocks(
            place, refs.next_out_rows, refs.next_out, refs.gather_next_out
        )

    def conv_middle():
        gather_next.relay()

    refs.after_turn, refs.after_mix, refs.conv_middle = after_turn, after_mix, conv_middle
    refs.finish_qkv, refs.finish_ci, refs.finish_co = (
        gather_qkv.finish,
        gather_ci.finish,
        lambda: held.co.finish(),
    )
    scatter = Scatter(place, refs.scatter, refs.attn_scatter)
    attention_forward(place, refs, gather, scatter)
    saved.append(traffic.save(attention_kept()))
    gather = Gather(place, refs.conv_blocks, refs.conv_ag)
    carry(place, scatter, gather, to_conv)
    scatter = Scatter(place, refs.scatter, refs.conv_scatter)
    conv_forward(place, refs, gather, scatter)
    held.next_out.relay()
    saved.append(traffic.save(conv_kept()))
    for part in place.parts:
        frames = place.parts.of(part)
        refs.stream_three[frames, :] = refs.stream_two[frames, :] + scatter.total(part)
    scatter.drain()
    gather_next.finish()
    held.next_out.finish()
    for finish in saved:
        finish()


def scratch_of(kept):
    return {name: VMEM(shape, dtype) for name, (shape, dtype) in kept.items()}


def forward_call(ins):
    kept = {**ffn_kept(), **attention_kept(), **conv_kept()}
    outs = dict(
        stream_one=((128, 1024), F32, VMEM),
        stream_two=((128, 1024), F32, VMEM),
        stream_three=((128, 1024), F32, VMEM),
        next_in=((16, 64, 512), BF16, pl.ANY),
        next_out=((4, 128, 1024), BF16, pl.ANY),
    )
    outs["row_lengths"] = ((2, 8, 128), F32, VMEM)
    for name, (shape, dtype) in kept.items():
        outs["keep_" + name] = (shape, dtype, pl.ANY)
    scratch = dict(
        scratch_of(kept),
        active=VMEM((8, 128, 512), BF16),
        gather_in=GatherRows.scratch(),
        gather_out=GatherBlocks.scratch(),
        gather_out_last=GatherBlocks.scratch(),
        gather_qkv=GatherRows.scratch(),
        gather_o=GatherHalf.scratch(),
        gather_ci=GatherRows.scratch(),
        gather_co=GatherHalf.scratch(),
        gather_next=GatherRows.scratch(),
        gather_next_out=GatherBlocks.scratch(),
        length_sems=DMA((2,)),
        **table_scratch(),
        traffic=DMA((len(kept),)),
        scatter=Scatter.scratch(FORWARD_PARTS, 128 // FORWARD_PARTS, 1024),
        scatter_columns=Scatter.scratch(2, 128, 512),
        ffn_ag=AG_SEMS,
        attn_ag=AG_SEMS,
        conv_ag=AG_SEMS,
        ffn_scatter=SCATTER_SEMS,
        attn_scatter=SCATTER_SEMS,
        conv_scatter=SCATTER_SEMS,
        q_rows=VMEM((8, 128, 128), BF16),
        k_rows=VMEM((8, 128, 128), BF16),
        v_rows=VMEM((8, 128, 128), BF16),
        turn_qk=Turn.scratch(512),
        turn_v=Turn.scratch(256),
        turn_mix=Turn.scratch(256),
        values_t=VMEM((64, 2048), BF16),
        glu=VMEM((8, 128, 128), BF16),
        edges=Edges.scratch(),
        stats=STATS,
    )
    return kernel_call(forward_body, 1, ins, outs, scratch)


class SmallSum:
    def __init__(self, place, refs):
        self.place, self.refs = place, refs
        self.first = Exchange(place, refs.small_first, refs.small_first_sems)
        self.last = Exchange(place, refs.small, refs.small_last_sems)
        self.sent = []

    def start(self):
        refs, place = self.refs, self.place

        def part(slot):
            return refs.gain_grads.at[:, columns_of(slot, 128)]

        self.first.blocks[place.slot(0)] = refs.gain_grads[:, columns_of(place.slot(0), 128)]
        self.first.start(lambda k: part(place.slot(k)))

    def along_z(self):
        refs, place = self.refs, self.place
        self.first.wait()
        refs.small_planes[place.z, 0:8, :] = jnp.sum(self.first.blocks[...], axis=0)
        refs.small_planes[place.z, 8:48, :] = refs.channel_grads[...]
        send, recv = refs.small_z_sems
        rows = refs.small_planes.at[place.z]
        for k in (1, 2, 3):
            copy = remote(rows, rows, send.at[k], recv.at[k], place.zdev(k))
            copy.start()
            self.sent.append(copy)

    def spread(self):
        refs, place = self.refs, self.place
        send, recv = refs.small_z_sems
        for k in (1, 2, 3):
            into = refs.small_planes.at[lax.rem(place.z + 4 - k, PLANES)]
            remote(into, into, send.at[k], recv.at[k], place.zdev(k)).wait_recv()
        for copy in self.sent:
            copy.wait_send()
        own = place.slot(0)
        self.last.blocks[own] = jnp.sum(refs.small_planes[...], axis=0)
        self.last.start(lambda k: self.last.blocks.at[own])

    def wait(self):
        self.last.wait()


def backward_step(place, refs, stream, gain, row, scale):
    saved = [
        norm_forward(stream[place.parts.of(part), :].astype(F32), gain)[1] for part in place.parts
    ]

    def step(part, total):
        frames = place.parts.of(part)
        input_part, gain_grad = norm_input_grad(total, gain, saved[part])
        value = refs.grad_stream[frames, :] + input_part
        refs.grad_stream[frames, :] = value
        refs.gain_grads[row : row + 1, :] += gain_grad
        return (scale * value).astype(BF16)

    return step


def backward_body(refs):
    place = Place(BACKWARD_PARTS)
    place.enter()
    traffic = Traffic(refs, refs.traffic)
    ready = traffic.start([(refs.next_in, refs.w_in), (refs.next_out, refs.w_out)])
    gather = Gather(place, refs.blocks, refs.ffn2_ag)
    for part in place.parts:
        frames = place.parts.of(part)
        gather.push(part, norm_rows(refs.stream_three[frames, :], refs.gain_ffn2[...])[0])
    refs.finish_conv = traffic.load(conv_kept())
    refs.finish_attn = traffic.load(attention_kept())
    refs.gain_grads[...] = jnp.zeros_like(refs.gain_grads)
    refs.channel_grads[...] = jnp.zeros_like(refs.channel_grads)
    scatter = Scatter(place, refs.scatter, refs.ffn2_scatter)
    ffn_forward(place, gather, refs.hidden, refs.w_in, refs.w_out, scatter, ready)
    gather.drain()
    fill_tables(refs)
    fill_channels(place, refs)

    def turn_round(part, total):
        frames = place.parts.of(part)
        final, saved = norm_forward(refs.stream_three[frames, :] + 0.5 * total, refs.gain_out[...])
        refs.output[frames, :] = final.astype(BF16)
        grad, gain_grad = norm_input_grad(
            refs.cotangent[frames, :].astype(F32), refs.gain_out[...], saved
        )
        refs.grad_stream[frames, :] = grad
        refs.gain_grads[4:5, :] += gain_grad
        return (0.5 * grad).astype(BF16)

    gather = Gather(place, refs.grads_even, refs.ffn2_ag_back)
    carry(place, scatter, gather, turn_round)
    scatter = Scatter(place, refs.scatter, refs.ffn2_scatter_back)
    ffn_backward(
        place,
        gather,
        refs.hidden,
        refs.hidden_grads,
        refs.active,
        refs.w_in,
        refs.w_out,
        scatter,
        lambda: None,
    )
    gather.drain()
    step = backward_step(place, refs, refs.stream_three, refs.gain_ffn2[...], 3, 1.0)
    weights_two = WeightGrads(place, refs, "ffn2", "ffn", True)
    weights_two.put_both(refs.active, refs.grads_even, refs.blocks, refs.hidden_grads)
    gather = Gather(place, refs.grads_odd, refs.conv_ag)
    carry(place, scatter, gather, step)
    load_first = traffic.load(ffn_kept())
    refs.conv_begin, refs.conv_middle = weights_two.sum_out.relay, weights_two.sum_in.relay
    scatter = Scatter(place, refs.scatter, refs.conv_scatter)
    inner, taps, weights_three = conv_backward(place, refs, gather, scatter)
    step = backward_step(place, refs, refs.stream_two, refs.gain_conv[...], 2, 1.0)
    refs.channel_grads[0:32, :] = taps
    refs.channel_grads[32:33, :] = inner
    weights_three.put_in(refs.conv_blocks, refs.gate_grads)
    gather = Gather(place, refs.grads_even, refs.attn_ag)
    carry(place, scatter, gather, step)

    refs.before_mix = weights_two.share
    refs.before_attend, refs.after_attend = weights_three.relay, weights_three.share
    scatter = Scatter(place, refs.scatter, refs.attn_scatter)
    weights_four = attention_backward(place, refs, gather, scatter)
    step = backward_step(place, refs, refs.stream_one, refs.gain_attn[...], 1, 0.5)
    weights_four.put_in(refs.attn_blocks, refs.qkv_grads)
    gather = Gather(place, refs.grads_odd, refs.ffn1_ag)
    carry(place, scatter, gather, step)
    weights_four.sum_in.relay()
    weights_two.wait()
    weights_three.wait()
    weights_one = WeightGrads(place, refs, "ffn1", "ffn", True)
    scatter = Scatter(place, refs.scatter, refs.ffn1_scatter)
    ffn_backward(
        place,
        gather,
        refs.hidden,
        refs.hidden_grads,
        refs.active,
        refs.w_in,
        refs.w_out,
        scatter,
        load_first,
        lambda: weights_one.put_both(
            refs.active, refs.grads_odd, refs.blocks, refs.hidden_grads
        ),
    )
    gather.drain()
    weights_four.share()
    weights_one.sum_out.relay()
    step = backward_step(place, refs, refs.stream, refs.gain_ffn1[...], 0, 1.0)
    for part in place.parts:
        step(part, scatter.total(part))
    scatter.drain()
    small = SmallSum(place, refs)
    small.start()
    weights_one.sum_in.relay()
    small.along_z()
    weights_one.share_rows()
    small.spread()
    weights_one.share_columns()
    weights_four.wait()
    small.wait()
    weights_one.wait()


MODULES = (("ffn1", 512, True), ("qkv", 384, False), ("conv", 256, False), ("ffn2", 512, True))


def backward_call(ins):
    kept = {**ffn_kept(), **attention_kept(), **conv_kept()}
    outs = dict(
        output=((128, 1024), BF16, VMEM),
        grad_stream=((128, 1024), F32, VMEM),
        small=((8, 48, 128), F32, VMEM),
    )
    scratch = dict(
        scratch_of(kept),
        active=VMEM((8, 128, 512), BF16),
        hidden_grads=VMEM((8, 128, 512), BF16),
        grads_even=VMEM((8, 128, 1024), BF16),
        grads_odd=VMEM((8, 128, 1024), BF16),
        traffic=DMA((2 + len(kept),)),
        scatter=Scatter.scratch(BACKWARD_PARTS, 128 // BACKWARD_PARTS, 1024),
        ffn2_ag=AG_SEMS,
        ffn2_ag_back=AG_SEMS,
        conv_ag=AG_SEMS,
        attn_ag=AG_SEMS,
        ffn1_ag=AG_SEMS,
        ffn2_scatter=SCATTER_SEMS,
        ffn2_scatter_back=SCATTER_SEMS,
        conv_scatter=SCATTER_SEMS,
        attn_scatter=SCATTER_SEMS,
        ffn1_scatter=SCATTER_SEMS,
        mix_rows=VMEM((8, 128, 128), BF16),
        mix_grads=VMEM((2048, 64), BF16),
        keys_t=VMEM((64, 2048), BF16),
        turn_qk=Turn.scratch(512),
        turn_v=Turn.scratch(256),
        turn_mix=Turn.scratch(256),
        key_grad=VMEM((2048, 64), F32),
        value_grad=VMEM((2048, 64), F32),
        qkv_grads=VMEM((8, 128, 384), BF16),
        **table_scratch(),
        inner_grad=VMEM((8, 128, 128), F32),
        grad_stats=VMEM((128, 128), F32),
        conv_grad=VMEM((8, 128, 128), BF16),
        conv_grad_padded=VMEM((8, 160, 128), F32),
        glu_grad=VMEM((8, 128, 128), F32),
        gate_grads=VMEM((8, 128, 256), BF16),
        tap_sums=VMEM((32, 8, 128), F32),
        edges=Edges.scratch(),
        stats=STATS,
        gain_grads=VMEM((8, 1024), F32),
        channel_grads=VMEM((40, 128), F32),
        small_first=VMEM((8, 8, 128), F32),
        small_planes=VMEM((PLANES, 48, 128), F32),
        small_first_sems=[DMA((8,)), DMA((8,))],
        small_z_sems=[DMA((4,)), DMA((4,))],
        small_last_sems=[DMA((8,)), DMA((8,))],
        **WeightGrads.sums("ffn", 512, True),
        **WeightGrads.sums("qkv", 384, False),
        **WeightGrads.sums("conv", 256, False),
    )
    for name, width, wide in MODULES:
        outs.update(WeightGrads.outs(name, width, wide))
        scratch.update(WeightGrads.scratch(name, width, wide))
    return kernel_call(backward_body, 2, ins, outs, scratch)


def unpack_body(count, *refs):
    sources, outs = refs[:count], refs[count : 2 * count + 8]
    (
        output,
        grad_stream,
        small,
        ffn1_in,
        ffn1_out,
        qkv_in,
        qkv_out,
        conv_in,
        conv_out,
        ffn2_in,
        ffn2_out,
    ) = sources
    outs[0][...] = output[...]
    outs[1][...] = grad_stream[...]
    for slot in range(8):
        x, yc = divmod(slot, 4)
        pair = ((x * 2 + yc % 2) * 2 + yc // 2) * 128
        for index, row in enumerate((0, 1, 2, None, 3, 4)):
            if row is not None:
                outs[2 + index][:, slot * 128 : slot * 128 + 128] = small[slot, row : row + 1, :]
        outs[5][:, pair : pair + 128] = small[slot, 40:41, :]
        outs[8][:, pair : pair + 128] = small[slot, 8 : 8 + KERNEL, :]
        for source, out in ((ffn1_in, outs[9]), (ffn2_in, outs[15])):
            for plane in range(PLANES):
                column = ((plane * 4 + yc) * 2 + x) * 128
                out[:, column : column + 128] = source[
                    slot, :, plane * 128 : plane * 128 + 128
                ].astype(F32)
        for source, out, kinds in ((qkv_in, outs[11], 3), (conv_in, outs[13], 2)):
            for kind in range(kinds):
                column = kind * 1024 + pair
                out[:, column : column + 128] = source[slot, :, kind * 128 : kind * 128 + 128].astype(
                    F32
                )
    for source, out in ((ffn1_out, outs[10]), (ffn2_out, outs[16])):
        out[0:128, :] = source[0].astype(F32)
        out[128:256, :] = source[1].astype(F32)
    outs[12][...] = qkv_out[...].astype(F32)
    outs[14][...] = conv_out[...].astype(F32)


def unpack_call(backward):
    arrays = list(backward.values())
    gain = jax.ShapeDtypeStruct((1, 1024), F32)
    shapes = [
        jax.ShapeDtypeStruct((128, 1024), BF16),
        jax.ShapeDtypeStruct((128, 1024), F32),
        *[gain] * 6,
        jax.ShapeDtypeStruct((KERNEL, 1024), F32),
    ] + [
        jax.ShapeDtypeStruct(shape, F32)
        for shape in (
            (64, 4096),
            (256, 1024),
            (64, 3072),
            (64, 1024),
            (64, 2048),
            (64, 1024),
            (64, 4096),
            (256, 1024),
        )
    ]
    whole = pl.BlockSpec(memory_space=VMEM)
    return pl.pallas_call(
        functools.partial(unpack_body, len(arrays)),
        out_shape=shapes,
        in_specs=[whole] * len(arrays),
        out_specs=[whole] * len(shapes),
        compiler_params=pltpu.CompilerParams(vmem_limit_bytes=VMEM_LIMIT),
    )(*arrays)


def local_planes(
    inputs,
    lengths,
    gain_ffn1,
    gain_attn,
    gain_conv,
    gain_inner,
    gain_ffn2,
    gain_out,
    conv_kernel,
    ffn1_in,
    ffn1_out,
    attn_qkv,
    attn_out,
    conv_in,
    conv_out,
    ffn2_in,
    ffn2_out,
    cotangent,
):
    plane = lax.axis_index("seq") // 4
    cos, sin = rotary_tables(plane * 512 + jnp.arange(512, dtype=jnp.int32))
    shared = dict(
        stream=(inputs[0], VMEM),
        gain_ffn1=(gain_ffn1[None], VMEM),
        gain_attn=(gain_attn[None], VMEM),
        gain_conv=(gain_conv[None], VMEM),
        all_inner=(gain_inner[None], VMEM),
        all_taps=(conv_kernel, VMEM),
        cos_rows=(cos, VMEM),
        sin_rows=(sin, VMEM),
    )
    forward = forward_call(
        dict(
            shared,
            own_lengths=(jnp.pad(lengths.astype(F32), ((0, 7), (0, 124))), VMEM),
            w_in_rows=(ffn1_in, pl.ANY),
            w_out_rows=(ffn1_out, pl.ANY),
            qkv_rows=(attn_qkv, pl.ANY),
            o_rows=(attn_out, pl.ANY),
            ci_rows=(conv_in, pl.ANY),
            co_rows=(conv_out, pl.ANY),
            next_in_rows=(ffn2_in, pl.ANY),
            next_out_rows=(ffn2_out, pl.ANY),
        )
    )
    ins = dict(
        shared,
        cotangent=(cotangent[0], VMEM),
        gain_ffn2=(gain_ffn2[None], VMEM),
        gain_out=(gain_out[None], VMEM),
    )
    for name, array in forward.items():
        held = name.startswith("stream") or name == "row_lengths"
        ins[name] = (array, VMEM if held else pl.ANY)
    results = unpack_call(backward_call(ins))
    return (
        results[0][None],
        results[1][None],
        *[gain[0] for gain in results[2:8]],
        *results[8:],
    )


def solution(mesh):
    return jax.shard_map(
        local_planes if mesh.shape["seq"] == 16 and mesh.shape["row"] == 2 else local,
        mesh=mesh,
        in_specs=(
            P("row", "seq", None),
            P("row", None),
            P(),
            P(),
            P(),
            P(),
            P(),
            P(),
            P(),
            P("seq", None),
            P("seq", None),
            P("seq", None),
            P("seq", None),
            P("seq", None),
            P("seq", None),
            P("seq", None),
            P("seq", None),
            P("row", "seq", None),
        ),
        out_specs=(
            P("row", "seq", None),
            P("row", "seq", None),
            P(),
            P(),
            P(),
            P(),
            P(),
            P(),
            P(),
            P("seq", None),
            P("seq", None),
            P("seq", None),
            P("seq", None),
            P("seq", None),
            P("seq", None),
            P("seq", None),
            P("seq", None),
        ),
        check_vma=False,
    )
```

```python
import functools
import math

import jax
import jax.numpy as jnp
from jax import lax
from jax.experimental import pallas as pl
from jax.experimental.pallas import tpu as pltpu
from jax.sharding import PartitionSpec as P

HEADS = 16
HEAD_DIM = 64
KERNEL = 31
HALF = 15


EPSILON = 1e-05
MASKED = -1e30


def with_halo(block, sides, width):
    for axis, dim in sides:
        count = lax.axis_size(axis)
        forward = [(i, i + 1) for i in range(count - 1)]
        backward = [(target, source) for source, target in forward]
        low = lax.ppermute(
            lax.slice_in_dim(block, block.shape[dim] - width, None, axis=dim), axis, forward
        )
        high = lax.ppermute(lax.slice_in_dim(block, 0, width, axis=dim), axis, backward)
        block = jnp.concatenate([low, block, high], axis=dim)
    return block


def shifted(array, axis, by):
    size = lax.axis_size(axis)
    return lax.ppermute(array, axis, [(i, (i + by) % size) for i in range(size)])


def segment_of(positions, seg_lengths):
    boundary = jnp.cumsum(seg_lengths)[:-1]
    return jnp.sum((positions[:, None] >= boundary[None, :]).astype(jnp.int32), axis=1)


def rotary_tables(positions):
    half_dim = HEAD_DIM // 2
    inverse = jnp.exp(-jnp.log(10000.0) * jnp.arange(half_dim, dtype=jnp.float32) / half_dim)
    angles = positions.astype(jnp.float32)[:, None] * inverse[None, :]
    return (jnp.cos(angles), jnp.sin(angles))


def split_heads(values):
    return values.reshape(values.shape[0], HEADS, HEAD_DIM)


def rotate(values, cos_table, sin_table):
    half_dim = HEAD_DIM // 2
    shaped = split_heads(values)
    first_half = shaped[..., :half_dim]
    second_half = shaped[..., half_dim:]
    cos_heads = cos_table[:, None, :]
    sin_heads = sin_table[:, None, :]
    turned = jnp.concatenate(
        [
            first_half * cos_heads - second_half * sin_heads,
            second_half * cos_heads + first_half * sin_heads,
        ],
        axis=-1,
    )
    return turned.reshape(values.shape)


def unrotate(grads, cos_table, sin_table):
    half_dim = HEAD_DIM // 2
    shaped = split_heads(grads)
    first_half = shaped[..., :half_dim]
    second_half = shaped[..., half_dim:]
    cos_heads = cos_table[:, None, :]
    sin_heads = sin_table[:, None, :]
    turned = jnp.concatenate(
        [
            first_half * cos_heads + second_half * sin_heads,
            second_half * cos_heads - first_half * sin_heads,
        ],
        axis=-1,
    )
    return turned.reshape(grads.shape)


def norm_forward(values, gain):
    center = values - jnp.mean(values, axis=-1, keepdims=True)
    spread = jnp.mean(center * center, axis=-1, keepdims=True)
    inverse = lax.rsqrt(spread + EPSILON)
    unit_part = center * inverse
    return (unit_part * gain, (unit_part, inverse))


def norm_backward(grads, gain, saved):
    unit_part, inverse = saved
    scaled = grads * gain
    gain_grad = jnp.sum(grads * unit_part, axis=0)
    input_part = inverse * (
        scaled
        - jnp.mean(scaled, axis=-1, keepdims=True)
        - unit_part * jnp.mean(scaled * unit_part, axis=-1, keepdims=True)
    )
    return (input_part, gain_grad)


def sigmoid_linear(values):
    return values * jax.nn.sigmoid(values)


def sigmoid_linear_grad(values):
    sigma = jax.nn.sigmoid(values)
    return sigma * (1.0 + values * (1.0 - sigma))


def project(left_side, weight):
    return (
        jnp.dot(
            left_side,
            lax.all_gather(weight, "seq", axis=0, tiled=True),
            preferred_element_type=jnp.float32,
        ),
        weight,
    )


def project_back(grad_side, weight):
    return lax.dot_general(
        grad_side,
        lax.all_gather(weight, "seq", axis=0, tiled=True),
        (((1,), (1,)), ((), ())),
        preferred_element_type=jnp.float32,
    )


def weight_grad(left_side, grad_side):
    return lax.psum_scatter(
        lax.dot_general(
            left_side, grad_side, (((0,), (0,)), ((), ())), preferred_element_type=jnp.float32
        ).astype(jnp.bfloat16),
        "seq",
        scatter_dimension=0,
        tiled=True,
    ).astype(jnp.float32)


def over_blocks(advance, running, pieces):
    total_rows = pieces[0].shape[0]
    block_size = math.gcd(total_rows, 512)
    number = total_rows // block_size
    stacked = tuple((piece.reshape((number, block_size) + piece.shape[1:]) for piece in pieces))

    def scan_step(current, block_item):
        block_index, blocks = block_item
        return (advance(current, blocks, block_index * block_size), None)

    running, unused = lax.scan(scan_step, running, (jnp.arange(number, dtype=jnp.int32), stacked))
    return running


def block_scores(query_heads, key_heads, query_segments, key_segments):
    scale = HEAD_DIM ** (-0.5)
    raw_scores = (
        jnp.einsum("qhd,khd->hqk", query_heads, key_heads, preferred_element_type=jnp.float32)
        * scale
    )
    return jnp.where((query_segments[:, None] == key_segments[None, :])[None], raw_scores, MASKED)


def pair_grads(
    query_rows, grad_rows, log_total, delta, query_segments, key_rows, value_rows, key_segments
):
    scale = HEAD_DIM ** (-0.5)
    query_heads = split_heads(query_rows)
    grad_heads = split_heads(grad_rows)
    key_heads = split_heads(key_rows)
    value_heads = split_heads(value_rows)
    probs = jnp.exp(
        block_scores(query_heads, key_heads, query_segments, key_segments) - log_total[:, :, None]
    )
    prob_grads = jnp.einsum(
        "qhd,khd->hqk", grad_heads, value_heads, preferred_element_type=jnp.float32
    )
    score_grads = (probs * (prob_grads - delta[:, :, None])).astype(jnp.bfloat16)
    query_grad = (
        jnp.einsum("hqk,khd->qhd", score_grads, key_heads, preferred_element_type=jnp.float32)
        * scale
    )
    key_grad = (
        jnp.einsum("hqk,qhd->khd", score_grads, query_heads, preferred_element_type=jnp.float32)
        * scale
    )
    value_grad = jnp.einsum(
        "hqk,qhd->khd", probs.astype(jnp.bfloat16), grad_heads, preferred_element_type=jnp.float32
    )
    return (
        query_grad.reshape(query_rows.shape),
        key_grad.reshape(key_rows.shape),
        value_grad.reshape(value_rows.shape),
    )


def local(
    inputs,
    lengths,
    gain_ffn1,
    gain_attn,
    gain_conv,
    gain_inner,
    gain_ffn2,
    gain_out,
    conv_kernel,
    ffn1_in,
    ffn1_out,
    attn_qkv,
    attn_out,
    conv_in,
    conv_out,
    ffn2_in,
    ffn2_out,
    cotangent,
):
    frame_count = inputs.shape[1]
    model_width = inputs.shape[2]
    device_count = lax.axis_size("seq")
    position_index = lax.axis_index("seq")
    seg_lengths = lengths[0]
    first_frame = position_index * frame_count
    local_frames = jnp.arange(frame_count, dtype=jnp.int32)
    positions = first_frame + local_frames
    query_segments = segment_of(positions, seg_lengths)
    cos_table, sin_table = rotary_tables(positions)
    stream = inputs[0].astype(jnp.float32)
    normed_one, saved_one = norm_forward(stream, gain_ffn1)
    normed_one_low = normed_one.astype(jnp.bfloat16)
    hidden_one, kept_ffn1_in = project(normed_one_low, ffn1_in)
    active_one = sigmoid_linear(hidden_one).astype(jnp.bfloat16)
    branch_one, kept_ffn1_out = project(active_one, ffn1_out)
    stream_one = stream + 0.5 * branch_one
    normed_two, saved_two = norm_forward(stream_one, gain_attn)
    normed_two_low = normed_two.astype(jnp.bfloat16)
    projected, kept_qkv = project(normed_two_low, attn_qkv)
    query_low = rotate(projected[:, :model_width], cos_table, sin_table).astype(jnp.bfloat16)
    key_low = rotate(projected[:, model_width : 2 * model_width], cos_table, sin_table).astype(
        jnp.bfloat16
    )
    value_low = projected[:, 2 * model_width :].astype(jnp.bfloat16)
    query_heads = split_heads(query_low)

    def stats_step(current, blocks, first_row):
        top_score, denominator = current
        key_block = blocks[0]
        key_segments = segment_of(
            first_row + jnp.arange(key_block.shape[0], dtype=jnp.int32), seg_lengths
        )
        masked = block_scores(query_heads, split_heads(key_block), query_segments, key_segments)
        new_top = jnp.maximum(top_score, jnp.max(masked, axis=-1))
        denominator = denominator * jnp.exp(top_score - new_top) + jnp.sum(
            jnp.exp(masked - new_top[:, :, None]), axis=-1
        )
        return (new_top, denominator)

    top_init = jnp.full((HEADS, frame_count), MASKED, jnp.float32)
    total_init = jnp.zeros((HEADS, frame_count), jnp.float32)
    top_score, denominator = over_blocks(
        stats_step, (top_init, total_init), (lax.all_gather(key_low, "seq", axis=0, tiled=True),)
    )
    log_total = top_score + jnp.log(denominator)

    def value_step(current, blocks, first_row):
        mixed_sum, rest_sum = current
        key_block, value_block = blocks
        key_segments = segment_of(
            first_row + jnp.arange(key_block.shape[0], dtype=jnp.int32), seg_lengths
        )
        probs = jnp.exp(
            block_scores(query_heads, split_heads(key_block), query_segments, key_segments)
            - log_total[:, :, None]
        )
        probs_high = probs.astype(jnp.bfloat16)
        probs_rest = (probs - probs_high.astype(jnp.float32)).astype(jnp.bfloat16)
        value_heads = split_heads(value_block)
        mixed_sum = mixed_sum + jnp.einsum(
            "hqk,khd->qhd", probs_high, value_heads, preferred_element_type=jnp.float32
        )
        rest_sum = rest_sum + jnp.einsum(
            "hqk,khd->qhd", probs_rest, value_heads, preferred_element_type=jnp.float32
        )
        return (mixed_sum, rest_sum)

    zero_heads = jnp.zeros((frame_count, HEADS, HEAD_DIM), jnp.float32)
    mixed_sum, rest_sum = over_blocks(
        value_step,
        (zero_heads, zero_heads),
        (
            lax.all_gather(key_low, "seq", axis=0, tiled=True),
            lax.all_gather(value_low, "seq", axis=0, tiled=True),
        ),
    )
    exact_sum = mixed_sum + rest_sum
    mixed_low = mixed_sum.reshape(frame_count, model_width).astype(jnp.bfloat16)
    branch_two, kept_attn_out = project(mixed_low, attn_out)
    stream_two = stream_one + branch_two
    normed_three, saved_three = norm_forward(stream_two, gain_conv)
    normed_three_low = normed_three.astype(jnp.bfloat16)
    gate_up, kept_conv_in = project(normed_three_low, conv_in)
    first_part = gate_up[:, :model_width]
    gate_sigma = jax.nn.sigmoid(gate_up[:, model_width:])
    glu_low = (first_part * gate_sigma).astype(jnp.bfloat16)
    padded = with_halo(glu_low, (("seq", 0),), HALF).astype(jnp.float32)
    padded_segments = segment_of(
        first_frame - HALF + jnp.arange(frame_count + 2 * HALF, dtype=jnp.int32), seg_lengths
    )
    kernel_taps = conv_kernel.astype(jnp.float32)
    conv_values = jnp.zeros((frame_count, model_width), jnp.float32)
    for offset in range(KERNEL):
        same_segment = (padded_segments[offset : offset + frame_count] == query_segments).astype(
            jnp.float32
        )
        conv_values = (
            conv_values
            + kernel_taps[offset] * padded[offset : offset + frame_count] * same_segment[:, None]
        )
    normed_four, saved_four = norm_forward(conv_values, gain_inner)
    active_four = sigmoid_linear(normed_four).astype(jnp.bfloat16)
    branch_three, kept_conv_out = project(active_four, conv_out)
    stream_three = stream_two + branch_three
    normed_five, saved_five = norm_forward(stream_three, gain_ffn2)
    normed_five_low = normed_five.astype(jnp.bfloat16)
    hidden_two, kept_ffn2_in = project(normed_five_low, ffn2_in)
    active_two = sigmoid_linear(hidden_two).astype(jnp.bfloat16)
    branch_four, kept_ffn2_out = project(active_two, ffn2_out)
    stream_four = stream_three + 0.5 * branch_four
    final_norm, saved_six = norm_forward(stream_four, gain_out)
    output = final_norm.astype(jnp.bfloat16)[None]
    grad_four, grad_gain_six = norm_backward(cotangent[0].astype(jnp.float32), gain_out, saved_six)
    out_two_low = (0.5 * grad_four).astype(jnp.bfloat16)
    grad_ffn_two_out = weight_grad(active_two, out_two_low)
    hidden_two_low = (project_back(out_two_low, ffn2_out) * sigmoid_linear_grad(hidden_two)).astype(
        jnp.bfloat16
    )
    grad_ffn_two_in = weight_grad(normed_five_low, hidden_two_low)
    input_part, grad_gain_five = norm_backward(
        project_back(hidden_two_low, ffn2_in), gain_ffn2, saved_five
    )
    grad_three = grad_four + input_part
    conv_out_low = grad_three.astype(jnp.bfloat16)
    grad_conv_weight_out = weight_grad(active_four, conv_out_low)
    active_grad = project_back(conv_out_low, conv_out) * sigmoid_linear_grad(normed_four)
    conv_grad, grad_gain_four = norm_backward(active_grad, gain_inner, saved_four)
    conv_grad_low = conv_grad.astype(jnp.bfloat16)
    conv_grad_value = conv_grad_low.astype(jnp.float32)
    rim_grad = with_halo(conv_grad_low, (("seq", 0),), HALF).astype(jnp.float32)
    tap_grads = []
    glu_grad = jnp.zeros((frame_count, model_width), jnp.float32)
    for offset in range(KERNEL):
        same_segment = (padded_segments[offset : offset + frame_count] == query_segments).astype(
            jnp.float32
        )
        tap_grads.append(
            jnp.sum(
                padded[offset : offset + frame_count] * same_segment[:, None] * conv_grad_value,
                axis=0,
            )
        )
        back_start = 2 * HALF - offset
        back_segment = (
            padded_segments[back_start : back_start + frame_count] == query_segments
        ).astype(jnp.float32)
        glu_grad = (
            glu_grad
            + kernel_taps[offset]
            * rim_grad[back_start : back_start + frame_count]
            * back_segment[:, None]
        )
    kernel_grad = jnp.stack(tap_grads, axis=0)
    gate_up_low = jnp.concatenate(
        [glu_grad * gate_sigma, glu_grad * first_part * gate_sigma * (1.0 - gate_sigma)], axis=1
    ).astype(jnp.bfloat16)
    grad_conv_weight_in = weight_grad(normed_three_low, gate_up_low)
    input_part, grad_gain_three = norm_backward(
        project_back(gate_up_low, conv_in), gain_conv, saved_three
    )
    grad_two = grad_three + input_part
    attn_grad_low = grad_two.astype(jnp.bfloat16)
    grad_attn_weight = weight_grad(mixed_low, attn_grad_low)
    mixed_grad_low = project_back(attn_grad_low, attn_out).astype(jnp.bfloat16)
    delta = jnp.transpose(
        jnp.sum(split_heads(mixed_grad_low).astype(jnp.float32) * exact_sum, axis=-1)
    )

    def key_turn(turn_index, current):
        key_rows, value_rows, key_acc, value_acc, query_acc = current
        owner = (position_index - turn_index) % device_count
        key_segments = segment_of(owner * frame_count + local_frames, seg_lengths)
        query_part, key_part, value_part = pair_grads(
            query_low,
            mixed_grad_low,
            log_total,
            delta,
            query_segments,
            key_rows,
            value_rows,
            key_segments,
        )
        key_rows, value_rows = shifted((key_rows, value_rows), "seq", 1)
        key_acc, value_acc = (
            shifted((key_acc + key_part).astype(jnp.bfloat16), "seq", 1).astype(jnp.float32),
            shifted((value_acc + value_part).astype(jnp.bfloat16), "seq", 1).astype(jnp.float32),
        )
        return (key_rows, value_rows, key_acc, value_acc, query_acc + query_part)

    zero_rows = jnp.zeros((frame_count, model_width), jnp.float32)
    unused_keys, unused_values, key_grad, value_grad, query_grad = lax.fori_loop(
        0, device_count, key_turn, (key_low, value_low, zero_rows, zero_rows, zero_rows)
    )
    projected_grad_low = jnp.concatenate(
        [
            unrotate(query_grad, cos_table, sin_table),
            unrotate(key_grad, cos_table, sin_table),
            value_grad,
        ],
        axis=1,
    ).astype(jnp.bfloat16)
    grad_qkv_weight = weight_grad(normed_two_low, projected_grad_low)
    input_part, grad_gain_two = norm_backward(
        project_back(projected_grad_low, attn_qkv), gain_attn, saved_two
    )
    grad_one = grad_two + input_part
    out_one_low = (0.5 * grad_one).astype(jnp.bfloat16)
    grad_ffn_one_out = weight_grad(active_one, out_one_low)
    hidden_one_low = (project_back(out_one_low, ffn1_out) * sigmoid_linear_grad(hidden_one)).astype(
        jnp.bfloat16
    )
    grad_ffn_one_in = weight_grad(normed_one_low, hidden_one_low)
    input_part, grad_gain_one = norm_backward(
        project_back(hidden_one_low, ffn1_in), gain_ffn1, saved_one
    )
    input_grad = (grad_one + input_part)[None]
    small_grads = lax.psum(
        (
            grad_gain_one,
            grad_gain_two,
            grad_gain_three,
            grad_gain_four,
            grad_gain_five,
            grad_gain_six,
            kernel_grad,
        ),
        ("seq", "row"),
    )
    large_grads = (
        grad_ffn_one_in,
        grad_ffn_one_out,
        grad_qkv_weight,
        grad_attn_weight,
        grad_conv_weight_in,
        grad_conv_weight_out,
        grad_ffn_two_in,
        grad_ffn_two_out,
    )
    large_grads = (
        lax.psum(grad_ffn_one_in.astype(jnp.bfloat16), "row").astype(jnp.float32),
        lax.psum(grad_ffn_one_out.astype(jnp.bfloat16), "row").astype(jnp.float32),
        lax.psum(grad_qkv_weight.astype(jnp.bfloat16), "row").astype(jnp.float32),
        lax.psum(grad_attn_weight.astype(jnp.bfloat16), "row").astype(jnp.float32),
        lax.psum(grad_conv_weight_in.astype(jnp.bfloat16), "row").astype(jnp.float32),
        lax.psum(grad_conv_weight_out.astype(jnp.bfloat16), "row").astype(jnp.float32),
        lax.psum(grad_ffn_two_in.astype(jnp.bfloat16), "row").astype(jnp.float32),
        lax.psum(grad_ffn_two_out.astype(jnp.bfloat16), "row").astype(jnp.float32),
    )
    return (
        output,
        input_grad,
        small_grads[0],
        small_grads[1],
        small_grads[2],
        small_grads[3],
        small_grads[4],
        small_grads[5],
        small_grads[6],
        large_grads[0],
        large_grads[1],
        large_grads[2],
        large_grads[3],
        large_grads[4],
        large_grads[5],
        large_grads[6],
        large_grads[7],
    )


BF16 = jnp.bfloat16
F32 = jnp.float32
PLANES = 4
VMEM = pltpu.VMEM
DMA = pltpu.SemaphoreType.DMA
VMEM_LIMIT = 60 * 1024 * 1024
FORWARD_PARTS = 1
BACKWARD_PARTS = 1


class Place:
    def __init__(self, parts):
        self.parts = Parts(parts)
        seq = lax.axis_index("seq")
        self.x = lax.axis_index("row")
        self.z = seq // 4
        self.yc = lax.rem(seq, 4)
        self.core = lax.rem(self.yc, 2)
        inside = lax.rem(self.z + self.z // 2, 2)
        self.end, self.middle = inside == 0, inside == 1
        self.beside, self.across, self.opposite = self.line(1 - inside), self.line(2), self.line(3)

    def flip(self, k):
        y, c, x = self.yc // 2, lax.rem(self.yc, 2), self.x
        c = 1 - c if k & 1 else c
        y = 1 - y if k & 2 else y
        x = 1 - x if k & 4 else x
        return x, y * 2 + c

    def dev(self, k):
        x, yc = self.flip(k)
        return {"seq": self.z * 4 + yc, "row": x}

    def slot(self, k):
        x, yc = self.flip(k)
        return x * 4 + yc

    def row(self, k):
        return self.flip(k)[0]

    def zdev(self, k):
        return self.at(lax.rem(self.z + k, PLANES))

    def at(self, plane, yc=None):
        return {"seq": plane * 4 + (self.yc if yc is None else yc), "row": self.x}

    def line(self, index):
        return index + self.z // 2 * (3 - 2 * index)

    def pair(self, x=None, yc=None):
        x = self.x if x is None else x
        yc = self.yc if yc is None else yc
        return (x * 2 + lax.rem(yc, 2)) * 2 + yc // 2

    def enter(self):
        barrier = pltpu.get_barrier_semaphore()
        partners = [self.dev(k) for k in range(1, 8)]
        for k in range(1, PLANES):
            plane = lax.rem(self.z + k, PLANES)
            partners += [self.at(plane), self.at(plane, self.flip(1)[1])]
        for partner in partners:
            pl.semaphore_signal(barrier, inc=1, device_id=partner)
        pl.semaphore_wait(barrier, len(partners))


def remote(src, dst, send_sem, recv_sem, dev):
    return pltpu.make_async_remote_copy(src, dst, send_sem, recv_sem, device_id=dev)


def dot(left, right, left_dim=1, right_dim=0):
    return lax.dot_general(
        left, right, (((left_dim,), (right_dim,)), ((), ())), preferred_element_type=F32
    )


PAIRS = (((0, 1),), ((2, 4), (3, 5)), ((6, 7),))
LAST_OF_ROW = {(3, 5): 0, (6, 7): 4}
OUT_PAIRS = ((7, 3), (5, 1), (6, 2), (4, 0))


class Parts:
    def __init__(self, count):
        self.count = count
        self.rows = 128 // count

    def __iter__(self):
        return iter(range(self.count))

    def of(self, part):
        return slice(part * self.rows, part * self.rows + self.rows)

    def take(self, ref, slots, part):
        return jnp.concatenate([ref[slot, self.of(part), :] for slot in slots], axis=0)

    def put(self, ref, slots, part, value):
        for index, slot in enumerate(slots):
            ref[slot, self.of(part), :] = value[index * self.rows : index * self.rows + self.rows]


class Gather:
    def __init__(self, place, blocks, sems):
        self.place, self.blocks = place, blocks
        self.send, self.recv = sems
        self.rows = place.parts.rows
        self.sent = []

    def at(self, slot, part, half=None):
        count = self.rows if half is None else self.rows // 2
        first = part * self.rows + (half or 0) * count
        return self.blocks.at[slot, pl.ds(first, count)]

    def copy(self, rows, to, part, sem):
        sem = part * 11 + sem
        return remote(rows, rows, self.send.at[sem], self.recv.at[sem], self.place.dev(to))

    def hand(self, rows, to, part, sem):
        copy = self.copy(rows, to, part, sem)
        copy.start()
        self.sent.append(copy)

    def push(self, part, value):
        own = self.place.slot(0)
        self.blocks[own, self.place.parts.of(part), :] = value
        for half in range(2):
            self.hand(self.at(own, part, 1 - half), 4, part, 4 + 5 * (half == 1))
            self.hand(self.at(own, part, half), 2, part, 2 + 8 * (half == 1))
        self.hand(self.at(own, part), 1, part, 1)

    def arrive(self, rows, part, sem):
        self.copy(rows, 1, part, sem).wait_recv()

    def fetch(self, ks, part):
        slots = {k: self.place.slot(k) for k in ks}
        if 2 in slots:
            self.arrive(self.at(slots[2], part, 0), part, 2)
            self.hand(self.at(slots[2], part, 0), 4, part, 6)
            self.arrive(self.at(slots[4], part, 1), part, 4)
            self.hand(self.at(slots[4], part, 1), 2, part, 8)
            self.arrive(self.at(slots[2], part, 1), part, 10)
            self.hand(self.at(slots[2], part), 1, part, 3)
            self.arrive(self.at(slots[4], part, 0), part, 9)
            self.hand(self.at(slots[4], part), 1, part, 5)
        if 6 in slots:
            self.arrive(self.at(slots[6], part, 0), part, 6)
            self.arrive(self.at(slots[6], part, 1), part, 8)
            self.hand(self.at(slots[6], part), 1, part, 7)
        for k in ks:
            if k % 2:
                self.arrive(self.at(slots[k], part), part, k)
        return slots

    def drain(self):
        for copy in self.sent:
            copy.wait_send()


class Scatter:
    def __init__(self, place, buffers, sems):
        self.place = place
        self.part, self.staged, self.sibling, self.reduced, self.received, self.relayed = buffers
        self.relays = False
        self.send, self.recv = sems
        self.sent = []

    @staticmethod
    def scratch(parts, rows, width):
        return [
            VMEM((parts, 4, rows, width), F32),
            VMEM((parts, 4, rows, width), BF16),
            VMEM((parts, 4, rows, width), BF16),
            VMEM((parts, 3, rows, width), BF16),
            VMEM((parts, 3, rows, width), BF16),
            VMEM((parts, 2, rows // 2, width), BF16),
        ]

    def copy(self, src, dst, part, sem, k):
        sem = part * 11 + sem
        return remote(src, dst, self.send.at[sem], self.recv.at[sem], self.place.dev(k))

    def push(self, *what):
        copy = self.copy(*what)
        copy.start()
        self.sent.append(copy)

    def emit(self, k, part, value):
        index = k // 2
        if k % 2:
            self.staged[part, index] = value.astype(BF16)
            self.push(
                self.staged.at[part, index], self.sibling.at[part, index], part, index, 1
            )
        else:
            self.part[part, index] = value

    def emit_pair(self, pair, part, value):
        rows = value.shape[0] // len(pair)
        for index, k in enumerate(pair):
            self.emit(k, part, value[index * rows : index * rows + rows])

    def of_chip(self, index, part):
        into = self.sibling.at[part, index]
        self.copy(into, into, part, index, 1).wait_recv()
        return self.part[part, index] + self.sibling[part, index].astype(F32)

    def finish_all(self, part):
        self.relays = True
        count = self.relayed.shape[2]
        halves = (pl.ds(0, count), pl.ds(count, count))
        self.reduced[part, 2] = self.of_chip(3, part).astype(BF16)
        for half, k in ((0, 4), (1, 2)):
            self.push(
                self.reduced.at[part, 2, halves[half]], self.relayed.at[part, half], part, 7 + half, k
            )
        sums = [self.of_chip(1, part), self.of_chip(2, part)]

        def send(index, half, value, sem):
            self.reduced[part, index, halves[half], :] = value.astype(BF16)
            self.push(
                self.reduced.at[part, index, halves[half]],
                self.received.at[part, index, halves[half]],
                part,
                sem,
                2 + 2 * index,
            )

        send(0, 1, sums[0][count:], 4)
        send(1, 0, sums[1][:count], 5)
        self.part[part, 0] = self.of_chip(0, part)
        for index, rows in ((0, slice(0, count)), (1, slice(count, 2 * count))):
            into = self.relayed.at[part, index]
            self.copy(into, into, part, 7 + index, 1).wait_recv()
            send(index, index, sums[index][rows] + self.relayed[part, index].astype(F32), 9 + index)

    def finish(self, k, part):
        index = k // 2
        total = self.of_chip(index, part)
        if k:
            self.reduced[part, index - 1] = total.astype(BF16)
            self.push(
                self.reduced.at[part, index - 1],
                self.received.at[part, index - 1],
                part,
                3 + index,
                k,
            )
        else:
            self.part[part, 0] = total

    def total(self, part):
        value = self.part[part, 0]
        if self.relays:
            count = self.relayed.shape[2]
            for index in range(2):
                for half in range(2):
                    into = self.received.at[part, index, pl.ds(half * count, count)]
                    sem = 9 + index if half == index else 4 + index
                    self.copy(into, into, part, sem, 1).wait_recv()
                value = value + self.received[part, index].astype(F32)
            return value
        for index in range(3):
            into = self.received.at[part, index]
            self.copy(into, into, part, 4 + index, 1).wait_recv()
            value = value + self.received[part, index].astype(F32)
        return value

    def drain(self):
        for copy in self.sent:
            copy.wait_send()


def gather_blocks(place, gather, process, scatter=None, before_last=None):
    for part in place.parts:
        for group in PAIRS:
            slots = gather.fetch([k for pair in group for k in pair], part)
            for pair in group:
                process(pair, [slots[k] for k in pair], part)
            if scatter and group == PAIRS[1]:
                scatter.finish(2, part)
                scatter.finish(4, part)
        if before_last and part == place.parts.count - 1:
            before_last()
        if scatter:
            scatter.finish(6, part)
            scatter.finish(0, part)


def scatter_blocks(place, scatter, rows, weight, side=0):
    for part in place.parts:
        for pair in OUT_PAIRS:
            slots = [place.slot(k) for k in pair]
            scatter.emit_pair(pair, part, dot(rows(slots, part), flat(weight), 1, side))
        scatter.finish_all(part)


def carry(place, scatter, gather, step):
    for part in place.parts:
        gather.push(part, step(part, scatter.total(part)))
    scatter.drain()


class Refs:
    pass


def kernel_call(body, collective, ins, outs, scratch):
    in_names = list(ins)
    out_names = list(outs)
    scratch_names = list(scratch)
    flat_scratch = []
    counts = []
    for name in scratch_names:
        item = scratch[name]
        counts.append(len(item) if isinstance(item, list) else 0)
        flat_scratch += item if isinstance(item, list) else [item]

    def kernel(*refs):
        held = Refs()
        at = 0
        for name in in_names + out_names:
            setattr(held, name, refs[at])
            at += 1
        for name, count in zip(scratch_names, counts):
            setattr(held, name, refs[at : at + count] if count else refs[at])
            at += max(count, 1)
        body(held)

    results = pl.pallas_call(
        kernel,
        out_shape=[jax.ShapeDtypeStruct(shape, dtype) for shape, dtype, unused in outs.values()],
        in_specs=[pl.BlockSpec(memory_space=space) for unused, space in ins.values()],
        out_specs=[pl.BlockSpec(memory_space=space) for unused, unused_type, space in outs.values()],
        scratch_shapes=flat_scratch,
        compiler_params=pltpu.CompilerParams(
            collective_id=collective, has_side_effects=True, vmem_limit_bytes=VMEM_LIMIT
        ),
    )(*[array for array, unused in ins.values()])
    return dict(zip(out_names, results))


class AlongZ:
    def __init__(self, place, sems, block):
        self.place = place
        self.send, self.recv = sems
        self.block = block
        self.sent = []

    def copy(self, source, owner, plane, sem):
        into = self.block(owner)
        return remote(
            source, into, self.send.at[sem], self.recv.at[owner], self.place.at(plane)
        )

    def arrive(self, owner):
        self.copy(self.block(owner), owner, owner, 0).wait_recv()

    def start(self, source):
        place = self.place
        self.sent = [
            self.copy(source, place.z, place.across, 0),
            self.copy(source, place.z, place.beside, 1),
        ]
        self.last = [
            self.copy(source, place.z, place.opposite, 2),
            self.copy(self.block(place.opposite), place.opposite, place.line(0), 3),
        ]
        for copy in self.sent:
            copy.start()

        @pl.when(place.middle)
        def start():
            self.last[0].start()

    def relay(self):
        @pl.when(self.place.middle)
        def hand_on():
            self.arrive(self.place.opposite)
            self.last[1].start()

    def finish(self):
        place = self.place
        self.arrive(place.beside)
        self.arrive(place.across)

        @pl.when(place.end)
        def last():
            self.arrive(place.opposite)

        for copy in self.sent:
            copy.wait_send()

        @pl.when(place.middle)
        def drain():
            for copy in self.last:
                copy.wait_send()


class GatherRows:
    def __init__(self, place, src, dst, sems, pieces):
        self.place, self.dst = place, dst
        self.send, self.recv, self.local = sems[:3]
        self.along = AlongZ(place, sems[3:], lambda plane: dst.at[pl.ds(plane * 4, 4)])
        mine = place.z * 4 + place.yc
        for k in (0, 2, 3, 1):
            x, to = place.flip(k)
            for index, column in enumerate(pieces(place, to)):
                source = src.at[:, pl.ds(pl.multiple_of(column * 128, 128), 128)]
                into = dst.at[mine, :, pl.ds(index * 128, 128)]
                if k:
                    remote(source, into, self.send.at[k], self.recv.at[k], place.dev(k)).start()
                else:
                    pltpu.make_async_copy(source, into, self.local).start()

    def along_z(self):
        place = self.place
        mine = self.dst.at[place.z * 4 + place.yc]
        pltpu.make_async_copy(mine, mine, self.local).wait()
        for k in (2, 3, 1):
            into = self.dst.at[place.z * 4 + place.flip(k)[1]]
            remote(into, into, self.send.at[k], self.recv.at[k], place.dev(k)).wait_recv()
        self.along.start(self.dst.at[pl.ds(place.z * 4, 4)])

    def relay(self):
        self.along.relay()

    def finish(self):
        place = self.place
        self.along.finish()
        mine = self.dst.at[place.z * 4 + place.yc]
        for k in (2, 3, 1):
            remote(mine, mine, self.send.at[k], self.recv.at[k], place.dev(k)).wait_send()

    @staticmethod
    def scratch():
        return [DMA((4,)), DMA((4,)), DMA, DMA((4,)), DMA((PLANES,))]


def ffn_pieces(place, yc):
    return [(plane * 4 + yc) * 2 + place.x for plane in range(PLANES)]


def head_pieces(place, yc):
    return [kind * 8 + place.pair(None, yc) for kind in range(3)]


def channel_pieces(place, yc):
    return [kind * 8 + place.pair(None, yc) for kind in range(2)]


class GatherBlocks:
    def __init__(self, place, src, dst, sems, columns=slice(0, 1024)):
        columns = pl.ds(columns.start, columns.stop - columns.start)
        src = src.at[pl.ds(place.x * 128, 128), columns]
        self.along = AlongZ(place, sems[1:], lambda plane: dst.at[plane, :, columns])
        self.own = pltpu.make_async_copy(src, dst.at[place.z, :, columns], sems[0])
        self.own.start()
        self.along.start(src)

    def relay(self):
        self.along.relay()

    def finish(self):
        self.own.wait()
        self.along.finish()

    @staticmethod
    def scratch():
        return [DMA, DMA((4,)), DMA((PLANES,))]


class PlaneSum:
    def __init__(self, place, refs):
        self.place = place
        self.own, self.staged, self.received, self.relayed, self.send, self.recv = refs

    @staticmethod
    def scratch(rows, width):
        return [
            VMEM((rows, width), F32),
            VMEM((3, rows, width), BF16),
            VMEM((3, rows, width), BF16),
            VMEM((rows, width), BF16),
            DMA((4,)),
            DMA((4,)),
        ]

    def term_copy(self, index, plane):
        slot = lax.rem(plane + 3 - self.place.z, PLANES)
        return remote(
            self.staged.at[index],
            self.received.at[slot],
            self.send.at[index],
            self.recv.at[slot],
            self.place.at(plane),
        )

    def relay_copy(self):
        return remote(
            self.staged.at[0],
            self.relayed,
            self.send.at[3],
            self.recv.at[3],
            self.place.at(self.place.beside),
        )

    def first(self, term):
        self.staged[0] = term(self.place.opposite).astype(BF16)

        @pl.when(self.place.end)
        def start():
            self.relay_copy().start()

    def rest(self, term):
        place = self.place
        self.staged[1] = term(place.across).astype(BF16)
        self.term_copy(1, place.across).start()
        self.staged[2] = term(place.beside).astype(BF16)
        self.term_copy(2, place.beside).start()
        self.own[...] = term(place.z)

    def relay(self):
        @pl.when(self.place.middle)
        def add():
            self.relay_copy().wait_recv()
            self.staged[0] = (
                self.staged[0].astype(F32) + self.relayed[...].astype(F32)
            ).astype(BF16)
            self.term_copy(0, self.place.opposite).start()

    def arrive(self, plane):
        slot = lax.rem(self.place.z + 3 - plane, PLANES)
        into = self.received.at[slot]
        remote(
            into, into, self.send.at[0], self.recv.at[slot], self.place.at(plane)
        ).wait_recv()

    def total(self):
        place = self.place
        self.arrive(place.beside)
        self.arrive(place.across)

        @pl.when(place.middle)
        def last():
            self.arrive(place.opposite)
            self.term_copy(0, place.opposite).wait_send()

        @pl.when(place.end)
        def nothing():
            self.received[lax.rem(place.z + 3 - place.opposite, PLANES)] = jnp.zeros(
                self.received.shape[1:], BF16
            )
            self.relay_copy().wait_send()

        self.term_copy(1, place.across).wait_send()
        self.term_copy(2, place.beside).wait_send()
        value = self.own[...]
        for index in range(3):
            value = value + self.received[index].astype(F32)
        return value


class Exchange:
    def __init__(self, place, blocks, sems, partners=tuple(range(1, 8)), slot=None):
        self.place = place
        self.blocks = blocks
        self.send, self.recv = sems
        self.partners = partners
        self.slot = slot or place.slot
        self.sent = []

    def start(self, source):
        own = self.slot(0)
        for k in self.partners:
            copy = remote(
                source(k), self.blocks.at[own], self.send.at[k], self.recv.at[k], self.place.dev(k)
            )
            copy.start()
            self.sent.append(copy)

    def wait(self):
        for k in self.partners:
            into = self.blocks.at[self.slot(k)]
            remote(into, into, self.send.at[k], self.recv.at[k], self.place.dev(k)).wait_recv()
        for copy in self.sent:
            copy.wait_send()


def flat(ref):
    value = ref[...]
    return value.reshape(value.shape[0] * value.shape[1], value.shape[2])


def ffn_forward(place, gather, hidden, w_in, w_out, scatter, ready):
    def process(pair, slots, part):
        if part == 0 and pair[0] == 0:
            ready()
        value = dot(place.parts.take(gather.blocks, slots, part), flat(w_in))
        place.parts.put(hidden, slots, part, value)
        scatter.emit_pair(pair, part, dot(sigmoid_linear(value).astype(BF16), flat(w_out)))

    gather_blocks(place, gather, process, scatter)


def ffn_backward(place, gather, hidden, hidden_grads, active, w_in, w_out, scatter, ready, before_last=None):
    def process(pair, slots, part):
        if part == 0 and pair[0] == 0:
            ready()
        value = place.parts.take(hidden, slots, part)
        sigma = jax.nn.sigmoid(value)
        place.parts.put(active, slots, part, (value * sigma).astype(BF16))
        back = dot(place.parts.take(gather.blocks, slots, part), flat(w_out), 1, 1)
        low = (back * (sigma * (1.0 + value * (1.0 - sigma)))).astype(BF16)
        place.parts.put(hidden_grads, slots, part, low)
        scatter.emit_pair(pair, part, dot(low, flat(w_in), 1, 1))

    gather_blocks(place, gather, process, scatter, before_last)


def token_dot(left, columns, right):
    count, rows, unused = left.shape
    taken = left[:, :, columns].reshape(count * rows, -1)
    return dot(taken, flat(right), 0, 0)


def columns_of(plane, width):
    return pl.ds(pl.multiple_of(plane * width, width), width)


class WeightGrads:
    def __init__(self, place, refs, name, sums, wide):
        self.place = place
        self.sum_in = PlaneSum(place, getattr(refs, sums + "_sum_in"))
        self.total_in = getattr(refs, name + "_total_in")
        self.share_in = Exchange(
            place, getattr(refs, name + "_grad_in"), getattr(refs, name + "_share_in")
        )
        self.wide = wide
        if wide:
            self.sum_out = PlaneSum(place, getattr(refs, sums + "_sum_out"))
            self.share_out = Exchange(
                place,
                getattr(refs, name + "_grad_out"),
                getattr(refs, name + "_share_out"),
                (4,),
                lambda k: place.flip(k)[0],
            )
        else:
            self.sum_out = HalfSum(
                place, getattr(refs, sums + "_sum_out"), getattr(refs, name + "_grad_out")
            )

    def put_out(self, active, grads):
        self.sum_out.put(dot(flat(active), flat(grads), 0, 0))

    def put_in(self, blocks, grads):
        def term(plane):
            return token_dot(blocks, columns_of(plane, 256), grads)

        self.sum_in.first(term)
        self.sum_in.rest(term)

    def put_both(self, active, grads, blocks, hidden_grads):
        def out(plane):
            return token_dot(active, columns_of(plane, 128), grads)

        def into(plane):
            return token_dot(blocks, columns_of(plane, 256), hidden_grads)

        self.sum_out.first(out)
        self.sum_in.first(into)
        self.sum_out.rest(out)
        self.sum_in.rest(into)

    def relay(self):
        self.sum_out.relay()
        self.sum_in.relay()

    def share(self):
        self.share_rows()
        self.share_columns()

    def share_rows(self):
        if self.wide:
            self.share_out.blocks[self.place.x] = self.sum_out.total().astype(BF16)
            self.share_out.start(lambda k: self.share_out.blocks.at[self.place.x])
        else:
            self.sum_out.add()

    def share_columns(self):
        self.total_in[...] = self.sum_in.total().astype(BF16).reshape(self.total_in.shape)
        self.share_in.blocks[self.place.slot(0)] = self.total_in[self.place.yc]
        self.share_in.start(lambda k: self.total_in.at[self.place.flip(k)[1]])

    def wait(self):
        (self.share_out if self.wide else self.sum_out).wait()
        self.share_in.wait()

    @staticmethod
    def sums(name, width, wide):
        return {
            name + "_sum_in": PlaneSum.scratch(256, width),
            name + "_sum_out": PlaneSum.scratch(128, 1024) if wide else HalfSum.scratch(1024),
        }

    @staticmethod
    def scratch(name, width, wide):
        held = {
            name + "_total_in": VMEM((4, 64, width), BF16),
            name + "_share_in": [DMA((8,)), DMA((8,))],
        }
        if wide:
            held[name + "_share_out"] = [DMA((8,)), DMA((8,))]
        return held

    @staticmethod
    def outs(name, width, wide):
        return {
            name + "_grad_in": ((8, 64, width), BF16, VMEM),
            name + "_grad_out": ((2, 128, 1024) if wide else (64, 1024), BF16, VMEM),
        }


AG_SEMS = [DMA((22,)), DMA((22,))]


def norm_rows(values, gain):
    normed, saved = norm_forward(values, gain)
    return normed.astype(BF16), saved


def norm_input_grad(grads, gain, saved):
    unit_part, inverse = saved
    scaled = grads * gain
    gain_grad = jnp.sum(grads * unit_part, axis=0, keepdims=True)
    input_part = inverse * (
        scaled
        - jnp.mean(scaled, axis=-1, keepdims=True)
        - unit_part * jnp.mean(scaled * unit_part, axis=-1, keepdims=True)
    )
    return input_part, gain_grad


class GatherHalf:
    def __init__(self, place, src, dst, sems):
        self.place, self.dst = place, dst
        self.send, self.recv, self.local = sems
        self.source = place.z // 2 == place.x
        self.first, self.last = 2 - place.x, 3 - 3 * place.x
        target = place.yc // 2 * 2 + lax.rem(place.z, 2)
        self.same = lax.rem(place.z, 2) == place.core
        self.own = pltpu.make_async_copy(src, dst.at[place.core], self.local)

        def copy(sem, plane):
            return remote(
                src,
                dst.at[place.core],
                self.send.at[sem],
                self.recv.at[place.core],
                place.at(plane, target),
            )

        self.far, self.near, self.sibling = (
            copy(0, self.first),
            copy(1, place.x * 2 + 1 - lax.rem(place.z, 2)),
            copy(2, place.z),
        )

        @pl.when(self.source)
        def start():
            self.far.start()
            self.near.start()

            @pl.when(self.same)
            def local():
                self.own.start()

            @pl.when(jnp.logical_not(self.same))
            def sibling():
                self.sibling.start()

    def on(self, half):
        rows = self.dst.at[half]
        return remote(
            rows, rows, self.send.at[half], self.recv.at[half], self.place.at(self.last)
        )

    def relay(self):
        @pl.when(self.place.z == self.first)
        def hand_on():
            for half in range(2):
                self.on(half).wait_recv()
                self.on(half).start()

    def finish(self):
        place = self.place
        at_home = place.z == place.x * 2 + place.core
        for half in range(2):
            here = jnp.logical_or(
                jnp.logical_and(at_home, place.core == half), place.z == self.first
            )

            @pl.when(jnp.logical_not(here))
            def arrive():
                self.on(half).wait_recv()

        @pl.when(self.source)
        def drain():
            self.far.wait_send()
            self.near.wait_send()

            @pl.when(self.same)
            def local():
                self.own.wait()

            @pl.when(jnp.logical_not(self.same))
            def sibling():
                self.sibling.wait_send()

        @pl.when(place.z == self.first)
        def drain_on():
            for half in range(2):
                self.on(half).wait_send()

    @staticmethod
    def scratch():
        return [DMA((3,)), DMA((2,)), DMA]


class HalfSum:
    def __init__(self, place, refs, result):
        self.place = place
        self.staged, self.received, self.relayed, self.send, self.recv, self.last = refs
        self.result = result
        self.near = place.z // 2 == place.x
        self.far_middle, self.far_end = 2 - place.x, 3 - 3 * place.x
        self.home = place.x * 2 + place.core

    @staticmethod
    def scratch(width):
        return [
            VMEM((2, 64, width), BF16),
            VMEM((3, 64, width), BF16),
            VMEM((2, 64, width), BF16),
            DMA((3,)),
            DMA((4,)),
            DMA((2,)),
        ]

    def term_copy(self, half, slot):
        place = self.place
        return remote(
            self.staged.at[half],
            self.received.at[slot],
            self.send.at[half],
            self.recv.at[slot],
            place.at(self.home, place.yc // 2 * 2 + half),
        )

    def relay_copy(self):
        return remote(
            self.staged,
            self.relayed,
            self.send.at[2],
            self.recv.at[3],
            self.place.at(self.far_middle),
        )

    def near_copies(self):
        place = self.place
        for half in range(2):
            here = jnp.logical_and(place.z == self.home, place.core == half)
            slot = lax.rem(place.z + self.home, 2)
            yield jnp.logical_and(self.near, jnp.logical_not(here)), self.term_copy(half, slot)

    def put(self, value):
        self.staged[...] = value.astype(BF16).reshape(self.staged.shape)

    def start(self):
        place = self.place

        @pl.when(place.z == self.far_end)
        def relay():
            self.relay_copy().start()

        for away, copy in self.near_copies():

            @pl.when(away)
            def start(copy=copy):
                copy.start()

    def relay(self):
        @pl.when(self.place.z == self.far_middle)
        def add():
            self.relay_copy().wait_recv()
            self.staged[...] = (
                self.staged[...].astype(F32) + self.relayed[...].astype(F32)
            ).astype(BF16)
            for half in range(2):
                self.term_copy(half, 2).start()

    def add(self):
        place = self.place
        at_home = jnp.logical_and(self.near, place.z == self.home)

        @pl.when(self.near)
        def reduce():
            @pl.when(at_home)
            def own():
                self.received[0] = self.staged[place.core]

            for slot in range(3):

                def arrive():
                    into = self.received.at[slot]
                    remote(
                        into, into, self.send.at[0], self.recv.at[slot], place.at(place.z)
                    ).wait_recv()

                if slot:
                    arrive()
                else:
                    pl.when(jnp.logical_not(at_home))(arrive)
            value = self.received[0].astype(F32)
            for slot in range(1, 3):
                value = value + self.received[slot].astype(F32)
            self.result[...] = value.astype(BF16)
            self.hand_over().start()

        for away, copy in self.near_copies():

            @pl.when(away)
            def drain(copy=copy):
                copy.wait_send()

        @pl.when(place.z == self.far_middle)
        def drain_sums():
            for half in range(2):
                self.term_copy(half, 2).wait_send()

        @pl.when(place.z == self.far_end)
        def drain_relay():
            self.relay_copy().wait_send()

    def hand_over(self):
        return remote(
            self.result, self.result, self.last.at[0], self.last.at[1], self.place.dev(4)
        )

    def wait(self):
        @pl.when(self.near)
        def sent():
            self.hand_over().wait_send()

        @pl.when(jnp.logical_not(self.near))
        def arrived():
            self.hand_over().wait_recv()


class Turn:
    def __init__(self, place, refs):
        self.place = place
        self.staged, self.received, self.send, self.recv = refs

    @staticmethod
    def scratch(rows):
        return [VMEM((PLANES, rows, 128), BF16), VMEM((PLANES, rows, 128), BF16), DMA((4,)), DMA((4,))]

    def copy(self, k):
        place = self.place
        return remote(
            self.staged.at[lax.rem(place.z + k, PLANES)],
            self.received.at[place.z],
            self.send.at[k],
            self.recv.at[k],
            place.zdev(k),
        )

    def start(self):
        for k in (2, 1, 3):
            self.copy(k).start()
        self.keep()

    def dispatch(self, pair):
        k = lax.rem(pair + PLANES - self.place.z, PLANES)

        @pl.when(k > 0)
        def start():
            self.copy(k).start()

        @pl.when(k == 0)
        def own():
            self.keep()

    def keep(self):
        self.received[self.place.z] = self.staged[self.place.z]

    def wait(self):
        for k in (1, 2, 3):
            into = self.received.at[lax.rem(self.place.z + 4 - k, PLANES)]
            remote(into, into, self.send.at[k], self.recv.at[k], self.place.zdev(k)).wait_recv()
        for k in (1, 2, 3):
            self.copy(k).wait_send()


def swap_halves(values):
    lane = lax.broadcasted_iota(jnp.int32, values.shape, 1)
    return jnp.where(lane % 64 < 32, pltpu.roll(values, 96, 1), pltpu.roll(values, 32, 1))


def head_part(values, head):
    return values[:, head * 64 : head * 64 + 64]


def pack_wide(turn, row, head, left, right):
    pair = row * 2 + head
    for block in range(4):
        turn.staged[pair, block * 128 : block * 128 + 128, :] = jnp.concatenate(
            [head_part(left[row * 4 + block], head), head_part(right[row * 4 + block], head)], axis=1
        )


def pack_narrow(turn, row, head, values):
    pair = row * 2 + head
    for block in range(2):
        turn.staged[pair, block * 128 : block * 128 + 128, :] = jnp.concatenate(
            [
                head_part(values[row * 4 + block], head),
                head_part(values[row * 4 + block + 2], head),
            ],
            axis=1,
        )


def unpack_narrow(turn, row, block):
    rows = slice((block % 2) * 128, (block % 2) * 128 + 128)
    return jnp.concatenate(
        [head_part(turn.received[row * 2 + head, rows, :], block // 2) for head in range(2)], axis=1
    )


def unpack_wide(turn, row, block, side):
    rows = slice(block * 128, block * 128 + 128)
    return jnp.concatenate(
        [head_part(turn.received[row * 2 + head, rows, :], side) for head in range(2)], axis=1
    )


QUERY_BLOCK = 256


def segment_ends(refs, row):
    lengths = refs.row_lengths[row]
    ends = [lengths[0:1, 0:1]]
    for index in range(1, 4):
        ends.append(ends[-1] + lengths[0:1, index : index + 1])
    return ends


def segment_features(refs, plane, row):
    frame = (plane * 512 + lax.broadcasted_iota(jnp.int32, (512, 64), 0)).astype(F32)
    lane = lax.broadcasted_iota(jnp.int32, (512, 64), 1).astype(F32)
    segment = jnp.zeros((512, 64), F32)
    for end in segment_ends(refs, row)[:3]:
        segment = segment + jnp.where(frame >= end, 1.0, 0.0)
    other = jnp.where(lane < 4.0, -MASKED, 0.0)
    return (
        jnp.where(lane == segment, 0.0, other).astype(BF16),
        jnp.where(lane == segment, -1.0, 0.0).astype(BF16),
    )


def segment_reach(place, refs, slot):
    row, block = slot // 4, slot % 4
    frame = place.z * 512 + block * 128 + lax.broadcasted_iota(jnp.int32, (128, 128), 0)
    frame = frame.astype(F32)
    ends = segment_ends(refs, row)
    first, last = jnp.zeros((128, 128), F32), ends[3]
    for end in ends[:3]:
        first = jnp.where(frame >= end, end, first)
    for end in ends[2::-1]:
        last = jnp.where(frame < end, end, last)
    return first - frame, last - frame


def open_heads(place, refs, turn_qk, turn_v):
    for plane in range(PLANES):
        seg_query, seg_key = segment_features(refs, plane, place.z // 2)
        rows = slice(plane * 512, plane * 512 + 512)
        pair = turn_qk.received[plane]
        scaled = (pair[:, :64].astype(F32) * HEAD_DIM ** (-0.5)).astype(BF16)
        refs.queries[rows, :] = jnp.concatenate([scaled, seg_query], axis=1)
        refs.keys[rows, :] = jnp.concatenate([pair[:, 64:], seg_key], axis=1)
        both = turn_v.received[plane]
        turned = jnp.transpose(both.astype(F32)).astype(BF16)
        refs.values[plane * 512 : plane * 512 + 256, :] = both[:, :64]
        refs.values[plane * 512 + 256 : plane * 512 + 512, :] = both[:, 64:]
        refs.values_t[:, plane * 512 : plane * 512 + 256] = turned[:64]
        refs.values_t[:, plane * 512 + 256 : plane * 512 + 512] = turned[64:]


def attend(place, refs, turn_mix):
    def plane_step(step, unused):
        k = lax.rem(step + 1, PLANES)
        plane = lax.rem(place.z + k, PLANES)
        parts = []
        for half in range(2):
            first = plane * 512 + half * 256
            query = refs.queries[pl.ds(pl.multiple_of(first, 256), QUERY_BLOCK), :]
            scores = dot(refs.keys[...], query, 1, 1)
            top = jnp.max(scores, axis=0, keepdims=True)
            weights = jnp.exp(scores - top)
            total = jnp.sum(weights, axis=0, keepdims=True)
            low = (weights * (1.0 / total)).astype(BF16)
            parts.append(jnp.transpose(dot(refs.values_t[...], low)))
            refs.log_total[plane * 2 + half] = jnp.broadcast_to(top + jnp.log(total), (8, 256))
        turn_mix.staged[plane] = jnp.concatenate(parts, axis=1).astype(BF16)

        @pl.when(step < PLANES - 1)
        def send():
            turn_mix.copy(k).start()

        return unused

    lax.fori_loop(0, PLANES, plane_step, 0)


def attention_forward(place, refs, gather, scatter):
    def process(pair, slots, part):
        if part == 0 and pair[0] == 0:
            refs.finish_qkv()
        value = dot(place.parts.take(gather.blocks, slots, part), flat(refs.w_qkv))

        def frames_of(slot, part):
            count = place.parts.rows
            first = lax.rem(slot, 4) * 128 + part * count
            return pl.ds(pl.multiple_of(first, count), count)

        def table(ref):
            return jnp.concatenate(
                [
                    ref[frames_of(slot, part), :]
                    for slot in slots
                ],
                axis=0,
            )

        cos, sin = table(refs.cos), table(refs.sin)
        query, key = value[:, :128], value[:, 128:256]
        place.parts.put(refs.q_rows, slots, part, (query * cos + swap_halves(query) * sin).astype(BF16))
        place.parts.put(refs.k_rows, slots, part, (key * cos + swap_halves(key) * sin).astype(BF16))
        place.parts.put(refs.v_rows, slots, part, value[:, 256:].astype(BF16))
        if part == place.parts.count - 1 and pair in LAST_OF_ROW:
            row = place.row(LAST_OF_ROW[pair])
            for head in range(2):
                pack_wide(turn_qk, row, head, refs.q_rows, refs.k_rows)
                turn_qk.dispatch(row * 2 + head)
            for head in range(2):
                pack_narrow(turn_v, row, head, refs.v_rows)
                turn_v.dispatch(row * 2 + head)

    turn_qk, turn_v = Turn(place, refs.turn_qk), Turn(place, refs.turn_v)
    gather_blocks(place, gather, process)
    gather.drain()
    turn_qk.wait()
    turn_v.wait()
    refs.after_turn()
    open_heads(place, refs, turn_qk, turn_v)
    turn_mix = Turn(place, refs.turn_mix)
    attend(place, refs, turn_mix)
    turn_mix.keep()
    turn_mix.wait()
    refs.after_mix()
    for slot in range(8):
        refs.mixed[slot] = unpack_narrow(turn_mix, slot // 4, slot % 4)
    scatter_blocks(
        place, scatter, lambda slots, part: place.parts.take(refs.mixed, slots, part), refs.w_o
    )


def attention_kept():
    return dict(
        attn_blocks=((8, 128, 1024), BF16),
        w_qkv=((16, 64, 384), BF16),
        w_o=((2, 64, 1024), BF16),
        queries=((2048, 128), BF16),
        keys=((2048, 128), BF16),
        values=((2048, 64), BF16),
        log_total=((8, 8, 256), F32),
        mixed=((8, 128, 128), BF16),
    )


def attend_back(place, refs, turn_kv, turn_q):
    refs.key_grad[...] = jnp.zeros_like(refs.key_grad)
    refs.value_grad[...] = jnp.zeros_like(refs.value_grad)

    def plane_step(step, unused):
        k = lax.rem(step + 1, PLANES)
        plane = lax.rem(place.z + k, PLANES)
        parts = []
        for half in range(2):
            first = pl.multiple_of(plane * 512 + half * 256, 256)
            query = refs.queries[pl.ds(first, QUERY_BLOCK), :]
            grad = refs.mix_grads[pl.ds(first, QUERY_BLOCK), :]
            log_total = refs.log_total[plane * 2 + half][:1]
            probs = jnp.exp(dot(refs.keys[...], query, 1, 1) - log_total)
            prob_grads = dot(refs.values[...], grad, 1, 1)
            delta = jnp.sum(probs * prob_grads, axis=0, keepdims=True)
            low = (probs * (prob_grads - delta)).astype(BF16)
            refs.key_grad[...] += dot(low, query[:, :64])
            refs.value_grad[...] += dot(probs.astype(BF16), grad)
            parts.append(jnp.transpose(dot(refs.keys_t[...], low)) * HEAD_DIM ** (-0.5))
        turn_q.staged[plane] = jnp.concatenate(parts, axis=1).astype(BF16)

        @pl.when(step < PLANES - 1)
        def send():
            turn_q.copy(k).start()

        return unused

    lax.fori_loop(0, PLANES, plane_step, 0)
    turn_q.keep()
    for plane in range(PLANES):
        rows = slice(plane * 512, plane * 512 + 512)
        turn_kv.staged[plane] = jnp.concatenate(
            [refs.key_grad[rows, :], refs.value_grad[rows, :]], axis=1
        ).astype(BF16)


def attention_backward(place, refs, gather, scatter):
    def process(pair, slots, part):
        if part == 0 and pair[0] == 0:
            refs.finish_attn()
        rows = dot(place.parts.take(gather.blocks, slots, part), flat(refs.w_o), 1, 1)
        place.parts.put(refs.mix_rows, slots, part, rows.astype(BF16))
        if part == place.parts.count - 1 and pair in LAST_OF_ROW:
            row = place.row(LAST_OF_ROW[pair])
            for head in range(2):
                pack_narrow(turn_mix, row, head, refs.mix_rows)
                turn_mix.dispatch(row * 2 + head)

    turn_mix = Turn(place, refs.turn_mix)
    gather_blocks(place, gather, process)
    gather.drain()
    weights = WeightGrads(place, refs, "qkv", "qkv", False)
    weights.put_out(refs.mixed, gather.blocks)
    turned = jnp.transpose(refs.keys[...].astype(F32))
    refs.keys_t[...] = turned[:64].astype(BF16)
    refs.before_mix()
    turn_mix.wait()
    for plane in range(PLANES):
        both = turn_mix.received[plane]
        refs.mix_grads[plane * 512 : plane * 512 + 256, :] = both[:, :64]
        refs.mix_grads[plane * 512 + 256 : plane * 512 + 512, :] = both[:, 64:]
    weights.sum_out.start()
    refs.before_attend()
    turn_kv, turn_q = Turn(place, refs.turn_qk), Turn(place, refs.turn_v)
    attend_back(place, refs, turn_kv, turn_q)
    turn_kv.start()
    weights.sum_out.relay()
    refs.after_attend()
    turn_q.wait()
    turn_kv.wait()
    for slot in range(8):
        row, block = divmod(slot, 4)
        cos = refs.cos[block * 128 : block * 128 + 128, :]
        sin = refs.sin[block * 128 : block * 128 + 128, :]
        query = unpack_narrow(turn_q, row, block).astype(F32)
        key = unpack_wide(turn_kv, row, block, 0).astype(F32)
        refs.qkv_grads[slot] = jnp.concatenate(
            [
                (query * cos - swap_halves(query) * sin).astype(BF16),
                (key * cos - swap_halves(key) * sin).astype(BF16),
                unpack_wide(turn_kv, row, block, 1),
            ],
            axis=1,
        )
    scatter_blocks(
        place, scatter, lambda slots, part: place.parts.take(refs.qkv_grads, slots, part), refs.w_qkv, 1
    )
    return weights


def fill_tables(refs):
    cos, sin = refs.cos_rows[...], refs.sin_rows[...]
    refs.cos[...] = jnp.concatenate([cos] * 4, axis=1)
    refs.sin[...] = jnp.concatenate([-sin, sin] * 2, axis=1)


def fill_channels(place, refs):
    columns = columns_of(place.pair(), 128)
    refs.taps[0:KERNEL, :] = refs.all_taps[:, columns].astype(F32)
    refs.gain_inner[...] = refs.all_inner[:, columns]
    for slot in range(8):
        refs.before[slot], refs.after[slot] = segment_reach(place, refs, slot)


def table_scratch():
    return dict(
        cos=VMEM((512, 128), F32),
        sin=VMEM((512, 128), F32),
        taps=VMEM((32, 128), F32),
        gain_inner=VMEM((1, 128), F32),
        before=VMEM((8, 128, 128), F32),
        after=VMEM((8, 128, 128), F32),
    )


class Edges:
    def __init__(self, place, refs):
        self.place = place
        self.staged, self.received, self.send, self.recv = refs

    @staticmethod
    def scratch():
        return [VMEM((2, 2, 16, 128), BF16), VMEM((2, 2, 16, 128), BF16), DMA((2,)), DMA((2,))]

    def copies(self):
        place = self.place
        for side, inside, step in ((0, place.z < PLANES - 1, 1), (1, place.z > 0, -1)):
            plane = jnp.clip(place.z + step, 0, PLANES - 1)
            yield (
                side,
                inside,
                remote(
                    self.staged.at[side],
                    self.received.at[side],
                    self.send.at[side],
                    self.recv.at[side],
                    {"seq": plane * 4 + place.yc, "row": place.x},
                ),
            )

    def start(self, blocks):
        for row in range(2):
            self.staged[0, row] = blocks[row * 4 + 3, 112:128, :]
            self.staged[1, row] = blocks[row * 4, 0:16, :]
        for side, inside, copy in self.copies():

            @pl.when(inside)
            def start(copy=copy):
                copy.start()

    def wait(self, blocks, padded):
        for slot in range(8):
            row, block = divmod(slot, 4)
            padded[slot, 16:144, :] = blocks[slot].astype(F32)
            if block > 0:
                padded[slot, 0:16, :] = blocks[slot - 1, 112:128, :].astype(F32)
            if block < 3:
                padded[slot, 144:160, :] = blocks[slot + 1, 0:16, :].astype(F32)
        place = self.place
        for side, outside in ((0, place.z == 0), (1, place.z == PLANES - 1)):
            first, rows = ((0, slice(0, 16)), (3, slice(144, 160)))[side]
            into = self.received.at[side]

            @pl.when(outside)
            def nothing():
                for row in range(2):
                    padded[row * 4 + first, rows, :] = jnp.zeros((16, 128), F32)

            @pl.when(jnp.logical_not(outside))
            def arrive():
                remote(
                    into, into, self.send.at[side], self.recv.at[side], place.zdev(1)
                ).wait_recv()
                for row in range(2):
                    padded[row * 4 + first, rows, :] = self.received[side, row].astype(F32)

        for side, inside, copy in self.copies():

            @pl.when(inside)
            def drain(copy=copy):
                copy.wait_send()


def lane_is(index, rows=128):
    return lax.broadcasted_iota(jnp.int32, (rows, 128), 1) == index


def put_columns(tile, slot, first, second):
    return jnp.where(lane_is(slot), first, jnp.where(lane_is(slot + 8), second, tile))


def share_columns(place, refs, tile):
    share = Exchange(place, refs[0], refs[1:])
    own = place.slot(0)
    share.blocks[own] = jnp.transpose(tile)[:16]
    share.start(lambda k: share.blocks.at[own])
    return share


def back_to_columns(first, second):
    rows = jnp.concatenate([first, second, jnp.zeros((112, 128), F32)], axis=0)
    return jnp.transpose(rows)


def column(tile, slot):
    return jnp.sum(jnp.where(lane_is(slot, tile.shape[0]), tile, 0.0), axis=1, keepdims=True)


def kept_frames(value, offset, before, after):
    if offset < 0:
        return jnp.where(before <= offset, value, 0.0)
    if offset > 0:
        return jnp.where(after > offset, value, 0.0)
    return value


CHUNK = 64


def convolve(refs):
    taps = [refs.taps[j : j + 1, :] for j in range(KERNEL)]

    def step(slot, tile):
        for first in range(0, 128, CHUNK):
            rows = slice(first, first + CHUNK)
            before, after = refs.before[slot, rows, :], refs.after[slot, rows, :]
            total = jnp.zeros((CHUNK, 128), F32)
            for j in range(KERNEL):
                start = first + j + 1
                value = refs.glu_padded[slot, start : start + CHUNK, :]
                total = total + taps[j] * kept_frames(value, j - HALF, before, after)
            refs.conv[slot, rows, :] = total
        value = refs.conv[slot]
        mean = jnp.mean(value, axis=1, keepdims=True)
        center = value - mean
        return put_columns(tile, slot, mean, jnp.sum(center * center, axis=1, keepdims=True))

    return lax.fori_loop(0, 8, step, jnp.zeros((128, 128), F32))


def inner_norm(refs, slot, rows=slice(0, 128)):
    tile = refs.inner_stats[rows, :]
    mean, inverse = column(tile, slot), column(tile, slot + 8)
    return (refs.conv[slot, rows, :] - mean) * inverse, inverse


def conv_forward(place, refs, gather, scatter):
    def process(pair, slots, part):
        if part == 0 and pair[0] == 0:
            refs.finish_ci()
        value = dot(place.parts.take(gather.blocks, slots, part), flat(refs.w_ci))
        place.parts.put(refs.gate_up, slots, part, value)
        place.parts.put(
            refs.glu,
            slots,
            part,
            (value[:, :128] * jax.nn.sigmoid(value[:, 128:])).astype(BF16),
        )

    gather_blocks(place, gather, process)
    edges = Edges(place, refs.edges)
    edges.start(refs.glu)
    gather.drain()
    edges.wait(refs.glu, refs.glu_padded)
    share = share_columns(place, refs.stats, convolve(refs))
    refs.conv_middle()
    share.wait()
    stats = share.blocks[...]
    means, spreads = stats[:, :8], stats[:, 8:]
    mean = jnp.mean(means, axis=0)
    spread = jnp.sum(spreads + 128.0 * jnp.square(means - mean[None]), axis=0) / 1024.0
    refs.inner_stats[...] = back_to_columns(mean, lax.rsqrt(spread + EPSILON))
    refs.finish_co()

    def active_rows(slots, part):
        rows = place.parts.of(part)
        parts = []
        for slot in slots:
            unit_part, unused = inner_norm(refs, slot, rows)
            parts.append(sigmoid_linear(unit_part * refs.gain_inner[...]).astype(BF16))
        value = jnp.concatenate(parts, axis=0)
        place.parts.put(refs.conv_active, slots, part, value)
        return value

    scatter_blocks(place, scatter, active_rows, refs.w_co)


def conv_kept():
    return dict(
        conv_blocks=((8, 128, 1024), BF16),
        w_ci=((16, 64, 256), BF16),
        w_co=((2, 64, 1024), BF16),
        gate_up=((8, 128, 256), F32),
        glu_padded=((8, 160, 128), F32),
        conv=((8, 128, 128), F32),
        inner_stats=((128, 128), F32),
        conv_active=((8, 128, 128), BF16),
    )


STATS = [VMEM((8, 16, 128), F32), DMA((8,)), DMA((8,))]


def convolve_back(refs):
    taps = [refs.taps[j : j + 1, :] for j in range(KERNEL)]
    refs.tap_sums[...] = jnp.zeros_like(refs.tap_sums)

    def step(slot, unused):
        for first in range(0, 128, CHUNK):
            rows = slice(first, first + CHUNK)
            before, after = refs.before[slot, rows, :], refs.after[slot, rows, :]
            total = jnp.zeros((CHUNK, 128), F32)
            grad = refs.conv_grad_padded[slot, first + 16 : first + 16 + CHUNK, :]
            for j in range(KERNEL):
                offset = j - HALF
                start = first + 16 - offset
                value = refs.conv_grad_padded[slot, start : start + CHUNK, :]
                total = total + taps[j] * kept_frames(value, -offset, before, after)
                start = first + 16 + offset
                value = refs.glu_padded[slot, start : start + CHUNK, :]
                product = kept_frames(value * grad, offset, before, after)
                refs.tap_sums[j] += jnp.sum(product.reshape(CHUNK // 8, 8, 128), axis=0)
            refs.glu_grad[slot, rows, :] = total
        return unused

    lax.fori_loop(0, 8, step, 0)
    return jnp.sum(refs.tap_sums[...], axis=1)


def conv_backward(place, refs, gather, scatter):
    gain = refs.gain_inner[...]

    def process(pair, slots, part):
        if part == 0 and pair[0] == 0:
            refs.finish_conv()
        back = dot(place.parts.take(gather.blocks, slots, part), flat(refs.w_co), 1, 1)
        rows = place.parts.of(part)
        units = jnp.concatenate([inner_norm(refs, slot, rows)[0] for slot in slots], axis=0)
        place.parts.put(refs.inner_grad, slots, part, back * sigmoid_linear_grad(units * gain))

    gather_blocks(place, gather, process)

    def sums(slot, current):
        tile, gain_grad = current
        value = refs.inner_grad[slot]
        unit_part, unused = inner_norm(refs, slot)
        scaled = value * gain
        tile = put_columns(
            tile,
            slot,
            jnp.sum(scaled, axis=1, keepdims=True),
            jnp.sum(scaled * unit_part, axis=1, keepdims=True),
        )
        return tile, gain_grad + jnp.sum(value * unit_part, axis=0, keepdims=True)

    tile, inner_gain_grad = lax.fori_loop(
        0, 8, sums, (jnp.zeros((128, 128), F32), jnp.zeros((1, 128), F32))
    )
    share = share_columns(place, refs.stats, tile)
    weights = WeightGrads(place, refs, "conv", "conv", False)
    weights.put_out(refs.conv_active, gather.blocks)
    gather.drain()
    share.wait()
    means = jnp.sum(share.blocks[...], axis=0) / 1024.0
    refs.grad_stats[...] = back_to_columns(means[:8], means[8:])

    def input_grad(slot, unused):
        unit_part, inverse = inner_norm(refs, slot)
        tile = refs.grad_stats[...]
        refs.conv_grad[slot] = (
            inverse
            * (
                refs.inner_grad[slot] * gain
                - column(tile, slot)
                - unit_part * column(tile, slot + 8)
            )
        ).astype(BF16)
        return unused

    lax.fori_loop(0, 8, input_grad, 0)
    edges = Edges(place, refs.edges)
    edges.start(refs.conv_grad)
    refs.conv_begin()
    edges.wait(refs.conv_grad, refs.conv_grad_padded)
    weights.sum_out.start()
    tap_grads = convolve_back(refs)
    refs.conv_middle()

    def gate_rows(slots, part):
        value, glu_grad = place.parts.take(refs.gate_up, slots, part), place.parts.take(refs.glu_grad, slots, part)
        sigma = jax.nn.sigmoid(value[:, 128:])
        low = jnp.concatenate(
            [glu_grad * sigma, glu_grad * value[:, :128] * sigma * (1.0 - sigma)], axis=1
        ).astype(BF16)
        place.parts.put(refs.gate_grads, slots, part, low)
        return low

    scatter_blocks(place, scatter, gate_rows, refs.w_ci, 1)
    return inner_gain_grad, tap_grads, weights


class Traffic:
    def __init__(self, refs, sems):
        self.refs, self.sems = refs, sems
        self.count = 0

    def start(self, pairs):
        copies = []
        for source, target in pairs:
            copy = pltpu.make_async_copy(source, target, self.sems.at[self.count])
            copy.start()
            copies.append(copy)
            self.count += 1

        def finish():
            for copy in copies:
                copy.wait()

        return finish

    def save(self, names):
        return self.start(
            [(getattr(self.refs, name), getattr(self.refs, "keep_" + name)) for name in names]
        )

    def load(self, names):
        return self.start(
            [(getattr(self.refs, "keep_" + name), getattr(self.refs, name)) for name in names]
        )


def ffn_kept():
    return dict(
        blocks=((8, 128, 1024), BF16),
        hidden=((8, 128, 512), F32),
        w_in=((16, 64, 512), BF16),
        w_out=((4, 128, 1024), BF16),
    )


SCATTER_SEMS = [DMA((22,)), DMA((22,))]


def forward_body(refs):
    place = Place(FORWARD_PARTS)
    place.enter()
    traffic = Traffic(refs, refs.traffic)
    gather_in = GatherRows(place, refs.w_in_rows, refs.w_in, refs.gather_in, ffn_pieces)
    refs.row_lengths[place.x] = refs.own_lengths[...]
    lengths = remote(
        refs.own_lengths,
        refs.row_lengths.at[place.x],
        refs.length_sems.at[0],
        refs.length_sems.at[1],
        place.dev(4),
    )
    lengths.start()
    halves = (slice(0, 512), slice(512, 1024))
    gather_out = [
        GatherBlocks(place, refs.w_out_rows, refs.w_out, refs.gather_out, halves[0])
    ]
    gather = Gather(place, refs.blocks, refs.ffn_ag)
    for part in place.parts:
        frames = place.parts.of(part)
        gather.push(part, norm_rows(refs.stream[frames, :].astype(F32), refs.gain_ffn1[...])[0])
    gather_in.along_z()
    gather_out.append(
        GatherBlocks(place, refs.w_out_rows, refs.w_out, refs.gather_out_last, halves[1])
    )
    gather_qkv = GatherRows(place, refs.qkv_rows, refs.w_qkv, refs.gather_qkv, head_pieces)
    held = Refs()
    gather_out[0].relay()
    gather_blocks(place, gather, lambda pair, slots, part: None)
    gather_in.relay()
    lengths.wait()
    fill_tables(refs)
    fill_channels(place, refs)
    gather_in.finish()
    for part in place.parts:
        for group in PAIRS:
            for pair in group:
                slots = [place.slot(k) for k in pair]
                value = dot(place.parts.take(refs.blocks, slots, part), flat(refs.w_in))
                place.parts.put(refs.hidden, slots, part, value)
                place.parts.put(refs.active, slots, part, sigmoid_linear(value).astype(BF16))
    gather.drain()
    scatter = Scatter(place, refs.scatter_columns, refs.ffn_scatter)
    for half, columns in enumerate(halves):
        if half:
            gather_out[half].relay()
        gather_out[half].finish()
        if half:
            gather_qkv.along_z()
            gather_o = GatherHalf(place, refs.o_rows, refs.w_o, refs.gather_o)
        weight = refs.w_out[:, :, columns].reshape(512, 512)
        for pair in OUT_PAIRS:
            rows = jnp.concatenate([refs.active[place.slot(k)] for k in pair], axis=0)
            scatter.emit_pair(pair, half, dot(rows, weight))
        for k in (6, 2, 4, 0):
            scatter.finish(k, half)
    saved = [traffic.save(ffn_kept())]
    gather_ci = GatherRows(place, refs.ci_rows, refs.w_ci, refs.gather_ci, channel_pieces)
    gather_next = GatherRows(place, refs.next_in_rows, refs.next_in, refs.gather_next, ffn_pieces)

    def to_attention(part, total):
        frames = place.parts.of(part)
        value = refs.stream[frames, :].astype(F32) + 0.5 * total
        refs.stream_one[frames, :] = value
        return norm_rows(value, refs.gain_attn[...])[0]

    def to_conv(part, total):
        frames = place.parts.of(part)
        value = refs.stream_one[frames, :] + total
        refs.stream_two[frames, :] = value
        return norm_rows(value, refs.gain_conv[...])[0]

    gather = Gather(place, refs.attn_blocks, refs.attn_ag)
    total = jnp.concatenate([scatter.total(half) for half in range(2)], axis=1)
    for part in place.parts:
        gather.push(part, to_attention(part, total[place.parts.of(part)]))
    scatter.drain()
    gather_qkv.relay()
    gather_o.relay()

    def after_turn():
        gather_ci.along_z()
        held.co = GatherHalf(place, refs.co_rows, refs.w_co, refs.gather_co)

    def after_mix():
        gather_ci.relay()
        held.co.relay()
        gather_o.finish()
        gather_next.along_z()
        held.next_out = GatherBlocks(
            place, refs.next_out_rows, refs.next_out, refs.gather_next_out
        )

    def conv_middle():
        gather_next.relay()

    refs.after_turn, refs.after_mix, refs.conv_middle = after_turn, after_mix, conv_middle
    refs.finish_qkv, refs.finish_ci, refs.finish_co = (
        gather_qkv.finish,
        gather_ci.finish,
        lambda: held.co.finish(),
    )
    scatter = Scatter(place, refs.scatter, refs.attn_scatter)
    attention_forward(place, refs, gather, scatter)
    saved.append(traffic.save(attention_kept()))
    gather = Gather(place, refs.conv_blocks, refs.conv_ag)
    carry(place, scatter, gather, to_conv)
    scatter = Scatter(place, refs.scatter, refs.conv_scatter)
    conv_forward(place, refs, gather, scatter)
    held.next_out.relay()
    saved.append(traffic.save(conv_kept()))
    for part in place.parts:
        frames = place.parts.of(part)
        refs.stream_three[frames, :] = refs.stream_two[frames, :] + scatter.total(part)
    scatter.drain()
    gather_next.finish()
    held.next_out.finish()
    for finish in saved:
        finish()


def scratch_of(kept):
    return {name: VMEM(shape, dtype) for name, (shape, dtype) in kept.items()}


def forward_call(ins):
    kept = {**ffn_kept(), **attention_kept(), **conv_kept()}
    outs = dict(
        stream_one=((128, 1024), F32, VMEM),
        stream_two=((128, 1024), F32, VMEM),
        stream_three=((128, 1024), F32, VMEM),
        next_in=((16, 64, 512), BF16, pl.ANY),
        next_out=((4, 128, 1024), BF16, pl.ANY),
    )
    outs["row_lengths"] = ((2, 8, 128), F32, VMEM)
    for name, (shape, dtype) in kept.items():
        outs["keep_" + name] = (shape, dtype, pl.ANY)
    scratch = dict(
        scratch_of(kept),
        active=VMEM((8, 128, 512), BF16),
        gather_in=GatherRows.scratch(),
        gather_out=GatherBlocks.scratch(),
        gather_out_last=GatherBlocks.scratch(),
        gather_qkv=GatherRows.scratch(),
        gather_o=GatherHalf.scratch(),
        gather_ci=GatherRows.scratch(),
        gather_co=GatherHalf.scratch(),
        gather_next=GatherRows.scratch(),
        gather_next_out=GatherBlocks.scratch(),
        length_sems=DMA((2,)),
        **table_scratch(),
        traffic=DMA((len(kept),)),
        scatter=Scatter.scratch(FORWARD_PARTS, 128 // FORWARD_PARTS, 1024),
        scatter_columns=Scatter.scratch(2, 128, 512),
        ffn_ag=AG_SEMS,
        attn_ag=AG_SEMS,
        conv_ag=AG_SEMS,
        ffn_scatter=SCATTER_SEMS,
        attn_scatter=SCATTER_SEMS,
        conv_scatter=SCATTER_SEMS,
        q_rows=VMEM((8, 128, 128), BF16),
        k_rows=VMEM((8, 128, 128), BF16),
        v_rows=VMEM((8, 128, 128), BF16),
        turn_qk=Turn.scratch(512),
        turn_v=Turn.scratch(256),
        turn_mix=Turn.scratch(256),
        values_t=VMEM((64, 2048), BF16),
        glu=VMEM((8, 128, 128), BF16),
        edges=Edges.scratch(),
        stats=STATS,
    )
    return kernel_call(forward_body, 1, ins, outs, scratch)


class SmallSum:
    def __init__(self, place, refs):
        self.place, self.refs = place, refs
        self.first = Exchange(place, refs.small_first, refs.small_first_sems)
        self.last = Exchange(place, refs.small, refs.small_last_sems)
        self.sent = []

    def start(self):
        refs, place = self.refs, self.place

        def part(slot):
            return refs.gain_grads.at[:, columns_of(slot, 128)]

        self.first.blocks[place.slot(0)] = refs.gain_grads[:, columns_of(place.slot(0), 128)]
        self.first.start(lambda k: part(place.slot(k)))

    def along_z(self):
        refs, place = self.refs, self.place
        self.first.wait()
        refs.small_planes[place.z, 0:8, :] = jnp.sum(self.first.blocks[...], axis=0)
        refs.small_planes[place.z, 8:48, :] = refs.channel_grads[...]
        send, recv = refs.small_z_sems
        rows = refs.small_planes.at[place.z]
        for k in (1, 2, 3):
            copy = remote(rows, rows, send.at[k], recv.at[k], place.zdev(k))
            copy.start()
            self.sent.append(copy)

    def spread(self):
        refs, place = self.refs, self.place
        send, recv = refs.small_z_sems
        for k in (1, 2, 3):
            into = refs.small_planes.at[lax.rem(place.z + 4 - k, PLANES)]
            remote(into, into, send.at[k], recv.at[k], place.zdev(k)).wait_recv()
        for copy in self.sent:
            copy.wait_send()
        own = place.slot(0)
        self.last.blocks[own] = jnp.sum(refs.small_planes[...], axis=0)
        self.last.start(lambda k: self.last.blocks.at[own])

    def wait(self):
        self.last.wait()


def backward_step(place, refs, stream, gain, row, scale):
    saved = [
        norm_forward(stream[place.parts.of(part), :].astype(F32), gain)[1] for part in place.parts
    ]

    def step(part, total):
        frames = place.parts.of(part)
        input_part, gain_grad = norm_input_grad(total, gain, saved[part])
        value = refs.grad_stream[frames, :] + input_part
        refs.grad_stream[frames, :] = value
        refs.gain_grads[row : row + 1, :] += gain_grad
        return (scale * value).astype(BF16)

    return step


def backward_body(refs):
    place = Place(BACKWARD_PARTS)
    place.enter()
    traffic = Traffic(refs, refs.traffic)
    ready = traffic.start([(refs.next_in, refs.w_in), (refs.next_out, refs.w_out)])
    gather = Gather(place, refs.blocks, refs.ffn2_ag)
    for part in place.parts:
        frames = place.parts.of(part)
        gather.push(part, norm_rows(refs.stream_three[frames, :], refs.gain_ffn2[...])[0])
    refs.finish_conv = traffic.load(conv_kept())
    refs.finish_attn = traffic.load(attention_kept())
    refs.gain_grads[...] = jnp.zeros_like(refs.gain_grads)
    refs.channel_grads[...] = jnp.zeros_like(refs.channel_grads)
    scatter = Scatter(place, refs.scatter, refs.ffn2_scatter)
    ffn_forward(place, gather, refs.hidden, refs.w_in, refs.w_out, scatter, ready)
    gather.drain()
    fill_tables(refs)
    fill_channels(place, refs)

    def turn_round(part, total):
        frames = place.parts.of(part)
        final, saved = norm_forward(refs.stream_three[frames, :] + 0.5 * total, refs.gain_out[...])
        refs.output[frames, :] = final.astype(BF16)
        grad, gain_grad = norm_input_grad(
            refs.cotangent[frames, :].astype(F32), refs.gain_out[...], saved
        )
        refs.grad_stream[frames, :] = grad
        refs.gain_grads[4:5, :] += gain_grad
        return (0.5 * grad).astype(BF16)

    gather = Gather(place, refs.grads_even, refs.ffn2_ag_back)
    carry(place, scatter, gather, turn_round)
    scatter = Scatter(place, refs.scatter, refs.ffn2_scatter_back)
    ffn_backward(
        place,
        gather,
        refs.hidden,
        refs.hidden_grads,
        refs.active,
        refs.w_in,
        refs.w_out,
        scatter,
        lambda: None,
    )
    gather.drain()
    step = backward_step(place, refs, refs.stream_three, refs.gain_ffn2[...], 3, 1.0)
    weights_two = WeightGrads(place, refs, "ffn2", "ffn", True)
    weights_two.put_both(refs.active, refs.grads_even, refs.blocks, refs.hidden_grads)
    gather = Gather(place, refs.grads_odd, refs.conv_ag)
    carry(place, scatter, gather, step)
    load_first = traffic.load(ffn_kept())
    refs.conv_begin, refs.conv_middle = weights_two.sum_out.relay, weights_two.sum_in.relay
    scatter = Scatter(place, refs.scatter, refs.conv_scatter)
    inner, taps, weights_three = conv_backward(place, refs, gather, scatter)
    step = backward_step(place, refs, refs.stream_two, refs.gain_conv[...], 2, 1.0)
    refs.channel_grads[0:32, :] = taps
    refs.channel_grads[32:33, :] = inner
    weights_three.put_in(refs.conv_blocks, refs.gate_grads)
    gather = Gather(place, refs.grads_even, refs.attn_ag)
    carry(place, scatter, gather, step)

    refs.before_mix = weights_two.share
    refs.before_attend, refs.after_attend = weights_three.relay, weights_three.share
    scatter = Scatter(place, refs.scatter, refs.attn_scatter)
    weights_four = attention_backward(place, refs, gather, scatter)
    step = backward_step(place, refs, refs.stream_one, refs.gain_attn[...], 1, 0.5)
    weights_four.put_in(refs.attn_blocks, refs.qkv_grads)
    gather = Gather(place, refs.grads_odd, refs.ffn1_ag)
    carry(place, scatter, gather, step)
    weights_four.sum_in.relay()
    weights_two.wait()
    weights_three.wait()
    weights_one = WeightGrads(place, refs, "ffn1", "ffn", True)
    scatter = Scatter(place, refs.scatter, refs.ffn1_scatter)
    ffn_backward(
        place,
        gather,
        refs.hidden,
        refs.hidden_grads,
        refs.active,
        refs.w_in,
        refs.w_out,
        scatter,
        load_first,
        lambda: weights_one.put_both(
            refs.active, refs.grads_odd, refs.blocks, refs.hidden_grads
        ),
    )
    gather.drain()
    weights_one.sum_out.relay()
    weights_four.share()
    step = backward_step(place, refs, refs.stream, refs.gain_ffn1[...], 0, 1.0)
    for part in place.parts:
        step(part, scatter.total(part))
    scatter.drain()
    small = SmallSum(place, refs)
    small.start()
    weights_one.sum_in.relay()
    small.along_z()
    weights_one.share_rows()
    small.spread()
    weights_one.share_columns()
    weights_four.wait()
    small.wait()
    weights_one.wait()


MODULES = (("ffn1", 512, True), ("qkv", 384, False), ("conv", 256, False), ("ffn2", 512, True))


def backward_call(ins):
    kept = {**ffn_kept(), **attention_kept(), **conv_kept()}
    outs = dict(
        output=((128, 1024), BF16, VMEM),
        grad_stream=((128, 1024), F32, VMEM),
        small=((8, 48, 128), F32, VMEM),
    )
    scratch = dict(
        scratch_of(kept),
        active=VMEM((8, 128, 512), BF16),
        hidden_grads=VMEM((8, 128, 512), BF16),
        grads_even=VMEM((8, 128, 1024), BF16),
        grads_odd=VMEM((8, 128, 1024), BF16),
        traffic=DMA((2 + len(kept),)),
        scatter=Scatter.scratch(BACKWARD_PARTS, 128 // BACKWARD_PARTS, 1024),
        ffn2_ag=AG_SEMS,
        ffn2_ag_back=AG_SEMS,
        conv_ag=AG_SEMS,
        attn_ag=AG_SEMS,
        ffn1_ag=AG_SEMS,
        ffn2_scatter=SCATTER_SEMS,
        ffn2_scatter_back=SCATTER_SEMS,
        conv_scatter=SCATTER_SEMS,
        attn_scatter=SCATTER_SEMS,
        ffn1_scatter=SCATTER_SEMS,
        mix_rows=VMEM((8, 128, 128), BF16),
        mix_grads=VMEM((2048, 64), BF16),
        keys_t=VMEM((64, 2048), BF16),
        turn_qk=Turn.scratch(512),
        turn_v=Turn.scratch(256),
        turn_mix=Turn.scratch(256),
        key_grad=VMEM((2048, 64), F32),
        value_grad=VMEM((2048, 64), F32),
        qkv_grads=VMEM((8, 128, 384), BF16),
        **table_scratch(),
        inner_grad=VMEM((8, 128, 128), F32),
        grad_stats=VMEM((128, 128), F32),
        conv_grad=VMEM((8, 128, 128), BF16),
        conv_grad_padded=VMEM((8, 160, 128), F32),
        glu_grad=VMEM((8, 128, 128), F32),
        gate_grads=VMEM((8, 128, 256), BF16),
        tap_sums=VMEM((32, 8, 128), F32),
        edges=Edges.scratch(),
        stats=STATS,
        gain_grads=VMEM((8, 1024), F32),
        channel_grads=VMEM((40, 128), F32),
        small_first=VMEM((8, 8, 128), F32),
        small_planes=VMEM((PLANES, 48, 128), F32),
        small_first_sems=[DMA((8,)), DMA((8,))],
        small_z_sems=[DMA((4,)), DMA((4,))],
        small_last_sems=[DMA((8,)), DMA((8,))],
        **WeightGrads.sums("ffn", 512, True),
        **WeightGrads.sums("qkv", 384, False),
        **WeightGrads.sums("conv", 256, False),
    )
    for name, width, wide in MODULES:
        outs.update(WeightGrads.outs(name, width, wide))
        scratch.update(WeightGrads.scratch(name, width, wide))
    return kernel_call(backward_body, 2, ins, outs, scratch)


def unpack_body(count, *refs):
    sources, outs = refs[:count], refs[count : 2 * count + 8]
    (
        output,
        grad_stream,
        small,
        ffn1_in,
        ffn1_out,
        qkv_in,
        qkv_out,
        conv_in,
        conv_out,
        ffn2_in,
        ffn2_out,
    ) = sources
    outs[0][...] = output[...]
    outs[1][...] = grad_stream[...]
    for slot in range(8):
        x, yc = divmod(slot, 4)
        pair = ((x * 2 + yc % 2) * 2 + yc // 2) * 128
        for index, row in enumerate((0, 1, 2, None, 3, 4)):
            if row is not None:
                outs[2 + index][:, slot * 128 : slot * 128 + 128] = small[slot, row : row + 1, :]
        outs[5][:, pair : pair + 128] = small[slot, 40:41, :]
        outs[8][:, pair : pair + 128] = small[slot, 8 : 8 + KERNEL, :]
        for source, out in ((ffn1_in, outs[9]), (ffn2_in, outs[15])):
            for plane in range(PLANES):
                column = ((plane * 4 + yc) * 2 + x) * 128
                out[:, column : column + 128] = source[
                    slot, :, plane * 128 : plane * 128 + 128
                ].astype(F32)
        for source, out, kinds in ((qkv_in, outs[11], 3), (conv_in, outs[13], 2)):
            for kind in range(kinds):
                column = kind * 1024 + pair
                out[:, column : column + 128] = source[slot, :, kind * 128 : kind * 128 + 128].astype(
                    F32
                )
    for source, out in ((ffn1_out, outs[10]), (ffn2_out, outs[16])):
        out[0:128, :] = source[0].astype(F32)
        out[128:256, :] = source[1].astype(F32)
    outs[12][...] = qkv_out[...].astype(F32)
    outs[14][...] = conv_out[...].astype(F32)


def unpack_call(backward):
    arrays = list(backward.values())
    gain = jax.ShapeDtypeStruct((1, 1024), F32)
    shapes = [
        jax.ShapeDtypeStruct((128, 1024), BF16),
        jax.ShapeDtypeStruct((128, 1024), F32),
        *[gain] * 6,
        jax.ShapeDtypeStruct((KERNEL, 1024), F32),
    ] + [
        jax.ShapeDtypeStruct(shape, F32)
        for shape in (
            (64, 4096),
            (256, 1024),
            (64, 3072),
            (64, 1024),
            (64, 2048),
            (64, 1024),
            (64, 4096),
            (256, 1024),
        )
    ]
    whole = pl.BlockSpec(memory_space=VMEM)
    return pl.pallas_call(
        functools.partial(unpack_body, len(arrays)),
        out_shape=shapes,
        in_specs=[whole] * len(arrays),
        out_specs=[whole] * len(shapes),
        compiler_params=pltpu.CompilerParams(vmem_limit_bytes=VMEM_LIMIT),
    )(*arrays)


def local_planes(
    inputs,
    lengths,
    gain_ffn1,
    gain_attn,
    gain_conv,
    gain_inner,
    gain_ffn2,
    gain_out,
    conv_kernel,
    ffn1_in,
    ffn1_out,
    attn_qkv,
    attn_out,
    conv_in,
    conv_out,
    ffn2_in,
    ffn2_out,
    cotangent,
):
    plane = lax.axis_index("seq") // 4
    cos, sin = rotary_tables(plane * 512 + jnp.arange(512, dtype=jnp.int32))
    shared = dict(
        stream=(inputs[0], VMEM),
        gain_ffn1=(gain_ffn1[None], VMEM),
        gain_attn=(gain_attn[None], VMEM),
        gain_conv=(gain_conv[None], VMEM),
        all_inner=(gain_inner[None], VMEM),
        all_taps=(conv_kernel, VMEM),
        cos_rows=(cos, VMEM),
        sin_rows=(sin, VMEM),
    )
    forward = forward_call(
        dict(
            shared,
            own_lengths=(jnp.pad(lengths.astype(F32), ((0, 7), (0, 124))), VMEM),
            w_in_rows=(ffn1_in, pl.ANY),
            w_out_rows=(ffn1_out, pl.ANY),
            qkv_rows=(attn_qkv, pl.ANY),
            o_rows=(attn_out, pl.ANY),
            ci_rows=(conv_in, pl.ANY),
            co_rows=(conv_out, pl.ANY),
            next_in_rows=(ffn2_in, pl.ANY),
            next_out_rows=(ffn2_out, pl.ANY),
        )
    )
    ins = dict(
        shared,
        cotangent=(cotangent[0], VMEM),
        gain_ffn2=(gain_ffn2[None], VMEM),
        gain_out=(gain_out[None], VMEM),
    )
    for name, array in forward.items():
        held = name.startswith("stream") or name == "row_lengths"
        ins[name] = (array, VMEM if held else pl.ANY)
    results = unpack_call(backward_call(ins))
    return (
        results[0][None],
        results[1][None],
        *[gain[0] for gain in results[2:8]],
        *results[8:],
    )


def solution(mesh):
    return jax.shard_map(
        local_planes if mesh.shape["seq"] == 16 and mesh.shape["row"] == 2 else local,
        mesh=mesh,
        in_specs=(
            P("row", "seq", None),
            P("row", None),
            P(),
            P(),
            P(),
            P(),
            P(),
            P(),
            P(),
            P("seq", None),
            P("seq", None),
            P("seq", None),
            P("seq", None),
            P("seq", None),
            P("seq", None),
            P("seq", None),
            P("seq", None),
            P("row", "seq", None),
        ),
        out_specs=(
            P("row", "seq", None),
            P("row", "seq", None),
            P(),
            P(),
            P(),
            P(),
            P(),
            P(),
            P(),
            P("seq", None),
            P("seq", None),
            P("seq", None),
            P("seq", None),
            P("seq", None),
            P("seq", None),
            P("seq", None),
            P("seq", None),
        ),
        check_vma=False,
    )
```
